32 devices in a mesh: wide: 8 (over y, x, core), narrow: 4 (over z).
Axes of the slice: x: 2, y: 2, z: 4, core: 2. Of those that a mesh axis runs over, the one named last changes fastest.
Arguments:
- piece_table: bfloat16 [32768, 512], P(('wide', 'narrow')), may hold values from -6 to 6
- piece_ids: int32 [4096, 7], P(('wide', 'narrow')), may hold values from 0 to 32767, as said below
- slot_mask: int32 [4096, 7], P(('wide', 'narrow')), may hold values from 0 to 1, as said below
- text_ids: int32 [8, 1024], replicated, may hold values from 0 to 4095
- text_mask: int32 [8, 1024], replicated, may hold values 0 or 1
- text_cot: bfloat16 [4096, 8192], P(('wide', 'narrow'))
- mat_master: float32 [4, 2560, 512], P('narrow')
- mat_momentum: float32 [4, 2560, 512], P('narrow')
- mat_ema: float32 [4, 2560, 512], P('narrow')
- vec_master: float32 [14336], replicated
- vec_moment1: float32 [14336], replicated
- vec_moment2: float32 [14336], replicated, as said below
- vec_ema: float32 [14336], replicated
Outputs:
- text_embeds: float32 [4096, 8192], P(('wide', 'narrow'))
- piece_grad: float32 [32768, 512], P(('wide', 'narrow'))
- mat_grad: float32 [4, 2560, 512], P('narrow')
- mat_momentum_new: float32 [4, 2560, 512], P('narrow')
- mat_weight: float32 [4, 2560, 512], P('narrow')
- mat_ema_new: float32 [4, 2560, 512], P('narrow')
- vec_grad: float32 [14336], replicated
- vec_moment1_new: float32 [14336], replicated
- vec_moment2_new: float32 [14336], replicated
- vec_weight: float32 [14336], replicated
- vec_ema_new: float32 [14336], replicated
The draws below stay inside these ranges and needn't reach their ends.
Inputs may be any that keep to these rules, and one draw needn't show every extreme that they name: `slot_mask`: the live piece slots of an entry are its first n slots, n from 1 to 7; the first entry of every block of 128 entries has all 7. `piece_ids`: call pieces j * 1024 to (j + 1) * 1024 - 1 group j. Of the 896 piece slots of each aligned block of 128 entries, at most 58 name pieces of any one group, and exactly 58 name pieces of some group. `vec_moment2`: every entry is positive.
All inputs are finite; a program needn't handle non-finite values.
Results may differ from the reference program's by a relative error of at most 0.0095.
Values may be sent and summed in bfloat16 or wider, within the bound.
A program may use at most 256 MiB of HBM per device.

```python
import math
import jax
import jax.numpy as jnp
import numpy as np
from jax import lax

D = 512
HEADS = 8
HDIM = 64
FF = 2048
OUTW = 4096
PIECES = 32768
SLOTS = 8
PSLOTS = 7
TEXT_LEN = 1024
STEP = 10
ENT_DEV = 128
TEXT_ROWS = 8
ENTRIES = 4096
RB = 2560
VLEN = 14336
PCAP = 58
N_NARROW = 4
DEVICES = 32


def narrow_blocks():
    return (4 * D + 2 * FF + OUTW) // RB


def row_scales(block_count, scale_list):
    segments = []
    for row_total, value_scale in zip((3 * D, D, FF, FF, OUTW), scale_list):
        segments.append(jnp.full((row_total // block_count,), value_scale, jnp.float32))
    return jnp.concatenate(segments)


def weight_values(key, block_count):
    scales = row_scales(block_count, (D ** (-0.5), 2.0 * D ** (-0.5), D ** (-0.5), FF ** (-0.5), D ** (-0.5)))
    base_values = jax.random.truncated_normal(key, -4.0, 4.0, (block_count, RB, D), jnp.float32)
    return base_values * scales[None, :, None]


def vector_values(key):
    keys_list = jax.random.split(key, 11)
    parts_list = [jax.random.truncated_normal(keys_list[0], -4.0, 4.0, (D,), jnp.float32), jax.random.truncated_normal(keys_list[1], -4.0, 4.0, (SLOTS * D,), jnp.float32)]
    for number in range(3):
        gain_noise = jax.random.truncated_normal(keys_list[2 + 2 * number], -3.0, 3.0, (D,), jnp.float32)
        parts_list.append(1.0 + 0.2 * gain_noise)
        parts_list.append(0.1 * jax.random.truncated_normal(keys_list[3 + 2 * number], -4.0, 4.0, (D,), jnp.float32))
    parts_list.append(0.1 * jax.random.truncated_normal(keys_list[8], -4.0, 4.0, (FF,), jnp.float32))
    parts_list.append(0.1 * jax.random.truncated_normal(keys_list[9], -4.0, 4.0, (D,), jnp.float32))
    parts_list.append(0.1 * jax.random.truncated_normal(keys_list[10], -4.0, 4.0, (OUTW,), jnp.float32))
    return jnp.concatenate(parts_list)


def vector_scale():
    return math.sqrt(TEXT_ROWS * TEXT_LEN * OUTW / D) / 2.0


def draw_piece_ids(key, part):
    key = jax.random.fold_in(key, 21)
    block_count = ENTRIES // ENT_DEV
    block_slots = ENT_DEV * PSLOTS
    group_rows = PIECES // DEVICES
    pool_size = (DEVICES - 1) * PCAP

    def one_block(block_key):
        key_a, key_b, key_c, key_d = jax.random.split(block_key, 4)
        heavy = jax.random.randint(key_a, (), 0, DEVICES)
        others = jax.random.permutation(key_b, pool_size)[:block_slots - PCAP] // PCAP
        others = others + (others >= heavy).astype(jnp.int32)
        owners = jnp.concatenate([jnp.full((PCAP,), heavy, jnp.int32), others.astype(jnp.int32)])
        owners = owners[jax.random.permutation(key_c, block_slots)]
        offsets = jax.random.randint(key_d, (block_slots,), 0, group_rows)
        return owners * group_rows + offsets
    chosen = jax.vmap(one_block)(jax.random.split(key, block_count))
    return chosen.reshape(ENTRIES, PSLOTS).astype(jnp.int32)


def draw_slot_mask(key, part):
    key = jax.random.fold_in(key, 17)
    counts = jax.random.randint(key, (ENTRIES,), 1, PSLOTS + 1)
    leading = jnp.arange(ENTRIES) % ENT_DEV == 0
    counts = jnp.where(leading, PSLOTS, counts)
    return (jnp.arange(PSLOTS)[None, :] < counts[:, None]).astype(jnp.int32)


def draw_text_cot(key, part):
    key = jax.random.fold_in(key, 14)
    key_a, key_b = jax.random.split(key, 2)
    tokens_all = TEXT_ROWS * TEXT_LEN
    feature_pos = jnp.arange(OUTW, dtype=jnp.float32) / max(OUTW - 1, 1)
    rise_factor = 3.0 ** feature_pos
    base_values = jax.random.truncated_normal(key_a, -4.0, 4.0, (OUTW, tokens_all), jnp.float32)
    row_factor = jnp.exp(jax.random.uniform(key_b, (OUTW,), jnp.float32, 0.0, math.log(3.2)))
    return (0.5 * base_values * (rise_factor * row_factor)[:, None]).astype(jnp.bfloat16)


def draw_mat_master(key, part):
    key = jax.random.fold_in(key, 11)
    return weight_values(key, narrow_blocks())


def draw_mat_ema(key, part):
    key = jax.random.fold_in(key, 12)
    return weight_values(key, narrow_blocks())


def draw_mat_momentum(key, part):
    key = jax.random.fold_in(key, 13)
    key_a, key_b, key_c = jax.random.split(key, 3)
    block_count = narrow_blocks()
    block_pos = jnp.arange(block_count, dtype=jnp.float32) / max(block_count - 1, 1)
    block_scale = 3.0 ** block_pos
    base_values = jax.random.truncated_normal(key_a, -4.0, 4.0, (block_count, RB, D), jnp.float32)
    row_factor = jnp.exp(jax.random.uniform(key_b, (block_count, RB), jnp.float32, 0.0, math.log(3.2)))
    col_factor = jnp.exp(jax.random.uniform(key_c, (D,), jnp.float32, 0.0, math.log(3.2)))
    magnitude = math.sqrt(TEXT_ROWS * TEXT_LEN) / 4.0
    return magnitude * base_values * block_scale[:, None, None] * row_factor[:, :, None] * col_factor[None, None, :]


def draw_vec_master(key, part):
    key = jax.random.fold_in(key, 15)
    return vector_values(key)


def draw_vec_ema(key, part):
    key = jax.random.fold_in(key, 16)
    return vector_values(key)


def draw_vec_moment1(key, part):
    key = jax.random.fold_in(key, 18)
    base_values = jax.random.truncated_normal(key, -4.0, 4.0, (VLEN,), jnp.float32)
    return base_values * (vector_scale() / 9.0)


def draw_vec_moment2(key, part):
    key = jax.random.fold_in(key, 19)
    center = 2.0 * (0.05 / 0.95) * vector_scale() * vector_scale()
    exponent = jax.random.uniform(key, (VLEN,), jnp.float32, math.log(0.5), math.log(2.0))
    return center * jnp.exp(exponent)


def place_ends(entries, rng, smallest, largest):
    longest = entries.shape.index(max(entries.shape))
    spots = []
    for shift in (0, 1):
        where = [jax.random.randint(jax.random.fold_in(rng, axis), (), 0, length) for axis, length in enumerate(entries.shape)]
        where[longest] = (where[longest] + shift) % entries.shape[longest]
        spots.append(tuple(where))
    return entries.at[spots[0]].set(smallest).at[spots[1]].set(largest)


def shard_levels(own_key, shape, shards, least, top_value):
    loudness = 1.0
    for position, parts in shards:
        draws = jax.random.uniform(jax.random.fold_in(jax.random.fold_in(own_key, 6), position), (parts,), jnp.float32, least / len(shards), top_value / len(shards))
        loudness = loudness * jnp.repeat(jnp.exp(draws), shape[position] // parts).reshape((-1,) + (1,) * (len(shape) - 1 - position))
    return loudness


def cumulative_ranks(amount, lean):
    portions = [(1 << 20) // math.isqrt(standing ** lean) + 1 for standing in range(1, amount + 1)]
    scale = 1 + sum(portions) // (1 << 30)
    return np.cumsum(np.array([max(1, weight // scale) for weight in portions]))


def ranked_ids(stream_key, dims, amount, lean):
    grid = cumulative_ranks(amount, lean)
    ticket = jax.random.randint(jax.random.fold_in(stream_key, 1), dims, 0, int(grid[amount - 1]))
    rank = jnp.searchsorted(jnp.asarray(grid, jnp.int32), ticket, side="right")
    return jax.random.permutation(jax.random.fold_in(stream_key, 2), amount)[rank].astype(jnp.int32)


def gaussian(own_key, shape, scale, most, cuts=(), kind=jnp.bfloat16):
    drawn = scale * jax.random.normal(own_key, shape, jnp.float32)
    if cuts:
        drawn = drawn * shard_levels(own_key, shape, cuts, -0.22, 0.18)
    return jnp.clip(drawn, -most, most).astype(kind)


def setup_inputs(seed: int = 0) -> dict:
    splits = jax.random.split(jax.random.key(seed), 14)
    return {
        "piece_table": gaussian(splits[0], (PIECES, D), 1.0, 6.0, ((0, 32),)),
        "piece_ids": draw_piece_ids(jax.random.fold_in(splits[13], 71), 0),
        "slot_mask": draw_slot_mask(jax.random.fold_in(splits[13], 71), 0),
        "text_ids": place_ends(ranked_ids(splits[3], (TEXT_ROWS, TEXT_LEN), ENTRIES, 2), jax.random.fold_in(splits[3], 3), 0, ENTRIES - 1).astype(jnp.int32),
        "text_mask": place_ends((jax.random.randint(splits[4], (TEXT_ROWS, TEXT_LEN), 0, 8) < 7).astype(jnp.int32), jax.random.fold_in(splits[4], 1), 0, 1),
        "text_cot": draw_text_cot(jax.random.fold_in(splits[13], 71), 0),
        "mat_master": draw_mat_master(jax.random.fold_in(splits[13], 71), 0),
        "mat_momentum": draw_mat_momentum(jax.random.fold_in(splits[13], 71), 0),
        "mat_ema": draw_mat_ema(jax.random.fold_in(splits[13], 71), 0),
        "vec_master": draw_vec_master(jax.random.fold_in(splits[13], 71), 0),
        "vec_moment1": draw_vec_moment1(jax.random.fold_in(splits[13], 71), 0),
        "vec_moment2": draw_vec_moment2(jax.random.fold_in(splits[13], 71), 0),
        "vec_ema": draw_vec_ema(jax.random.fold_in(splits[13], 71), 0),
    }


@jax.custom_vjp
def low(v):
    return lax.optimization_barrier(v.astype(jnp.bfloat16)).astype(jnp.float32)

@jax.custom_vjp
def low_back(v):
    return v

def low_keep(v):
    return (low(v), None)

def low_pass(kept, grad):
    return (grad,)

def back_keep(v):
    return (v, None)

def back_low(kept, grad):
    return (low(grad),)
low.defvjp(low_keep, low_pass)
low_back.defvjp(back_keep, back_low)
HIGHEST = lax.Precision.HIGHEST
MUON_RATE = 0.5
MUON_DECAY = 0.01
MUON_BETA = 0.95
ADAM_RATE = 0.5
ADAM_BETA1 = 0.9
ADAM_BETA2 = 0.95
ADAM_EPSILON = 1e-08
EMA_DECAY = 0.8
NEWTON_A = 3.4445
NEWTON_B = -4.775
NEWTON_C = 2.0315

def matrix_rows():
    return (3 * D, D, FF, FF, OUTW)

def unpack(packed):
    matrices = []
    offset = 0
    for row_total in matrix_rows():
        height = row_total // N_NARROW
        matrices.append(packed[:, offset:offset + height, :].reshape(row_total, D))
        offset = offset + height
    return matrices

def pack(matrices):
    return jnp.concatenate([matrix.reshape(N_NARROW, matrix.shape[0] // N_NARROW, D) for matrix in matrices], axis=1)

def split_vectors(vector):
    lengths = (D, SLOTS * D, D, D, D, D, D, D, FF, D, OUTW)
    chosen = []
    offset = 0
    for length in lengths:
        chosen.append(vector[offset:offset + length])
        offset = offset + length
    chosen[1] = chosen[1].reshape(SLOTS, D)
    return chosen

def layer_norm(values, gain, shift):
    center = values - lax.optimization_barrier(jnp.mean(values, axis=-1, keepdims=True))
    spread = lax.optimization_barrier(jnp.mean(center * center, axis=-1, keepdims=True))
    return center * lax.rsqrt(spread + 1e-05) * gain + shift

def gelu_tanh(values):
    return jax.nn.gelu(values, approximate=True)

def attend(query_rows, key_rows, value_rows, live_slots):
    entry_count = query_rows.shape[0]
    query_heads = query_rows.reshape(entry_count, HEADS, HDIM)
    key_heads = key_rows.reshape(entry_count, SLOTS, HEADS, HDIM)
    value_heads = value_rows.reshape(entry_count, SLOTS, HEADS, HDIM)
    scores = jnp.einsum('ehd,eshd->ehs', query_heads, key_heads, precision=HIGHEST) / math.sqrt(HDIM)
    scores = jnp.where(live_slots[:, None, :], scores, -1e+30)
    scores = scores - lax.optimization_barrier(jnp.max(scores, axis=-1, keepdims=True))
    expped = jnp.exp(scores)
    probabilities = expped / lax.optimization_barrier(jnp.sum(expped, axis=-1, keepdims=True))
    mixed_heads = jnp.einsum('ehs,eshd->ehd', probabilities, value_heads, precision=HIGHEST)
    return mixed_heads.reshape(entry_count, D)

def hyper_layer(table_in, mats_in, vector_in, piece_ids, slot_mask):
    w_qkv, w_out, w_up, w_down, w_proj = unpack(low(mats_in))
    cls_vec, positions, ln1_gain, ln1_shift, ln2_gain, ln2_shift, final_gain, final_shift, bias_up, bias_down, bias_out = split_vectors(vector_in)
    entry_count = piece_ids.shape[0]
    pieces = low_back(jnp.take(table_in, piece_ids, axis=0))
    first_slot = jnp.broadcast_to(cls_vec + positions[0], (entry_count, 1, D))
    slots_x = jnp.concatenate([first_slot, pieces + positions[1:]], axis=1)
    live_slots = jnp.concatenate([jnp.ones((entry_count, 1), jnp.int32), slot_mask], axis=1) > 0
    normed = low(layer_norm(slots_x, ln1_gain, ln1_shift))
    query_rows = low_back(jnp.dot(normed[:, 0], w_qkv[:D].T, precision=HIGHEST))
    key_rows = low_back(jnp.einsum('esd,fd->esf', normed, w_qkv[D:2 * D], precision=HIGHEST))
    value_rows = low_back(jnp.einsum('esd,fd->esf', normed, w_qkv[2 * D:], precision=HIGHEST))
    attended = low(attend(query_rows, key_rows, value_rows, live_slots))
    residual = slots_x[:, 0] + low_back(jnp.dot(attended, w_out.T, precision=HIGHEST))
    normed_two = low(layer_norm(residual, ln2_gain, ln2_shift))
    gate_in = low_back(jnp.dot(normed_two, w_up.T, precision=HIGHEST) + bias_up)
    active = low(gelu_tanh(gate_in))
    second_residual = residual + low_back(jnp.dot(active, w_down, precision=HIGHEST) + bias_down)
    normed_three = low(layer_norm(second_residual, final_gain, final_shift))
    output_rows = jnp.dot(normed_three, w_proj.T, precision=HIGHEST) + bias_out
    return low_back(output_rows)

def text_lookup(table_out, text_ids, text_mask):
    flat_ids = text_ids.reshape(-1)
    keep_mask = text_mask.reshape(-1).astype(jnp.float32)
    return (jnp.take(table_out, flat_ids, axis=0) * keep_mask[:, None]).T

def reference(piece_table, piece_ids, slot_mask, text_ids, text_mask, text_cot, mat_master, mat_momentum, mat_ema, vec_master, vec_moment1, vec_moment2, vec_ema):
    table_float = piece_table.astype(jnp.float32)

    def whole_pass(table_in, mats_in, vector_in):
        return text_lookup(hyper_layer(table_in, mats_in, vector_in, piece_ids, slot_mask), text_ids, text_mask)
    text_out, pullback = jax.vjp(whole_pass, table_float, mat_master, vec_master)
    piece_grad, mat_grad, vec_grad = pullback(text_cot.astype(jnp.float32))
    new_moments = []
    new_weights = []
    for row_total, gradient, momentum, master in zip(matrix_rows(), unpack(mat_grad), unpack(mat_momentum), unpack(mat_master)):
        momentum_new = MUON_BETA * momentum + gradient
        update = gradient + MUON_BETA * momentum_new
        ortho_block = update / (jnp.sqrt(jnp.sum(update * update)) + 1e-07)
        for sweep_index in range(5):
            gram = jnp.dot(ortho_block.T, ortho_block, precision=HIGHEST)
            poly = NEWTON_B * gram + NEWTON_C * jnp.dot(gram, gram, precision=HIGHEST)
            ortho_block = NEWTON_A * ortho_block + jnp.dot(ortho_block, poly, precision=HIGHEST)
        new_moments.append(momentum_new)
        new_weights.append(master * (1.0 - MUON_RATE * MUON_DECAY) - MUON_RATE * math.sqrt(row_total / D) * ortho_block)
    mat_momentum_new = pack(new_moments)
    mat_weight = pack(new_weights)
    mat_ema_new = EMA_DECAY * mat_ema + (1.0 - EMA_DECAY) * mat_weight
    moment_one = ADAM_BETA1 * vec_moment1 + (1.0 - ADAM_BETA1) * vec_grad
    moment_two = ADAM_BETA2 * vec_moment2 + (1.0 - ADAM_BETA2) * vec_grad * vec_grad
    corrected_one = moment_one / (1.0 - ADAM_BETA1 ** STEP)
    corrected_two = moment_two / (1.0 - ADAM_BETA2 ** STEP)
    vec_weight = vec_master - ADAM_RATE * corrected_one / (jnp.sqrt(corrected_two) + ADAM_EPSILON)
    vec_ema_new = EMA_DECAY * vec_ema + (1.0 - EMA_DECAY) * vec_weight
    return (text_out, piece_grad, mat_grad, mat_momentum_new, mat_weight, mat_ema_new, vec_grad, moment_one, moment_two, vec_weight, vec_ema_new)
```

```python
from functools import partial
import math

import jax
import jax.numpy as jnp
from jax import lax
from jax.sharding import PartitionSpec as P

D = 512
HEADS = 8
HDIM = 64
FF = 2048
OUTW = 4096
SLOTS = 8
PSLOTS = 7
STEP = 10


HIGHEST = lax.Precision.HIGHEST
HIGH = lax.Precision.HIGH
MUON_RATE = 0.5
MUON_DECAY = 0.01
MUON_BETA = 0.95
ADAM_RATE = 0.5
ADAM_BETA1 = 0.9
ADAM_BETA2 = 0.95
ADAM_EPSILON = 1e-08
EMA_DECAY = 0.8
NEWTON_A = 3.4445
NEWTON_B = -4.775
NEWTON_C = 2.0315


def matrix_rows():
    return (3 * D, D, FF, FF, OUTW)


def unpack(packed, narrow_count):
    matrices = []
    offset = 0
    for row_total in matrix_rows():
        height = row_total // narrow_count
        matrices.append(packed[:, offset : offset + height, :].reshape(row_total, packed.shape[2]))
        offset = offset + height
    return matrices


def pack(matrices, narrow_count):
    return jnp.concatenate(
        [
            matrix.reshape(narrow_count, matrix.shape[0] // narrow_count, matrix.shape[1])
            for matrix in matrices
        ],
        axis=1,
    )


def block_slices(block, narrow_count):
    segments = []
    offset = 0
    for row_total in matrix_rows():
        height = row_total // narrow_count
        segments.append(block[offset : offset + height])
        offset = offset + height
    return segments


def split_vectors(vector):
    lengths = (D, SLOTS * D, D, D, D, D, D, D, FF, D, OUTW)
    chosen = []
    offset = 0
    for length in lengths:
        chosen.append(vector[offset : offset + length])
        offset = offset + length
    chosen[1] = chosen[1].reshape(SLOTS, D)
    return chosen


def layer_norm(values, gain, shift):
    center = values - jnp.mean(values, axis=-1, keepdims=True)
    spread = jnp.mean(center * center, axis=-1, keepdims=True)
    return center * lax.rsqrt(spread + 1e-05) * gain + shift


def gelu_tanh(values):
    return jax.nn.gelu(values, approximate=True)


def attend(query_rows, key_rows, value_rows, live_slots):
    entry_count = query_rows.shape[0]
    query_heads = query_rows.reshape(entry_count, HEADS, HDIM)
    key_heads = key_rows.reshape(entry_count, SLOTS, HEADS, HDIM)
    value_heads = value_rows.reshape(entry_count, SLOTS, HEADS, HDIM)
    scores = jnp.einsum("ehd,eshd->ehs", query_heads, key_heads, precision=HIGHEST) / math.sqrt(
        HDIM
    )
    scores = jnp.where(live_slots[:, None, :], scores, -1e30)
    scores = scores - jnp.max(scores, axis=-1, keepdims=True)
    expped = jnp.exp(scores)
    probabilities = expped / jnp.sum(expped, axis=-1, keepdims=True)
    mixed_heads = jnp.einsum("ehs,eshd->ehd", probabilities, value_heads, precision=HIGHEST)
    return mixed_heads.reshape(entry_count, D)


PIECE_CAPS = {1024: 58, 256: 16}
BOTH = ("wide", "narrow")


def piece_cap(group_rows):
    cap = PIECE_CAPS.get(group_rows, group_rows)
    return -(-cap // 16) * 16


def contract_rows(left, right):
    return lax.dot_general(
        left, right, (((0,), (0,)), ((), ())), preferred_element_type=jnp.float32
    )


def gram_of(block):
    return lax.dot_general(block, block, (((0,), (0,)), ((), ())), precision=HIGHEST)


def on_device(
    piece_table,
    piece_ids,
    slot_mask,
    text_ids,
    text_mask,
    text_cot,
    mat_master,
    mat_momentum,
    mat_ema,
    vec_master,
    vec_moment1,
    vec_moment2,
    vec_ema,
):
    narrow_count = lax.axis_size("narrow")
    wide_count = lax.axis_size("wide")
    device_count = narrow_count * wide_count
    wide_at = lax.axis_index("wide")
    narrow_at = lax.axis_index("narrow")
    me = wide_at * narrow_count + narrow_at
    block_rows = mat_master.shape[1]
    own_rows = block_rows // wide_count
    own_part = lax.dynamic_slice_in_dim(mat_master[0], wide_at * own_rows, own_rows, 0)
    packed_bf = lax.all_gather(
        own_part.astype(jnp.bfloat16), ("narrow", "wide"), axis=0, tiled=True
    ).reshape(narrow_count, block_rows, D)
    w_qkv, w_out, w_up, w_down, w_proj = unpack(packed_bf, narrow_count)
    (
        cls_vec,
        positions,
        ln1_gain,
        ln1_shift,
        ln2_gain,
        ln2_shift,
        final_gain,
        final_shift,
        bias_up,
        bias_down,
        bias_out,
    ) = split_vectors(vec_master)
    entries = piece_ids.shape[0]
    slot_ids = piece_ids.reshape(-1)
    slot_count = slot_ids.shape[0]
    group_rows = piece_table.shape[0]
    cap = piece_cap(group_rows)
    every_ids = lax.all_gather(slot_ids, BOTH, axis=0, tiled=False)
    asked = every_ids // group_rows == me
    before = (
        lax.broadcasted_iota(jnp.int32, (slot_count, slot_count), 0)
        < lax.broadcasted_iota(jnp.int32, (slot_count, slot_count), 1)
    )
    asked_rank = jnp.dot(
        asked.astype(jnp.bfloat16), before.astype(jnp.bfloat16), preferred_element_type=jnp.float32
    ).astype(jnp.int32)
    asked_rank = jnp.where(asked, asked_rank, -1)
    chosen = asked_rank[:, None, :] == lax.iota(jnp.int32, cap)[None, :, None]
    local_ids = every_ids - me * group_rows + 1
    asked_rows = jnp.sum(jnp.where(chosen, local_ids[:, None, :], 0), axis=2).reshape(-1) - 1
    asked_onehot = (
        asked_rows[:, None] == lax.iota(jnp.int32, group_rows)[None, :]
    ).astype(jnp.bfloat16)
    outgoing = jnp.dot(asked_onehot, piece_table, preferred_element_type=jnp.float32)
    incoming = lax.all_to_all(
        outgoing.astype(jnp.bfloat16).reshape(device_count, cap, D), BOTH, 0, 0, tiled=True
    ).reshape(device_count * cap, D)
    own_group = slot_ids // group_rows
    same = (own_group[:, None] == own_group[None, :]) & before.T
    own_rank = jnp.sum(same.astype(jnp.int32), axis=1)
    own_spot = own_group * cap + own_rank
    own_onehot = (
        own_spot[:, None] == lax.iota(jnp.int32, device_count * cap)[None, :]
    ).astype(jnp.bfloat16)
    looked = jnp.dot(own_onehot, incoming, preferred_element_type=jnp.float32)
    pieces = looked.reshape(entries, PSLOTS, D)

    flat_ids = text_ids.reshape(-1)
    flat_mask = text_mask.reshape(-1)
    token_count = flat_ids.shape[0]
    feature_rows = text_cot.shape[0]
    all_entries = entries * device_count
    block_len = min(512, token_count)
    entry_index = lax.iota(jnp.int32, all_entries)

    def text_block(step_index, grad_cols):
        begin_at = step_index * block_len
        ids_now = lax.dynamic_slice_in_dim(flat_ids, begin_at, block_len)
        keep_mask = lax.dynamic_slice_in_dim(flat_mask, begin_at, block_len)
        onehot = (entry_index[:, None] == ids_now[None, :]).astype(jnp.bfloat16)
        cot_now = lax.dynamic_slice_in_dim(text_cot, begin_at, block_len, 1)
        masked_cot = jnp.where(keep_mask[None, :] > 0, cot_now, jnp.zeros_like(cot_now))
        return grad_cols + lax.dot_general(
            masked_cot, onehot, (((1,), (1,)), ((), ())), preferred_element_type=jnp.float32
        )

    grad_cols = lax.fori_loop(
        0, token_count // block_len, text_block, jnp.zeros((feature_rows, all_entries), jnp.float32)
    )
    grad_table_cols = grad_cols.astype(jnp.bfloat16)
    grad_table = lax.all_to_all(grad_table_cols, BOTH, split_axis=1, concat_axis=0, tiled=True)
    grad_bias_own = jnp.sum(grad_table_cols.astype(jnp.float32), axis=1)
    grad_normed_three = contract_rows(grad_table, w_proj)

    first_slot = jnp.broadcast_to(cls_vec + positions[0], (entries, 1, D))
    slots_x = jnp.concatenate([first_slot, pieces + positions[1:]], axis=1)
    live_slots = jnp.concatenate([jnp.ones((entries, 1), jnp.int32), slot_mask], axis=1) > 0
    normed, norm1_pull = jax.vjp(layer_norm, slots_x, ln1_gain, ln1_shift)
    normed_bf = normed.astype(jnp.bfloat16)
    query_rows = jnp.einsum(
        "ed,fd->ef", normed_bf[:, 0], w_qkv[:D], preferred_element_type=jnp.float32
    )
    key_value = jnp.einsum("esd,fd->esf", normed_bf, w_qkv[D:], preferred_element_type=jnp.float32)
    attended, attend_pull = jax.vjp(
        partial(attend, live_slots=live_slots), query_rows, key_value[:, :, :D], key_value[:, :, D:]
    )
    attended_bf = attended.astype(jnp.bfloat16)
    residual = slots_x[:, 0] + jnp.einsum(
        "ed,fd->ef", attended_bf, w_out, preferred_element_type=jnp.float32
    )
    normed_two, norm2_pull = jax.vjp(layer_norm, residual, ln2_gain, ln2_shift)
    normed_two_bf = normed_two.astype(jnp.bfloat16)
    gate_in = (
        jnp.einsum("ed,fd->ef", normed_two_bf, w_up, preferred_element_type=jnp.float32) + bias_up
    )
    active, gelu_pull = jax.vjp(gelu_tanh, gate_in)
    active_bf = active.astype(jnp.bfloat16)
    second_residual = residual + (
        jnp.dot(active_bf, w_down, preferred_element_type=jnp.float32) + bias_down
    )
    normed_three, norm3_pull = jax.vjp(layer_norm, second_residual, final_gain, final_shift)
    normed_three_bf = normed_three.astype(jnp.bfloat16)
    every_normed = lax.all_gather(normed_three_bf, BOTH, axis=0, tiled=True)
    proj_own = lax.dynamic_slice_in_dim(w_proj, me * feature_rows, feature_rows, 0)
    bias_own = lax.dynamic_slice_in_dim(bias_out, me * feature_rows, feature_rows, 0)
    table_cols = (
        jnp.einsum("fd,ed->fe", proj_own, every_normed, preferred_element_type=jnp.float32)
        + bias_own[:, None]
    )
    text_embeds = jnp.take(table_cols, flat_ids, axis=1) * flat_mask[None, :].astype(jnp.float32)
    grad_proj_own = jnp.dot(grad_table_cols, every_normed, preferred_element_type=jnp.float32)

    grad_second, grad_final_gain, grad_final_shift = norm3_pull(grad_normed_three)
    grad_branch_two = grad_second.astype(jnp.bfloat16)
    grad_bias_down = jnp.sum(grad_branch_two.astype(jnp.float32), axis=0)
    grad_down = contract_rows(active_bf, grad_branch_two)
    grad_active = jnp.einsum(
        "ed,fd->ef", grad_branch_two, w_down, preferred_element_type=jnp.float32
    )
    (grad_gate,) = gelu_pull(grad_active)
    grad_gate_bf = grad_gate.astype(jnp.bfloat16)
    grad_bias_up = jnp.sum(grad_gate_bf.astype(jnp.float32), axis=0)
    grad_up = contract_rows(grad_gate_bf, normed_two_bf)
    grad_normed_two = jnp.dot(grad_gate_bf, w_up, preferred_element_type=jnp.float32)
    grad_residual_norm, grad_ln2_gain, grad_ln2_shift = norm2_pull(grad_normed_two)
    grad_residual = grad_second + grad_residual_norm
    grad_branch_one = grad_residual.astype(jnp.bfloat16)
    grad_out_w = contract_rows(grad_branch_one, attended_bf)
    grad_attended = jnp.dot(grad_branch_one, w_out, preferred_element_type=jnp.float32)
    grad_query, grad_keys, grad_values = attend_pull(grad_attended)
    grad_query_bf = grad_query.astype(jnp.bfloat16)
    grad_kv = jnp.concatenate(
        [grad_keys.astype(jnp.bfloat16), grad_values.astype(jnp.bfloat16)], axis=2
    )
    grad_q_w = contract_rows(grad_query_bf, normed_bf[:, 0])
    grad_kv_w = jnp.einsum("esf,esd->fd", grad_kv, normed_bf, preferred_element_type=jnp.float32)
    grad_normed = jnp.einsum("esf,fd->esd", grad_kv, w_qkv[D:], preferred_element_type=jnp.float32)
    grad_normed = grad_normed.at[:, 0].add(
        jnp.dot(grad_query_bf, w_qkv[:D], preferred_element_type=jnp.float32)
    )
    grad_slots, grad_ln1_gain, grad_ln1_shift = norm1_pull(grad_normed)
    grad_first = grad_slots[:, 0] + grad_residual
    grad_cls = jnp.sum(grad_first, axis=0)
    grad_pos = jnp.concatenate([grad_cls[None], jnp.sum(grad_slots[:, 1:], axis=0)], axis=0)
    grad_pieces = grad_slots[:, 1:].astype(jnp.bfloat16).reshape(-1, D)
    grad_outgoing = contract_rows(own_onehot, grad_pieces).astype(jnp.bfloat16)
    grad_incoming = lax.all_to_all(
        grad_outgoing.reshape(device_count, cap, D), BOTH, 0, 0, tiled=True
    ).reshape(device_count * cap, D)
    piece_grad = contract_rows(asked_onehot, grad_incoming)

    vec_local = jnp.concatenate(
        [
            grad_cls,
            grad_pos.reshape(-1),
            grad_ln1_gain,
            grad_ln1_shift,
            grad_ln2_gain,
            grad_ln2_shift,
            grad_final_gain,
            grad_final_shift,
            grad_bias_up,
            grad_bias_down,
            lax.dynamic_update_slice_in_dim(
                jnp.zeros((OUTW,), jnp.float32), grad_bias_own, me * feature_rows, 0
            ),
        ]
    )
    vec_grad = lax.psum(vec_local, BOTH)
    grad_qkv = jnp.concatenate([grad_q_w, grad_kv_w], axis=0)
    packed_term = jnp.concatenate(
        [
            matrix.reshape(narrow_count, matrix.shape[0] // narrow_count, D)
            for matrix in (grad_qkv, grad_out_w, grad_up, grad_down)
        ],
        axis=1,
    )
    term_rows = packed_term.shape[1]
    share = term_rows // wide_count
    packed_term = (
        packed_term.astype(jnp.bfloat16)
        .reshape(narrow_count, wide_count, share, D)
        .transpose(1, 0, 2, 3)
        .reshape(device_count, share, D)
    )
    terms = lax.all_to_all(packed_term, BOTH, 0, 0, tiled=True)
    share_sum = jnp.sum(terms.astype(jnp.float32), axis=0)
    main_grad = lax.all_gather(share_sum.astype(jnp.bfloat16), "wide", axis=0, tiled=True)
    proj_grad = lax.all_gather(grad_proj_own.astype(jnp.bfloat16), BOTH, axis=0, tiled=True)
    proj_rows = OUTW // narrow_count
    proj_grad = lax.dynamic_slice_in_dim(proj_grad, narrow_at * proj_rows, proj_rows, 0)
    grad_block = jnp.concatenate([main_grad, proj_grad], axis=0).astype(jnp.float32)
    momentum_block = MUON_BETA * mat_momentum[0] + grad_block
    update_block = grad_block + MUON_BETA * momentum_block
    segments = block_slices(update_block, narrow_count)
    grams = lax.psum(jnp.stack([gram_of(segment) for segment in segments]), "narrow")
    new_segments = []
    for position, (row_total, master_seg, segment) in enumerate(
        zip(matrix_rows(), block_slices(mat_master[0], narrow_count), segments)
    ):
        square = jnp.sum(jnp.diagonal(grams[position]))
        norm = jnp.sqrt(square) + 1e-07
        gram = grams[position] / (norm * norm)
        chain = None
        for sweep_index in range(5):
            squared = jnp.dot(gram, gram, precision=HIGH)
            poly = NEWTON_B * gram + NEWTON_C * squared + NEWTON_A * jnp.eye(D, dtype=jnp.float32)
            chain = poly if chain is None else jnp.dot(chain, poly, precision=HIGH)
            if sweep_index < 4:
                gram = jnp.dot(jnp.dot(gram, poly, precision=HIGH), poly, precision=HIGH)
        ortho = jnp.dot(segment / norm, chain, precision=HIGH)
        new_segments.append(
            master_seg * (1.0 - MUON_RATE * MUON_DECAY)
            - MUON_RATE * math.sqrt(row_total / D) * ortho
        )
    weight_block = jnp.concatenate(new_segments, axis=0)[None]
    ema_block = EMA_DECAY * mat_ema + (1.0 - EMA_DECAY) * weight_block
    moment_one = ADAM_BETA1 * vec_moment1 + (1.0 - ADAM_BETA1) * vec_grad
    moment_two = ADAM_BETA2 * vec_moment2 + (1.0 - ADAM_BETA2) * vec_grad * vec_grad
    corrected_one = moment_one / (1.0 - ADAM_BETA1**STEP)
    corrected_two = moment_two / (1.0 - ADAM_BETA2**STEP)
    vec_weight = vec_master - ADAM_RATE * corrected_one / (jnp.sqrt(corrected_two) + ADAM_EPSILON)
    vec_ema_new = EMA_DECAY * vec_ema + (1.0 - EMA_DECAY) * vec_weight
    return (
        text_embeds,
        piece_grad,
        grad_block[None],
        momentum_block[None],
        weight_block,
        ema_block,
        vec_grad,
        moment_one,
        moment_two,
        vec_weight,
        vec_ema_new,
    )


def solution(mesh):
    in_specs = (
        P(("wide", "narrow"), None),
        P(("wide", "narrow"), None),
        P(("wide", "narrow"), None),
        P(),
        P(),
        P(("wide", "narrow"), None),
        P("narrow", None, None),
        P("narrow", None, None),
        P("narrow", None, None),
        P(),
        P(),
        P(),
        P(),
    )
    out_specs = (
        P(("wide", "narrow"), None),
        P(("wide", "narrow"), None),
        P("narrow", None, None),
        P("narrow", None, None),
        P("narrow", None, None),
        P("narrow", None, None),
        P(),
        P(),
        P(),
        P(),
        P(),
    )
    return jax.shard_map(
        on_device, mesh=mesh, in_specs=in_specs, out_specs=out_specs, check_vma=False
    )
```

```python
from functools import partial
import math

import jax
import jax.numpy as jnp
from jax import lax
from jax.experimental import pallas as pl
from jax.experimental.pallas import tpu as pltpu
from jax.sharding import PartitionSpec as P

D = 512
HEADS = 8
HDIM = 64
FF = 2048
OUTW = 4096
SLOTS = 8
PSLOTS = 7
STEP = 10


HIGHEST = lax.Precision.HIGHEST
HIGH = lax.Precision.HIGH
MUON_RATE = 0.5
MUON_DECAY = 0.01
MUON_BETA = 0.95
ADAM_RATE = 0.5
ADAM_BETA1 = 0.9
ADAM_BETA2 = 0.95
ADAM_EPSILON = 1e-08
EMA_DECAY = 0.8
NEWTON_A = 3.4445
NEWTON_B = -4.775
NEWTON_C = 2.0315


def matrix_rows():
    return (3 * D, D, FF, FF, OUTW)


def block_slices(block, narrow_count):
    segments = []
    offset = 0
    for row_total in matrix_rows():
        height = row_total // narrow_count
        segments.append(block[offset : offset + height])
        offset = offset + height
    return segments


def split_vectors(vector):
    lengths = (D, SLOTS * D, D, D, D, D, D, D, FF, D, OUTW)
    chosen = []
    offset = 0
    for length in lengths:
        chosen.append(vector[offset : offset + length])
        offset = offset + length
    chosen[1] = chosen[1].reshape(SLOTS, D)
    return chosen


def layer_norm(values, gain, shift):
    center = values - jnp.mean(values, axis=-1, keepdims=True)
    spread = jnp.mean(center * center, axis=-1, keepdims=True)
    return center * lax.rsqrt(spread + 1e-05) * gain + shift


def gelu_tanh(values):
    return jax.nn.gelu(values, approximate=True)


def attend(query_rows, key_rows, value_rows, live_slots):
    entry_count = query_rows.shape[0]
    query_heads = query_rows.reshape(entry_count, HEADS, HDIM)
    key_heads = key_rows.reshape(entry_count, SLOTS, HEADS, HDIM)
    value_heads = value_rows.reshape(entry_count, SLOTS, HEADS, HDIM)
    scores = jnp.einsum("ehd,eshd->ehs", query_heads, key_heads, precision=HIGHEST) / math.sqrt(
        HDIM
    )
    scores = jnp.where(live_slots[:, None, :], scores, -1e30)
    scores = scores - jnp.max(scores, axis=-1, keepdims=True)
    expped = jnp.exp(scores)
    probabilities = expped / jnp.sum(expped, axis=-1, keepdims=True)
    mixed_heads = jnp.einsum("ehs,eshd->ehd", probabilities, value_heads, precision=HIGHEST)
    return mixed_heads.reshape(entry_count, D)


PIECE_CAPS = {1024: 58, 256: 16}
BOTH = ("wide", "narrow")


def piece_cap(group_rows):
    cap = PIECE_CAPS.get(group_rows, group_rows)
    return -(-cap // 16) * 16


def contract_rows(left, right):
    return lax.dot_general(
        left, right, (((0,), (0,)), ((), ())), preferred_element_type=jnp.float32
    )


def gram_of(block):
    return lax.dot_general(block, block, (((0,), (0,)), ((), ())), precision=HIGHEST)


MESH_ID = pl.DeviceIdType.MESH
CORES = 2
CHIPS = 4
PLANES = 4
MAIN = 192
CHUNKS = 4
CHUNK = MAIN // CHUNKS
PROJ = 32
PART = MAIN + PLANES * PROJ
VROWS = 16


def place():
    wide_at = lax.axis_index("wide")
    plane = lax.axis_index("narrow")
    chip = wide_at // CORES
    core = lax.rem(wide_at, CORES)
    return wide_at, plane, chip, core


def enter(targets):
    barrier = pltpu.get_barrier_semaphore()
    for target in targets:
        pl.semaphore_signal(barrier, inc=1, device_id=target, device_id_type=MESH_ID)
    pl.semaphore_wait(barrier, len(targets))


def neighbours(wide_at, plane, chip, core):
    sibling = (chip * CORES + 1 - core, plane)
    chips = [(lax.rem(chip + k, CHIPS) * CORES + core, plane) for k in range(1, CHIPS)]
    planes = [(wide_at, lax.rem(plane + k, PLANES)) for k in range(1, PLANES)]
    return sibling, chips, planes


def remote(src, dst, sems, index, target):
    return pltpu.make_async_remote_copy(
        src_ref=src,
        dst_ref=dst,
        send_sem=sems[0].at[index],
        recv_sem=sems[1].at[index],
        device_id=target,
        device_id_type=MESH_ID,
    )


def reduce_kernel(
    main_ref,
    proj_ref,
    vec_ref,
    out_ref,
    vec_out_ref,
    near,
    first,
    far,
    second,
    deep,
    proj_far,
    part,
    vec_near,
    vec_far,
    vec_deep,
    load_sem,
    main_send,
    main_recv,
    far_send,
    far_recv,
    deep_send,
    deep_recv,
    done_send,
    done_recv,
    pass_send,
    pass_recv,
    proj_send,
    proj_recv,
    vec_send,
    vec_recv,
):
    wide_at, plane, chip, core = place()
    sibling, chips, planes = neighbours(wide_at, plane, chip, core)
    other = 1 - core
    own_main = pltpu.make_async_copy(main_ref.at[core], first, load_sem.at[0])
    own_main.start()
    enter([sibling] + chips + planes)

    vec_sems = (vec_send, vec_recv)
    vec_copies = [remote(vec_ref.at[other], vec_near, vec_sems, 0, sibling)]
    vec_copies[0].start()
    main_sems = (main_send, main_recv)
    near_copies = []
    for chunk in range(CHUNKS):
        copy = remote(main_ref.at[other, chunk], near.at[chunk], main_sems, chunk, sibling)
        copy.start()
        near_copies.append(copy)
    proj_sems = (proj_send, proj_recv)
    proj_copies = []
    for k, target in enumerate(chips):
        to_chip = lax.rem(chip + k + 1, CHIPS)
        copy = remote(proj_ref.at[to_chip], proj_far.at[chip], proj_sems, k, target)
        copy.start()
        proj_copies.append(copy)
    own_proj = pltpu.make_async_copy(proj_ref.at[chip], proj_far.at[chip], load_sem.at[1])
    own_proj.start()
    own_main.wait()

    vec_copies[0].wait_recv()
    vec_far[chip] = vec_ref[core] + vec_near[...]
    for k, target in enumerate(chips):
        copy = remote(vec_far.at[chip], vec_far.at[chip], vec_sems, 1 + k, target)
        copy.start()
        vec_copies.append(copy)

    far_sems = (far_send, far_recv)
    far_copies = []
    for chunk in range(CHUNKS):
        near_copies[chunk].wait_recv()

        @pl.loop(0, CHIPS * PLANES)
        def _(step, chunk=chunk):
            q = step // PLANES
            m = lax.rem(step, PLANES)
            first[chunk, q, m] = (
                first[chunk, q, m].astype(jnp.float32) + near[chunk, q, m].astype(jnp.float32)
            ).astype(jnp.bfloat16)

        copies = []
        for k, target in enumerate(chips):
            to_chip = lax.rem(chip + k + 1, CHIPS)
            copy = remote(
                first.at[chunk, to_chip],
                far.at[chunk, k],
                far_sems,
                chunk * 3 + k,
                target,
            )
            copy.start()
            copies.append(copy)
        far_copies.append(copies)

    for copy in vec_copies[1:4]:
        copy.wait()
    vec_deep[plane] = (vec_far[0] + vec_far[1]) + (vec_far[2] + vec_far[3])
    for k, target in enumerate(planes):
        copy = remote(vec_deep.at[plane], vec_deep.at[plane], vec_sems, 4 + k, target)
        copy.start()
        vec_copies.append(copy)

    deep_sems = (deep_send, deep_recv)
    own_proj.wait()
    for copy in proj_copies:
        copy.wait()
    proj_copies = []
    for k, target in enumerate(planes):
        to_plane = lax.rem(plane + k + 1, PLANES)
        copy = remote(
            proj_far.at[to_plane],
            part.at[pl.ds(MAIN + plane * PROJ, PROJ)],
            proj_sems,
            3 + k,
            target,
        )
        copy.start()
        proj_copies.append(copy)
    part[pl.ds(pl.multiple_of(MAIN + plane * PROJ, PROJ), PROJ), :] = proj_far[plane]

    deep_copies = []
    for chunk in range(CHUNKS):
        for copy in far_copies[chunk]:
            copy.wait_recv()

        @pl.loop(0, PLANES)
        def _(m, chunk=chunk):
            total = first[chunk, chip, m].astype(jnp.float32)
            for k in range(3):
                total = total + far[chunk, k, m].astype(jnp.float32)
            second[chunk, m] = total.astype(jnp.bfloat16)

        copies = []
        for k, target in enumerate(planes):
            to_plane = lax.rem(plane + k + 1, PLANES)
            copy = remote(
                second.at[chunk, to_plane],
                deep.at[chunk, k],
                deep_sems,
                chunk * 3 + k,
                target,
            )
            copy.start()
            copies.append(copy)
        deep_copies.append(copies)

    for copy in vec_copies[4:7]:
        copy.wait()
    vec_out_ref[core] = (vec_deep[0] + vec_deep[1]) + (vec_deep[2] + vec_deep[3])
    copy = remote(vec_out_ref.at[core], vec_out_ref.at[core], vec_sems, 7, sibling)
    copy.start()
    vec_copies.append(copy)

    done_sems = (done_send, done_recv)
    done_copies = []
    pieces = [(chunk * CHUNK, CHUNK) for chunk in range(CHUNKS)] + [(MAIN, PART - MAIN)]
    for index, (offset, size) in enumerate(pieces):
        rows = pl.ds(offset, size)
        if index < CHUNKS:
            for copy in deep_copies[index]:
                copy.wait_recv()
            total = second[index, plane].astype(jnp.float32)
            for k in range(3):
                total = total + deep[index, k].astype(jnp.float32)
            part[rows, :] = total.astype(jnp.bfloat16)
        else:
            for copy in proj_copies:
                copy.wait()
        copies = []
        for k, target in enumerate([sibling] + chips):
            copy = remote(
                part.at[rows], out_ref.at[wide_at, rows], done_sems, index * 4 + k, target
            )
            copy.start()
            copies.append(copy)
        done_copies.append(copies)
    own_part = pltpu.make_async_copy(part, out_ref.at[wide_at], load_sem.at[2])
    own_part.start()

    pass_sems = (pass_send, pass_recv)
    pass_copies = []
    for index, (offset, size) in enumerate(pieces):
        rows = pl.ds(offset, size)
        for k in range(3):
            done_copies[index][1 + k].wait_recv()
            source = lax.rem(chip + CHIPS - 1 - k, CHIPS) * CORES + core
            copy = remote(
                out_ref.at[source, rows], out_ref.at[source, rows], pass_sems, index * 3 + k, sibling
            )
            copy.start()
            pass_copies.append(copy)
    own_part.wait()
    for copies in done_copies:
        copies[0].wait_recv()
        for copy in copies:
            copy.wait_send()
    for copy in pass_copies:
        copy.wait()
    for copies in [near_copies] + far_copies + deep_copies:
        for copy in copies:
            copy.wait_send()
    vec_copies[0].wait_send()
    vec_copies[7].wait()


def reduce_grads(main, proj, vec):
    dma = pltpu.SemaphoreType.DMA
    bf = jnp.bfloat16
    return pl.pallas_call(
        reduce_kernel,
        out_shape=(
            jax.ShapeDtypeStruct((CORES * CHIPS, PART, D), bf),
            jax.ShapeDtypeStruct((CORES, VROWS, D), jnp.float32),
        ),
        in_specs=[
            pl.BlockSpec(memory_space=pl.ANY),
            pl.BlockSpec(memory_space=pl.ANY),
            pl.BlockSpec(memory_space=pltpu.VMEM),
        ],
        out_specs=(
            pl.BlockSpec(memory_space=pl.ANY),
            pl.BlockSpec(memory_space=pltpu.VMEM),
        ),
        scratch_shapes=[
            pltpu.VMEM((CHUNKS, CHIPS, PLANES, CHUNK, D), bf),
            pltpu.VMEM((CHUNKS, CHIPS, PLANES, CHUNK, D), bf),
            pltpu.VMEM((CHUNKS, 3, PLANES, CHUNK, D), bf),
            pltpu.VMEM((CHUNKS, PLANES, CHUNK, D), bf),
            pltpu.VMEM((CHUNKS, 3, CHUNK, D), bf),
            pltpu.VMEM((CHIPS, PROJ, D), bf),
            pltpu.VMEM((PART, D), bf),
            pltpu.VMEM((VROWS, D), jnp.float32),
            pltpu.VMEM((CHIPS, VROWS, D), jnp.float32),
            pltpu.VMEM((PLANES, VROWS, D), jnp.float32),
            dma((3,)),
            dma((CHUNKS,)),
            dma((CHUNKS,)),
            dma((CHUNKS * 3,)),
            dma((CHUNKS * 3,)),
            dma((CHUNKS * 3,)),
            dma((CHUNKS * 3,)),
            dma(((CHUNKS + 1) * 4,)),
            dma(((CHUNKS + 1) * 4,)),
            dma(((CHUNKS + 1) * 3,)),
            dma(((CHUNKS + 1) * 3,)),
            dma((6,)),
            dma((6,)),
            dma((8,)),
            dma((8,)),
        ],
        compiler_params=pltpu.CompilerParams(
            collective_id=3, has_side_effects=True, vmem_limit_bytes=40 * 2**20
        ),
        name="reduce_grads",
    )(main, proj, vec)


TILE = 128
STRIP = D // PLANES
OWNERS = (6, 7, 2, 4, 0)
BLOCK_TILES = (3, 1, 4, 4, 8)
MOST_TILES = max(BLOCK_TILES)


def halves(value):
    high = value.astype(jnp.bfloat16)
    return high, (value - high.astype(jnp.float32)).astype(jnp.bfloat16)


def plain_dot(left, right):
    return jnp.dot(left, right, preferred_element_type=jnp.float32)


def split_dot(left, right):
    return plain_dot(left[0], right[0]) + (
        plain_dot(left[0], right[1]) + plain_dot(left[1], right[0])
    )


def newton_kernel(
    grad_ref,
    momentum_ref,
    out_ref,
    grad_tiles,
    momentum_tiles,
    update_high,
    update_low,
    gram,
    poly,
    chain,
    pieces,
    rows_out,
    load_sem,
    gram_send,
    gram_recv,
    sum_send,
    sum_recv,
    rows_send,
    rows_recv,
    pass_send,
    pass_recv,
    local_sem,
):
    wide_at, plane, chip, core = place()
    sibling, chips, planes = neighbours(wide_at, plane, chip, core)
    tile_count = jnp.int32(0)
    tile_first = jnp.int32(0)
    begin = 0
    for owner, count in zip(OWNERS, BLOCK_TILES):
        tile_count = tile_count + jnp.where(wide_at == owner, count, 0)
        tile_first = tile_first + jnp.where(wide_at == owner, begin, 0)
        begin = begin + count
    owning = tile_count > 0

    def tile_rows(tile):
        return pl.ds(pl.multiple_of(tile * TILE, TILE), TILE)

    def loads(tile):
        source = tile_rows(tile_first + tile)
        return (
            pltpu.make_async_copy(grad_ref.at[source], grad_tiles.at[tile], load_sem.at[0, tile]),
            pltpu.make_async_copy(
                momentum_ref.at[source], momentum_tiles.at[tile], load_sem.at[1, tile]
            ),
        )

    @pl.loop(0, tile_count)
    def _(tile):
        for copy in loads(tile):
            copy.start()

    enter([sibling] + chips + planes)

    gram_sems = (gram_send, gram_recv)
    sum_sems = (sum_send, sum_recv)

    def transposed_dot(left, right):
        return lax.dot_general(
            left, right, (((0,), (0,)), ((), ())), preferred_element_type=jnp.float32
        )

    @pl.when(owning)
    def _():
        gram[...] = jnp.zeros_like(gram)
        poly[...] = jnp.zeros_like(poly)

        @pl.loop(0, tile_count)
        def _(tile):
            for copy in loads(tile):
                copy.wait()
            update = grad_tiles[tile] + MUON_BETA * momentum_tiles[tile]
            high, low = halves(update)
            update_high[tile] = high
            update_low[tile] = low
            gram[...] += transposed_dot(high, high)
            poly[...] += transposed_dot(high, low)

        gram[...] += poly[...] + poly[...].T
        copies = []
        for k, target in enumerate(planes):
            to_plane = lax.rem(plane + k + 1, PLANES)
            copy = remote(
                gram.at[pl.ds(pl.multiple_of(to_plane * STRIP, STRIP), STRIP)],
                pieces.at[plane],
                gram_sems,
                k,
                target,
            )
            copy.start()
            copies.append(copy)
        own_strip = pl.ds(pl.multiple_of(plane * STRIP, STRIP), STRIP)
        pieces[plane] = gram[own_strip, :]
        for copy in copies:
            copy.wait()
        chain[own_strip, :] = (pieces[0] + pieces[1]) + (pieces[2] + pieces[3])
        copies = []
        for k, target in enumerate(planes):
            copy = remote(chain.at[own_strip], chain.at[own_strip], sum_sems, k, target)
            copy.start()
            copies.append(copy)
        for copy in copies:
            copy.wait()

        diagonal = lax.broadcasted_iota(jnp.int32, (D, D), 0) == lax.broadcasted_iota(
            jnp.int32, (D, D), 1
        )
        square = jnp.sum(jnp.where(diagonal, chain[...], 0.0))
        norm = jnp.sqrt(jnp.full((1, 1), square)) + 1e-07
        inverse = 1.0 / norm
        gram[...] = chain[...] * (inverse * inverse)

        def make_poly():
            value = gram[...]
            parts = halves(value)
            diagonal = lax.broadcasted_iota(jnp.int32, (D, D), 0) == lax.broadcasted_iota(
                jnp.int32, (D, D), 1
            )
            poly[...] = (
                NEWTON_B * value
                + NEWTON_C * split_dot(parts, parts)
                + jnp.where(diagonal, NEWTON_A, 0.0)
            )

        def next_gram():
            parts = halves(poly[...])
            half_way = split_dot(halves(gram[...]), parts)
            gram[...] = split_dot(halves(half_way), parts)

        def extend():
            chain[...] = split_dot(halves(chain[...]), halves(poly[...]))

        make_poly()
        chain[...] = poly[...]
        next_gram()

        @pl.loop(0, 3)
        def _(sweep):
            make_poly()
            extend()
            next_gram()

        make_poly()
        extend()
        chain_parts = halves(chain[...] * inverse)

        @pl.loop(0, tile_count)
        def _(tile):
            rows_out[tile] = split_dot((update_high[tile], update_low[tile]), chain_parts).astype(
                jnp.bfloat16
            )

    row_sems = (rows_send, rows_recv)
    pass_sems = (pass_send, pass_recv)
    begin = 0
    for index, (owner, count) in enumerate(zip(OWNERS, BLOCK_TILES)):
        owner_chip, owner_core = divmod(owner, CORES)
        span = pl.ds(begin, count)
        begin = begin + count

        @pl.when(wide_at == owner)
        def _(index=index, count=count, span=span):
            for k, target in enumerate(chips + [sibling]):
                remote(
                    rows_out.at[pl.ds(0, count)], out_ref.at[span], row_sems, index * 4 + k, target
                ).start()
            pltpu.make_async_copy(
                rows_out.at[pl.ds(0, count)], out_ref.at[span], local_sem.at[0]
            ).start()

    begin = 0
    for index, (owner, count) in enumerate(zip(OWNERS, BLOCK_TILES)):
        owner_chip, owner_core = divmod(owner, CORES)
        span = pl.ds(begin, count)
        begin = begin + count
        for k in range(3):
            receiver = (owner_chip + k + 1) % CHIPS * CORES + owner_core

            @pl.when(wide_at == receiver)
            def _(index=index, span=span, k=k):
                remote(
                    out_ref.at[span], out_ref.at[span], row_sems, index * 4 + k, sibling
                ).wait_recv()
                remote(out_ref.at[span], out_ref.at[span], pass_sems, index, sibling).start()

    begin = 0
    for index, (owner, count) in enumerate(zip(OWNERS, BLOCK_TILES)):
        owner_chip, owner_core = divmod(owner, CORES)
        span = pl.ds(begin, count)
        begin = begin + count

        @pl.when(wide_at == owner)
        def _(index=index, count=count, span=span):
            for k, target in enumerate(chips + [sibling]):
                remote(
                    rows_out.at[pl.ds(0, count)], out_ref.at[span], row_sems, index * 4 + k, target
                ).wait_send()
            pltpu.make_async_copy(
                rows_out.at[pl.ds(0, count)], out_ref.at[span], local_sem.at[0]
            ).wait()

        @pl.when((core == owner_core) & (chip != owner_chip))
        def _(index=index, span=span):
            remote(out_ref.at[span], out_ref.at[span], pass_sems, index, sibling).wait_send()

        @pl.when((core != owner_core) & (chip != owner_chip))
        def _(index=index, span=span):
            remote(out_ref.at[span], out_ref.at[span], pass_sems, index, sibling).wait_recv()

        @pl.when((core != owner_core) & (chip == owner_chip))
        def _(index=index, span=span):
            remote(
                out_ref.at[span], out_ref.at[span], row_sems, index * 4 + 3, sibling
            ).wait_recv()


def newton_rows(grad_block, momentum_block):
    dma = pltpu.SemaphoreType.DMA
    tiles = grad_block.shape[0] // TILE
    scratch = [
        pltpu.VMEM((MOST_TILES, TILE, D), jnp.float32),
        pltpu.VMEM((MOST_TILES, TILE, D), jnp.float32),
        pltpu.VMEM((MOST_TILES, TILE, D), jnp.bfloat16),
        pltpu.VMEM((MOST_TILES, TILE, D), jnp.bfloat16),
        pltpu.VMEM((D, D), jnp.float32),
        pltpu.VMEM((D, D), jnp.float32),
        pltpu.VMEM((D, D), jnp.float32),
        pltpu.VMEM((PLANES, STRIP, D), jnp.float32),
        pltpu.VMEM((MOST_TILES, TILE, D), jnp.bfloat16),
        dma((2, MOST_TILES)),
        dma((3,)),
        dma((3,)),
        dma((3,)),
        dma((3,)),
        dma((20,)),
        dma((20,)),
        dma((5,)),
        dma((5,)),
        dma((1,)),
    ]
    return pl.pallas_call(
        newton_kernel,
        out_shape=jax.ShapeDtypeStruct((tiles, TILE, D), jnp.bfloat16),
        in_specs=[pl.BlockSpec(memory_space=pl.ANY)] * 2,
        out_specs=pl.BlockSpec(memory_space=pl.ANY),
        scratch_shapes=scratch,
        compiler_params=pltpu.CompilerParams(
            collective_id=4, has_side_effects=True, vmem_limit_bytes=48 * 2**20
        ),
        name="newton_rows",
    )(grad_block, momentum_block).reshape(grad_block.shape)


def spread_kernel(count, *refs):
    own = refs[:count]
    outs = refs[count : 2 * count]
    local_sem, send_sem, recv_sem = refs[2 * count :]
    wide_at, plane, chip, core = place()
    sibling, chips, planes = neighbours(wide_at, plane, chip, core)
    enter([sibling] + chips + planes)
    sems = (send_sem, recv_sem)
    pending = []
    firsts = []

    def send(src, dst, index, target):
        copy = remote(src, dst, sems, index, target)
        copy.start()
        pending.append(copy)
        return copy

    for item in range(count):
        base = item * 31
        spot = outs[item].at[plane, wide_at]
        local = pltpu.make_async_copy(own[item], spot, local_sem.at[item])
        local.start()
        pending.append(local)
        from_planes = [send(own[item], spot, base + k, planes[k]) for k in range(3)]
        from_chips = [send(own[item], spot, base + 3 + k, chips[k]) for k in range(3)]
        send(own[item], spot, base + 6, sibling)
        firsts.append((from_planes, [from_chips]))
    for k in range(3):
        for item in range(count):
            base = item * 31 + 7 + k * 4
            from_planes, from_chips = firsts[item]
            from_planes[k].wait_recv()
            spot = outs[item].at[lax.rem(plane + PLANES - 1 - k, PLANES), wide_at]
            from_chips.append([send(spot, spot, base + j, chips[j]) for j in range(3)])
            send(spot, spot, base + 3, sibling)
    for step in range(PLANES):
        for item in range(count):
            base = item * 31 + 19 + step * 3
            source_plane = plane if step == 0 else lax.rem(plane + PLANES - step, PLANES)
            for j in range(3):
                firsts[item][1][step][j].wait_recv()
                source = lax.rem(chip + CHIPS - 1 - j, CHIPS) * CORES + core
                spot = outs[item].at[source_plane, source]
                send(spot, spot, base + j, sibling)
    received = {id(copy) for from_planes, _ in firsts for copy in from_planes}
    received |= {id(copy) for _, groups in firsts for group in groups for copy in group}
    for copy in pending:
        if id(copy) in received:
            copy.wait_send()
        else:
            copy.wait()


def spread(parts, collective_id, name):
    dma = pltpu.SemaphoreType.DMA
    count = len(parts)
    return pl.pallas_call(
        partial(spread_kernel, count),
        out_shape=tuple(
            jax.ShapeDtypeStruct((PLANES, CHIPS * CORES) + part.shape, part.dtype)
            for part in parts
        ),
        in_specs=[pl.BlockSpec(memory_space=pl.ANY)] * count,
        out_specs=tuple(pl.BlockSpec(memory_space=pl.ANY) for _ in parts),
        scratch_shapes=[dma((count,)), dma((31 * count,)), dma((31 * count,))],
        compiler_params=pltpu.CompilerParams(collective_id=collective_id, has_side_effects=True),
        name=name,
    )(*parts)


def tell_kernel(own_ref, out_ref, send_sem, recv_sem):
    wide_at, plane, chip, core = place()
    wide_count = CHIPS * CORES
    peers = [
        (lax.rem(wide_at + k // PLANES, wide_count), lax.rem(plane + k % PLANES, PLANES))
        for k in range(1, wide_count * PLANES)
    ]
    enter(peers)
    spot = out_ref.at[wide_at * PLANES + plane]
    copies = [
        remote(own_ref, spot, (send_sem, recv_sem), k, target) for k, target in enumerate(peers)
    ]
    for copy in copies:
        copy.start()
    out_ref[wide_at * PLANES + plane] = own_ref[...]
    for copy in copies:
        copy.wait()


def tell(values, collective_id):
    dma = pltpu.SemaphoreType.DMA
    every = PLANES * CHIPS * CORES
    return pl.pallas_call(
        tell_kernel,
        out_shape=jax.ShapeDtypeStruct((every,) + values.shape, values.dtype),
        in_specs=[pl.BlockSpec(memory_space=pltpu.VMEM)],
        out_specs=pl.BlockSpec(memory_space=pltpu.VMEM),
        scratch_shapes=[dma((every - 1,)), dma((every - 1,))],
        compiler_params=pltpu.CompilerParams(collective_id=collective_id, has_side_effects=True),
        name="tell_ids",
    )(values)


def meshed():
    return lax.axis_size("wide") == CHIPS * CORES and lax.axis_size("narrow") == PLANES


def gather_weights(mat_master):
    narrow_count = lax.axis_size("narrow")
    wide_count = lax.axis_size("wide")
    wide_at = lax.axis_index("wide")
    gathered = []
    for segment in block_slices(mat_master[0], narrow_count):
        rows = segment.shape[0] // wide_count
        own_part = lax.dynamic_slice_in_dim(segment, wide_at * rows, rows, 0)
        gathered.append(
            lax.all_gather(own_part.astype(jnp.bfloat16), ("narrow", "wide"), axis=0, tiled=True)
        )
    return gathered


def gather_ids(slot_ids):
    if not meshed():
        return lax.all_gather(slot_ids, BOTH, axis=0, tiled=False)
    count = slot_ids.shape[0]
    lanes = 128
    rows = -(-count // (8 * lanes)) * 8
    padded = jnp.pad(slot_ids, (0, rows * lanes - count)).reshape(rows, lanes)
    every = tell(padded, 1)
    return every.reshape(every.shape[0], rows * lanes)[:, :count]


def gather_entries(rows):
    if not meshed():
        return lax.all_gather(rows, BOTH, axis=0, tiled=True)
    (every,) = spread([rows], 2, "spread_entries")
    return every.transpose(1, 0, 2, 3).reshape(-1, rows.shape[1])


def total_grads(matrices, grad_proj_own, vec_local):
    narrow_count = lax.axis_size("narrow")
    wide_count = lax.axis_size("wide")
    narrow_at = lax.axis_index("narrow")
    packed_term = jnp.concatenate(
        [
            matrix.reshape(narrow_count, wide_count, -1, D).astype(jnp.bfloat16)
            for matrix in matrices
        ],
        axis=2,
    )
    proj_bf = grad_proj_own.astype(jnp.bfloat16)
    if meshed():
        main = packed_term.reshape(PLANES, CHIPS, CORES, CHUNKS, CHUNK, D)
        main = main.transpose(2, 3, 1, 0, 4, 5)
        vec_rows = CORES * VROWS
        vec_in = jnp.pad(vec_local.reshape(-1, D), ((0, vec_rows - vec_local.shape[0] // D), (0, 0)))
        parts, vec_sum = reduce_grads(
            main, proj_bf.reshape(CHIPS, PROJ, D), vec_in.reshape(CORES, VROWS, D)
        )
        vec_grad = vec_sum.reshape(-1)[: vec_local.shape[0]]
        segments = []
        offset = 0
        for matrix in matrices:
            height = matrix.shape[0] // (narrow_count * wide_count)
            segments.append(parts[:, offset : offset + height].reshape(-1, D))
            offset = offset + height
        proj = parts[:, MAIN:].reshape(CHIPS, CORES, PLANES, PROJ, D)
        segments.append(proj.transpose(1, 2, 0, 3, 4).reshape(-1, D))
        return jnp.concatenate(segments, axis=0).astype(jnp.float32), vec_grad
    vec_grad = lax.psum(vec_local, BOTH)
    share = packed_term.shape[2]
    terms = lax.all_to_all(
        packed_term.transpose(1, 0, 2, 3).reshape(-1, share, D), BOTH, 0, 0, tiled=True
    )
    share_sum = jnp.sum(terms.astype(jnp.float32), axis=0)
    parts = lax.all_gather(share_sum.astype(jnp.bfloat16), "wide", axis=0, tiled=False)
    segments = []
    offset = 0
    for matrix in matrices:
        height = matrix.shape[0] // (narrow_count * wide_count)
        segments.append(parts[:, offset : offset + height].reshape(-1, D))
        offset = offset + height
    proj_grad = lax.all_gather(proj_bf, BOTH, axis=0, tiled=True)
    proj_rows = OUTW // narrow_count
    segments.append(lax.dynamic_slice_in_dim(proj_grad, narrow_at * proj_rows, proj_rows, 0))
    return jnp.concatenate(segments, axis=0).astype(jnp.float32), vec_grad


def orthogonal_rows(grad_block, momentum_block):
    if meshed():
        return newton_rows(grad_block, momentum_block)
    narrow_count = lax.axis_size("narrow")
    segments = block_slices(grad_block + MUON_BETA * momentum_block, narrow_count)
    grams = lax.psum(jnp.stack([gram_of(segment) for segment in segments]), "narrow")
    rows = []
    for position, segment in enumerate(segments):
        square = jnp.sum(jnp.diagonal(grams[position]))
        norm = jnp.sqrt(square) + 1e-07
        gram = grams[position] / (norm * norm)
        chain = None
        for sweep_index in range(5):
            squared = jnp.dot(gram, gram, precision=HIGH)
            poly = NEWTON_B * gram + NEWTON_C * squared + NEWTON_A * jnp.eye(D, dtype=jnp.float32)
            chain = poly if chain is None else jnp.dot(chain, poly, precision=HIGH)
            if sweep_index < 4:
                gram = jnp.dot(jnp.dot(gram, poly, precision=HIGH), poly, precision=HIGH)
        rows.append(jnp.dot(segment / norm, chain, precision=HIGH))
    return jnp.concatenate(rows, axis=0)


def on_device(
    piece_table,
    piece_ids,
    slot_mask,
    text_ids,
    text_mask,
    text_cot,
    mat_master,
    mat_momentum,
    mat_ema,
    vec_master,
    vec_moment1,
    vec_moment2,
    vec_ema,
):
    narrow_count = lax.axis_size("narrow")
    wide_count = lax.axis_size("wide")
    device_count = narrow_count * wide_count
    wide_at = lax.axis_index("wide")
    narrow_at = lax.axis_index("narrow")
    me = wide_at * narrow_count + narrow_at
    w_qkv, w_out, w_up, w_down, w_proj = gather_weights(mat_master)
    (
        cls_vec,
        positions,
        ln1_gain,
        ln1_shift,
        ln2_gain,
        ln2_shift,
        final_gain,
        final_shift,
        bias_up,
        bias_down,
        bias_out,
    ) = split_vectors(vec_master)
    entries = piece_ids.shape[0]
    slot_ids = piece_ids.reshape(-1)
    slot_count = slot_ids.shape[0]
    group_rows = piece_table.shape[0]
    cap = piece_cap(group_rows)
    every_ids = gather_ids(slot_ids)
    asked = every_ids // group_rows == me
    before = (
        lax.broadcasted_iota(jnp.int32, (slot_count, slot_count), 0)
        < lax.broadcasted_iota(jnp.int32, (slot_count, slot_count), 1)
    )
    asked_rank = jnp.dot(
        asked.astype(jnp.bfloat16), before.astype(jnp.bfloat16), preferred_element_type=jnp.float32
    ).astype(jnp.int32)
    asked_rank = jnp.where(asked, asked_rank, -1)
    chosen = asked_rank[:, None, :] == lax.iota(jnp.int32, cap)[None, :, None]
    local_ids = every_ids - me * group_rows + 1
    asked_rows = jnp.sum(jnp.where(chosen, local_ids[:, None, :], 0), axis=2).reshape(-1) - 1
    asked_onehot = (
        asked_rows[:, None] == lax.iota(jnp.int32, group_rows)[None, :]
    ).astype(jnp.bfloat16)
    outgoing = jnp.dot(asked_onehot, piece_table, preferred_element_type=jnp.float32)
    incoming = lax.all_to_all(
        outgoing.astype(jnp.bfloat16).reshape(device_count, cap, D), BOTH, 0, 0, tiled=True
    ).reshape(device_count * cap, D)
    own_group = slot_ids // group_rows
    same = (own_group[:, None] == own_group[None, :]) & before.T
    own_rank = jnp.sum(same.astype(jnp.int32), axis=1)
    own_spot = own_group * cap + own_rank
    own_onehot = (
        own_spot[:, None] == lax.iota(jnp.int32, device_count * cap)[None, :]
    ).astype(jnp.bfloat16)
    looked = jnp.dot(own_onehot, incoming, preferred_element_type=jnp.float32)
    pieces = looked.reshape(entries, PSLOTS, D)

    flat_ids = text_ids.reshape(-1)
    flat_mask = text_mask.reshape(-1)
    token_count = flat_ids.shape[0]
    feature_rows = text_cot.shape[0]
    all_entries = entries * device_count
    block_len = min(512, token_count)
    entry_index = lax.iota(jnp.int32, all_entries)

    def text_block(step_index, grad_cols):
        begin_at = step_index * block_len
        ids_now = lax.dynamic_slice_in_dim(flat_ids, begin_at, block_len)
        keep_mask = lax.dynamic_slice_in_dim(flat_mask, begin_at, block_len)
        onehot = (entry_index[:, None] == ids_now[None, :]).astype(jnp.bfloat16)
        cot_now = lax.dynamic_slice_in_dim(text_cot, begin_at, block_len, 1)
        masked_cot = jnp.where(keep_mask[None, :] > 0, cot_now, jnp.zeros_like(cot_now))
        return grad_cols + lax.dot_general(
            masked_cot, onehot, (((1,), (1,)), ((), ())), preferred_element_type=jnp.float32
        )

    grad_cols = lax.fori_loop(
        0, token_count // block_len, text_block, jnp.zeros((feature_rows, all_entries), jnp.float32)
    )
    grad_table_cols = grad_cols.astype(jnp.bfloat16)
    grad_table = lax.all_to_all(grad_table_cols, BOTH, split_axis=1, concat_axis=0, tiled=True)
    grad_bias_own = jnp.sum(grad_table_cols.astype(jnp.float32), axis=1)
    grad_normed_three = contract_rows(grad_table, w_proj)

    first_slot = jnp.broadcast_to(cls_vec + positions[0], (entries, 1, D))
    slots_x = jnp.concatenate([first_slot, pieces + positions[1:]], axis=1)
    live_slots = jnp.concatenate([jnp.ones((entries, 1), jnp.int32), slot_mask], axis=1) > 0
    normed, norm1_pull = jax.vjp(layer_norm, slots_x, ln1_gain, ln1_shift)
    normed_bf = normed.astype(jnp.bfloat16)
    query_rows = jnp.einsum(
        "ed,fd->ef", normed_bf[:, 0], w_qkv[:D], preferred_element_type=jnp.float32
    )
    key_value = jnp.einsum("esd,fd->esf", normed_bf, w_qkv[D:], preferred_element_type=jnp.float32)
    attended, attend_pull = jax.vjp(
        partial(attend, live_slots=live_slots), query_rows, key_value[:, :, :D], key_value[:, :, D:]
    )
    attended_bf = attended.astype(jnp.bfloat16)
    residual = slots_x[:, 0] + jnp.einsum(
        "ed,fd->ef", attended_bf, w_out, preferred_element_type=jnp.float32
    )
    normed_two, norm2_pull = jax.vjp(layer_norm, residual, ln2_gain, ln2_shift)
    normed_two_bf = normed_two.astype(jnp.bfloat16)
    gate_in = (
        jnp.einsum("ed,fd->ef", normed_two_bf, w_up, preferred_element_type=jnp.float32) + bias_up
    )
    active, gelu_pull = jax.vjp(gelu_tanh, gate_in)
    active_bf = active.astype(jnp.bfloat16)
    second_residual = residual + (
        jnp.dot(active_bf, w_down, preferred_element_type=jnp.float32) + bias_down
    )
    normed_three, norm3_pull = jax.vjp(layer_norm, second_residual, final_gain, final_shift)
    normed_three_bf = normed_three.astype(jnp.bfloat16)
    every_normed = gather_entries(normed_three_bf)
    proj_own = lax.dynamic_slice_in_dim(w_proj, me * feature_rows, feature_rows, 0)
    bias_own = lax.dynamic_slice_in_dim(bias_out, me * feature_rows, feature_rows, 0)
    table_cols = (
        jnp.einsum("fd,ed->fe", proj_own, every_normed, preferred_element_type=jnp.float32)
        + bias_own[:, None]
    )
    text_embeds = jnp.take(table_cols, flat_ids, axis=1) * flat_mask[None, :].astype(jnp.float32)
    grad_proj_own = jnp.dot(grad_table_cols, every_normed, preferred_element_type=jnp.float32)

    grad_second, grad_final_gain, grad_final_shift = norm3_pull(grad_normed_three)
    grad_branch_two = grad_second.astype(jnp.bfloat16)
    grad_bias_down = jnp.sum(grad_branch_two.astype(jnp.float32), axis=0)
    grad_down = contract_rows(active_bf, grad_branch_two)
    grad_active = jnp.einsum(
        "ed,fd->ef", grad_branch_two, w_down, preferred_element_type=jnp.float32
    )
    (grad_gate,) = gelu_pull(grad_active)
    grad_gate_bf = grad_gate.astype(jnp.bfloat16)
    grad_bias_up = jnp.sum(grad_gate_bf.astype(jnp.float32), axis=0)
    grad_up = contract_rows(grad_gate_bf, normed_two_bf)
    grad_normed_two = jnp.dot(grad_gate_bf, w_up, preferred_element_type=jnp.float32)
    grad_residual_norm, grad_ln2_gain, grad_ln2_shift = norm2_pull(grad_normed_two)
    grad_residual = grad_second + grad_residual_norm
    grad_branch_one = grad_residual.astype(jnp.bfloat16)
    grad_out_w = contract_rows(grad_branch_one, attended_bf)
    grad_attended = jnp.dot(grad_branch_one, w_out, preferred_element_type=jnp.float32)
    grad_query, grad_keys, grad_values = attend_pull(grad_attended)
    grad_query_bf = grad_query.astype(jnp.bfloat16)
    grad_kv = jnp.concatenate(
        [grad_keys.astype(jnp.bfloat16), grad_values.astype(jnp.bfloat16)], axis=2
    )
    grad_q_w = contract_rows(grad_query_bf, normed_bf[:, 0])
    grad_kv_w = jnp.einsum("esf,esd->fd", grad_kv, normed_bf, preferred_element_type=jnp.float32)
    grad_normed = jnp.einsum("esf,fd->esd", grad_kv, w_qkv[D:], preferred_element_type=jnp.float32)
    grad_normed = grad_normed.at[:, 0].add(
        jnp.dot(grad_query_bf, w_qkv[:D], preferred_element_type=jnp.float32)
    )
    grad_slots, grad_ln1_gain, grad_ln1_shift = norm1_pull(grad_normed)
    grad_first = grad_slots[:, 0] + grad_residual
    grad_cls = jnp.sum(grad_first, axis=0)
    grad_pos = jnp.concatenate([grad_cls[None], jnp.sum(grad_slots[:, 1:], axis=0)], axis=0)
    grad_pieces = grad_slots[:, 1:].astype(jnp.bfloat16).reshape(-1, D)
    grad_outgoing = contract_rows(own_onehot, grad_pieces).astype(jnp.bfloat16)
    grad_incoming = lax.all_to_all(
        grad_outgoing.reshape(device_count, cap, D), BOTH, 0, 0, tiled=True
    ).reshape(device_count * cap, D)
    piece_grad = contract_rows(asked_onehot, grad_incoming)

    vec_local = jnp.concatenate(
        [
            grad_cls,
            grad_pos.reshape(-1),
            grad_ln1_gain,
            grad_ln1_shift,
            grad_ln2_gain,
            grad_ln2_shift,
            grad_final_gain,
            grad_final_shift,
            grad_bias_up,
            grad_bias_down,
            lax.dynamic_update_slice_in_dim(
                jnp.zeros((OUTW,), jnp.float32), grad_bias_own, me * feature_rows, 0
            ),
        ]
    )
    grad_qkv = jnp.concatenate([grad_q_w, grad_kv_w], axis=0)
    grad_block, vec_grad = total_grads(
        (grad_qkv, grad_out_w, grad_up, grad_down), grad_proj_own, vec_local
    )
    momentum_block = MUON_BETA * mat_momentum[0] + grad_block
    ortho = orthogonal_rows(grad_block, momentum_block).astype(jnp.float32)
    row_scale = jnp.concatenate(
        [
            jnp.full((row_total // narrow_count, 1), MUON_RATE * math.sqrt(row_total / D))
            for row_total in matrix_rows()
        ],
        axis=0,
    ).astype(jnp.float32)
    weight_block = (mat_master[0] * (1.0 - MUON_RATE * MUON_DECAY) - row_scale * ortho)[None]
    ema_block = EMA_DECAY * mat_ema + (1.0 - EMA_DECAY) * weight_block
    moment_one = ADAM_BETA1 * vec_moment1 + (1.0 - ADAM_BETA1) * vec_grad
    moment_two = ADAM_BETA2 * vec_moment2 + (1.0 - ADAM_BETA2) * vec_grad * vec_grad
    corrected_one = moment_one / (1.0 - ADAM_BETA1**STEP)
    corrected_two = moment_two / (1.0 - ADAM_BETA2**STEP)
    vec_weight = vec_master - ADAM_RATE * corrected_one / (jnp.sqrt(corrected_two) + ADAM_EPSILON)
    vec_ema_new = EMA_DECAY * vec_ema + (1.0 - EMA_DECAY) * vec_weight
    return (
        text_embeds,
        piece_grad,
        grad_block[None],
        momentum_block[None],
        weight_block,
        ema_block,
        vec_grad,
        moment_one,
        moment_two,
        vec_weight,
        vec_ema_new,
    )


def solution(mesh):
    in_specs = (
        P(("wide", "narrow"), None),
        P(("wide", "narrow"), None),
        P(("wide", "narrow"), None),
        P(),
        P(),
        P(("wide", "narrow"), None),
        P("narrow", None, None),
        P("narrow", None, None),
        P("narrow", None, None),
        P(),
        P(),
        P(),
        P(),
    )
    out_specs = (
        P(("wide", "narrow"), None),
        P(("wide", "narrow"), None),
        P("narrow", None, None),
        P("narrow", None, None),
        P("narrow", None, None),
        P("narrow", None, None),
        P(),
        P(),
        P(),
        P(),
        P(),
    )
    return jax.shard_map(
        on_device, mesh=mesh, in_specs=in_specs, out_specs=out_specs, check_vma=False
    )
```

```python
from functools import partial
import math

import jax
import jax.numpy as jnp
from jax import lax
from jax.experimental import pallas as pl
from jax.experimental.pallas import tpu as pltpu
from jax.sharding import PartitionSpec as P

D = 512
HEADS = 8
HDIM = 64
FF = 2048
OUTW = 4096
SLOTS = 8
PSLOTS = 7
STEP = 10


HIGHEST = lax.Precision.HIGHEST
HIGH = lax.Precision.HIGH
MUON_RATE = 0.5
MUON_DECAY = 0.01
MUON_BETA = 0.95
ADAM_RATE = 0.5
ADAM_BETA1 = 0.9
ADAM_BETA2 = 0.95
ADAM_EPSILON = 1e-08
EMA_DECAY = 0.8
NEWTON_A = 3.4445
NEWTON_B = -4.775
NEWTON_C = 2.0315


def matrix_rows():
    return (3 * D, D, FF, FF, OUTW)


def unpack(packed, narrow_count):
    matrices = []
    offset = 0
    for row_total in matrix_rows():
        height = row_total // narrow_count
        matrices.append(packed[:, offset : offset + height, :].reshape(row_total, packed.shape[2]))
        offset = offset + height
    return matrices


def pack(matrices, narrow_count):
    return jnp.concatenate(
        [
            matrix.reshape(narrow_count, matrix.shape[0] // narrow_count, matrix.shape[1])
            for matrix in matrices
        ],
        axis=1,
    )


def block_slices(block, narrow_count):
    segments = []
    offset = 0
    for row_total in matrix_rows():
        height = row_total // narrow_count
        segments.append(block[offset : offset + height])
        offset = offset + height
    return segments


def split_vectors(vector):
    lengths = (D, SLOTS * D, D, D, D, D, D, D, FF, D, OUTW)
    chosen = []
    offset = 0
    for length in lengths:
        chosen.append(vector[offset : offset + length])
        offset = offset + length
    chosen[1] = chosen[1].reshape(SLOTS, D)
    return chosen


def layer_norm(values, gain, shift):
    center = values - jnp.mean(values, axis=-1, keepdims=True)
    spread = jnp.mean(center * center, axis=-1, keepdims=True)
    return center * lax.rsqrt(spread + 1e-05) * gain + shift


def gelu_tanh(values):
    return jax.nn.gelu(values, approximate=True)


def attend(query_rows, key_rows, value_rows, live_slots):
    entry_count = query_rows.shape[0]
    query_heads = query_rows.reshape(entry_count, HEADS, HDIM)
    key_heads = key_rows.reshape(entry_count, SLOTS, HEADS, HDIM)
    value_heads = value_rows.reshape(entry_count, SLOTS, HEADS, HDIM)
    scores = jnp.einsum("ehd,eshd->ehs", query_heads, key_heads, precision=HIGHEST) / math.sqrt(
        HDIM
    )
    scores = jnp.where(live_slots[:, None, :], scores, -1e30)
    scores = scores - jnp.max(scores, axis=-1, keepdims=True)
    expped = jnp.exp(scores)
    probabilities = expped / jnp.sum(expped, axis=-1, keepdims=True)
    mixed_heads = jnp.einsum("ehs,eshd->ehd", probabilities, value_heads, precision=HIGHEST)
    return mixed_heads.reshape(entry_count, D)


PIECE_CAPS = {1024: 58, 256: 16}
BOTH = ("wide", "narrow")


def piece_cap(group_rows):
    cap = PIECE_CAPS.get(group_rows, group_rows)
    return -(-cap // 16) * 16


def contract_rows(left, right):
    return lax.dot_general(
        left, right, (((0,), (0,)), ((), ())), preferred_element_type=jnp.float32
    )


def gram_of(block):
    return lax.dot_general(block, block, (((0,), (0,)), ((), ())), precision=HIGHEST)


def adam(vec_grad, vec_master, vec_moment1, vec_moment2, vec_ema):
    moment_one = ADAM_BETA1 * vec_moment1 + (1.0 - ADAM_BETA1) * vec_grad
    moment_two = ADAM_BETA2 * vec_moment2 + (1.0 - ADAM_BETA2) * vec_grad * vec_grad
    corrected_one = moment_one / (1.0 - ADAM_BETA1**STEP)
    corrected_two = moment_two / (1.0 - ADAM_BETA2**STEP)
    vec_weight = vec_master - ADAM_RATE * corrected_one / (jnp.sqrt(corrected_two) + ADAM_EPSILON)
    vec_ema_new = EMA_DECAY * vec_ema + (1.0 - EMA_DECAY) * vec_weight
    return vec_grad, moment_one, moment_two, vec_weight, vec_ema_new


def on_device_plain(
    piece_table,
    piece_ids,
    slot_mask,
    text_ids,
    text_mask,
    text_cot,
    mat_master,
    mat_momentum,
    mat_ema,
    vec_master,
    vec_moment1,
    vec_moment2,
    vec_ema,
):
    narrow_count = lax.axis_size("narrow")
    wide_count = lax.axis_size("wide")
    device_count = narrow_count * wide_count
    wide_at = lax.axis_index("wide")
    narrow_at = lax.axis_index("narrow")
    me = wide_at * narrow_count + narrow_at
    block_rows = mat_master.shape[1]
    own_rows = block_rows // wide_count
    own_part = lax.dynamic_slice_in_dim(mat_master[0], wide_at * own_rows, own_rows, 0)
    packed_bf = lax.all_gather(
        own_part.astype(jnp.bfloat16), ("narrow", "wide"), axis=0, tiled=True
    ).reshape(narrow_count, block_rows, D)
    w_qkv, w_out, w_up, w_down, w_proj = unpack(packed_bf, narrow_count)
    (
        cls_vec,
        positions,
        ln1_gain,
        ln1_shift,
        ln2_gain,
        ln2_shift,
        final_gain,
        final_shift,
        bias_up,
        bias_down,
        bias_out,
    ) = split_vectors(vec_master)
    entries = piece_ids.shape[0]
    slot_ids = piece_ids.reshape(-1)
    slot_count = slot_ids.shape[0]
    group_rows = piece_table.shape[0]
    cap = piece_cap(group_rows)
    every_ids = lax.all_gather(slot_ids, BOTH, axis=0, tiled=False)
    asked = every_ids // group_rows == me
    before = (
        lax.broadcasted_iota(jnp.int32, (slot_count, slot_count), 0)
        < lax.broadcasted_iota(jnp.int32, (slot_count, slot_count), 1)
    )
    asked_rank = jnp.dot(
        asked.astype(jnp.bfloat16), before.astype(jnp.bfloat16), preferred_element_type=jnp.float32
    ).astype(jnp.int32)
    asked_rank = jnp.where(asked, asked_rank, -1)
    chosen = asked_rank[:, None, :] == lax.iota(jnp.int32, cap)[None, :, None]
    local_ids = every_ids - me * group_rows + 1
    asked_rows = jnp.sum(jnp.where(chosen, local_ids[:, None, :], 0), axis=2).reshape(-1) - 1
    asked_onehot = (
        asked_rows[:, None] == lax.iota(jnp.int32, group_rows)[None, :]
    ).astype(jnp.bfloat16)
    outgoing = jnp.dot(asked_onehot, piece_table, preferred_element_type=jnp.float32)
    incoming = lax.all_to_all(
        outgoing.astype(jnp.bfloat16).reshape(device_count, cap, D), BOTH, 0, 0, tiled=True
    ).reshape(device_count * cap, D)
    own_group = slot_ids // group_rows
    same = (own_group[:, None] == own_group[None, :]) & before.T
    own_rank = jnp.sum(same.astype(jnp.int32), axis=1)
    own_spot = own_group * cap + own_rank
    own_onehot = (
        own_spot[:, None] == lax.iota(jnp.int32, device_count * cap)[None, :]
    ).astype(jnp.bfloat16)
    looked = jnp.dot(own_onehot, incoming, preferred_element_type=jnp.float32)
    pieces = looked.reshape(entries, PSLOTS, D)

    flat_ids = text_ids.reshape(-1)
    flat_mask = text_mask.reshape(-1)
    token_count = flat_ids.shape[0]
    feature_rows = text_cot.shape[0]
    all_entries = entries * device_count
    block_len = min(512, token_count)
    entry_index = lax.iota(jnp.int32, all_entries)

    def text_block(step_index, grad_cols):
        begin_at = step_index * block_len
        ids_now = lax.dynamic_slice_in_dim(flat_ids, begin_at, block_len)
        keep_mask = lax.dynamic_slice_in_dim(flat_mask, begin_at, block_len)
        onehot = (entry_index[:, None] == ids_now[None, :]).astype(jnp.bfloat16)
        cot_now = lax.dynamic_slice_in_dim(text_cot, begin_at, block_len, 1)
        masked_cot = jnp.where(keep_mask[None, :] > 0, cot_now, jnp.zeros_like(cot_now))
        return grad_cols + lax.dot_general(
            masked_cot, onehot, (((1,), (1,)), ((), ())), preferred_element_type=jnp.float32
        )

    grad_cols = lax.fori_loop(
        0, token_count // block_len, text_block, jnp.zeros((feature_rows, all_entries), jnp.float32)
    )
    grad_table_cols = grad_cols.astype(jnp.bfloat16)
    grad_table = lax.all_to_all(grad_table_cols, BOTH, split_axis=1, concat_axis=0, tiled=True)
    grad_bias_own = jnp.sum(grad_table_cols.astype(jnp.float32), axis=1)
    grad_normed_three = contract_rows(grad_table, w_proj)

    first_slot = jnp.broadcast_to(cls_vec + positions[0], (entries, 1, D))
    slots_x = jnp.concatenate([first_slot, pieces + positions[1:]], axis=1)
    live_slots = jnp.concatenate([jnp.ones((entries, 1), jnp.int32), slot_mask], axis=1) > 0
    normed, norm1_pull = jax.vjp(layer_norm, slots_x, ln1_gain, ln1_shift)
    normed_bf = normed.astype(jnp.bfloat16)
    query_rows = jnp.einsum(
        "ed,fd->ef", normed_bf[:, 0], w_qkv[:D], preferred_element_type=jnp.float32
    )
    key_value = jnp.einsum("esd,fd->esf", normed_bf, w_qkv[D:], preferred_element_type=jnp.float32)
    attended, attend_pull = jax.vjp(
        partial(attend, live_slots=live_slots), query_rows, key_value[:, :, :D], key_value[:, :, D:]
    )
    attended_bf = attended.astype(jnp.bfloat16)
    residual = slots_x[:, 0] + jnp.einsum(
        "ed,fd->ef", attended_bf, w_out, preferred_element_type=jnp.float32
    )
    normed_two, norm2_pull = jax.vjp(layer_norm, residual, ln2_gain, ln2_shift)
    normed_two_bf = normed_two.astype(jnp.bfloat16)
    gate_in = (
        jnp.einsum("ed,fd->ef", normed_two_bf, w_up, preferred_element_type=jnp.float32) + bias_up
    )
    active, gelu_pull = jax.vjp(gelu_tanh, gate_in)
    active_bf = active.astype(jnp.bfloat16)
    second_residual = residual + (
        jnp.dot(active_bf, w_down, preferred_element_type=jnp.float32) + bias_down
    )
    normed_three, norm3_pull = jax.vjp(layer_norm, second_residual, final_gain, final_shift)
    normed_three_bf = normed_three.astype(jnp.bfloat16)
    every_normed = lax.all_gather(normed_three_bf, BOTH, axis=0, tiled=True)
    proj_own = lax.dynamic_slice_in_dim(w_proj, me * feature_rows, feature_rows, 0)
    bias_own = lax.dynamic_slice_in_dim(bias_out, me * feature_rows, feature_rows, 0)
    table_cols = (
        jnp.einsum("fd,ed->fe", proj_own, every_normed, preferred_element_type=jnp.float32)
        + bias_own[:, None]
    )
    text_embeds = jnp.take(table_cols, flat_ids, axis=1) * flat_mask[None, :].astype(jnp.float32)
    grad_proj_own = jnp.dot(grad_table_cols, every_normed, preferred_element_type=jnp.float32)

    grad_second, grad_final_gain, grad_final_shift = norm3_pull(grad_normed_three)
    grad_branch_two = grad_second.astype(jnp.bfloat16)
    grad_bias_down = jnp.sum(grad_branch_two.astype(jnp.float32), axis=0)
    grad_down = contract_rows(active_bf, grad_branch_two)
    grad_active = jnp.einsum(
        "ed,fd->ef", grad_branch_two, w_down, preferred_element_type=jnp.float32
    )
    (grad_gate,) = gelu_pull(grad_active)
    grad_gate_bf = grad_gate.astype(jnp.bfloat16)
    grad_bias_up = jnp.sum(grad_gate_bf.astype(jnp.float32), axis=0)
    grad_up = contract_rows(grad_gate_bf, normed_two_bf)
    grad_normed_two = jnp.dot(grad_gate_bf, w_up, preferred_element_type=jnp.float32)
    grad_residual_norm, grad_ln2_gain, grad_ln2_shift = norm2_pull(grad_normed_two)
    grad_residual = grad_second + grad_residual_norm
    grad_branch_one = grad_residual.astype(jnp.bfloat16)
    grad_out_w = contract_rows(grad_branch_one, attended_bf)
    grad_attended = jnp.dot(grad_branch_one, w_out, preferred_element_type=jnp.float32)
    grad_query, grad_keys, grad_values = attend_pull(grad_attended)
    grad_query_bf = grad_query.astype(jnp.bfloat16)
    grad_kv = jnp.concatenate(
        [grad_keys.astype(jnp.bfloat16), grad_values.astype(jnp.bfloat16)], axis=2
    )
    grad_q_w = contract_rows(grad_query_bf, normed_bf[:, 0])
    grad_kv_w = jnp.einsum("esf,esd->fd", grad_kv, normed_bf, preferred_element_type=jnp.float32)
    grad_normed = jnp.einsum("esf,fd->esd", grad_kv, w_qkv[D:], preferred_element_type=jnp.float32)
    grad_normed = grad_normed.at[:, 0].add(
        jnp.dot(grad_query_bf, w_qkv[:D], preferred_element_type=jnp.float32)
    )
    grad_slots, grad_ln1_gain, grad_ln1_shift = norm1_pull(grad_normed)
    grad_first = grad_slots[:, 0] + grad_residual
    grad_cls = jnp.sum(grad_first, axis=0)
    grad_pos = jnp.concatenate([grad_cls[None], jnp.sum(grad_slots[:, 1:], axis=0)], axis=0)
    grad_pieces = grad_slots[:, 1:].astype(jnp.bfloat16).reshape(-1, D)
    grad_outgoing = contract_rows(own_onehot, grad_pieces).astype(jnp.bfloat16)
    grad_incoming = lax.all_to_all(
        grad_outgoing.reshape(device_count, cap, D), BOTH, 0, 0, tiled=True
    ).reshape(device_count * cap, D)
    piece_grad = contract_rows(asked_onehot, grad_incoming)

    vec_local = jnp.concatenate(
        [
            grad_cls,
            grad_pos.reshape(-1),
            grad_ln1_gain,
            grad_ln1_shift,
            grad_ln2_gain,
            grad_ln2_shift,
            grad_final_gain,
            grad_final_shift,
            grad_bias_up,
            grad_bias_down,
            lax.dynamic_update_slice_in_dim(
                jnp.zeros((OUTW,), jnp.float32), grad_bias_own, me * feature_rows, 0
            ),
        ]
    )
    vec_grad = lax.psum(vec_local, BOTH)
    grad_qkv = jnp.concatenate([grad_q_w, grad_kv_w], axis=0)
    packed_term = jnp.concatenate(
        [
            matrix.reshape(narrow_count, matrix.shape[0] // narrow_count, D)
            for matrix in (grad_qkv, grad_out_w, grad_up, grad_down)
        ],
        axis=1,
    )
    term_rows = packed_term.shape[1]
    share = term_rows // wide_count
    packed_term = (
        packed_term.astype(jnp.bfloat16)
        .reshape(narrow_count, wide_count, share, D)
        .transpose(1, 0, 2, 3)
        .reshape(device_count, share, D)
    )
    terms = lax.all_to_all(packed_term, BOTH, 0, 0, tiled=True)
    share_sum = jnp.sum(terms.astype(jnp.float32), axis=0)
    main_grad = lax.all_gather(share_sum.astype(jnp.bfloat16), "wide", axis=0, tiled=True)
    proj_grad = lax.all_gather(grad_proj_own.astype(jnp.bfloat16), BOTH, axis=0, tiled=True)
    proj_rows = OUTW // narrow_count
    proj_grad = lax.dynamic_slice_in_dim(proj_grad, narrow_at * proj_rows, proj_rows, 0)
    grad_block = jnp.concatenate([main_grad, proj_grad], axis=0).astype(jnp.float32)
    momentum_block = MUON_BETA * mat_momentum[0] + grad_block
    update_block = grad_block + MUON_BETA * momentum_block
    segments = block_slices(update_block, narrow_count)
    grams = lax.psum(jnp.stack([gram_of(segment) for segment in segments]), "narrow")
    new_segments = []
    for position, (row_total, master_seg, segment) in enumerate(
        zip(matrix_rows(), block_slices(mat_master[0], narrow_count), segments)
    ):
        square = jnp.sum(jnp.diagonal(grams[position]))
        norm = jnp.sqrt(square) + 1e-07
        gram = grams[position] / (norm * norm)
        chain = None
        for sweep_index in range(5):
            squared = jnp.dot(gram, gram, precision=HIGH)
            poly = NEWTON_B * gram + NEWTON_C * squared + NEWTON_A * jnp.eye(D, dtype=jnp.float32)
            chain = poly if chain is None else jnp.dot(chain, poly, precision=HIGH)
            if sweep_index < 4:
                gram = jnp.dot(jnp.dot(gram, poly, precision=HIGH), poly, precision=HIGH)
        ortho = jnp.dot(segment / norm, chain, precision=HIGH)
        new_segments.append(
            master_seg * (1.0 - MUON_RATE * MUON_DECAY)
            - MUON_RATE * math.sqrt(row_total / D) * ortho
        )
    weight_block = jnp.concatenate(new_segments, axis=0)[None]
    ema_block = EMA_DECAY * mat_ema + (1.0 - EMA_DECAY) * weight_block
    return (
        text_embeds,
        piece_grad,
        grad_block[None],
        momentum_block[None],
        weight_block,
        ema_block,
    ) + adam(vec_grad, vec_master, vec_moment1, vec_moment2, vec_ema)


MESH_ID = pl.DeviceIdType.MESH
CORES = 2
CHIPS = 4
PLANES = 4
MAIN = 192
CHUNKS = 3
CHUNK = MAIN // CHUNKS
PROJ = 32
PART = MAIN + PLANES * PROJ
VROWS = 16


def place():
    wide_at = lax.axis_index("wide")
    plane = lax.axis_index("narrow")
    chip = wide_at // CORES
    core = lax.rem(wide_at, CORES)
    return wide_at, plane, chip, core


def enter(targets):
    barrier = pltpu.get_barrier_semaphore()
    for target in targets:
        pl.semaphore_signal(barrier, inc=1, device_id=target, device_id_type=MESH_ID)
    pl.semaphore_wait(barrier, len(targets))


def neighbours(wide_at, plane, chip, core):
    sibling = (chip * CORES + 1 - core, plane)
    chips = [(lax.rem(chip + k, CHIPS) * CORES + core, plane) for k in range(1, CHIPS)]
    planes = [(wide_at, lax.rem(plane + k, PLANES)) for k in range(1, PLANES)]
    return sibling, chips, planes


def remote(src, dst, sems, index, target):
    return pltpu.make_async_remote_copy(
        src_ref=src,
        dst_ref=dst,
        send_sem=sems[0].at[index],
        recv_sem=sems[1].at[index],
        device_id=target,
        device_id_type=MESH_ID,
    )


def reduce_kernel(
    main_ref,
    proj_ref,
    vec_ref,
    out_ref,
    vec_out_ref,
    near,
    first,
    far,
    second,
    deep,
    proj_far,
    part,
    vec_near,
    vec_far,
    vec_deep,
    load_sem,
    main_send,
    main_recv,
    far_send,
    far_recv,
    deep_send,
    deep_recv,
    done_send,
    done_recv,
    pass_send,
    pass_recv,
    proj_send,
    proj_recv,
    vec_send,
    vec_recv,
):
    wide_at, plane, chip, core = place()
    sibling, chips, planes = neighbours(wide_at, plane, chip, core)
    other = 1 - core
    own_main = pltpu.make_async_copy(main_ref.at[core], first, load_sem.at[0])
    own_main.start()
    enter([sibling] + chips + planes)

    vec_sems = (vec_send, vec_recv)
    vec_copies = [remote(vec_ref.at[other], vec_near, vec_sems, 0, sibling)]
    vec_copies[0].start()
    main_sems = (main_send, main_recv)
    near_copies = []
    for chunk in range(CHUNKS):
        copy = remote(main_ref.at[other, chunk], near.at[chunk], main_sems, chunk, sibling)
        copy.start()
        near_copies.append(copy)
    proj_sems = (proj_send, proj_recv)
    proj_copies = []
    for k, target in enumerate(chips):
        to_chip = lax.rem(chip + k + 1, CHIPS)
        copy = remote(proj_ref.at[to_chip], proj_far.at[chip], proj_sems, k, target)
        copy.start()
        proj_copies.append(copy)
    own_proj = pltpu.make_async_copy(proj_ref.at[chip], proj_far.at[chip], load_sem.at[1])
    own_proj.start()
    own_main.wait()

    vec_copies[0].wait_recv()
    vec_far[chip] = vec_ref[core] + vec_near[...]
    for k, target in enumerate(chips):
        copy = remote(vec_far.at[chip], vec_far.at[chip], vec_sems, 1 + k, target)
        copy.start()
        vec_copies.append(copy)

    far_sems = (far_send, far_recv)
    far_copies = []
    for chunk in range(CHUNKS):
        near_copies[chunk].wait_recv()

        @pl.loop(0, CHIPS * PLANES)
        def _(step, chunk=chunk):
            q = step // PLANES
            m = lax.rem(step, PLANES)
            first[chunk, q, m] = (
                first[chunk, q, m].astype(jnp.float32) + near[chunk, q, m].astype(jnp.float32)
            ).astype(jnp.bfloat16)

        copies = []
        for k, target in enumerate(chips):
            to_chip = lax.rem(chip + k + 1, CHIPS)
            copy = remote(
                first.at[chunk, to_chip],
                far.at[chunk, k],
                far_sems,
                chunk * 3 + k,
                target,
            )
            copy.start()
            copies.append(copy)
        far_copies.append(copies)

    for copy in vec_copies[1:4]:
        copy.wait()
    vec_deep[plane] = (vec_far[0] + vec_far[1]) + (vec_far[2] + vec_far[3])
    for k, target in enumerate(planes):
        copy = remote(vec_deep.at[plane], vec_deep.at[plane], vec_sems, 4 + k, target)
        copy.start()
        vec_copies.append(copy)

    deep_sems = (deep_send, deep_recv)
    own_proj.wait()
    for copy in proj_copies:
        copy.wait()
    proj_copies = []
    for k, target in enumerate(planes):
        to_plane = lax.rem(plane + k + 1, PLANES)
        copy = remote(
            proj_far.at[to_plane],
            part.at[pl.ds(MAIN + plane * PROJ, PROJ)],
            proj_sems,
            3 + k,
            target,
        )
        copy.start()
        proj_copies.append(copy)
    part[pl.ds(pl.multiple_of(MAIN + plane * PROJ, PROJ), PROJ), :] = proj_far[plane]

    deep_copies = []
    for chunk in range(CHUNKS):
        for copy in far_copies[chunk]:
            copy.wait_recv()

        @pl.loop(0, PLANES)
        def _(m, chunk=chunk):
            total = first[chunk, chip, m].astype(jnp.float32)
            for k in range(3):
                total = total + far[chunk, k, m].astype(jnp.float32)
            second[chunk, m] = total.astype(jnp.bfloat16)

        copies = []
        for k, target in enumerate(planes):
            to_plane = lax.rem(plane + k + 1, PLANES)
            copy = remote(
                second.at[chunk, to_plane],
                deep.at[chunk, k],
                deep_sems,
                chunk * 3 + k,
                target,
            )
            copy.start()
            copies.append(copy)
        deep_copies.append(copies)

    for copy in vec_copies[4:7]:
        copy.wait()
    vec_out_ref[core] = (vec_deep[0] + vec_deep[1]) + (vec_deep[2] + vec_deep[3])
    copy = remote(vec_out_ref.at[core], vec_out_ref.at[core], vec_sems, 7, sibling)
    copy.start()
    vec_copies.append(copy)

    done_sems = (done_send, done_recv)
    done_copies = []
    pieces = [(chunk * CHUNK, CHUNK) for chunk in range(CHUNKS)] + [(MAIN, PART - MAIN)]
    for index, (offset, size) in enumerate(pieces):
        rows = pl.ds(offset, size)
        if index < CHUNKS:
            for copy in deep_copies[index]:
                copy.wait_recv()
            total = second[index, plane].astype(jnp.float32)
            for k in range(3):
                total = total + deep[index, k].astype(jnp.float32)
            part[rows, :] = total.astype(jnp.bfloat16)
        else:
            for copy in proj_copies:
                copy.wait()
        copies = []
        for k, target in enumerate([sibling] + chips):
            copy = remote(
                part.at[rows], out_ref.at[wide_at, rows], done_sems, index * 4 + k, target
            )
            copy.start()
            copies.append(copy)
        done_copies.append(copies)
    own_part = pltpu.make_async_copy(part, out_ref.at[wide_at], load_sem.at[2])
    own_part.start()

    pass_sems = (pass_send, pass_recv)
    pass_copies = []
    for index, (offset, size) in enumerate(pieces):
        rows = pl.ds(offset, size)
        for k in range(3):
            done_copies[index][1 + k].wait_recv()
            source = lax.rem(chip + CHIPS - 1 - k, CHIPS) * CORES + core
            copy = remote(
                out_ref.at[source, rows], out_ref.at[source, rows], pass_sems, index * 3 + k, sibling
            )
            copy.start()
            pass_copies.append(copy)
    own_part.wait()
    for copies in done_copies:
        copies[0].wait_recv()
        for copy in copies:
            copy.wait_send()
    for copy in pass_copies:
        copy.wait()
    for copies in [near_copies] + far_copies + deep_copies:
        for copy in copies:
            copy.wait_send()
    vec_copies[0].wait_send()
    vec_copies[7].wait()


def reduce_grads(main, proj, vec):
    dma = pltpu.SemaphoreType.DMA
    bf = jnp.bfloat16
    return pl.pallas_call(
        reduce_kernel,
        out_shape=(
            jax.ShapeDtypeStruct((CORES * CHIPS, PART, D), bf),
            jax.ShapeDtypeStruct((CORES, VROWS, D), jnp.float32),
        ),
        in_specs=[
            pl.BlockSpec(memory_space=pl.ANY),
            pl.BlockSpec(memory_space=pl.ANY),
            pl.BlockSpec(memory_space=pltpu.VMEM),
        ],
        out_specs=(
            pl.BlockSpec(memory_space=pl.ANY),
            pl.BlockSpec(memory_space=pltpu.VMEM),
        ),
        scratch_shapes=[
            pltpu.VMEM((CHUNKS, CHIPS, PLANES, CHUNK, D), bf),
            pltpu.VMEM((CHUNKS, CHIPS, PLANES, CHUNK, D), bf),
            pltpu.VMEM((CHUNKS, 3, PLANES, CHUNK, D), bf),
            pltpu.VMEM((CHUNKS, PLANES, CHUNK, D), bf),
            pltpu.VMEM((CHUNKS, 3, CHUNK, D), bf),
            pltpu.VMEM((CHIPS, PROJ, D), bf),
            pltpu.VMEM((PART, D), bf),
            pltpu.VMEM((VROWS, D), jnp.float32),
            pltpu.VMEM((CHIPS, VROWS, D), jnp.float32),
            pltpu.VMEM((PLANES, VROWS, D), jnp.float32),
            dma((3,)),
            dma((CHUNKS,)),
            dma((CHUNKS,)),
            dma((CHUNKS * 3,)),
            dma((CHUNKS * 3,)),
            dma((CHUNKS * 3,)),
            dma((CHUNKS * 3,)),
            dma(((CHUNKS + 1) * 4,)),
            dma(((CHUNKS + 1) * 4,)),
            dma(((CHUNKS + 1) * 3,)),
            dma(((CHUNKS + 1) * 3,)),
            dma((6,)),
            dma((6,)),
            dma((8,)),
            dma((8,)),
        ],
        compiler_params=pltpu.CompilerParams(
            collective_id=3, has_side_effects=True, vmem_limit_bytes=40 * 2**20
        ),
        name="reduce_grads",
    )(main, proj, vec)

TILE = 128
STRIP = D // PLANES
OWNERS = (6, 7, 2, 4, 0)
BLOCK_TILES = (3, 1, 4, 4, 8)
MOST_TILES = max(BLOCK_TILES)


def halves(value):
    high = value.astype(jnp.bfloat16)
    return high, (value - high.astype(jnp.float32)).astype(jnp.bfloat16)


def plain_dot(left, right):
    return jnp.dot(left, right, preferred_element_type=jnp.float32)


def split_dot(left, right):
    return plain_dot(left[0], right[0]) + (
        plain_dot(left[0], right[1]) + plain_dot(left[1], right[0])
    )


def newton_kernel(
    grad_ref,
    momentum_ref,
    out_ref,
    grad_tiles,
    momentum_tiles,
    update_high,
    update_low,
    gram,
    poly,
    chain,
    pieces,
    rows_out,
    load_sem,
    gram_send,
    gram_recv,
    sum_send,
    sum_recv,
    rows_send,
    rows_recv,
    pass_send,
    pass_recv,
    local_sem,
):
    wide_at, plane, chip, core = place()
    sibling, chips, planes = neighbours(wide_at, plane, chip, core)
    tile_count = jnp.int32(0)
    tile_first = jnp.int32(0)
    begin = 0
    for owner, count in zip(OWNERS, BLOCK_TILES):
        tile_count = tile_count + jnp.where(wide_at == owner, count, 0)
        tile_first = tile_first + jnp.where(wide_at == owner, begin, 0)
        begin = begin + count
    owning = tile_count > 0

    def tile_rows(tile):
        return pl.ds(pl.multiple_of(tile * TILE, TILE), TILE)

    def loads(tile):
        source = tile_rows(tile_first + tile)
        return (
            pltpu.make_async_copy(grad_ref.at[source], grad_tiles.at[tile], load_sem.at[0, tile]),
            pltpu.make_async_copy(
                momentum_ref.at[source], momentum_tiles.at[tile], load_sem.at[1, tile]
            ),
        )

    @pl.loop(0, tile_count)
    def _(tile):
        for copy in loads(tile):
            copy.start()

    enter([sibling] + chips + planes)

    gram_sems = (gram_send, gram_recv)
    sum_sems = (sum_send, sum_recv)

    def transposed_dot(left, right):
        return lax.dot_general(
            left, right, (((0,), (0,)), ((), ())), preferred_element_type=jnp.float32
        )

    @pl.when(owning)
    def _():
        gram[...] = jnp.zeros_like(gram)
        poly[...] = jnp.zeros_like(poly)

        @pl.loop(0, tile_count)
        def _(tile):
            for copy in loads(tile):
                copy.wait()
            update = grad_tiles[tile] + MUON_BETA * momentum_tiles[tile]
            high, low = halves(update)
            update_high[tile] = high
            update_low[tile] = low
            gram[...] += transposed_dot(high, high)
            poly[...] += transposed_dot(high, low)

        gram[...] += poly[...] + poly[...].T
        copies = []
        for k, target in enumerate(planes):
            to_plane = lax.rem(plane + k + 1, PLANES)
            copy = remote(
                gram.at[pl.ds(pl.multiple_of(to_plane * STRIP, STRIP), STRIP)],
                pieces.at[plane],
                gram_sems,
                k,
                target,
            )
            copy.start()
            copies.append(copy)
        own_strip = pl.ds(pl.multiple_of(plane * STRIP, STRIP), STRIP)
        pieces[plane] = gram[own_strip, :]
        for copy in copies:
            copy.wait()
        chain[own_strip, :] = (pieces[0] + pieces[1]) + (pieces[2] + pieces[3])
        copies = []
        for k, target in enumerate(planes):
            copy = remote(chain.at[own_strip], chain.at[own_strip], sum_sems, k, target)
            copy.start()
            copies.append(copy)
        for copy in copies:
            copy.wait()

        diagonal = lax.broadcasted_iota(jnp.int32, (D, D), 0) == lax.broadcasted_iota(
            jnp.int32, (D, D), 1
        )
        square = jnp.sum(jnp.where(diagonal, chain[...], 0.0))
        norm = jnp.sqrt(jnp.full((1, 1), square)) + 1e-07
        inverse = 1.0 / norm
        gram[...] = chain[...] * (inverse * inverse)

        def make_poly():
            value = gram[...]
            parts = halves(value)
            diagonal = lax.broadcasted_iota(jnp.int32, (D, D), 0) == lax.broadcasted_iota(
                jnp.int32, (D, D), 1
            )
            poly[...] = (
                NEWTON_B * value
                + NEWTON_C * split_dot(parts, parts)
                + jnp.where(diagonal, NEWTON_A, 0.0)
            )

        def next_gram():
            parts = halves(poly[...])
            half_way = split_dot(halves(gram[...]), parts)
            gram[...] = split_dot(halves(half_way), parts)

        def extend():
            chain[...] = split_dot(halves(chain[...]), halves(poly[...]))

        make_poly()
        chain[...] = poly[...]
        next_gram()

        @pl.loop(0, 3)
        def _(sweep):
            make_poly()
            extend()
            next_gram()

        make_poly()
        extend()
        chain_parts = halves(chain[...] * inverse)

        @pl.loop(0, tile_count)
        def _(tile):
            rows_out[tile] = split_dot((update_high[tile], update_low[tile]), chain_parts).astype(
                jnp.bfloat16
            )

    row_sems = (rows_send, rows_recv)
    pass_sems = (pass_send, pass_recv)
    begin = 0
    for index, (owner, count) in enumerate(zip(OWNERS, BLOCK_TILES)):
        owner_chip, owner_core = divmod(owner, CORES)
        span = pl.ds(begin, count)
        begin = begin + count

        @pl.when(wide_at == owner)
        def _(index=index, count=count, span=span):
            for k, target in enumerate(chips + [sibling]):
                remote(
                    rows_out.at[pl.ds(0, count)], out_ref.at[span], row_sems, index * 4 + k, target
                ).start()
            pltpu.make_async_copy(
                rows_out.at[pl.ds(0, count)], out_ref.at[span], local_sem.at[0]
            ).start()

    begin = 0
    for index, (owner, count) in enumerate(zip(OWNERS, BLOCK_TILES)):
        owner_chip, owner_core = divmod(owner, CORES)
        span = pl.ds(begin, count)
        begin = begin + count
        for k in range(3):
            receiver = (owner_chip + k + 1) % CHIPS * CORES + owner_core

            @pl.when(wide_at == receiver)
            def _(index=index, span=span, k=k):
                remote(
                    out_ref.at[span], out_ref.at[span], row_sems, index * 4 + k, sibling
                ).wait_recv()
                remote(out_ref.at[span], out_ref.at[span], pass_sems, index, sibling).start()

    begin = 0
    for index, (owner, count) in enumerate(zip(OWNERS, BLOCK_TILES)):
        owner_chip, owner_core = divmod(owner, CORES)
        span = pl.ds(begin, count)
        begin = begin + count

        @pl.when(wide_at == owner)
        def _(index=index, count=count, span=span):
            for k, target in enumerate(chips + [sibling]):
                remote(
                    rows_out.at[pl.ds(0, count)], out_ref.at[span], row_sems, index * 4 + k, target
                ).wait_send()
            pltpu.make_async_copy(
                rows_out.at[pl.ds(0, count)], out_ref.at[span], local_sem.at[0]
            ).wait()

        @pl.when((core == owner_core) & (chip != owner_chip))
        def _(index=index, span=span):
            remote(out_ref.at[span], out_ref.at[span], pass_sems, index, sibling).wait_send()

        @pl.when((core != owner_core) & (chip != owner_chip))
        def _(index=index, span=span):
            remote(out_ref.at[span], out_ref.at[span], pass_sems, index, sibling).wait_recv()

        @pl.when((core != owner_core) & (chip == owner_chip))
        def _(index=index, span=span):
            remote(
                out_ref.at[span], out_ref.at[span], row_sems, index * 4 + 3, sibling
            ).wait_recv()


def newton_rows(grad_block, momentum_block):
    dma = pltpu.SemaphoreType.DMA
    tiles = grad_block.shape[0] // TILE
    scratch = [
        pltpu.VMEM((MOST_TILES, TILE, D), jnp.float32),
        pltpu.VMEM((MOST_TILES, TILE, D), jnp.float32),
        pltpu.VMEM((MOST_TILES, TILE, D), jnp.bfloat16),
        pltpu.VMEM((MOST_TILES, TILE, D), jnp.bfloat16),
        pltpu.VMEM((D, D), jnp.float32),
        pltpu.VMEM((D, D), jnp.float32),
        pltpu.VMEM((D, D), jnp.float32),
        pltpu.VMEM((PLANES, STRIP, D), jnp.float32),
        pltpu.VMEM((MOST_TILES, TILE, D), jnp.bfloat16),
        dma((2, MOST_TILES)),
        dma((3,)),
        dma((3,)),
        dma((3,)),
        dma((3,)),
        dma((20,)),
        dma((20,)),
        dma((5,)),
        dma((5,)),
        dma((1,)),
    ]
    return pl.pallas_call(
        newton_kernel,
        out_shape=jax.ShapeDtypeStruct((tiles, TILE, D), jnp.bfloat16),
        in_specs=[pl.BlockSpec(memory_space=pl.ANY)] * 2,
        out_specs=pl.BlockSpec(memory_space=pl.ANY),
        scratch_shapes=scratch,
        compiler_params=pltpu.CompilerParams(
            collective_id=4, has_side_effects=True, vmem_limit_bytes=48 * 2**20
        ),
        name="newton_rows",
    )(grad_block, momentum_block).reshape(grad_block.shape)

def spread_kernel(count, *refs):
    own = refs[:count]
    outs = refs[count : 2 * count]
    local_sem, send_sem, recv_sem = refs[2 * count :]
    wide_at, plane, chip, core = place()
    sibling, chips, planes = neighbours(wide_at, plane, chip, core)
    enter([sibling] + chips + planes)
    sems = (send_sem, recv_sem)
    pending = []
    firsts = []

    def send(src, dst, index, target):
        copy = remote(src, dst, sems, index, target)
        copy.start()
        pending.append(copy)
        return copy

    for item in range(count):
        base = item * 31
        spot = outs[item].at[plane, wide_at]
        local = pltpu.make_async_copy(own[item], spot, local_sem.at[item])
        local.start()
        pending.append(local)
        from_planes = [send(own[item], spot, base + k, planes[k]) for k in range(3)]
        from_chips = [send(own[item], spot, base + 3 + k, chips[k]) for k in range(3)]
        send(own[item], spot, base + 6, sibling)
        firsts.append((from_planes, [from_chips]))
    for k in range(3):
        for item in range(count):
            base = item * 31 + 7 + k * 4
            from_planes, from_chips = firsts[item]
            from_planes[k].wait_recv()
            spot = outs[item].at[lax.rem(plane + PLANES - 1 - k, PLANES), wide_at]
            from_chips.append([send(spot, spot, base + j, chips[j]) for j in range(3)])
            send(spot, spot, base + 3, sibling)
    for step in range(PLANES):
        for item in range(count):
            base = item * 31 + 19 + step * 3
            source_plane = plane if step == 0 else lax.rem(plane + PLANES - step, PLANES)
            for j in range(3):
                firsts[item][1][step][j].wait_recv()
                source = lax.rem(chip + CHIPS - 1 - j, CHIPS) * CORES + core
                spot = outs[item].at[source_plane, source]
                send(spot, spot, base + j, sibling)
    received = {id(copy) for from_planes, _ in firsts for copy in from_planes}
    received |= {id(copy) for _, groups in firsts for group in groups for copy in group}
    for copy in pending:
        if id(copy) in received:
            copy.wait_send()
        else:
            copy.wait()


def spread(parts, collective_id, name):
    dma = pltpu.SemaphoreType.DMA
    count = len(parts)
    return pl.pallas_call(
        partial(spread_kernel, count),
        out_shape=tuple(
            jax.ShapeDtypeStruct((PLANES, CHIPS * CORES) + part.shape, part.dtype)
            for part in parts
        ),
        in_specs=[pl.BlockSpec(memory_space=pl.ANY)] * count,
        out_specs=tuple(pl.BlockSpec(memory_space=pl.ANY) for _ in parts),
        scratch_shapes=[dma((count,)), dma((31 * count,)), dma((31 * count,))],
        compiler_params=pltpu.CompilerParams(collective_id=collective_id, has_side_effects=True),
        name=name,
    )(*parts)


def tell_kernel(own_ref, out_ref, send_sem, recv_sem):
    wide_at, plane, chip, core = place()
    wide_count = CHIPS * CORES
    peers = [
        (lax.rem(wide_at + k // PLANES, wide_count), lax.rem(plane + k % PLANES, PLANES))
        for k in range(1, wide_count * PLANES)
    ]
    enter(peers)
    spot = out_ref.at[wide_at * PLANES + plane]
    copies = [
        remote(own_ref, spot, (send_sem, recv_sem), k, target) for k, target in enumerate(peers)
    ]
    for copy in copies:
        copy.start()
    out_ref[wide_at * PLANES + plane] = own_ref[...]
    for copy in copies:
        copy.wait()


def tell(values, collective_id):
    dma = pltpu.SemaphoreType.DMA
    every = PLANES * CHIPS * CORES
    return pl.pallas_call(
        tell_kernel,
        out_shape=jax.ShapeDtypeStruct((every,) + values.shape, values.dtype),
        in_specs=[pl.BlockSpec(memory_space=pltpu.VMEM)],
        out_specs=pl.BlockSpec(memory_space=pltpu.VMEM),
        scratch_shapes=[dma((every - 1,)), dma((every - 1,))],
        compiler_params=pltpu.CompilerParams(collective_id=collective_id, has_side_effects=True),
        name="tell_ids",
    )(values)

BANDS = 4
TEXT_TILE = 512


def band_onehot(ids, rows):
    place_in = lax.rem(ids, rows)
    spots = lax.broadcasted_iota(jnp.int32, (rows, ids.shape[1]), 0)
    return jnp.where(spots == place_in, 1.0, 0.0).astype(jnp.bfloat16)


def text_grad_kernel(ids_ref, mask_ref, cot_ref, out_ref, bias_ref, total):
    step = pl.program_id(0)
    rows = out_ref.shape[1]
    ids = ids_ref[...]
    onehot = band_onehot(ids, rows)
    band = jnp.where(mask_ref[...] > 0, ids // rows, -1)
    cot = cot_ref[...].astype(jnp.float32)
    banded = jnp.concatenate(
        [jnp.where(band == b, cot, 0.0).astype(jnp.bfloat16) for b in range(BANDS)], axis=0
    )

    @pl.when(step == 0)
    def _():
        total[...] = jnp.zeros_like(total)

    total[...] += lax.dot_general(
        onehot, banded, (((1,), (1,)), ((), ())), preferred_element_type=jnp.float32
    )

    @pl.when(step == pl.num_programs(0) - 1)
    def _():
        features = cot_ref.shape[0]
        sums = jnp.zeros((1, features), jnp.float32)
        for b in range(BANDS):
            rounded = total[:, b * features : (b + 1) * features].astype(jnp.bfloat16)
            out_ref[b] = rounded
            sums = sums + jnp.sum(rounded.astype(jnp.float32), axis=0, keepdims=True)
        bias_ref[...] = sums


def text_grad(flat_ids, flat_mask, text_cot, all_entries):
    features, tokens = text_cot.shape
    rows = all_entries // BANDS
    row_spec = pl.BlockSpec((1, TEXT_TILE), lambda i: (0, i))
    return pl.pallas_call(
        text_grad_kernel,
        grid=(tokens // TEXT_TILE,),
        out_shape=(
            jax.ShapeDtypeStruct((BANDS, rows, features), jnp.bfloat16),
            jax.ShapeDtypeStruct((1, features), jnp.float32),
        ),
        in_specs=[row_spec, row_spec, pl.BlockSpec((features, TEXT_TILE), lambda i: (0, i))],
        out_specs=(
            pl.BlockSpec((BANDS, rows, features), lambda i: (0, 0, 0)),
            pl.BlockSpec((1, features), lambda i: (0, 0)),
        ),
        scratch_shapes=[pltpu.VMEM((rows, BANDS * features), jnp.float32)],
        compiler_params=pltpu.CompilerParams(vmem_limit_bytes=32 * 2**20),
        cost_estimate=pl.CostEstimate(
            flops=2 * rows * tokens * BANDS * features, bytes_accessed=4 * 2**20, transcendentals=0
        ),
        name="text_grad",
    )(flat_ids[None], flat_mask[None], text_cot)


def table_kernel(entries_ref, proj_ref, bias_ref, grad_ref, table_ref, out_ref):
    features = proj_ref.shape[0]
    count = entries_ref.shape[2]
    wide_count = entries_ref.shape[1]
    per_band = grad_ref.shape[1] // count
    total = jnp.zeros(out_ref.shape, jnp.float32)
    for block in range(PLANES * wide_count):
        rows = entries_ref[block % PLANES, block // PLANES]
        band, spot = divmod(block, per_band)
        values = lax.dot_general(
            proj_ref[...], rows, (((1,), (1,)), ((), ())), preferred_element_type=jnp.float32
        )
        table_ref[band * features : (band + 1) * features, spot * count : (spot + 1) * count] = (
            values + bias_ref[...]
        ).astype(jnp.bfloat16)
        total = total + lax.dot_general(
            grad_ref[band, spot * count : (spot + 1) * count, :],
            rows,
            (((0,), (0,)), ((), ())),
            preferred_element_type=jnp.float32,
        )
    out_ref[...] = total.astype(jnp.bfloat16)


def table_and_grad(every, proj_own, bias_own, grad_own):
    features = proj_own.shape[0]
    rows = grad_own.shape[1]
    return pl.pallas_call(
        table_kernel,
        out_shape=(
            jax.ShapeDtypeStruct((BANDS * features, rows), jnp.bfloat16),
            jax.ShapeDtypeStruct((features, D), jnp.bfloat16),
        ),
        in_specs=[pl.BlockSpec(memory_space=pltpu.VMEM)] * 4,
        out_specs=(pl.BlockSpec(memory_space=pltpu.VMEM),) * 2,
        compiler_params=pltpu.CompilerParams(vmem_limit_bytes=32 * 2**20),
        name="table_and_grad",
    )(every, proj_own, bias_own, grad_own)


def text_kernel(ids_ref, mask_ref, table_ref, out_ref):
    features = out_ref.shape[0]
    rows = table_ref.shape[1]
    ids = ids_ref[...]
    values = jnp.dot(
        table_ref[...], band_onehot(ids, rows), preferred_element_type=jnp.float32
    )
    band = jnp.where(mask_ref[...] > 0, ids // rows, -1)
    total = jnp.zeros(out_ref.shape, jnp.float32)
    for b in range(BANDS):
        total = jnp.where(band == b, values[b * features : (b + 1) * features], total)
    out_ref[...] = total


def text_lookup(flat_ids, flat_mask, table):
    tokens = flat_ids.shape[0]
    features = table.shape[0] // BANDS
    row_spec = pl.BlockSpec((1, TEXT_TILE), lambda i: (0, i))
    return pl.pallas_call(
        text_kernel,
        grid=(tokens // TEXT_TILE,),
        out_shape=jax.ShapeDtypeStruct((features, tokens), jnp.float32),
        in_specs=[row_spec, row_spec, pl.BlockSpec(table.shape, lambda i: (0, 0))],
        out_specs=pl.BlockSpec((features, TEXT_TILE), lambda i: (0, i)),
        compiler_params=pltpu.CompilerParams(vmem_limit_bytes=32 * 2**20),
        cost_estimate=pl.CostEstimate(
            flops=2 * table.size * tokens, bytes_accessed=6 * 2**20, transcendentals=0
        ),
        name="text_lookup",
    )(flat_ids[None], flat_mask[None], table)

def dot_nt(left, right):
    return lax.dot_general(
        left, right, (((1,), (1,)), ((), ())), preferred_element_type=jnp.float32
    )


def dot_tn(left, right):
    return lax.dot_general(
        left, right, (((0,), (0,)), ((), ())), preferred_element_type=jnp.float32
    )


def two_part_dot(left, right):
    high, low = halves(left)
    return plain_dot(high, right) + plain_dot(low, right)


def normalize(values):
    center = values - jnp.mean(values, axis=-1, keepdims=True)
    spread = jnp.mean(center * center, axis=-1, keepdims=True)
    scale = lax.rsqrt(spread + 1e-05)
    return center * scale, scale


def normalize_back(grad, gain, hat, scale):
    grad_hat = grad * gain
    return scale * (
        grad_hat
        - jnp.mean(grad_hat, axis=-1, keepdims=True)
        - hat * jnp.mean(grad_hat * hat, axis=-1, keepdims=True)
    )


def over_rows(values):
    return jnp.sum(values, axis=0, keepdims=True)


def body_kernel(
    incoming_ref,
    spots_ref,
    live_ref,
    packed_ref,
    grad_ref,
    cls_ref,
    pos_ref,
    norms_ref,
    bias_up_ref,
    bias_down_ref,
    z_ref,
    main_ref,
    outgoing_ref,
    vec_ref,
    wide_ref,
    onehot,
    hats,
    scales,
    normed,
    keys,
    probs,
    grad_kv,
    grad_normed,
    grad_pieces,
    active,
    slope,
    sums,
    qkv_parts,
    out_parts,
    up_parts,
    down_parts,
    proj_parts,
    load_sem,
):
    loads = []
    begin = 0
    for index, part in enumerate((qkv_parts, out_parts, up_parts, down_parts, proj_parts)):
        size = part.shape[2]
        copy = pltpu.make_async_copy(
            packed_ref.at[:, :, pl.ds(begin, size)], part, load_sem.at[index]
        )
        copy.start()
        loads.append(copy)
        begin = begin + size
    entries = z_ref.shape[0]
    spot_count = incoming_ref.shape[0]
    gain_one, shift_one = norms_ref[0:1, :], norms_ref[1:2, :]
    gain_two, shift_two = norms_ref[2:3, :], norms_ref[3:4, :]
    gain_end, shift_end = norms_ref[4:5, :], norms_ref[5:6, :]

    def slot_rows(slot):
        return pl.ds(pl.multiple_of(slot * entries, entries), entries)

    def piece_lanes(slot):
        return pl.ds(pl.multiple_of((slot - 1) * entries, entries), entries)

    @pl.loop(1, SLOTS)
    def _(slot):
        places = lax.broadcasted_iota(jnp.int32, (spot_count, entries), 0)
        chosen = jnp.where(places == spots_ref[pl.ds(slot, 1), :], 1.0, 0.0).astype(jnp.bfloat16)
        onehot[:, piece_lanes(slot)] = chosen
        hats[slot_rows(slot), :] = dot_tn(chosen, incoming_ref[...]) + pos_ref[pl.ds(slot, 1), :]

    def matrix_rows_of(part, begin, end):
        size = part.shape[2] * part.shape[1]
        return part[...].reshape(part.shape[0] * size, D)[begin:end, :]

    for copy in loads:
        copy.wait()
    first_row = cls_ref[...] + pos_ref[0:1, :]
    hats[0:entries, :] = jnp.broadcast_to(first_row, (entries, D))
    sums[...] = jnp.zeros_like(sums)

    @pl.loop(0, SLOTS)
    def _(slot):
        rows = slot_rows(slot)
        hat, scale = normalize(hats[rows, :])
        hats[rows, :] = hat
        scales[rows, :] = jnp.broadcast_to(scale, (entries, 128))
        part = (hat * gain_one + shift_one).astype(jnp.bfloat16)
        normed[rows, :] = part
        keys[rows, :] = dot_nt(part, matrix_rows_of(qkv_parts, D, 3 * D))

    query = dot_nt(normed[0:entries, :], matrix_rows_of(qkv_parts, 0, D))
    lane_head = lax.broadcasted_iota(jnp.int32, (D, 128), 0) // HDIM
    to_heads = jnp.where(
        lane_head == lax.broadcasted_iota(jnp.int32, (D, 128), 1), 1.0, 0.0
    ).astype(jnp.bfloat16)
    head_lane = lax.broadcasted_iota(jnp.int32, (128, D), 1) // HDIM
    from_heads = jnp.where(
        head_lane == lax.broadcasted_iota(jnp.int32, (128, D), 0), 1.0, 0.0
    ).astype(jnp.bfloat16)
    root = 1.0 / math.sqrt(HDIM)
    scores = []
    for slot in range(SLOTS):
        rows = slice(slot * entries, (slot + 1) * entries)
        value = two_part_dot(query * keys[rows, 0:D], to_heads) * root
        scores.append(jnp.where(live_ref[:, slot : slot + 1] > 0, value, -1e30))
    top = scores[0]
    for value in scores[1:]:
        top = jnp.maximum(top, value)
    scores = [jnp.exp(value - top) for value in scores]
    whole = scores[0]
    for value in scores[1:]:
        whole = whole + value
    attended = jnp.zeros((entries, D), jnp.float32)
    for slot in range(SLOTS):
        rows = slice(slot * entries, (slot + 1) * entries)
        share = scores[slot] / whole
        probs[rows, :] = share
        attended = attended + two_part_dot(share, from_heads) * keys[rows, D:]
    attended_bf = attended.astype(jnp.bfloat16)
    residual = first_row + dot_nt(attended_bf, matrix_rows_of(out_parts, 0, D))
    hat_two, scale_two = normalize(residual)
    normed_two = (hat_two * gain_two + shift_two).astype(jnp.bfloat16)
    span = 512
    second = residual + bias_down_ref[...]
    for begin in range(0, FF, span):
        lanes = slice(begin, begin + span)
        gate = dot_nt(normed_two, up_parts[begin // span].reshape(span, D)) + bias_up_ref[:, lanes]
        square = gate * gate
        bend = jnp.tanh(math.sqrt(2.0 / math.pi) * (gate + 0.044715 * square * gate))
        part = (0.5 * gate * (1.0 + bend)).astype(jnp.bfloat16)
        active[:, lanes] = part
        slope[:, lanes] = 0.5 * (1.0 + bend) + 0.5 * gate * (1.0 - bend * bend) * (
            math.sqrt(2.0 / math.pi) * (1.0 + 3.0 * 0.044715 * square)
        )
        second = second + plain_dot(part, down_parts[begin // span].reshape(span, D))
    hat_end, scale_end = normalize(second)
    z_ref[...] = (hat_end * gain_end + shift_end).astype(jnp.bfloat16)

    count = grad_ref.shape[0]
    width = grad_ref.shape[2]
    grad_z = jnp.zeros((entries, D), jnp.float32)
    for source in range(count):
        grad_z = grad_z + plain_dot(
            grad_ref[source], proj_parts[source // 8, source % 8]
        )
    vec_ref[...] = jnp.zeros_like(vec_ref)
    vec_ref[13:14, :] = over_rows(grad_z * hat_end)
    vec_ref[14:15, :] = over_rows(grad_z)
    grad_second = normalize_back(grad_z, gain_end, hat_end, scale_end)
    branch_two = grad_second.astype(jnp.bfloat16)
    vec_ref[15:16, :] = over_rows(branch_two.astype(jnp.float32))

    def store(value, plane, chunk, height, offset):
        for chip in range(CHIPS):
            for core in range(CORES):
                at = (chip * CORES + core) * height
                main_ref[core, chunk, chip, plane, offset : offset + height, :] = value[
                    at : at + height, :
                ].astype(jnp.bfloat16)

    grad_two = jnp.zeros((entries, D), jnp.float32)
    for plane in range(PLANES):
        lanes = slice(plane * span, (plane + 1) * span)
        store(dot_tn(active[:, lanes], branch_two), plane, 0, 64, 0)
        gate_grad = (dot_nt(branch_two, down_parts[plane].reshape(span, D)) * slope[:, lanes]).astype(jnp.bfloat16)
        wide_ref[:, lanes] = over_rows(gate_grad.astype(jnp.float32))
        store(dot_tn(gate_grad, normed_two), plane, 1, 64, 0)
        grad_two = grad_two + plain_dot(gate_grad, up_parts[plane].reshape(span, D))
    vec_ref[11:12, :] = over_rows(grad_two * hat_two)
    vec_ref[12:13, :] = over_rows(grad_two)
    grad_residual = grad_second + normalize_back(grad_two, gain_two, hat_two, scale_two)
    branch_one = grad_residual.astype(jnp.bfloat16)
    grad_out = dot_tn(branch_one, attended_bf)
    for plane in range(PLANES):
        store(grad_out[plane * 128 : (plane + 1) * 128, :], plane, 2, 16, 0)
    grad_attended = plain_dot(branch_one, matrix_rows_of(out_parts, 0, D))

    inner = jnp.zeros((entries, 128), jnp.float32)
    slides = []
    for slot in range(SLOTS):
        rows = slice(slot * entries, (slot + 1) * entries)
        value = two_part_dot(grad_attended * keys[rows, D:], to_heads)
        slides.append(value)
        inner = inner + probs[rows, :] * value
    grad_query = jnp.zeros((entries, D), jnp.float32)
    for slot in range(SLOTS):
        rows = slice(slot * entries, (slot + 1) * entries)
        share = probs[rows, :]
        grad_kv[rows, D:] = (two_part_dot(share, from_heads) * grad_attended).astype(jnp.bfloat16)
        push = two_part_dot(share * (slides[slot] - inner), from_heads) * root
        grad_query = grad_query + push * keys[rows, 0:D]
        grad_kv[rows, 0:D] = (push * query).astype(jnp.bfloat16)
    query_bf = grad_query.astype(jnp.bfloat16)

    grad_q = dot_tn(query_bf, normed[0:entries, :])
    grad_k = dot_tn(grad_kv[:, 0:D], normed[...])
    grad_v = dot_tn(grad_kv[:, D:], normed[...])
    third = D * 3 // PLANES
    every = jnp.concatenate([grad_q, grad_k, grad_v], axis=0)
    for plane in range(PLANES):
        store(every[plane * third : (plane + 1) * third, :], plane, 2, 48, 16)

    @pl.loop(0, SLOTS)
    def _(slot):
        rows = slot_rows(slot)
        grad_normed[rows, :] = plain_dot(grad_kv[rows, :], matrix_rows_of(qkv_parts, D, 3 * D))

    grad_normed[0:entries, :] += plain_dot(query_bf, matrix_rows_of(qkv_parts, 0, D))

    @pl.loop(0, SLOTS)
    def _(slot):
        rows = slot_rows(slot)
        grad = grad_normed[rows, :]
        hat = hats[rows, :]
        sums[0:1, :] += over_rows(grad * hat)
        sums[1:2, :] += over_rows(grad)
        grad_x = normalize_back(grad, gain_one, hat, scales[rows, 0:1])
        vec_ref[pl.ds(1 + slot, 1), :] = over_rows(grad_x)

        @pl.when(slot > 0)
        def _():
            grad_pieces[pl.ds(pl.multiple_of((slot - 1) * entries, entries), entries), :] = (
                grad_x.astype(jnp.bfloat16)
            )

    vec_ref[9:11, :] = sums[0:2, :]
    vec_ref[1:2, :] += over_rows(grad_residual)
    vec_ref[0:1, :] = vec_ref[1:2, :]
    tile = 256
    for begin in range(0, spot_count, tile):
        outgoing_ref[begin : begin + tile, :] = plain_dot(
            onehot[begin : begin + tile, :], grad_pieces[...]
        ).astype(jnp.bfloat16)


def body(incoming, spots, live, packed, grad_table, vectors):
    cls_vec, positions, norms, bias_up, bias_down = vectors
    entries = live.shape[0]
    spot_count = incoming.shape[0]
    rows = entries * SLOTS
    f32, bf = jnp.float32, jnp.bfloat16
    vmem = pl.BlockSpec(memory_space=pltpu.VMEM)
    return pl.pallas_call(
        body_kernel,
        out_shape=(
            jax.ShapeDtypeStruct((entries, D), bf),
            jax.ShapeDtypeStruct((CORES, CHUNKS, CHIPS, PLANES, CHUNK, D), bf),
            jax.ShapeDtypeStruct((spot_count, D), bf),
            jax.ShapeDtypeStruct((16, D), f32),
            jax.ShapeDtypeStruct((1, FF), f32),
        ),
        in_specs=[vmem] * 3 + [pl.BlockSpec(memory_space=pl.ANY)] + [vmem] * 6,
        out_specs=(vmem,) * 5,
        scratch_shapes=[
            pltpu.VMEM((spot_count, entries * PSLOTS), bf),
            pltpu.VMEM((rows, D), f32),
            pltpu.VMEM((rows, 128), f32),
            pltpu.VMEM((rows, D), bf),
            pltpu.VMEM((rows, 2 * D), f32),
            pltpu.VMEM((rows, 128), f32),
            pltpu.VMEM((rows, 2 * D), bf),
            pltpu.VMEM((rows, D), f32),
            pltpu.VMEM((entries * PSLOTS, D), bf),
            pltpu.VMEM((entries, FF), bf),
            pltpu.VMEM((entries, FF), f32),
            pltpu.VMEM((8, D), f32),
        ]
        + [
            pltpu.VMEM((PLANES, CHIPS * CORES, size // (PLANES * CHIPS * CORES), D), bf)
            for size in matrix_rows()
        ]
        + [pltpu.SemaphoreType.DMA((5,))],
        compiler_params=pltpu.CompilerParams(vmem_limit_bytes=60 * 2**20),
        name="body",
    )(
        incoming,
        spots,
        live,
        packed,
        grad_table,
        cls_vec,
        positions,
        norms,
        bias_up,
        bias_down,
    )


def own_weight_part(mat_master):
    wide_count = CHIPS * CORES
    wide_at = lax.axis_index("wide")
    parts = []
    for segment in block_slices(mat_master[0], PLANES):
        rows = segment.shape[0] // wide_count
        parts.append(
            lax.dynamic_slice_in_dim(segment, wide_at * rows, rows, 0).astype(jnp.bfloat16)
        )
    return jnp.concatenate(parts, axis=0)


def gather_ids(slot_ids):
    count = slot_ids.shape[0]
    lanes = 128
    rows = -(-count // (8 * lanes)) * 8
    padded = jnp.pad(slot_ids, (0, rows * lanes - count)).reshape(rows, lanes)
    every = tell(padded, 1)
    return every.reshape(every.shape[0], rows * lanes)[:, :count]


def asked_onehot_of(every_ids, group_rows, cap):
    me = lax.axis_index("wide") * PLANES + lax.axis_index("narrow")
    slot_count = every_ids.shape[1]
    asked = every_ids // group_rows == me
    before = (
        lax.broadcasted_iota(jnp.int32, (slot_count, slot_count), 0)
        < lax.broadcasted_iota(jnp.int32, (slot_count, slot_count), 1)
    )
    asked_rank = jnp.dot(
        asked.astype(jnp.bfloat16), before.astype(jnp.bfloat16), preferred_element_type=jnp.float32
    ).astype(jnp.int32)
    asked_rank = jnp.where(asked, asked_rank, -1)
    chosen = asked_rank[:, None, :] == lax.iota(jnp.int32, cap)[None, :, None]
    local_ids = every_ids - me * group_rows + 1
    asked_rows = jnp.sum(jnp.where(chosen, local_ids[:, None, :], 0), axis=2).reshape(-1) - 1
    return (asked_rows[:, None] == lax.iota(jnp.int32, group_rows)[None, :]).astype(jnp.bfloat16)


def own_spots_of(slot_ids, group_rows, cap):
    slot_count = slot_ids.shape[0]
    before = (
        lax.broadcasted_iota(jnp.int32, (slot_count, slot_count), 0)
        > lax.broadcasted_iota(jnp.int32, (slot_count, slot_count), 1)
    )
    own_group = slot_ids // group_rows
    same = (own_group[:, None] == own_group[None, :]) & before
    own_rank = jnp.sum(same.astype(jnp.int32), axis=1)
    return (own_group * cap + own_rank).reshape(-1, PSLOTS)


def total_grads(main, grad_proj, vec_local):
    vec_rows = CORES * VROWS
    rows = vec_local.reshape(-1, D)
    vec_in = jnp.pad(rows, ((0, vec_rows - rows.shape[0]), (0, 0)))
    parts, vec_sum = reduce_grads(
        main, grad_proj.reshape(CHIPS, PROJ, D), vec_in.reshape(CORES, VROWS, D)
    )
    vec_grad = vec_sum.reshape(-1)[: vec_local.shape[0]]
    spans = ((144, 48), (128, 16), (64, 64), (0, 64))
    segments = [parts[:, begin : begin + size].reshape(-1, D) for begin, size in spans]
    proj = parts[:, MAIN:].reshape(CHIPS, CORES, PLANES, PROJ, D)
    segments.append(proj.transpose(1, 2, 0, 3, 4).reshape(-1, D))
    return jnp.concatenate(segments, axis=0).astype(jnp.float32), vec_grad


def on_device(
    piece_table,
    piece_ids,
    slot_mask,
    text_ids,
    text_mask,
    text_cot,
    mat_master,
    mat_momentum,
    mat_ema,
    vec_master,
    vec_moment1,
    vec_moment2,
    vec_ema,
):
    device_count = PLANES * CHIPS * CORES
    me = lax.axis_index("wide") * PLANES + lax.axis_index("narrow")
    (
        cls_vec,
        positions,
        ln1_gain,
        ln1_shift,
        ln2_gain,
        ln2_shift,
        final_gain,
        final_shift,
        bias_up,
        bias_down,
        bias_out,
    ) = split_vectors(vec_master)
    entries = piece_ids.shape[0]
    slot_ids = piece_ids.reshape(-1)
    group_rows = piece_table.shape[0]
    cap = piece_cap(group_rows)
    flat_ids = text_ids.reshape(-1)
    flat_mask = text_mask.reshape(-1)
    feature_rows = text_cot.shape[0]

    every_ids = gather_ids(slot_ids)
    asked_onehot = asked_onehot_of(every_ids, group_rows, cap)
    outgoing = jnp.dot(asked_onehot, piece_table, preferred_element_type=jnp.float32)
    outgoing = outgoing.astype(jnp.bfloat16).reshape(device_count, cap, D)
    incoming = lax.all_to_all(outgoing, BOTH, 0, 0, tiled=True).reshape(device_count * cap, D)
    spots = own_spots_of(slot_ids, group_rows, cap)
    spots = jnp.pad(spots.T, ((1, 0), (0, 0)))
    live = jnp.concatenate([jnp.ones((entries, 1), jnp.int32), slot_mask], axis=1)
    live = jnp.pad(live.astype(jnp.float32), ((0, 0), (0, 128 - SLOTS)))

    flat_ids, _ = lax.optimization_barrier((flat_ids, outgoing))
    grad_own, grad_bias_own = text_grad(flat_ids, flat_mask, text_cot, entries * device_count)
    grad_table = lax.all_to_all(
        grad_own.reshape(device_count, entries, feature_rows), BOTH, 0, 0, tiled=True
    )
    packed = lax.all_gather(own_weight_part(mat_master), ("narrow", "wide"), axis=0)
    packed = packed.reshape(PLANES, CHIPS * CORES, -1, D)

    norms = jnp.stack([ln1_gain, ln1_shift, ln2_gain, ln2_shift, final_gain, final_shift])
    normed_three, main, grad_outgoing, vec_rows, grad_bias_up = body(
        incoming,
        spots,
        live,
        packed,
        grad_table,
        (cls_vec[None], positions, norms, bias_up[None], bias_down[None]),
    )
    grad_incoming = lax.all_to_all(
        grad_outgoing.reshape(device_count, cap, D), BOTH, 0, 0, tiled=True
    ).reshape(device_count * cap, D)
    (every_normed,) = spread([normed_three], 2, "spread_entries")
    proj_own = lax.dynamic_slice(
        packed, (me // (CHIPS * CORES), me % (CHIPS * CORES), MAIN, 0), (1, 1, feature_rows, D)
    )[0, 0]
    bias_own = lax.dynamic_slice_in_dim(bias_out, me * feature_rows, feature_rows, 0)
    table, grad_proj = table_and_grad(every_normed, proj_own, bias_own[:, None], grad_own)
    text_embeds = text_lookup(flat_ids, flat_mask, table)
    piece_grad = contract_rows(asked_onehot, grad_incoming)

    vec_local = jnp.concatenate(
        [
            vec_rows[:15].reshape(-1),
            grad_bias_up[0],
            vec_rows[15],
            lax.dynamic_update_slice_in_dim(
                jnp.zeros((OUTW,), jnp.float32), grad_bias_own[0], me * feature_rows, 0
            ),
        ]
    )
    grad_block, vec_grad = total_grads(main, grad_proj, vec_local)
    momentum_block = MUON_BETA * mat_momentum[0] + grad_block
    ortho = newton_rows(grad_block, momentum_block).astype(jnp.float32)
    row_scale = jnp.concatenate(
        [
            jnp.full((row_total // PLANES, 1), MUON_RATE * math.sqrt(row_total / D), jnp.float32)
            for row_total in matrix_rows()
        ],
        axis=0,
    )
    weight_block = (mat_master[0] * (1.0 - MUON_RATE * MUON_DECAY) - row_scale * ortho)[None]
    ema_block = EMA_DECAY * mat_ema + (1.0 - EMA_DECAY) * weight_block
    return (
        text_embeds,
        piece_grad,
        grad_block[None],
        momentum_block[None],
        weight_block,
        ema_block,
    ) + adam(vec_grad, vec_master, vec_moment1, vec_moment2, vec_ema)


def solution(mesh):
    in_specs = (
        P(("wide", "narrow"), None),
        P(("wide", "narrow"), None),
        P(("wide", "narrow"), None),
        P(),
        P(),
        P(("wide", "narrow"), None),
        P("narrow", None, None),
        P("narrow", None, None),
        P("narrow", None, None),
        P(),
        P(),
        P(),
        P(),
    )
    out_specs = (
        P(("wide", "narrow"), None),
        P(("wide", "narrow"), None),
        P("narrow", None, None),
        P("narrow", None, None),
        P("narrow", None, None),
        P("narrow", None, None),
        P(),
        P(),
        P(),
        P(),
        P(),
    )
    fits = mesh.shape["wide"] == CHIPS * CORES and mesh.shape["narrow"] == PLANES
    step = on_device if fits else on_device_plain
    return jax.shard_map(
        step, mesh=mesh, in_specs=in_specs, out_specs=out_specs, check_vma=False
    )
```

```python
from functools import partial
import math

import jax
import jax.numpy as jnp
from jax import lax
from jax.experimental import pallas as pl
from jax.experimental.pallas import tpu as pltpu
from jax.sharding import PartitionSpec as P

D = 512
HEADS = 8
HDIM = 64
FF = 2048
OUTW = 4096
SLOTS = 8
PSLOTS = 7
STEP = 10


HIGHEST = lax.Precision.HIGHEST
HIGH = lax.Precision.HIGH
MUON_RATE = 0.5
MUON_DECAY = 0.01
MUON_BETA = 0.95
ADAM_RATE = 0.5
ADAM_BETA1 = 0.9
ADAM_BETA2 = 0.95
ADAM_EPSILON = 1e-08
EMA_DECAY = 0.8
NEWTON_A = 3.4445
NEWTON_B = -4.775
NEWTON_C = 2.0315


def matrix_rows():
    return (3 * D, D, FF, FF, OUTW)


def unpack(packed, narrow_count):
    matrices = []
    offset = 0
    for row_total in matrix_rows():
        height = row_total // narrow_count
        matrices.append(packed[:, offset : offset + height, :].reshape(row_total, packed.shape[2]))
        offset = offset + height
    return matrices


def pack(matrices, narrow_count):
    return jnp.concatenate(
        [
            matrix.reshape(narrow_count, matrix.shape[0] // narrow_count, matrix.shape[1])
            for matrix in matrices
        ],
        axis=1,
    )


def block_slices(block, narrow_count):
    segments = []
    offset = 0
    for row_total in matrix_rows():
        height = row_total // narrow_count
        segments.append(block[offset : offset + height])
        offset = offset + height
    return segments


def split_vectors(vector):
    lengths = (D, SLOTS * D, D, D, D, D, D, D, FF, D, OUTW)
    chosen = []
    offset = 0
    for length in lengths:
        chosen.append(vector[offset : offset + length])
        offset = offset + length
    chosen[1] = chosen[1].reshape(SLOTS, D)
    return chosen


def layer_norm(values, gain, shift):
    center = values - jnp.mean(values, axis=-1, keepdims=True)
    spread = jnp.mean(center * center, axis=-1, keepdims=True)
    return center * lax.rsqrt(spread + 1e-05) * gain + shift


def gelu_tanh(values):
    return jax.nn.gelu(values, approximate=True)


def attend(query_rows, key_rows, value_rows, live_slots):
    entry_count = query_rows.shape[0]
    query_heads = query_rows.reshape(entry_count, HEADS, HDIM)
    key_heads = key_rows.reshape(entry_count, SLOTS, HEADS, HDIM)
    value_heads = value_rows.reshape(entry_count, SLOTS, HEADS, HDIM)
    scores = jnp.einsum("ehd,eshd->ehs", query_heads, key_heads, precision=HIGHEST) / math.sqrt(
        HDIM
    )
    scores = jnp.where(live_slots[:, None, :], scores, -1e30)
    scores = scores - jnp.max(scores, axis=-1, keepdims=True)
    expped = jnp.exp(scores)
    probabilities = expped / jnp.sum(expped, axis=-1, keepdims=True)
    mixed_heads = jnp.einsum("ehs,eshd->ehd", probabilities, value_heads, precision=HIGHEST)
    return mixed_heads.reshape(entry_count, D)


PIECE_CAPS = {1024: 58, 256: 16}
BOTH = ("wide", "narrow")


def piece_cap(group_rows):
    cap = PIECE_CAPS.get(group_rows, group_rows)
    return -(-cap // 16) * 16


def contract_rows(left, right):
    return lax.dot_general(
        left, right, (((0,), (0,)), ((), ())), preferred_element_type=jnp.float32
    )


def gram_of(block):
    return lax.dot_general(block, block, (((0,), (0,)), ((), ())), precision=HIGHEST)


def adam(vec_grad, vec_master, vec_moment1, vec_moment2, vec_ema):
    moment_one = ADAM_BETA1 * vec_moment1 + (1.0 - ADAM_BETA1) * vec_grad
    moment_two = ADAM_BETA2 * vec_moment2 + (1.0 - ADAM_BETA2) * vec_grad * vec_grad
    corrected_one = moment_one / (1.0 - ADAM_BETA1**STEP)
    corrected_two = moment_two / (1.0 - ADAM_BETA2**STEP)
    vec_weight = vec_master - ADAM_RATE * corrected_one / (jnp.sqrt(corrected_two) + ADAM_EPSILON)
    vec_ema_new = EMA_DECAY * vec_ema + (1.0 - EMA_DECAY) * vec_weight
    return vec_grad, moment_one, moment_two, vec_weight, vec_ema_new


def on_device_plain(
    piece_table,
    piece_ids,
    slot_mask,
    text_ids,
    text_mask,
    text_cot,
    mat_master,
    mat_momentum,
    mat_ema,
    vec_master,
    vec_moment1,
    vec_moment2,
    vec_ema,
):
    narrow_count = lax.axis_size("narrow")
    wide_count = lax.axis_size("wide")
    device_count = narrow_count * wide_count
    wide_at = lax.axis_index("wide")
    narrow_at = lax.axis_index("narrow")
    me = wide_at * narrow_count + narrow_at
    block_rows = mat_master.shape[1]
    own_rows = block_rows // wide_count
    own_part = lax.dynamic_slice_in_dim(mat_master[0], wide_at * own_rows, own_rows, 0)
    packed_bf = lax.all_gather(
        own_part.astype(jnp.bfloat16), ("narrow", "wide"), axis=0, tiled=True
    ).reshape(narrow_count, block_rows, D)
    w_qkv, w_out, w_up, w_down, w_proj = unpack(packed_bf, narrow_count)
    (
        cls_vec,
        positions,
        ln1_gain,
        ln1_shift,
        ln2_gain,
        ln2_shift,
        final_gain,
        final_shift,
        bias_up,
        bias_down,
        bias_out,
    ) = split_vectors(vec_master)
    entries = piece_ids.shape[0]
    slot_ids = piece_ids.reshape(-1)
    slot_count = slot_ids.shape[0]
    group_rows = piece_table.shape[0]
    cap = piece_cap(group_rows)
    every_ids = lax.all_gather(slot_ids, BOTH, axis=0, tiled=False)
    asked = every_ids // group_rows == me
    before = (
        lax.broadcasted_iota(jnp.int32, (slot_count, slot_count), 0)
        < lax.broadcasted_iota(jnp.int32, (slot_count, slot_count), 1)
    )
    asked_rank = jnp.dot(
        asked.astype(jnp.bfloat16), before.astype(jnp.bfloat16), preferred_element_type=jnp.float32
    ).astype(jnp.int32)
    asked_rank = jnp.where(asked, asked_rank, -1)
    chosen = asked_rank[:, None, :] == lax.iota(jnp.int32, cap)[None, :, None]
    local_ids = every_ids - me * group_rows + 1
    asked_rows = jnp.sum(jnp.where(chosen, local_ids[:, None, :], 0), axis=2).reshape(-1) - 1
    asked_onehot = (
        asked_rows[:, None] == lax.iota(jnp.int32, group_rows)[None, :]
    ).astype(jnp.bfloat16)
    outgoing = jnp.dot(asked_onehot, piece_table, preferred_element_type=jnp.float32)
    incoming = lax.all_to_all(
        outgoing.astype(jnp.bfloat16).reshape(device_count, cap, D), BOTH, 0, 0, tiled=True
    ).reshape(device_count * cap, D)
    own_group = slot_ids // group_rows
    same = (own_group[:, None] == own_group[None, :]) & before.T
    own_rank = jnp.sum(same.astype(jnp.int32), axis=1)
    own_spot = own_group * cap + own_rank
    own_onehot = (
        own_spot[:, None] == lax.iota(jnp.int32, device_count * cap)[None, :]
    ).astype(jnp.bfloat16)
    looked = jnp.dot(own_onehot, incoming, preferred_element_type=jnp.float32)
    pieces = looked.reshape(entries, PSLOTS, D)

    flat_ids = text_ids.reshape(-1)
    flat_mask = text_mask.reshape(-1)
    token_count = flat_ids.shape[0]
    feature_rows = text_cot.shape[0]
    all_entries = entries * device_count
    block_len = min(512, token_count)
    entry_index = lax.iota(jnp.int32, all_entries)

    def text_block(step_index, grad_cols):
        begin_at = step_index * block_len
        ids_now = lax.dynamic_slice_in_dim(flat_ids, begin_at, block_len)
        keep_mask = lax.dynamic_slice_in_dim(flat_mask, begin_at, block_len)
        onehot = (entry_index[:, None] == ids_now[None, :]).astype(jnp.bfloat16)
        cot_now = lax.dynamic_slice_in_dim(text_cot, begin_at, block_len, 1)
        masked_cot = jnp.where(keep_mask[None, :] > 0, cot_now, jnp.zeros_like(cot_now))
        return grad_cols + lax.dot_general(
            masked_cot, onehot, (((1,), (1,)), ((), ())), preferred_element_type=jnp.float32
        )

    grad_cols = lax.fori_loop(
        0, token_count // block_len, text_block, jnp.zeros((feature_rows, all_entries), jnp.float32)
    )
    grad_table_cols = grad_cols.astype(jnp.bfloat16)
    grad_table = lax.all_to_all(grad_table_cols, BOTH, split_axis=1, concat_axis=0, tiled=True)
    grad_bias_own = jnp.sum(grad_table_cols.astype(jnp.float32), axis=1)
    grad_normed_three = contract_rows(grad_table, w_proj)

    first_slot = jnp.broadcast_to(cls_vec + positions[0], (entries, 1, D))
    slots_x = jnp.concatenate([first_slot, pieces + positions[1:]], axis=1)
    live_slots = jnp.concatenate([jnp.ones((entries, 1), jnp.int32), slot_mask], axis=1) > 0
    normed, norm1_pull = jax.vjp(layer_norm, slots_x, ln1_gain, ln1_shift)
    normed_bf = normed.astype(jnp.bfloat16)
    query_rows = jnp.einsum(
        "ed,fd->ef", normed_bf[:, 0], w_qkv[:D], preferred_element_type=jnp.float32
    )
    key_value = jnp.einsum("esd,fd->esf", normed_bf, w_qkv[D:], preferred_element_type=jnp.float32)
    attended, attend_pull = jax.vjp(
        partial(attend, live_slots=live_slots), query_rows, key_value[:, :, :D], key_value[:, :, D:]
    )
    attended_bf = attended.astype(jnp.bfloat16)
    residual = slots_x[:, 0] + jnp.einsum(
        "ed,fd->ef", attended_bf, w_out, preferred_element_type=jnp.float32
    )
    normed_two, norm2_pull = jax.vjp(layer_norm, residual, ln2_gain, ln2_shift)
    normed_two_bf = normed_two.astype(jnp.bfloat16)
    gate_in = (
        jnp.einsum("ed,fd->ef", normed_two_bf, w_up, preferred_element_type=jnp.float32) + bias_up
    )
    active, gelu_pull = jax.vjp(gelu_tanh, gate_in)
    active_bf = active.astype(jnp.bfloat16)
    second_residual = residual + (
        jnp.dot(active_bf, w_down, preferred_element_type=jnp.float32) + bias_down
    )
    normed_three, norm3_pull = jax.vjp(layer_norm, second_residual, final_gain, final_shift)
    normed_three_bf = normed_three.astype(jnp.bfloat16)
    every_normed = lax.all_gather(normed_three_bf, BOTH, axis=0, tiled=True)
    proj_own = lax.dynamic_slice_in_dim(w_proj, me * feature_rows, feature_rows, 0)
    bias_own = lax.dynamic_slice_in_dim(bias_out, me * feature_rows, feature_rows, 0)
    table_cols = (
        jnp.einsum("fd,ed->fe", proj_own, every_normed, preferred_element_type=jnp.float32)
        + bias_own[:, None]
    )
    text_embeds = jnp.take(table_cols, flat_ids, axis=1) * flat_mask[None, :].astype(jnp.float32)
    grad_proj_own = jnp.dot(grad_table_cols, every_normed, preferred_element_type=jnp.float32)

    grad_second, grad_final_gain, grad_final_shift = norm3_pull(grad_normed_three)
    grad_branch_two = grad_second.astype(jnp.bfloat16)
    grad_bias_down = jnp.sum(grad_branch_two.astype(jnp.float32), axis=0)
    grad_down = contract_rows(active_bf, grad_branch_two)
    grad_active = jnp.einsum(
        "ed,fd->ef", grad_branch_two, w_down, preferred_element_type=jnp.float32
    )
    (grad_gate,) = gelu_pull(grad_active)
    grad_gate_bf = grad_gate.astype(jnp.bfloat16)
    grad_bias_up = jnp.sum(grad_gate_bf.astype(jnp.float32), axis=0)
    grad_up = contract_rows(grad_gate_bf, normed_two_bf)
    grad_normed_two = jnp.dot(grad_gate_bf, w_up, preferred_element_type=jnp.float32)
    grad_residual_norm, grad_ln2_gain, grad_ln2_shift = norm2_pull(grad_normed_two)
    grad_residual = grad_second + grad_residual_norm
    grad_branch_one = grad_residual.astype(jnp.bfloat16)
    grad_out_w = contract_rows(grad_branch_one, attended_bf)
    grad_attended = jnp.dot(grad_branch_one, w_out, preferred_element_type=jnp.float32)
    grad_query, grad_keys, grad_values = attend_pull(grad_attended)
    grad_query_bf = grad_query.astype(jnp.bfloat16)
    grad_kv = jnp.concatenate(
        [grad_keys.astype(jnp.bfloat16), grad_values.astype(jnp.bfloat16)], axis=2
    )
    grad_q_w = contract_rows(grad_query_bf, normed_bf[:, 0])
    grad_kv_w = jnp.einsum("esf,esd->fd", grad_kv, normed_bf, preferred_element_type=jnp.float32)
    grad_normed = jnp.einsum("esf,fd->esd", grad_kv, w_qkv[D:], preferred_element_type=jnp.float32)
    grad_normed = grad_normed.at[:, 0].add(
        jnp.dot(grad_query_bf, w_qkv[:D], preferred_element_type=jnp.float32)
    )
    grad_slots, grad_ln1_gain, grad_ln1_shift = norm1_pull(grad_normed)
    grad_first = grad_slots[:, 0] + grad_residual
    grad_cls = jnp.sum(grad_first, axis=0)
    grad_pos = jnp.concatenate([grad_cls[None], jnp.sum(grad_slots[:, 1:], axis=0)], axis=0)
    grad_pieces = grad_slots[:, 1:].astype(jnp.bfloat16).reshape(-1, D)
    grad_outgoing = contract_rows(own_onehot, grad_pieces).astype(jnp.bfloat16)
    grad_incoming = lax.all_to_all(
        grad_outgoing.reshape(device_count, cap, D), BOTH, 0, 0, tiled=True
    ).reshape(device_count * cap, D)
    piece_grad = contract_rows(asked_onehot, grad_incoming)

    vec_local = jnp.concatenate(
        [
            grad_cls,
            grad_pos.reshape(-1),
            grad_ln1_gain,
            grad_ln1_shift,
            grad_ln2_gain,
            grad_ln2_shift,
            grad_final_gain,
            grad_final_shift,
            grad_bias_up,
            grad_bias_down,
            lax.dynamic_update_slice_in_dim(
                jnp.zeros((OUTW,), jnp.float32), grad_bias_own, me * feature_rows, 0
            ),
        ]
    )
    vec_grad = lax.psum(vec_local, BOTH)
    grad_qkv = jnp.concatenate([grad_q_w, grad_kv_w], axis=0)
    packed_term = jnp.concatenate(
        [
            matrix.reshape(narrow_count, matrix.shape[0] // narrow_count, D)
            for matrix in (grad_qkv, grad_out_w, grad_up, grad_down)
        ],
        axis=1,
    )
    term_rows = packed_term.shape[1]
    share = term_rows // wide_count
    packed_term = (
        packed_term.astype(jnp.bfloat16)
        .reshape(narrow_count, wide_count, share, D)
        .transpose(1, 0, 2, 3)
        .reshape(device_count, share, D)
    )
    terms = lax.all_to_all(packed_term, BOTH, 0, 0, tiled=True)
    share_sum = jnp.sum(terms.astype(jnp.float32), axis=0)
    main_grad = lax.all_gather(share_sum.astype(jnp.bfloat16), "wide", axis=0, tiled=True)
    proj_grad = lax.all_gather(grad_proj_own.astype(jnp.bfloat16), BOTH, axis=0, tiled=True)
    proj_rows = OUTW // narrow_count
    proj_grad = lax.dynamic_slice_in_dim(proj_grad, narrow_at * proj_rows, proj_rows, 0)
    grad_block = jnp.concatenate([main_grad, proj_grad], axis=0).astype(jnp.float32)
    momentum_block = MUON_BETA * mat_momentum[0] + grad_block
    update_block = grad_block + MUON_BETA * momentum_block
    segments = block_slices(update_block, narrow_count)
    grams = lax.psum(jnp.stack([gram_of(segment) for segment in segments]), "narrow")
    new_segments = []
    for position, (row_total, master_seg, segment) in enumerate(
        zip(matrix_rows(), block_slices(mat_master[0], narrow_count), segments)
    ):
        square = jnp.sum(jnp.diagonal(grams[position]))
        norm = jnp.sqrt(square) + 1e-07
        gram = grams[position] / (norm * norm)
        chain = None
        for sweep_index in range(5):
            squared = jnp.dot(gram, gram, precision=HIGH)
            poly = NEWTON_B * gram + NEWTON_C * squared + NEWTON_A * jnp.eye(D, dtype=jnp.float32)
            chain = poly if chain is None else jnp.dot(chain, poly, precision=HIGH)
            if sweep_index < 4:
                gram = jnp.dot(jnp.dot(gram, poly, precision=HIGH), poly, precision=HIGH)
        ortho = jnp.dot(segment / norm, chain, precision=HIGH)
        new_segments.append(
            master_seg * (1.0 - MUON_RATE * MUON_DECAY)
            - MUON_RATE * math.sqrt(row_total / D) * ortho
        )
    weight_block = jnp.concatenate(new_segments, axis=0)[None]
    ema_block = EMA_DECAY * mat_ema + (1.0 - EMA_DECAY) * weight_block
    return (
        text_embeds,
        piece_grad,
        grad_block[None],
        momentum_block[None],
        weight_block,
        ema_block,
    ) + adam(vec_grad, vec_master, vec_moment1, vec_moment2, vec_ema)


MESH_ID = pl.DeviceIdType.MESH
CORES = 2
CHIPS = 4
PLANES = 4
MAIN = 192
CHUNKS = 3
CHUNK = MAIN // CHUNKS
PROJ = 32
PART = MAIN + PLANES * PROJ
VROWS = 16


def place():
    wide_at = lax.axis_index("wide")
    plane = lax.axis_index("narrow")
    chip = wide_at // CORES
    core = lax.rem(wide_at, CORES)
    return wide_at, plane, chip, core


def enter(targets):
    barrier = pltpu.get_barrier_semaphore()
    for target in targets:
        pl.semaphore_signal(barrier, inc=1, device_id=target, device_id_type=MESH_ID)
    pl.semaphore_wait(barrier, len(targets))


def neighbours(wide_at, plane, chip, core):
    sibling = (chip * CORES + 1 - core, plane)
    chips = [(lax.rem(chip + k, CHIPS) * CORES + core, plane) for k in range(1, CHIPS)]
    planes = [(wide_at, lax.rem(plane + k, PLANES)) for k in range(1, PLANES)]
    return sibling, chips, planes


def remote(src, dst, sems, index, target):
    return pltpu.make_async_remote_copy(
        src_ref=src,
        dst_ref=dst,
        send_sem=sems[0].at[index],
        recv_sem=sems[1].at[index],
        device_id=target,
        device_id_type=MESH_ID,
    )

OWNERS = (6, 7, 2, 4, 0)
BLOCK_TILES = (3, 1, 4, 4, 8)
MOST_TILES = max(BLOCK_TILES)
MAIN_TILES = 12
BANDS = 4
TEXT_TILE = 512
TILE = 128
SIDE = 2
STRIPS = 8
STRIP = D // STRIPS
PACKED = 640
PIECES = ((0, 64, 1024), (64, 64, 512), (128, 16, 384), (144, 48, 0))


def halves(value):
    high = value.astype(jnp.bfloat16)
    return high, (value - high.astype(jnp.float32)).astype(jnp.bfloat16)


def plain_dot(left, right):
    return jnp.dot(left, right, preferred_element_type=jnp.float32)


def split_dot(left, right):
    return plain_dot(left[0], right[0]) + (
        plain_dot(left[0], right[1]) + plain_dot(left[1], right[0])
    )


def dot_nt(left, right):
    return lax.dot_general(
        left, right, (((1,), (1,)), ((), ())), preferred_element_type=jnp.float32
    )


def dot_tn(left, right):
    return lax.dot_general(
        left, right, (((0,), (0,)), ((), ())), preferred_element_type=jnp.float32
    )


def band_onehot(ids, rows):
    place_in = lax.rem(ids, rows)
    spots = lax.broadcasted_iota(jnp.int32, (rows, ids.shape[1]), 0)
    return jnp.where(spots == place_in, 1.0, 0.0).astype(jnp.bfloat16)


def across(wide_at, plane, chip, core):
    x_at = lax.rem(chip, SIDE)
    x_chip = chip + 1 - 2 * x_at
    y_chip = lax.rem(chip + SIDE, CHIPS)
    return x_chip * CORES + core, y_chip * CORES + core


def owner_tiles(wide_at):
    tile_count = jnp.int32(0)
    tile_first = jnp.int32(0)
    begin = 0
    for owner, count in zip(OWNERS, BLOCK_TILES):
        tile_count = tile_count + jnp.where(wide_at == owner, count, 0)
        tile_first = tile_first + jnp.where(wide_at == owner, begin, 0)
        begin = begin + count
    return tile_count, tile_first


def settle_kernel(
    every,
    main_ref,
    vec_ref,
    grad_ref,
    proj_ref,
    bias_ref,
    momentum_ref,
    ids_ref,
    mask_ref,
    text_ref,
    sum_ref,
    proj_sum_ref,
    vec_out_ref,
    gram_ref,
    high_ref,
    low_ref,
    table_ref,
    text_tiles,
    near,
    first,
    x_first,
    y_first,
    x_second,
    y_second,
    second,
    deep,
    proj_own,
    proj_far,
    part,
    proj_part,
    vec_near,
    vec_far,
    vec_deep,
    main_tiles,
    proj_tiles,
    momentum_tiles,
    packs,
    pieces,
    totals,
    local_sem,
    tile_sem,
    text_sem,
    main_send,
    main_recv,
    far_send,
    far_recv,
    deep_send,
    deep_recv,
    done_send,
    done_recv,
    pass_send,
    pass_recv,
    proj_send,
    proj_recv,
    vec_send,
    vec_recv,
    gram_send,
    gram_recv,
):
    wide_at, plane, chip, core = place()
    sibling, chips, planes = neighbours(wide_at, plane, chip, core)
    x_wide, y_wide = across(wide_at, plane, chip, core)
    x_near, y_near = (x_wide, plane), (y_wide, plane)
    diagonal_wide = (CHIPS - 1 - chip) * CORES + core
    other = 1 - core
    x_at = lax.rem(chip, SIDE)
    y_at = chip // SIDE
    tile_count, tile_first = owner_tiles(wide_at)

    own_main = pltpu.make_async_copy(main_ref.at[core], first, local_sem.at[0])
    own_main.start()

    def momentum_load(tile):
        source = pl.ds(pl.multiple_of((tile_first + tile) * TILE, TILE), TILE)
        return pltpu.make_async_copy(
            momentum_ref.at[source], momentum_tiles.at[tile], tile_sem.at[0, tile]
        )

    @pl.loop(0, tile_count)
    def _(tile):
        momentum_load(tile).start()

    enter([sibling] + chips + planes)

    vec_sems = (vec_send, vec_recv)
    vec_copies = [remote(vec_ref.at[other], vec_near, vec_sems, 0, sibling)]
    vec_copies[0].start()
    main_sems = (main_send, main_recv)
    near_copies = []
    for chunk in range(CHUNKS):
        copy = remote(main_ref.at[other, chunk], near.at[chunk], main_sems, chunk, sibling)
        copy.start()
        near_copies.append(copy)

    count = every.shape[2]
    features = proj_ref.shape[0]
    wide_count = CHIPS * CORES
    per_band = grad_ref.shape[0] // BANDS
    total = jnp.zeros((features, D), jnp.float32)
    for block in range(PLANES * wide_count):
        rows = every[block % PLANES, block // PLANES]
        total = total + dot_tn(grad_ref[block], rows)
    proj_own[...] = total.astype(jnp.bfloat16).reshape(CHIPS, PROJ, D)

    proj_sems = (proj_send, proj_recv)
    proj_copies = []
    for k, target in enumerate(chips):
        to_chip = lax.rem(chip + k + 1, CHIPS)
        copy = remote(proj_own.at[to_chip], proj_far.at[chip], proj_sems, k, target)
        copy.start()
        proj_copies.append(copy)
    proj_far[chip] = proj_own[chip]

    own_main.wait()
    vec_copies[0].wait_recv()
    vec_far[chip] = vec_ref[core] + vec_near[...]
    for k, target in enumerate(chips):
        copy = remote(vec_far.at[chip], vec_far.at[chip], vec_sems, 1 + k, target)
        copy.start()
        vec_copies.append(copy)

    far_sems = (far_send, far_recv)
    lows, highs = pl.ds(0, 2), pl.ds(2, 2)
    firsts = []
    for chunk in range(CHUNKS):
        near_copies[chunk].wait_recv()

        @pl.loop(0, CHIPS * PLANES)
        def _(step, chunk=chunk):
            y, x, m = step // (SIDE * PLANES), lax.rem(step // PLANES, SIDE), lax.rem(step, PLANES)
            first[chunk, y, x, m] = (
                first[chunk, y, x, m].astype(jnp.float32)
                + near[chunk, y, x, m].astype(jnp.float32)
            ).astype(jnp.bfloat16)

        by_x = remote(
            first.at[chunk, :, 1 - x_at, lows], x_first.at[chunk], far_sems, chunk * 4, x_near
        )
        by_y = remote(
            first.at[chunk, 1 - y_at, :, highs], y_first.at[chunk], far_sems, chunk * 4 + 1, y_near
        )
        by_x.start()
        by_y.start()
        firsts.append((by_x, by_y))

    seconds = []

    def second_step(chunk):
        by_x, by_y = firsts[chunk]
        by_x.wait_recv()
        for y in range(SIDE):
            for m in range(2):
                first[chunk, y, x_at, m] = (
                    first[chunk, y, x_at, m].astype(jnp.float32)
                    + x_first[chunk, y, m].astype(jnp.float32)
                ).astype(jnp.bfloat16)
        next_y = remote(
            first.at[chunk, 1 - y_at, x_at, lows],
            y_second.at[chunk],
            far_sems,
            chunk * 4 + 2,
            y_near,
        )
        next_y.start()
        by_y.wait_recv()
        for x in range(SIDE):
            for m in range(2):
                first[chunk, y_at, x, 2 + m] = (
                    first[chunk, y_at, x, 2 + m].astype(jnp.float32)
                    + y_first[chunk, x, m].astype(jnp.float32)
                ).astype(jnp.bfloat16)
        next_x = remote(
            first.at[chunk, y_at, 1 - x_at, highs],
            x_second.at[chunk],
            far_sems,
            chunk * 4 + 3,
            x_near,
        )
        next_x.start()
        seconds.append((next_y, next_x))

    deep_sems = (deep_send, deep_recv)
    deep_copies = []

    def deep_step(chunk):
        next_y, next_x = seconds[chunk]
        next_y.wait_recv()
        for m in range(2):
            second[chunk, m] = (
                first[chunk, y_at, x_at, m].astype(jnp.float32)
                + y_second[chunk, m].astype(jnp.float32)
            ).astype(jnp.bfloat16)
        next_x.wait_recv()
        for m in range(2):
            second[chunk, 2 + m] = (
                first[chunk, y_at, x_at, 2 + m].astype(jnp.float32)
                + x_second[chunk, m].astype(jnp.float32)
            ).astype(jnp.bfloat16)
        copies = []
        for k, target in enumerate(planes):
            to_plane = lax.rem(plane + k + 1, PLANES)
            copy = remote(
                second.at[chunk, to_plane], deep.at[chunk, k], deep_sems, chunk * 3 + k, target
            )
            copy.start()
            copies.append(copy)
        deep_copies.append(copies)

    for block in range(PLANES * wide_count):
        rows = every[block % PLANES, block // PLANES]
        band, spot = divmod(block, per_band)
        table_ref[band * features : (band + 1) * features, spot * count : (spot + 1) * count] = (
            dot_nt(proj_ref[...], rows) + bias_ref[...]
        ).astype(jnp.bfloat16)

    text_rows = table_ref.shape[1]
    text_count = ids_ref.shape[1] // TEXT_TILE

    def text_copy(step):
        slot = lax.rem(step, 2)
        lanes = pl.ds(pl.multiple_of(step * TEXT_TILE, TEXT_TILE), TEXT_TILE)
        return pltpu.make_async_copy(text_tiles.at[slot], text_ref.at[:, lanes], text_sem.at[slot])

    def text_steps(begin, end):
        @pl.loop(begin, end)
        def _(step):
            lanes = pl.ds(pl.multiple_of(step * TEXT_TILE, TEXT_TILE), TEXT_TILE)
            ids = ids_ref[:, lanes]
            values = plain_dot(table_ref[...], band_onehot(ids, text_rows))
            band = jnp.where(mask_ref[:, lanes] > 0, ids // text_rows, -1)
            total = jnp.zeros((features, TEXT_TILE), jnp.float32)
            for b in range(BANDS):
                total = jnp.where(band == b, values[b * features : (b + 1) * features], total)

            @pl.when(step >= 2)
            def _():
                text_copy(step - 2).wait()

            text_tiles[lax.rem(step, 2)] = total
            text_copy(step).start()

    text_steps(0, 4)
    second_step(0)
    second_step(1)
    second_step(2)
    text_steps(4, 6)
    deep_step(0)
    deep_step(1)
    deep_step(2)

    for copy in vec_copies[1:4]:
        copy.wait()
    vec_deep[plane] = (vec_far[0] + vec_far[1]) + (vec_far[2] + vec_far[3])
    for k, target in enumerate(planes):
        copy = remote(vec_deep.at[plane], vec_deep.at[plane], vec_sems, 4 + k, target)
        copy.start()
        vec_copies.append(copy)

    for copy in proj_copies:
        copy.wait()
    proj_copies = []
    for k, target in enumerate(planes):
        to_plane = lax.rem(plane + k + 1, PLANES)
        copy = remote(proj_far.at[to_plane], proj_part.at[plane], proj_sems, 3 + k, target)
        copy.start()
        proj_copies.append(copy)
    proj_part[plane] = proj_far[plane]
    text_steps(6, 12)

    done_sems = (done_send, done_recv)
    pass_sems = (pass_send, pass_recv)
    done_copies = []
    locals_done = []

    def natural(index, wide):
        _, size, base = PIECES[index]
        return sum_ref.at[pl.ds(pl.multiple_of(base + wide * size, 16), size)]

    def proj_natural(at_chip, at_core):
        return proj_sum_ref.at[at_core, :, at_chip]

    def publish(index, src, spot):
        copies = []
        for k, target in enumerate([sibling] + chips):
            copy = remote(src, spot, done_sems, index * 4 + k, target)
            copy.start()
            copies.append(copy)
        done_copies.append(copies)
        copy = pltpu.make_async_copy(src, spot, local_sem.at[2 + index])
        copy.start()
        locals_done.append(copy)

    for chunk in range(CHUNKS):
        for copy in deep_copies[chunk]:
            copy.wait_recv()
        value = second[chunk, plane].astype(jnp.float32)
        for k in range(3):
            value = value + deep[chunk, k].astype(jnp.float32)
        part[chunk * CHUNK : (chunk + 1) * CHUNK, :] = value.astype(jnp.bfloat16)
        for index, (offset, size, _) in enumerate(PIECES):
            if offset // CHUNK == chunk:
                publish(index, part.at[pl.ds(offset, size)], natural(index, wide_at))
    for copy in proj_copies:
        copy.wait()
    publish(len(PIECES), proj_part, proj_natural(chip, core))

    for copy in vec_copies[4:7]:
        copy.wait()
    vec_out_ref[core] = (vec_deep[0] + vec_deep[1]) + (vec_deep[2] + vec_deep[3])
    copy = remote(vec_out_ref.at[core], vec_out_ref.at[core], vec_sems, 7, sibling)
    copy.start()
    vec_copies.append(copy)

    pass_copies = []
    for index in range(len(PIECES) + 1):
        for k in range(3):
            done_copies[index][1 + k].wait_recv()
            from_chip = lax.rem(chip + CHIPS - 1 - k, CHIPS)
            if index < len(PIECES):
                spot = natural(index, from_chip * CORES + core)
            else:
                spot = proj_natural(from_chip, core)
            copy = remote(spot, spot, pass_sems, index * 3 + k, sibling)
            copy.start()
            pass_copies.append(copy)

    text_steps(12, text_count)
    for copies in done_copies:
        copies[0].wait_recv()
    for copy in pass_copies:
        copy.wait_recv()
    for copy in locals_done:
        copy.wait()

    gram_sems = (gram_send, gram_recv)

    def add_tile(tile, gradient):
        momentum_load(tile).wait()
        gradient = gradient.astype(jnp.float32)
        update = gradient + MUON_BETA * (MUON_BETA * momentum_tiles[tile] + gradient)
        high, low = halves(update)
        high_ref[tile] = high
        low_ref[tile] = low
        gram_ref[...] += dot_tn(high, high)
        cross = dot_tn(high, low)
        gram_ref[...] += cross + cross.T

    @pl.when(tile_count > 0)
    def _():
        gram_ref[...] = jnp.zeros_like(gram_ref)

    @pl.when(wide_at == OWNERS[4])
    def _():
        loads = [
            pltpu.make_async_copy(
                proj_sum_ref.at[tile // PLANES, tile % PLANES],
                proj_tiles.at[tile],
                tile_sem.at[1, tile],
            )
            for tile in range(MOST_TILES)
        ]
        for copy in loads:
            copy.start()
        for copy in loads:
            copy.wait()

        @pl.loop(0, MOST_TILES)
        def _(tile):
            add_tile(tile, proj_tiles[tile].reshape(TILE, D))

    @pl.when((tile_count > 0) & (wide_at != OWNERS[4]))
    def _():
        def load(tile):
            source = pl.ds(pl.multiple_of((tile_first + tile) * TILE, TILE), TILE)
            return pltpu.make_async_copy(
                sum_ref.at[source], main_tiles.at[tile], tile_sem.at[1, tile]
            )

        @pl.loop(0, tile_count)
        def _(tile):
            load(tile).start()

        @pl.loop(0, tile_count)
        def _(tile):
            load(tile).wait()
            add_tile(tile, main_tiles[tile])

    @pl.when(tile_count > 0)
    def _():
        for t in range(PLANES):
            for strip, lane in ((t, 0), (STRIPS - 1 - t, 1)):
                begin = strip // 2 * TILE
                value = gram_ref[strip * STRIP : (strip + 1) * STRIP, begin:]
                width = D - begin
                at = 0 if lane == 0 else PACKED - width
                packs[t, :, at : at + width] = value
        copies = []
        for k, target in enumerate(planes):
            to_plane = lax.rem(plane + k + 1, PLANES)
            copy = remote(packs.at[to_plane], pieces.at[plane], gram_sems, k, target)
            copy.start()
            copies.append(copy)
        pieces[plane] = packs[plane]
        for copy in copies:
            copy.wait()
        totals[plane] = (pieces[0] + pieces[1]) + (pieces[2] + pieces[3])
        copies = []
        for k, target in enumerate(planes):
            copy = remote(totals.at[plane], totals.at[plane], gram_sems, 3 + k, target)
            copy.start()
            copies.append(copy)
        for copy in copies:
            copy.wait()
        for t in range(PLANES):
            for strip, lane in ((t, 0), (STRIPS - 1 - t, 1)):
                begin = strip // 2 * TILE
                width = D - begin
                at = 0 if lane == 0 else PACKED - width
                gram_ref[strip * STRIP : (strip + 1) * STRIP, begin:] = totals[
                    t, :, at : at + width
                ]
        row_block = lax.broadcasted_iota(jnp.int32, (D, D), 0) // TILE
        lane_block = lax.broadcasted_iota(jnp.int32, (D, D), 1) // TILE
        value = gram_ref[...]
        gram_ref[...] = jnp.where(lane_block >= row_block, value, value.T)

    for copies in done_copies:
        for copy in copies:
            copy.wait_send()
    for copy in pass_copies:
        copy.wait_send()
    for copy in near_copies:
        copy.wait_send()
    for pair in firsts + seconds:
        for copy in pair:
            copy.wait_send()
    for copies in deep_copies:
        for copy in copies:
            copy.wait_send()
    vec_copies[0].wait_send()
    vec_copies[7].wait()
    text_copy(text_count - 2).wait()
    text_copy(text_count - 1).wait()


def settle(every, main, vec, grad_own, proj_own, bias_own, momentum, flat_ids, flat_mask):
    dma = pltpu.SemaphoreType.DMA
    f32, bf = jnp.float32, jnp.bfloat16
    features, tokens = proj_own.shape[0], flat_ids.shape[0]
    rows = grad_own.shape[0] * grad_own.shape[1] // BANDS
    hbm = pl.BlockSpec(memory_space=pl.ANY)
    vmem = pl.BlockSpec(memory_space=pltpu.VMEM)
    grid = (CHUNKS, SIDE, SIDE, PLANES, CHUNK, D)
    return pl.pallas_call(
        settle_kernel,
        out_shape=(
            jax.ShapeDtypeStruct((features, tokens), f32),
            jax.ShapeDtypeStruct((MAIN_TILES * TILE, D), bf),
            jax.ShapeDtypeStruct((CORES, PLANES, CHIPS, PROJ, D), bf),
            jax.ShapeDtypeStruct((CORES, VROWS, D), f32),
            jax.ShapeDtypeStruct((D, D), f32),
            jax.ShapeDtypeStruct((MOST_TILES, TILE, D), bf),
            jax.ShapeDtypeStruct((MOST_TILES, TILE, D), bf),
        ),
        in_specs=[vmem, hbm, vmem, vmem, vmem, vmem, hbm, vmem, vmem],
        out_specs=(hbm, hbm, hbm, vmem, vmem, vmem, vmem),
        scratch_shapes=[
            pltpu.VMEM((BANDS * features, rows), bf),
            pltpu.VMEM((2, features, TEXT_TILE), f32),
            pltpu.VMEM(grid, bf),
            pltpu.VMEM(grid, bf),
            pltpu.VMEM((CHUNKS, SIDE, 2, CHUNK, D), bf),
            pltpu.VMEM((CHUNKS, SIDE, 2, CHUNK, D), bf),
            pltpu.VMEM((CHUNKS, 2, CHUNK, D), bf),
            pltpu.VMEM((CHUNKS, 2, CHUNK, D), bf),
            pltpu.VMEM((CHUNKS, PLANES, CHUNK, D), bf),
            pltpu.VMEM((CHUNKS, 3, CHUNK, D), bf),
            pltpu.VMEM((CHIPS, PROJ, D), bf),
            pltpu.VMEM((CHIPS, PROJ, D), bf),
            pltpu.VMEM((MAIN, D), bf),
            pltpu.VMEM((PLANES, PROJ, D), bf),
            pltpu.VMEM((VROWS, D), f32),
            pltpu.VMEM((CHIPS, VROWS, D), f32),
            pltpu.VMEM((PLANES, VROWS, D), f32),
            pltpu.VMEM((4, TILE, D), bf),
            pltpu.VMEM((MOST_TILES, CHIPS, PROJ, D), bf),
            pltpu.VMEM((MOST_TILES, TILE, D), f32),
            pltpu.VMEM((PLANES, STRIP, PACKED), f32),
            pltpu.VMEM((PLANES, STRIP, PACKED), f32),
            pltpu.VMEM((PLANES, STRIP, PACKED), f32),
            dma((8,)),
            dma((2, MOST_TILES)),
            dma((2,)),
            dma((CHUNKS,)),
            dma((CHUNKS,)),
            dma((CHUNKS * 4,)),
            dma((CHUNKS * 4,)),
            dma((CHUNKS * 3,)),
            dma((CHUNKS * 3,)),
            dma((20,)),
            dma((20,)),
            dma((15,)),
            dma((15,)),
            dma((6,)),
            dma((6,)),
            dma((8,)),
            dma((8,)),
            dma((6,)),
            dma((6,)),
        ],
        compiler_params=pltpu.CompilerParams(
            collective_id=3, has_side_effects=True, vmem_limit_bytes=58 * 2**20
        ),
        name="settle",
    )(
        every,
        main.reshape((CORES,) + grid),
        vec,
        grad_own,
        proj_own,
        bias_own,
        momentum,
        flat_ids[None],
        flat_mask[None],
    )


SHARES = ((6, 0, 0, 384), (7, 0, 384, 128), (2, 0, 512, 512), (4, 0, 1024, 512)) + (
    (0, 0, 1536, 512),
    (0, 512, 2048, 512),
)


def muon_kernel(
    gram_ref,
    high_ref,
    low_ref,
    out_ref,
    gram,
    poly,
    chain,
    rows_out,
    local_sem,
    rows_send,
    rows_recv,
):
    wide_at, plane, chip, core = place()
    sibling, chips, planes = neighbours(wide_at, plane, chip, core)
    x_wide, y_wide = across(wide_at, plane, chip, core)
    x_near, y_near = (x_wide, plane), (y_wide, plane)
    tile_count, _ = owner_tiles(wide_at)
    enter([sibling, x_near, y_near])

    @pl.when(tile_count > 0)
    def _():
        diagonal = lax.broadcasted_iota(jnp.int32, (D, D), 0) == lax.broadcasted_iota(
            jnp.int32, (D, D), 1
        )
        square = jnp.sum(jnp.where(diagonal, gram_ref[...], 0.0))
        inverse = 1.0 / (jnp.sqrt(jnp.full((1, 1), square)) + 1e-07)
        gram[...] = gram_ref[...] * (inverse * inverse)

        def make_poly():
            value = gram[...]
            parts = halves(value)
            diagonal = lax.broadcasted_iota(jnp.int32, (D, D), 0) == lax.broadcasted_iota(
                jnp.int32, (D, D), 1
            )
            poly[...] = (
                NEWTON_B * value
                + NEWTON_C * split_dot(parts, parts)
                + jnp.where(diagonal, NEWTON_A, 0.0)
            )

        def next_gram():
            parts = halves(poly[...])
            half_way = split_dot(halves(gram[...]), parts)
            gram[...] = split_dot(halves(half_way), parts)

        def extend():
            chain[...] = split_dot(halves(chain[...]), halves(poly[...]))

        make_poly()
        chain[...] = poly[...]
        next_gram()

        @pl.loop(0, 3)
        def _(sweep):
            make_poly()
            extend()
            next_gram()

        make_poly()
        extend()
        chain_parts = halves(chain[...] * inverse)

        @pl.loop(0, tile_count)
        def _(tile):
            rows = pl.ds(pl.multiple_of(tile * TILE, TILE), TILE)
            rows_out[rows, :] = split_dot((high_ref[tile], low_ref[tile]), chain_parts).astype(
                jnp.bfloat16
            )

    sems = (rows_send, rows_recv)

    def share_copies(index):
        owner, source, begin, size = SHARES[index]
        owner_chip, owner_core = divmod(owner, CORES)
        mine = rows_out.at[pl.ds(source, size)]
        spot = out_ref.at[pl.ds(begin, size)]
        first = out_ref.at[pl.ds(begin, size // 2)]
        last = out_ref.at[pl.ds(begin + size // 2, size // 2)]
        base = index * 9
        roles = {
            "x": (owner_chip ^ 1) * CORES + owner_core,
            "y": (owner_chip ^ 2) * CORES + owner_core,
            "d": (owner_chip ^ 3) * CORES + owner_core,
        }
        sends = {
            "o": [
                (mine, spot, base, x_near),
                (mine, spot, base + 1, y_near),
                (mine, spot, base + 2, sibling),
            ],
            "x": [(first, first, base + 3, y_near), (spot, spot, base + 5, sibling)],
            "y": [(last, last, base + 4, x_near), (spot, spot, base + 6, sibling)],
            "d": [(first, first, base + 7, sibling), (last, last, base + 8, sibling)],
        }
        gets = {
            "x": [(spot, base)],
            "y": [(spot, base + 1)],
            "d": [(first, base + 3), (last, base + 4)],
            "so": [(spot, base + 2)],
            "sx": [(spot, base + 5)],
            "sy": [(spot, base + 6)],
            "sd": [(first, base + 7), (last, base + 8)],
        }
        roles["o"] = owner
        for role in ("o", "x", "y", "d"):
            at = roles[role]
            roles["s" + role] = at // CORES * CORES + 1 - at % CORES
        local = (mine, spot, local_sem.at[index])
        return roles, sends, gets, local

    def started(entry):
        src, dst, index, target = entry
        return remote(src, dst, sems, index, target)

    def arriving(entry):
        spot, index = entry
        return remote(spot, spot, sems, index, sibling)

    plans = [share_copies(index) for index in range(len(SHARES))]
    for roles, sends, gets, local in plans:

        @pl.when(wide_at == roles["o"])
        def _(sends=sends, local=local):
            for entry in sends["o"]:
                started(entry).start()
            pltpu.make_async_copy(*local).start()

    for phase in (("x", "y"), ("d",)):
        for roles, sends, gets, local in plans:
            for role in phase:

                @pl.when(wide_at == roles[role])
                def _(sends=sends, gets=gets, role=role):
                    for got, entry in zip(gets[role] * 2, sends[role]):
                        if role == "d" or entry is sends[role][0]:
                            arriving(got).wait_recv()
                        started(entry).start()

    for roles, sends, gets, local in plans:
        for role in ("so", "sx", "sy", "sd"):

            @pl.when(wide_at == roles[role])
            def _(gets=gets, role=role):
                for got in gets[role]:
                    arriving(got).wait_recv()

        for role in ("o", "x", "y", "d"):

            @pl.when(wide_at == roles[role])
            def _(sends=sends, local=local, role=role):
                for entry in sends[role]:
                    started(entry).wait_send()
                if role == "o":
                    pltpu.make_async_copy(*local).wait()


def muon_rows(gram, high, low):
    dma = pltpu.SemaphoreType.DMA
    vmem = pl.BlockSpec(memory_space=pltpu.VMEM)
    total = (MAIN_TILES + MOST_TILES) * TILE
    return pl.pallas_call(
        muon_kernel,
        out_shape=jax.ShapeDtypeStruct((total, D), jnp.bfloat16),
        in_specs=[vmem] * 3,
        out_specs=pl.BlockSpec(memory_space=pl.ANY),
        scratch_shapes=[
            pltpu.VMEM((D, D), jnp.float32),
            pltpu.VMEM((D, D), jnp.float32),
            pltpu.VMEM((D, D), jnp.float32),
            pltpu.VMEM((MOST_TILES * TILE, D), jnp.bfloat16),
            dma((len(SHARES),)),
            dma((len(SHARES) * 9,)),
            dma((len(SHARES) * 9,)),
        ],
        compiler_params=pltpu.CompilerParams(
            collective_id=4, has_side_effects=True, vmem_limit_bytes=40 * 2**20
        ),
        name="muon_rows",
    )(gram, high, low)


def finish_kernel(main_ref, proj_ref, rows_ref, momentum_ref, master_ref, ema_ref, *outs):
    grad_ref, momentum_new_ref, weight_ref, ema_new_ref = outs
    tile = pl.program_id(0)
    main = main_ref[...].astype(jnp.float32)
    proj = proj_ref[...].reshape(TILE, D).astype(jnp.float32)
    gradient = jnp.where(tile < MAIN_TILES, main, proj)
    grad_ref[0] = gradient
    momentum_new_ref[0] = MUON_BETA * momentum_ref[0] + gradient
    scale = jnp.float32(0.0)
    begin = 0
    for row_total, count in zip(matrix_rows(), BLOCK_TILES):
        inside = (tile >= begin) & (tile < begin + count)
        scale = jnp.where(inside, MUON_RATE * math.sqrt(row_total / D), scale)
        begin = begin + count
    weight = master_ref[0] * (1.0 - MUON_RATE * MUON_DECAY) - scale * rows_ref[...].astype(
        jnp.float32
    )
    weight_ref[0] = weight
    ema_new_ref[0] = EMA_DECAY * ema_ref[0] + (1.0 - EMA_DECAY) * weight


def finish(main_sum, proj_sum, rows, momentum, master, ema):
    block = pl.BlockSpec((1, TILE, D), lambda i: (0, i, 0))
    proj = proj_sum.reshape((MOST_TILES,) + proj_sum.shape[2:])
    return pl.pallas_call(
        finish_kernel,
        grid=(MAIN_TILES + MOST_TILES,),
        out_shape=(jax.ShapeDtypeStruct(master.shape, jnp.float32),) * 4,
        in_specs=[
            pl.BlockSpec((TILE, D), lambda i: (jnp.minimum(i, MAIN_TILES - 1), 0)),
            pl.BlockSpec(
                (1,) + proj.shape[1:], lambda i: (jnp.maximum(i - MAIN_TILES, 0), 0, 0, 0)
            ),
            pl.BlockSpec((TILE, D), lambda i: (i, 0)),
            block,
            block,
            block,
        ],
        out_specs=(block,) * 4,
        cost_estimate=pl.CostEstimate(
            flops=12 * master.size, bytes_accessed=32 * master.size, transcendentals=0
        ),
        name="finish",
    )(main_sum, proj, rows, momentum, master, ema)

def tell_kernel(own_ref, out_ref, send_sem, recv_sem):
    wide_at, plane, chip, core = place()
    wide_count = CHIPS * CORES
    peers = [
        (lax.rem(wide_at + k // PLANES, wide_count), lax.rem(plane + k % PLANES, PLANES))
        for k in range(1, wide_count * PLANES)
    ]
    enter(peers)
    spot = out_ref.at[wide_at * PLANES + plane]
    copies = [
        remote(own_ref, spot, (send_sem, recv_sem), k, target) for k, target in enumerate(peers)
    ]
    for copy in copies:
        copy.start()
    out_ref[wide_at * PLANES + plane] = own_ref[...]
    for copy in copies:
        copy.wait()


def tell(values, collective_id):
    dma = pltpu.SemaphoreType.DMA
    every = PLANES * CHIPS * CORES
    return pl.pallas_call(
        tell_kernel,
        out_shape=jax.ShapeDtypeStruct((every,) + values.shape, values.dtype),
        in_specs=[pl.BlockSpec(memory_space=pltpu.VMEM)],
        out_specs=pl.BlockSpec(memory_space=pltpu.VMEM),
        scratch_shapes=[dma((every - 1,)), dma((every - 1,))],
        compiler_params=pltpu.CompilerParams(collective_id=collective_id, has_side_effects=True),
        name="tell_ids",
    )(values)

def two_part_dot(left, right):
    high, low = halves(left)
    return plain_dot(high, right) + plain_dot(low, right)


def normalize(values):
    center = values - jnp.mean(values, axis=-1, keepdims=True)
    spread = jnp.mean(center * center, axis=-1, keepdims=True)
    scale = lax.rsqrt(spread + 1e-05)
    return center * scale, scale


def normalize_back(grad, gain, hat, scale):
    grad_hat = grad * gain
    return scale * (
        grad_hat
        - jnp.mean(grad_hat, axis=-1, keepdims=True)
        - hat * jnp.mean(grad_hat * hat, axis=-1, keepdims=True)
    )


def over_rows(values):
    return jnp.sum(values, axis=0, keepdims=True)


def spread_steps(own, held, sems, base, at):
    wide_at, plane, chip, core = at
    sibling = (chip * CORES + 1 - core, plane)
    x_wide, y_wide = across(wide_at, plane, chip, core)
    x_near, y_near = (x_wide, plane), (y_wide, plane)
    diagonal_wide = (CHIPS - 1 - chip) * CORES + core
    half = own.shape[0] // 2
    tops, bottoms = pl.ds(0, half), pl.ds(half, half)
    above, below = (wide_at, plane + 1), (wide_at, plane - 1)

    def climb(distance, source, src):
        spot = held.at[source, wide_at]
        return remote(spot if src is None else src, spot, sems, base + distance - 1, above)

    def sink(distance, source, src):
        spot = held.at[source, wide_at]
        return remote(spot if src is None else src, spot, sems, base + 2 + distance, below)

    def plane_copy(source, kind, src=None):
        index = base + 6 + 9 * source + kind
        own_spot = held.at[source, wide_at]
        x_spot, y_spot = held.at[source, x_wide], held.at[source, y_wide]
        far_spot = held.at[source, diagonal_wide]
        if kind in (0, 1, 2):
            target = (x_near, y_near, sibling)[kind]
            return remote(own_spot if src is None else src, own_spot, sems, index, target)
        if kind == 3:
            return remote(x_spot.at[tops], x_spot.at[tops], sems, index, y_near)
        if kind == 5:
            return remote(y_spot.at[bottoms], y_spot.at[bottoms], sems, index, x_near)
        if kind in (4, 6):
            spot = x_spot if kind == 4 else y_spot
            return remote(spot, spot, sems, index, sibling)
        rows = tops if kind == 7 else bottoms
        return remote(far_spot.at[rows], far_spot.at[rows], sems, index, sibling)

    def plane_send(source, src=None):
        for kind in (0, 1, 2):
            plane_copy(source, kind, src).start()

    def begin():
        @pl.when(plane < PLANES - 1)
        def _():
            climb(1, plane, own).start()

        @pl.when(plane > 0)
        def _():
            sink(1, plane, own).start()

        plane_send(plane, own)

    def arrive(distance):
        @pl.when(plane >= distance)
        def _():
            source = plane - distance
            climb(distance, source, None).wait_recv()
            if distance < PLANES - 1:

                @pl.when(plane < PLANES - 1)
                def _():
                    climb(distance + 1, source, None).start()

            plane_send(source)

        @pl.when(plane + distance < PLANES)
        def _():
            source = plane + distance
            sink(distance, source, None).wait_recv()
            if distance < PLANES - 1:

                @pl.when(plane > 0)
                def _():
                    sink(distance + 1, source, None).start()

            plane_send(source)

    def at_distance(distance, step):
        if distance == 0:
            step(plane)
            return

        @pl.when(plane >= distance)
        def _():
            step(plane - distance)

        @pl.when(plane + distance < PLANES)
        def _():
            step(plane + distance)

    def relay_one(source):
        plane_copy(source, 0).wait_recv()
        plane_copy(source, 3).start()
        plane_copy(source, 4).start()
        plane_copy(source, 1).wait_recv()
        plane_copy(source, 5).start()
        plane_copy(source, 6).start()

    def finish_one(source):
        plane_copy(source, 3).wait_recv()
        plane_copy(source, 7).start()
        plane_copy(source, 5).wait_recv()
        plane_copy(source, 8).start()

    def settle_one(source):
        for kind in (2, 4, 6, 7, 8):
            plane_copy(source, kind).wait_recv()
        for kind in range(9):
            plane_copy(source, kind).wait_send()

    def relay(distance):
        at_distance(distance, relay_one)

    def finish(distance):
        at_distance(distance, finish_one)

    def settled():
        for distance in range(PLANES):
            at_distance(distance, settle_one)
        for distance in range(1, PLANES):
            source = plane - distance + 1

            @pl.when((plane < PLANES - 1) & (source >= 0))
            def _(distance=distance, source=source):
                climb(distance, source, None).wait_send()

            down_source = plane + distance - 1

            @pl.when((plane > 0) & (down_source < PLANES))
            def _(distance=distance, down_source=down_source):
                sink(distance, down_source, None).wait_send()

    return begin, arrive, relay, finish, settled


def layer_kernel(
    outgoing_in_ref,
    own_ref,
    ids_ref,
    mask_ref,
    cot_ref,
    spots_ref,
    live_ref,
    cls_ref,
    pos_ref,
    norms_ref,
    bias_up_ref,
    bias_down_ref,
    every_ref,
    main_ref,
    outgoing_ref,
    vec_ref,
    wide_ref,
    own_grad_ref,
    own_bias_ref,
    own_proj_ref,
    incoming_ref,
    grad_ref,
    packed,
    text_total,
    z_ref,
    onehot,
    hats,
    scales,
    normed,
    keys,
    probs,
    grad_kv,
    grad_normed,
    grad_pieces,
    active,
    slope,
    sums,
    local_sem,
    piece_send,
    piece_recv,
    table_send,
    table_recv,
    body_send,
    body_recv,
    proj_send,
    proj_recv,
    z_send,
    z_recv,
):
    at = place()
    wide_at, plane, chip, core = at
    me = wide_at * PLANES + plane
    wide_count = CHIPS * CORES
    cap = outgoing_in_ref.shape[1]
    peers = [
        (lax.rem(wide_at + k // PLANES, wide_count), lax.rem(plane + k % PLANES, PLANES))
        for k in range(1, wide_count * PLANES)
    ]

    def spread_of(own, held, sems):
        return spread_steps(own, held, sems, 0, at)

    body_part, proj_part = own_ref.at[pl.ds(0, MAIN)], own_ref.at[pl.ds(MAIN, PART - MAIN)]
    body_spread = spread_of(body_part, packed.at[:, :, pl.ds(0, MAIN)], (body_send, body_recv))
    proj_spread = spread_of(
        proj_part, packed.at[:, :, pl.ds(MAIN, PART - MAIN)], (proj_send, proj_recv)
    )
    z_spread = spread_of(z_ref, every_ref, (z_send, z_recv))
    body_begin, body_arrive, body_relay, body_finish, body_settled = body_spread
    proj_begin, proj_arrive, proj_relay, proj_finish, proj_settled = proj_spread
    z_begin, z_arrive, z_relay, z_finish, z_settled = z_spread

    own_copies = [
        pltpu.make_async_copy(own_ref, packed.at[plane, wide_at], local_sem.at[0]),
        pltpu.make_async_copy(
            outgoing_in_ref.at[me],
            incoming_ref.at[pl.ds(pl.multiple_of(me * cap, cap), cap)],
            local_sem.at[1],
        ),
    ]
    for copy in own_copies:
        copy.start()
    enter(peers)
    piece_copies = []
    for index, (wide_to, plane_to) in enumerate(peers):
        copy = remote(
            outgoing_in_ref.at[wide_to * PLANES + plane_to],
            incoming_ref.at[pl.ds(pl.multiple_of(me * cap, cap), cap)],
            (piece_send, piece_recv),
            index,
            (wide_to, plane_to),
        )
        copy.start()
        piece_copies.append(copy)
    body_begin()

    text_rows = own_grad_ref.shape[0] * own_grad_ref.shape[1] // BANDS
    features = cot_ref.shape[0]
    text_total[...] = jnp.zeros_like(text_total)

    def text_steps(begin, end):
        @pl.loop(begin, end)
        def _(step):
            lanes = pl.ds(pl.multiple_of(step * TEXT_TILE, TEXT_TILE), TEXT_TILE)
            ids = ids_ref[:, lanes]
            chosen = band_onehot(ids, text_rows)
            band = jnp.where(mask_ref[:, lanes] > 0, ids // text_rows, -1)
            cot = cot_ref[:, lanes].astype(jnp.float32)
            banded = jnp.concatenate(
                [jnp.where(band == b, cot, 0.0).astype(jnp.bfloat16) for b in range(BANDS)], axis=0
            )
            text_total[...] += dot_nt(chosen, banded)

    text_tiles = ids_ref.shape[1] // TEXT_TILE
    text_steps(0, text_tiles // 4)
    body_arrive(1)
    text_steps(text_tiles // 4, text_tiles // 2)
    body_relay(0)
    body_arrive(2)
    text_steps(text_tiles // 2, text_tiles * 3 // 4)
    body_relay(1)
    body_arrive(3)
    text_steps(text_tiles * 3 // 4, text_tiles)
    bias_total = jnp.zeros((1, features), jnp.float32)
    blocks = own_grad_ref.shape[0] // BANDS
    for b in range(BANDS):
        rounded = text_total[:, b * features : (b + 1) * features].astype(jnp.bfloat16)
        own_grad_ref[b * blocks : (b + 1) * blocks] = rounded.reshape(
            (blocks,) + own_grad_ref.shape[1:]
        )
        bias_total = bias_total + over_rows(rounded.astype(jnp.float32))
    own_bias_ref[...] = bias_total
    proj_begin()
    table_copies = []
    for index, (wide_to, plane_to) in enumerate(peers):
        copy = remote(
            own_grad_ref.at[wide_to * PLANES + plane_to],
            grad_ref.at[me],
            (table_send, table_recv),
            index,
            (wide_to, plane_to),
        )
        copy.start()
        table_copies.append(copy)
    grad_ref[me] = own_grad_ref[me]
    body_relay(2)
    body_relay(3)
    for distance in range(PLANES):
        body_finish(distance)
    proj_arrive(1)
    proj_arrive(2)
    proj_arrive(3)
    for copy in own_copies:
        copy.wait()
    body_settled()
    for copy in piece_copies:
        copy.wait()
    def weight_rows(begin, size, plane_at=None):
        rows = slice(begin, begin + size)
        if plane_at is None:
            return packed[:, :, rows, :].reshape(PLANES * wide_count * size, D)
        return packed[plane_at, :, rows, :].reshape(wide_count * size, D)

    qkv_at, out_at, up_at, down_at, proj_at = 0, 48, 64, 128, MAIN
    entries = z_ref.shape[0]
    spot_count = incoming_ref.shape[0]
    gain_one, shift_one = norms_ref[0:1, :], norms_ref[1:2, :]
    gain_two, shift_two = norms_ref[2:3, :], norms_ref[3:4, :]
    gain_end, shift_end = norms_ref[4:5, :], norms_ref[5:6, :]

    def slot_rows(slot):
        return pl.ds(pl.multiple_of(slot * entries, entries), entries)

    def piece_lanes(slot):
        return pl.ds(pl.multiple_of((slot - 1) * entries, entries), entries)

    @pl.loop(1, SLOTS)
    def _(slot):
        places = lax.broadcasted_iota(jnp.int32, (spot_count, entries), 0)
        chosen = jnp.where(places == spots_ref[pl.ds(slot, 1), :], 1.0, 0.0).astype(jnp.bfloat16)
        onehot[:, piece_lanes(slot)] = chosen
        hats[slot_rows(slot), :] = dot_tn(chosen, incoming_ref[...]) + pos_ref[pl.ds(slot, 1), :]

    first_row = cls_ref[...] + pos_ref[0:1, :]
    hats[0:entries, :] = jnp.broadcast_to(first_row, (entries, D))
    sums[...] = jnp.zeros_like(sums)

    @pl.loop(0, SLOTS)
    def _(slot):
        rows = slot_rows(slot)
        hat, scale = normalize(hats[rows, :])
        hats[rows, :] = hat
        scales[rows, :] = jnp.broadcast_to(scale, (entries, 128))
        part = (hat * gain_one + shift_one).astype(jnp.bfloat16)
        normed[rows, :] = part
        keys[rows, :] = dot_nt(part, weight_rows(qkv_at, 48)[D:, :])

    query = dot_nt(normed[0:entries, :], weight_rows(qkv_at, 48)[0:D, :])
    lane_head = lax.broadcasted_iota(jnp.int32, (D, 128), 0) // HDIM
    to_heads = jnp.where(
        lane_head == lax.broadcasted_iota(jnp.int32, (D, 128), 1), 1.0, 0.0
    ).astype(jnp.bfloat16)
    head_lane = lax.broadcasted_iota(jnp.int32, (128, D), 1) // HDIM
    from_heads = jnp.where(
        head_lane == lax.broadcasted_iota(jnp.int32, (128, D), 0), 1.0, 0.0
    ).astype(jnp.bfloat16)
    root = 1.0 / math.sqrt(HDIM)
    scores = []
    for slot in range(SLOTS):
        rows = slice(slot * entries, (slot + 1) * entries)
        value = two_part_dot(query * keys[rows, 0:D], to_heads) * root
        scores.append(jnp.where(live_ref[:, slot : slot + 1] > 0, value, -1e30))
    top = scores[0]
    for value in scores[1:]:
        top = jnp.maximum(top, value)
    scores = [jnp.exp(value - top) for value in scores]
    whole = scores[0]
    for value in scores[1:]:
        whole = whole + value
    attended = jnp.zeros((entries, D), jnp.float32)
    for slot in range(SLOTS):
        rows = slice(slot * entries, (slot + 1) * entries)
        share = scores[slot] / whole
        probs[rows, :] = share
        attended = attended + two_part_dot(share, from_heads) * keys[rows, D:]
    attended_bf = attended.astype(jnp.bfloat16)
    residual = first_row + dot_nt(attended_bf, weight_rows(out_at, 16))
    hat_two, scale_two = normalize(residual)
    normed_two = (hat_two * gain_two + shift_two).astype(jnp.bfloat16)
    span = 512
    second = residual + bias_down_ref[...]
    for begin in range(0, FF, span):
        lanes = slice(begin, begin + span)
        gate = dot_nt(normed_two, weight_rows(up_at, 64, begin // span)) + bias_up_ref[:, lanes]
        square = gate * gate
        bend = jnp.tanh(math.sqrt(2.0 / math.pi) * (gate + 0.044715 * square * gate))
        part = (0.5 * gate * (1.0 + bend)).astype(jnp.bfloat16)
        active[:, lanes] = part
        slope[:, lanes] = 0.5 * (1.0 + bend) + 0.5 * gate * (1.0 - bend * bend) * (
            math.sqrt(2.0 / math.pi) * (1.0 + 3.0 * 0.044715 * square)
        )
        second = second + plain_dot(part, weight_rows(down_at, 64, begin // span))
    hat_end, scale_end = normalize(second)
    z_ref[...] = (hat_end * gain_end + shift_end).astype(jnp.bfloat16)

    z_begin()
    own_z = pltpu.make_async_copy(z_ref, every_ref.at[plane, wide_at], local_sem.at[2])
    own_z.start()
    for distance in range(PLANES):
        proj_relay(distance)
    for distance in range(PLANES):
        proj_finish(distance)
    z_arrive(1)
    proj_settled()
    for copy in table_copies:
        copy.wait()
    own_proj_ref[...] = packed[me // wide_count, lax.rem(me, wide_count), MAIN:, :]
    grad_z = jnp.zeros((entries, D), jnp.float32)
    for source in range(grad_ref.shape[0]):
        grad_z = grad_z + plain_dot(
            grad_ref[source], packed[source // wide_count, source % wide_count, MAIN:, :]
        )
    vec_ref[...] = jnp.zeros_like(vec_ref)
    vec_ref[13:14, :] = over_rows(grad_z * hat_end)
    vec_ref[14:15, :] = over_rows(grad_z)
    grad_second = normalize_back(grad_z, gain_end, hat_end, scale_end)
    branch_two = grad_second.astype(jnp.bfloat16)
    vec_ref[15:16, :] = over_rows(branch_two.astype(jnp.float32))

    def store(value, block, chunk, height, offset):
        for chip_at in range(CHIPS):
            for core_at in range(CORES):
                top = (chip_at * CORES + core_at) * height
                main_ref[core_at, chunk, chip_at, block, offset : offset + height, :] = value[
                    top : top + height, :
                ].astype(jnp.bfloat16)

    z_arrive(2)
    z_relay(0)
    grad_two = jnp.zeros((entries, D), jnp.float32)
    for block in range(PLANES):
        lanes = slice(block * span, (block + 1) * span)
        store(dot_tn(active[:, lanes], branch_two), block, 0, 64, 0)
        gate_grad = (dot_nt(branch_two, weight_rows(down_at, 64, block)) * slope[:, lanes]).astype(jnp.bfloat16)
        wide_ref[:, lanes] = over_rows(gate_grad.astype(jnp.float32))
        store(dot_tn(gate_grad, normed_two), block, 1, 64, 0)
        grad_two = grad_two + plain_dot(gate_grad, weight_rows(up_at, 64, block))
    z_arrive(3)
    z_relay(1)
    vec_ref[11:12, :] = over_rows(grad_two * hat_two)
    vec_ref[12:13, :] = over_rows(grad_two)
    grad_residual = grad_second + normalize_back(grad_two, gain_two, hat_two, scale_two)
    branch_one = grad_residual.astype(jnp.bfloat16)
    grad_out = dot_tn(branch_one, attended_bf)
    for block in range(PLANES):
        store(grad_out[block * 128 : (block + 1) * 128, :], block, 2, 16, 0)
    grad_attended = plain_dot(branch_one, weight_rows(out_at, 16))

    z_relay(2)
    z_finish(0)
    inner = jnp.zeros((entries, 128), jnp.float32)
    slides = []
    for slot in range(SLOTS):
        rows = slice(slot * entries, (slot + 1) * entries)
        value = two_part_dot(grad_attended * keys[rows, D:], to_heads)
        slides.append(value)
        inner = inner + probs[rows, :] * value
    grad_query = jnp.zeros((entries, D), jnp.float32)
    for slot in range(SLOTS):
        rows = slice(slot * entries, (slot + 1) * entries)
        share = probs[rows, :]
        grad_kv[rows, D:] = (two_part_dot(share, from_heads) * grad_attended).astype(jnp.bfloat16)
        push = two_part_dot(share * (slides[slot] - inner), from_heads) * root
        grad_query = grad_query + push * keys[rows, 0:D]
        grad_kv[rows, 0:D] = (push * query).astype(jnp.bfloat16)
    z_relay(3)
    z_finish(1)
    query_bf = grad_query.astype(jnp.bfloat16)

    grad_q = dot_tn(query_bf, normed[0:entries, :])
    grad_k = dot_tn(grad_kv[:, 0:D], normed[...])
    grad_v = dot_tn(grad_kv[:, D:], normed[...])
    third = D * 3 // PLANES
    every = jnp.concatenate([grad_q, grad_k, grad_v], axis=0)
    for block in range(PLANES):
        store(every[block * third : (block + 1) * third, :], block, 2, 48, 16)

    @pl.loop(0, SLOTS)
    def _(slot):
        rows = slot_rows(slot)
        grad_normed[rows, :] = plain_dot(grad_kv[rows, :], weight_rows(qkv_at, 48)[D:, :])

    grad_normed[0:entries, :] += plain_dot(query_bf, weight_rows(qkv_at, 48)[0:D, :])

    @pl.loop(0, SLOTS)
    def _(slot):
        rows = slot_rows(slot)
        grad = grad_normed[rows, :]
        hat = hats[rows, :]
        sums[0:1, :] += over_rows(grad * hat)
        sums[1:2, :] += over_rows(grad)
        grad_x = normalize_back(grad, gain_one, hat, scales[rows, 0:1])
        vec_ref[pl.ds(1 + slot, 1), :] = over_rows(grad_x)

        @pl.when(slot > 0)
        def _():
            grad_pieces[pl.ds(pl.multiple_of((slot - 1) * entries, entries), entries), :] = (
                grad_x.astype(jnp.bfloat16)
            )

    z_finish(2)
    z_finish(3)
    vec_ref[9:11, :] = sums[0:2, :]
    vec_ref[1:2, :] += over_rows(grad_residual)
    vec_ref[0:1, :] = vec_ref[1:2, :]
    tile = 256
    for begin in range(0, spot_count, tile):
        outgoing_ref[begin : begin + tile, :] = plain_dot(
            onehot[begin : begin + tile, :], grad_pieces[...]
        ).astype(jnp.bfloat16)
    own_z.wait()
    z_settled()


def layer(outgoing, own_part, flat_ids, flat_mask, text_cot, spots, live, vectors):
    f32, bf = jnp.float32, jnp.bfloat16
    dma = pltpu.SemaphoreType.DMA
    count, cap = outgoing.shape[:2]
    entries = live.shape[0]
    features = text_cot.shape[0]
    rows = entries * SLOTS
    hbm = pl.BlockSpec(memory_space=pl.ANY)
    vmem = pl.BlockSpec(memory_space=pltpu.VMEM)
    spread_count = 6 + 9 * PLANES
    return pl.pallas_call(
        layer_kernel,
        out_shape=(
            jax.ShapeDtypeStruct((PLANES, CHIPS * CORES, entries, D), bf),
            jax.ShapeDtypeStruct((CORES, CHUNKS, CHIPS, PLANES, CHUNK, D), bf),
            jax.ShapeDtypeStruct((count * cap, D), bf),
            jax.ShapeDtypeStruct((16, D), f32),
            jax.ShapeDtypeStruct((1, FF), f32),
            jax.ShapeDtypeStruct((count, entries, features), bf),
            jax.ShapeDtypeStruct((1, features), f32),
            jax.ShapeDtypeStruct((features, D), bf),
        ),
        in_specs=[hbm, hbm] + [vmem] * 10,
        out_specs=(hbm,) + (vmem,) * 7,
        scratch_shapes=[
            pltpu.VMEM((count * cap, D), bf),
            pltpu.VMEM((count, entries, features), bf),
            pltpu.VMEM((PLANES, CHIPS * CORES, PART, D), bf),
            pltpu.VMEM((count * entries // BANDS, BANDS * features), f32),
            pltpu.VMEM((entries, D), bf),
            pltpu.VMEM((count * cap, entries * PSLOTS), bf),
            pltpu.VMEM((rows, D), f32),
            pltpu.VMEM((rows, 128), f32),
            pltpu.VMEM((rows, D), bf),
            pltpu.VMEM((rows, 2 * D), f32),
            pltpu.VMEM((rows, 128), f32),
            pltpu.VMEM((rows, 2 * D), bf),
            pltpu.VMEM((rows, D), f32),
            pltpu.VMEM((entries * PSLOTS, D), bf),
            pltpu.VMEM((entries, FF), bf),
            pltpu.VMEM((entries, FF), f32),
            pltpu.VMEM((8, D), f32),
            dma((3,)),
            dma((count - 1,)),
            dma((count - 1,)),
            dma((count - 1,)),
            dma((count - 1,)),
            dma((spread_count,)),
            dma((spread_count,)),
            dma((spread_count,)),
            dma((spread_count,)),
            dma((spread_count,)),
            dma((spread_count,)),
        ],
        compiler_params=pltpu.CompilerParams(
            collective_id=5, has_side_effects=True, vmem_limit_bytes=62 * 2**20
        ),
        name="layer",
    )(outgoing, own_part, flat_ids[None], flat_mask[None], text_cot, spots, live, *vectors)


def own_weight_part(mat_master):
    wide_count = CHIPS * CORES
    wide_at = lax.axis_index("wide")
    parts = []
    for segment in block_slices(mat_master[0], PLANES):
        rows = segment.shape[0] // wide_count
        parts.append(
            lax.dynamic_slice_in_dim(segment, wide_at * rows, rows, 0).astype(jnp.bfloat16)
        )
    return jnp.concatenate(parts, axis=0)


def gather_ids(slot_ids):
    count = slot_ids.shape[0]
    lanes = 128
    rows = -(-count // (8 * lanes)) * 8
    padded = jnp.pad(slot_ids, (0, rows * lanes - count)).reshape(rows, lanes)
    every = tell(padded, 1)
    return every.reshape(every.shape[0], rows * lanes)[:, :count]


def asked_onehot_of(every_ids, group_rows, cap):
    me = lax.axis_index("wide") * PLANES + lax.axis_index("narrow")
    slot_count = every_ids.shape[1]
    asked = every_ids // group_rows == me
    before = (
        lax.broadcasted_iota(jnp.int32, (slot_count, slot_count), 0)
        < lax.broadcasted_iota(jnp.int32, (slot_count, slot_count), 1)
    )
    asked_rank = jnp.dot(
        asked.astype(jnp.bfloat16), before.astype(jnp.bfloat16), preferred_element_type=jnp.float32
    ).astype(jnp.int32)
    asked_rank = jnp.where(asked, asked_rank, -1)
    chosen = asked_rank[:, None, :] == lax.iota(jnp.int32, cap)[None, :, None]
    local_ids = every_ids - me * group_rows + 1
    asked_rows = jnp.sum(jnp.where(chosen, local_ids[:, None, :], 0), axis=2).reshape(-1) - 1
    return (asked_rows[:, None] == lax.iota(jnp.int32, group_rows)[None, :]).astype(jnp.bfloat16)


def own_spots_of(slot_ids, group_rows, cap):
    slot_count = slot_ids.shape[0]
    before = (
        lax.broadcasted_iota(jnp.int32, (slot_count, slot_count), 0)
        > lax.broadcasted_iota(jnp.int32, (slot_count, slot_count), 1)
    )
    own_group = slot_ids // group_rows
    same = (own_group[:, None] == own_group[None, :]) & before
    own_rank = jnp.sum(same.astype(jnp.int32), axis=1)
    return (own_group * cap + own_rank).reshape(-1, PSLOTS)


def on_device(
    piece_table,
    piece_ids,
    slot_mask,
    text_ids,
    text_mask,
    text_cot,
    mat_master,
    mat_momentum,
    mat_ema,
    vec_master,
    vec_moment1,
    vec_moment2,
    vec_ema,
):
    device_count = PLANES * CHIPS * CORES
    me = lax.axis_index("wide") * PLANES + lax.axis_index("narrow")
    (
        cls_vec,
        positions,
        ln1_gain,
        ln1_shift,
        ln2_gain,
        ln2_shift,
        final_gain,
        final_shift,
        bias_up,
        bias_down,
        bias_out,
    ) = split_vectors(vec_master)
    entries = piece_ids.shape[0]
    slot_ids = piece_ids.reshape(-1)
    group_rows = piece_table.shape[0]
    cap = piece_cap(group_rows)
    flat_ids = text_ids.reshape(-1)
    flat_mask = text_mask.reshape(-1)
    feature_rows = text_cot.shape[0]

    every_ids = gather_ids(slot_ids)
    asked_onehot = asked_onehot_of(every_ids, group_rows, cap)
    outgoing = jnp.dot(asked_onehot, piece_table, preferred_element_type=jnp.float32)
    outgoing = outgoing.astype(jnp.bfloat16).reshape(device_count, cap, D)
    spots = own_spots_of(slot_ids, group_rows, cap)
    spots = jnp.pad(spots.T, ((1, 0), (0, 0)))
    live = jnp.concatenate([jnp.ones((entries, 1), jnp.int32), slot_mask], axis=1)
    live = jnp.pad(live.astype(jnp.float32), ((0, 0), (0, 128 - SLOTS)))

    norms = jnp.stack([ln1_gain, ln1_shift, ln2_gain, ln2_shift, final_gain, final_shift])
    (
        every_normed,
        main,
        grad_outgoing,
        vec_rows,
        grad_bias_up,
        grad_own,
        grad_bias_own,
        proj_own,
    ) = layer(
        outgoing,
        own_weight_part(mat_master),
        flat_ids,
        flat_mask,
        text_cot,
        spots,
        live,
        (cls_vec[None], positions, norms, bias_up[None], bias_down[None]),
    )
    bias_own = lax.dynamic_slice_in_dim(bias_out, me * feature_rows, feature_rows, 0)
    vec_local = jnp.concatenate(
        [
            vec_rows[:15].reshape(-1),
            grad_bias_up[0],
            vec_rows[15],
            lax.dynamic_update_slice_in_dim(
                jnp.zeros((OUTW,), jnp.float32), grad_bias_own[0], me * feature_rows, 0
            ),
        ]
    )
    vec_rows = vec_local.reshape(-1, D)
    vec_rows = jnp.pad(vec_rows, ((0, CORES * VROWS - vec_rows.shape[0]), (0, 0)))
    text_embeds, main_sum, proj_sum, vec_sum, gram, high, low = settle(
        every_normed,
        main,
        vec_rows.reshape(CORES, VROWS, D),
        grad_own,
        proj_own,
        bias_own[:, None],
        mat_momentum[0],
        flat_ids,
        flat_mask,
    )
    vec_grad = vec_sum.reshape(-1)[: vec_local.shape[0]]
    grad_outgoing, _ = lax.optimization_barrier((grad_outgoing, gram))
    grad_incoming = lax.all_to_all(
        grad_outgoing.reshape(device_count, cap, D), BOTH, 0, 0, tiled=True
    ).reshape(device_count * cap, D)
    rows = muon_rows(gram, high, low)
    grad_block, momentum_block, weight_block, ema_block = finish(
        main_sum, proj_sum, rows, mat_momentum, mat_master, mat_ema
    )
    piece_grad = contract_rows(asked_onehot, grad_incoming)
    return (
        text_embeds,
        piece_grad,
        grad_block,
        momentum_block,
        weight_block,
        ema_block,
    ) + adam(vec_grad, vec_master, vec_moment1, vec_moment2, vec_ema)


def solution(mesh):
    in_specs = (
        P(("wide", "narrow"), None),
        P(("wide", "narrow"), None),
        P(("wide", "narrow"), None),
        P(),
        P(),
        P(("wide", "narrow"), None),
        P("narrow", None, None),
        P("narrow", None, None),
        P("narrow", None, None),
        P(),
        P(),
        P(),
        P(),
    )
    out_specs = (
        P(("wide", "narrow"), None),
        P(("wide", "narrow"), None),
        P("narrow", None, None),
        P("narrow", None, None),
        P("narrow", None, None),
        P("narrow", None, None),
        P(),
        P(),
        P(),
        P(),
        P(),
    )
    fits = mesh.shape["wide"] == CHIPS * CORES and mesh.shape["narrow"] == PLANES
    step = on_device if fits else on_device_plain
    return jax.shard_map(
        step, mesh=mesh, in_specs=in_specs, out_specs=out_specs, check_vma=False
    )
```

```python
from functools import partial
import math

import jax
import jax.numpy as jnp
from jax import lax
from jax.experimental import pallas as pl
from jax.experimental.pallas import tpu as pltpu
from jax.sharding import PartitionSpec as P

D = 512
HEADS = 8
HDIM = 64
FF = 2048
OUTW = 4096
SLOTS = 8
PSLOTS = 7
STEP = 10


HIGHEST = lax.Precision.HIGHEST
HIGH = lax.Precision.HIGH
MUON_RATE = 0.5
MUON_DECAY = 0.01
MUON_BETA = 0.95
ADAM_RATE = 0.5
ADAM_BETA1 = 0.9
ADAM_BETA2 = 0.95
ADAM_EPSILON = 1e-08
EMA_DECAY = 0.8
NEWTON_A = 3.4445
NEWTON_B = -4.775
NEWTON_C = 2.0315


def matrix_rows():
    return (3 * D, D, FF, FF, OUTW)


def unpack(packed, narrow_count):
    matrices = []
    offset = 0
    for row_total in matrix_rows():
        height = row_total // narrow_count
        matrices.append(packed[:, offset : offset + height, :].reshape(row_total, packed.shape[2]))
        offset = offset + height
    return matrices


def pack(matrices, narrow_count):
    return jnp.concatenate(
        [
            matrix.reshape(narrow_count, matrix.shape[0] // narrow_count, matrix.shape[1])
            for matrix in matrices
        ],
        axis=1,
    )


def block_slices(block, narrow_count):
    segments = []
    offset = 0
    for row_total in matrix_rows():
        height = row_total // narrow_count
        segments.append(block[offset : offset + height])
        offset = offset + height
    return segments


def split_vectors(vector):
    lengths = (D, SLOTS * D, D, D, D, D, D, D, FF, D, OUTW)
    chosen = []
    offset = 0
    for length in lengths:
        chosen.append(vector[offset : offset + length])
        offset = offset + length
    chosen[1] = chosen[1].reshape(SLOTS, D)
    return chosen


def layer_norm(values, gain, shift):
    center = values - jnp.mean(values, axis=-1, keepdims=True)
    spread = jnp.mean(center * center, axis=-1, keepdims=True)
    return center * lax.rsqrt(spread + 1e-05) * gain + shift


def gelu_tanh(values):
    return jax.nn.gelu(values, approximate=True)


def attend(query_rows, key_rows, value_rows, live_slots):
    entry_count = query_rows.shape[0]
    query_heads = query_rows.reshape(entry_count, HEADS, HDIM)
    key_heads = key_rows.reshape(entry_count, SLOTS, HEADS, HDIM)
    value_heads = value_rows.reshape(entry_count, SLOTS, HEADS, HDIM)
    scores = jnp.einsum("ehd,eshd->ehs", query_heads, key_heads, precision=HIGHEST) / math.sqrt(
        HDIM
    )
    scores = jnp.where(live_slots[:, None, :], scores, -1e30)
    scores = scores - jnp.max(scores, axis=-1, keepdims=True)
    expped = jnp.exp(scores)
    probabilities = expped / jnp.sum(expped, axis=-1, keepdims=True)
    mixed_heads = jnp.einsum("ehs,eshd->ehd", probabilities, value_heads, precision=HIGHEST)
    return mixed_heads.reshape(entry_count, D)


PIECE_CAPS = {1024: 58, 256: 16}
BOTH = ("wide", "narrow")


def piece_cap(group_rows):
    cap = PIECE_CAPS.get(group_rows, group_rows)
    return -(-cap // 16) * 16


def contract_rows(left, right):
    return lax.dot_general(
        left, right, (((0,), (0,)), ((), ())), preferred_element_type=jnp.float32
    )


def gram_of(block):
    return lax.dot_general(block, block, (((0,), (0,)), ((), ())), precision=HIGHEST)


def adam(vec_grad, vec_master, vec_moment1, vec_moment2, vec_ema):
    moment_one = ADAM_BETA1 * vec_moment1 + (1.0 - ADAM_BETA1) * vec_grad
    moment_two = ADAM_BETA2 * vec_moment2 + (1.0 - ADAM_BETA2) * vec_grad * vec_grad
    corrected_one = moment_one / (1.0 - ADAM_BETA1**STEP)
    corrected_two = moment_two / (1.0 - ADAM_BETA2**STEP)
    vec_weight = vec_master - ADAM_RATE * corrected_one / (jnp.sqrt(corrected_two) + ADAM_EPSILON)
    vec_ema_new = EMA_DECAY * vec_ema + (1.0 - EMA_DECAY) * vec_weight
    return vec_grad, moment_one, moment_two, vec_weight, vec_ema_new


def on_device_plain(
    piece_table,
    piece_ids,
    slot_mask,
    text_ids,
    text_mask,
    text_cot,
    mat_master,
    mat_momentum,
    mat_ema,
    vec_master,
    vec_moment1,
    vec_moment2,
    vec_ema,
):
    narrow_count = lax.axis_size("narrow")
    wide_count = lax.axis_size("wide")
    device_count = narrow_count * wide_count
    wide_at = lax.axis_index("wide")
    narrow_at = lax.axis_index("narrow")
    me = wide_at * narrow_count + narrow_at
    block_rows = mat_master.shape[1]
    own_rows = block_rows // wide_count
    own_part = lax.dynamic_slice_in_dim(mat_master[0], wide_at * own_rows, own_rows, 0)
    packed_bf = lax.all_gather(
        own_part.astype(jnp.bfloat16), ("narrow", "wide"), axis=0, tiled=True
    ).reshape(narrow_count, block_rows, D)
    w_qkv, w_out, w_up, w_down, w_proj = unpack(packed_bf, narrow_count)
    (
        cls_vec,
        positions,
        ln1_gain,
        ln1_shift,
        ln2_gain,
        ln2_shift,
        final_gain,
        final_shift,
        bias_up,
        bias_down,
        bias_out,
    ) = split_vectors(vec_master)
    entries = piece_ids.shape[0]
    slot_ids = piece_ids.reshape(-1)
    slot_count = slot_ids.shape[0]
    group_rows = piece_table.shape[0]
    cap = piece_cap(group_rows)
    every_ids = lax.all_gather(slot_ids, BOTH, axis=0, tiled=False)
    asked = every_ids // group_rows == me
    before = (
        lax.broadcasted_iota(jnp.int32, (slot_count, slot_count), 0)
        < lax.broadcasted_iota(jnp.int32, (slot_count, slot_count), 1)
    )
    asked_rank = jnp.dot(
        asked.astype(jnp.bfloat16), before.astype(jnp.bfloat16), preferred_element_type=jnp.float32
    ).astype(jnp.int32)
    asked_rank = jnp.where(asked, asked_rank, -1)
    chosen = asked_rank[:, None, :] == lax.iota(jnp.int32, cap)[None, :, None]
    local_ids = every_ids - me * group_rows + 1
    asked_rows = jnp.sum(jnp.where(chosen, local_ids[:, None, :], 0), axis=2).reshape(-1) - 1
    asked_onehot = (
        asked_rows[:, None] == lax.iota(jnp.int32, group_rows)[None, :]
    ).astype(jnp.bfloat16)
    outgoing = jnp.dot(asked_onehot, piece_table, preferred_element_type=jnp.float32)
    incoming = lax.all_to_all(
        outgoing.astype(jnp.bfloat16).reshape(device_count, cap, D), BOTH, 0, 0, tiled=True
    ).reshape(device_count * cap, D)
    own_group = slot_ids // group_rows
    same = (own_group[:, None] == own_group[None, :]) & before.T
    own_rank = jnp.sum(same.astype(jnp.int32), axis=1)
    own_spot = own_group * cap + own_rank
    own_onehot = (
        own_spot[:, None] == lax.iota(jnp.int32, device_count * cap)[None, :]
    ).astype(jnp.bfloat16)
    looked = jnp.dot(own_onehot, incoming, preferred_element_type=jnp.float32)
    pieces = looked.reshape(entries, PSLOTS, D)

    flat_ids = text_ids.reshape(-1)
    flat_mask = text_mask.reshape(-1)
    token_count = flat_ids.shape[0]
    feature_rows = text_cot.shape[0]
    all_entries = entries * device_count
    block_len = min(512, token_count)
    entry_index = lax.iota(jnp.int32, all_entries)

    def text_block(step_index, grad_cols):
        begin_at = step_index * block_len
        ids_now = lax.dynamic_slice_in_dim(flat_ids, begin_at, block_len)
        keep_mask = lax.dynamic_slice_in_dim(flat_mask, begin_at, block_len)
        onehot = (entry_index[:, None] == ids_now[None, :]).astype(jnp.bfloat16)
        cot_now = lax.dynamic_slice_in_dim(text_cot, begin_at, block_len, 1)
        masked_cot = jnp.where(keep_mask[None, :] > 0, cot_now, jnp.zeros_like(cot_now))
        return grad_cols + lax.dot_general(
            masked_cot, onehot, (((1,), (1,)), ((), ())), preferred_element_type=jnp.float32
        )

    grad_cols = lax.fori_loop(
        0, token_count // block_len, text_block, jnp.zeros((feature_rows, all_entries), jnp.float32)
    )
    grad_table_cols = grad_cols.astype(jnp.bfloat16)
    grad_table = lax.all_to_all(grad_table_cols, BOTH, split_axis=1, concat_axis=0, tiled=True)
    grad_bias_own = jnp.sum(grad_table_cols.astype(jnp.float32), axis=1)
    grad_normed_three = contract_rows(grad_table, w_proj)

    first_slot = jnp.broadcast_to(cls_vec + positions[0], (entries, 1, D))
    slots_x = jnp.concatenate([first_slot, pieces + positions[1:]], axis=1)
    live_slots = jnp.concatenate([jnp.ones((entries, 1), jnp.int32), slot_mask], axis=1) > 0
    normed, norm1_pull = jax.vjp(layer_norm, slots_x, ln1_gain, ln1_shift)
    normed_bf = normed.astype(jnp.bfloat16)
    query_rows = jnp.einsum(
        "ed,fd->ef", normed_bf[:, 0], w_qkv[:D], preferred_element_type=jnp.float32
    )
    key_value = jnp.einsum("esd,fd->esf", normed_bf, w_qkv[D:], preferred_element_type=jnp.float32)
    attended, attend_pull = jax.vjp(
        partial(attend, live_slots=live_slots), query_rows, key_value[:, :, :D], key_value[:, :, D:]
    )
    attended_bf = attended.astype(jnp.bfloat16)
    residual = slots_x[:, 0] + jnp.einsum(
        "ed,fd->ef", attended_bf, w_out, preferred_element_type=jnp.float32
    )
    normed_two, norm2_pull = jax.vjp(layer_norm, residual, ln2_gain, ln2_shift)
    normed_two_bf = normed_two.astype(jnp.bfloat16)
    gate_in = (
        jnp.einsum("ed,fd->ef", normed_two_bf, w_up, preferred_element_type=jnp.float32) + bias_up
    )
    active, gelu_pull = jax.vjp(gelu_tanh, gate_in)
    active_bf = active.astype(jnp.bfloat16)
    second_residual = residual + (
        jnp.dot(active_bf, w_down, preferred_element_type=jnp.float32) + bias_down
    )
    normed_three, norm3_pull = jax.vjp(layer_norm, second_residual, final_gain, final_shift)
    normed_three_bf = normed_three.astype(jnp.bfloat16)
    every_normed = lax.all_gather(normed_three_bf, BOTH, axis=0, tiled=True)
    proj_own = lax.dynamic_slice_in_dim(w_proj, me * feature_rows, feature_rows, 0)
    bias_own = lax.dynamic_slice_in_dim(bias_out, me * feature_rows, feature_rows, 0)
    table_cols = (
        jnp.einsum("fd,ed->fe", proj_own, every_normed, preferred_element_type=jnp.float32)
        + bias_own[:, None]
    )
    text_embeds = jnp.take(table_cols, flat_ids, axis=1) * flat_mask[None, :].astype(jnp.float32)
    grad_proj_own = jnp.dot(grad_table_cols, every_normed, preferred_element_type=jnp.float32)

    grad_second, grad_final_gain, grad_final_shift = norm3_pull(grad_normed_three)
    grad_branch_two = grad_second.astype(jnp.bfloat16)
    grad_bias_down = jnp.sum(grad_branch_two.astype(jnp.float32), axis=0)
    grad_down = contract_rows(active_bf, grad_branch_two)
    grad_active = jnp.einsum(
        "ed,fd->ef", grad_branch_two, w_down, preferred_element_type=jnp.float32
    )
    (grad_gate,) = gelu_pull(grad_active)
    grad_gate_bf = grad_gate.astype(jnp.bfloat16)
    grad_bias_up = jnp.sum(grad_gate_bf.astype(jnp.float32), axis=0)
    grad_up = contract_rows(grad_gate_bf, normed_two_bf)
    grad_normed_two = jnp.dot(grad_gate_bf, w_up, preferred_element_type=jnp.float32)
    grad_residual_norm, grad_ln2_gain, grad_ln2_shift = norm2_pull(grad_normed_two)
    grad_residual = grad_second + grad_residual_norm
    grad_branch_one = grad_residual.astype(jnp.bfloat16)
    grad_out_w = contract_rows(grad_branch_one, attended_bf)
    grad_attended = jnp.dot(grad_branch_one, w_out, preferred_element_type=jnp.float32)
    grad_query, grad_keys, grad_values = attend_pull(grad_attended)
    grad_query_bf = grad_query.astype(jnp.bfloat16)
    grad_kv = jnp.concatenate(
        [grad_keys.astype(jnp.bfloat16), grad_values.astype(jnp.bfloat16)], axis=2
    )
    grad_q_w = contract_rows(grad_query_bf, normed_bf[:, 0])
    grad_kv_w = jnp.einsum("esf,esd->fd", grad_kv, normed_bf, preferred_element_type=jnp.float32)
    grad_normed = jnp.einsum("esf,fd->esd", grad_kv, w_qkv[D:], preferred_element_type=jnp.float32)
    grad_normed = grad_normed.at[:, 0].add(
        jnp.dot(grad_query_bf, w_qkv[:D], preferred_element_type=jnp.float32)
    )
    grad_slots, grad_ln1_gain, grad_ln1_shift = norm1_pull(grad_normed)
    grad_first = grad_slots[:, 0] + grad_residual
    grad_cls = jnp.sum(grad_first, axis=0)
    grad_pos = jnp.concatenate([grad_cls[None], jnp.sum(grad_slots[:, 1:], axis=0)], axis=0)
    grad_pieces = grad_slots[:, 1:].astype(jnp.bfloat16).reshape(-1, D)
    grad_outgoing = contract_rows(own_onehot, grad_pieces).astype(jnp.bfloat16)
    grad_incoming = lax.all_to_all(
        grad_outgoing.reshape(device_count, cap, D), BOTH, 0, 0, tiled=True
    ).reshape(device_count * cap, D)
    piece_grad = contract_rows(asked_onehot, grad_incoming)

    vec_local = jnp.concatenate(
        [
            grad_cls,
            grad_pos.reshape(-1),
            grad_ln1_gain,
            grad_ln1_shift,
            grad_ln2_gain,
            grad_ln2_shift,
            grad_final_gain,
            grad_final_shift,
            grad_bias_up,
            grad_bias_down,
            lax.dynamic_update_slice_in_dim(
                jnp.zeros((OUTW,), jnp.float32), grad_bias_own, me * feature_rows, 0
            ),
        ]
    )
    vec_grad = lax.psum(vec_local, BOTH)
    grad_qkv = jnp.concatenate([grad_q_w, grad_kv_w], axis=0)
    packed_term = jnp.concatenate(
        [
            matrix.reshape(narrow_count, matrix.shape[0] // narrow_count, D)
            for matrix in (grad_qkv, grad_out_w, grad_up, grad_down)
        ],
        axis=1,
    )
    term_rows = packed_term.shape[1]
    share = term_rows // wide_count
    packed_term = (
        packed_term.astype(jnp.bfloat16)
        .reshape(narrow_count, wide_count, share, D)
        .transpose(1, 0, 2, 3)
        .reshape(device_count, share, D)
    )
    terms = lax.all_to_all(packed_term, BOTH, 0, 0, tiled=True)
    share_sum = jnp.sum(terms.astype(jnp.float32), axis=0)
    main_grad = lax.all_gather(share_sum.astype(jnp.bfloat16), "wide", axis=0, tiled=True)
    proj_grad = lax.all_gather(grad_proj_own.astype(jnp.bfloat16), BOTH, axis=0, tiled=True)
    proj_rows = OUTW // narrow_count
    proj_grad = lax.dynamic_slice_in_dim(proj_grad, narrow_at * proj_rows, proj_rows, 0)
    grad_block = jnp.concatenate([main_grad, proj_grad], axis=0).astype(jnp.float32)
    momentum_block = MUON_BETA * mat_momentum[0] + grad_block
    update_block = grad_block + MUON_BETA * momentum_block
    segments = block_slices(update_block, narrow_count)
    grams = lax.psum(jnp.stack([gram_of(segment) for segment in segments]), "narrow")
    new_segments = []
    for position, (row_total, master_seg, segment) in enumerate(
        zip(matrix_rows(), block_slices(mat_master[0], narrow_count), segments)
    ):
        square = jnp.sum(jnp.diagonal(grams[position]))
        norm = jnp.sqrt(square) + 1e-07
        gram = grams[position] / (norm * norm)
        chain = None
        for sweep_index in range(5):
            squared = jnp.dot(gram, gram, precision=HIGH)
            poly = NEWTON_B * gram + NEWTON_C * squared + NEWTON_A * jnp.eye(D, dtype=jnp.float32)
            chain = poly if chain is None else jnp.dot(chain, poly, precision=HIGH)
            if sweep_index < 4:
                gram = jnp.dot(jnp.dot(gram, poly, precision=HIGH), poly, precision=HIGH)
        ortho = jnp.dot(segment / norm, chain, precision=HIGH)
        new_segments.append(
            master_seg * (1.0 - MUON_RATE * MUON_DECAY)
            - MUON_RATE * math.sqrt(row_total / D) * ortho
        )
    weight_block = jnp.concatenate(new_segments, axis=0)[None]
    ema_block = EMA_DECAY * mat_ema + (1.0 - EMA_DECAY) * weight_block
    return (
        text_embeds,
        piece_grad,
        grad_block[None],
        momentum_block[None],
        weight_block,
        ema_block,
    ) + adam(vec_grad, vec_master, vec_moment1, vec_moment2, vec_ema)


MESH_ID = pl.DeviceIdType.MESH
CORES = 2
CHIPS = 4
PLANES = 4
MAIN = 192
CHUNKS = 3
CHUNK = MAIN // CHUNKS
PROJ = 32
PART = MAIN + PLANES * PROJ
VROWS = 16


def place():
    wide_at = lax.axis_index("wide")
    plane = lax.axis_index("narrow")
    chip = wide_at // CORES
    core = lax.rem(wide_at, CORES)
    return wide_at, plane, chip, core


def enter(targets):
    barrier = pltpu.get_barrier_semaphore()
    for target in targets:
        pl.semaphore_signal(barrier, inc=1, device_id=target, device_id_type=MESH_ID)
    pl.semaphore_wait(barrier, len(targets))


def neighbours(wide_at, plane, chip, core):
    sibling = (chip * CORES + 1 - core, plane)
    chips = [(lax.rem(chip + k, CHIPS) * CORES + core, plane) for k in range(1, CHIPS)]
    planes = [(wide_at, lax.rem(plane + k, PLANES)) for k in range(1, PLANES)]
    return sibling, chips, planes


def remote(src, dst, sems, index, target):
    return pltpu.make_async_remote_copy(
        src_ref=src,
        dst_ref=dst,
        send_sem=sems[0].at[index],
        recv_sem=sems[1].at[index],
        device_id=target,
        device_id_type=MESH_ID,
    )

OWNERS = (6, 7, 2, 4, 0)
BLOCK_TILES = (3, 1, 4, 4, 8)
MOST_TILES = max(BLOCK_TILES)
MAIN_TILES = 12
BANDS = 4
TEXT_TILE = 512
TILE = 128
SIDE = 2
STRIPS = 8
STRIP = D // STRIPS
PACKED = 640
PIECES = ((0, 64, 1024), (64, 64, 512), (128, 16, 384), (144, 48, 0))


def halves(value):
    high = value.astype(jnp.bfloat16)
    return high, (value - high.astype(jnp.float32)).astype(jnp.bfloat16)


def plain_dot(left, right):
    return jnp.dot(left, right, preferred_element_type=jnp.float32)


def split_dot(left, right):
    return plain_dot(left[0], right[0]) + (
        plain_dot(left[0], right[1]) + plain_dot(left[1], right[0])
    )


def dot_nt(left, right):
    return lax.dot_general(
        left, right, (((1,), (1,)), ((), ())), preferred_element_type=jnp.float32
    )


def dot_tn(left, right):
    return lax.dot_general(
        left, right, (((0,), (0,)), ((), ())), preferred_element_type=jnp.float32
    )


def band_onehot(ids, rows):
    place_in = lax.rem(ids, rows)
    spots = lax.broadcasted_iota(jnp.int32, (rows, ids.shape[1]), 0)
    return jnp.where(spots == place_in, 1.0, 0.0).astype(jnp.bfloat16)


def across(wide_at, plane, chip, core):
    x_at = lax.rem(chip, SIDE)
    x_chip = chip + 1 - 2 * x_at
    y_chip = lax.rem(chip + SIDE, CHIPS)
    return x_chip * CORES + core, y_chip * CORES + core


def owner_tiles(wide_at):
    tile_count = jnp.int32(0)
    tile_first = jnp.int32(0)
    begin = 0
    for owner, count in zip(OWNERS, BLOCK_TILES):
        tile_count = tile_count + jnp.where(wide_at == owner, count, 0)
        tile_first = tile_first + jnp.where(wide_at == owner, begin, 0)
        begin = begin + count
    return tile_count, tile_first


def spread_steps(own, held, sems, base, at):
    wide_at, plane, chip, core = at
    sibling = (chip * CORES + 1 - core, plane)
    x_wide, y_wide = across(wide_at, plane, chip, core)
    x_near, y_near = (x_wide, plane), (y_wide, plane)
    diagonal_wide = (CHIPS - 1 - chip) * CORES + core
    half = own.shape[0] // 2
    tops, bottoms = pl.ds(0, half), pl.ds(half, half)
    above, below = (wide_at, plane + 1), (wide_at, plane - 1)

    def climb(distance, source, src):
        spot = held.at[source, wide_at]
        return remote(spot if src is None else src, spot, sems, base + distance - 1, above)

    def sink(distance, source, src):
        spot = held.at[source, wide_at]
        return remote(spot if src is None else src, spot, sems, base + 2 + distance, below)

    def plane_copy(source, kind, src=None):
        index = base + 6 + 9 * source + kind
        own_spot = held.at[source, wide_at]
        x_spot, y_spot = held.at[source, x_wide], held.at[source, y_wide]
        far_spot = held.at[source, diagonal_wide]
        if kind in (0, 1, 2):
            target = (x_near, y_near, sibling)[kind]
            return remote(own_spot if src is None else src, own_spot, sems, index, target)
        if kind == 3:
            return remote(x_spot.at[tops], x_spot.at[tops], sems, index, y_near)
        if kind == 5:
            return remote(y_spot.at[bottoms], y_spot.at[bottoms], sems, index, x_near)
        if kind in (4, 6):
            spot = x_spot if kind == 4 else y_spot
            return remote(spot, spot, sems, index, sibling)
        rows = tops if kind == 7 else bottoms
        return remote(far_spot.at[rows], far_spot.at[rows], sems, index, sibling)

    def plane_send(source, src=None):
        for kind in (0, 1, 2):
            plane_copy(source, kind, src).start()

    def begin():
        @pl.when(plane < PLANES - 1)
        def _():
            climb(1, plane, own).start()

        @pl.when(plane > 0)
        def _():
            sink(1, plane, own).start()

        plane_send(plane, own)

    def arrive(distance):
        @pl.when(plane >= distance)
        def _():
            source = plane - distance
            climb(distance, source, None).wait_recv()
            if distance < PLANES - 1:

                @pl.when(plane < PLANES - 1)
                def _():
                    climb(distance + 1, source, None).start()

            plane_send(source)

        @pl.when(plane + distance < PLANES)
        def _():
            source = plane + distance
            sink(distance, source, None).wait_recv()
            if distance < PLANES - 1:

                @pl.when(plane > 0)
                def _():
                    sink(distance + 1, source, None).start()

            plane_send(source)

    def at_distance(distance, step):
        if distance == 0:
            step(plane)
            return

        @pl.when(plane >= distance)
        def _():
            step(plane - distance)

        @pl.when(plane + distance < PLANES)
        def _():
            step(plane + distance)

    def relay_one(source):
        plane_copy(source, 0).wait_recv()
        plane_copy(source, 3).start()
        plane_copy(source, 4).start()
        plane_copy(source, 1).wait_recv()
        plane_copy(source, 5).start()
        plane_copy(source, 6).start()

    def finish_one(source):
        plane_copy(source, 3).wait_recv()
        plane_copy(source, 7).start()
        plane_copy(source, 5).wait_recv()
        plane_copy(source, 8).start()

    def settle_one(source):
        for kind in (2, 4, 6, 7, 8):
            plane_copy(source, kind).wait_recv()
        for kind in range(9):
            plane_copy(source, kind).wait_send()

    def relay(distance):
        at_distance(distance, relay_one)

    def finish(distance):
        at_distance(distance, finish_one)

    def settled():
        for distance in range(PLANES):
            at_distance(distance, settle_one)
        for distance in range(1, PLANES):
            source = plane - distance + 1

            @pl.when((plane < PLANES - 1) & (source >= 0))
            def _(distance=distance, source=source):
                climb(distance, source, None).wait_send()

            down_source = plane + distance - 1

            @pl.when((plane > 0) & (down_source < PLANES))
            def _(distance=distance, down_source=down_source):
                sink(distance, down_source, None).wait_send()

    return begin, arrive, relay, finish, settled


def settle_kernel(
    z_ref,
    main_ref,
    vec_ref,
    grad_ref,
    proj_ref,
    bias_ref,
    momentum_ref,
    ids_ref,
    mask_ref,
    text_ref,
    sum_ref,
    proj_sum_ref,
    vec_out_ref,
    gram_ref,
    high_ref,
    low_ref,
    every,
    table_ref,
    text_tiles,
    near,
    first,
    x_first,
    y_first,
    x_second,
    y_second,
    second,
    deep,
    proj_own,
    proj_far,
    part,
    proj_part,
    vec_near,
    vec_far,
    vec_deep,
    main_tiles,
    proj_tiles,
    momentum_tiles,
    packs,
    pieces,
    totals,
    local_sem,
    tile_sem,
    text_sem,
    z_send,
    z_recv,
    main_send,
    main_recv,
    far_send,
    far_recv,
    deep_send,
    deep_recv,
    done_send,
    done_recv,
    pass_send,
    pass_recv,
    proj_send,
    proj_recv,
    vec_send,
    vec_recv,
    gram_send,
    gram_recv,
):
    wide_at, plane, chip, core = place()
    sibling, chips, planes = neighbours(wide_at, plane, chip, core)
    x_wide, y_wide = across(wide_at, plane, chip, core)
    x_near, y_near = (x_wide, plane), (y_wide, plane)
    diagonal_wide = (CHIPS - 1 - chip) * CORES + core
    other = 1 - core
    x_at = lax.rem(chip, SIDE)
    y_at = chip // SIDE
    tile_count, tile_first = owner_tiles(wide_at)

    own_main = pltpu.make_async_copy(main_ref.at[core], first, local_sem.at[0])
    own_main.start()

    def momentum_load(tile):
        source = pl.ds(pl.multiple_of((tile_first + tile) * TILE, TILE), TILE)
        return pltpu.make_async_copy(
            momentum_ref.at[source], momentum_tiles.at[tile], tile_sem.at[0, tile]
        )

    @pl.loop(0, tile_count)
    def _(tile):
        momentum_load(tile).start()

    enter([sibling] + chips + planes)

    vec_sems = (vec_send, vec_recv)
    vec_copies = [remote(vec_ref.at[other], vec_near, vec_sems, 0, sibling)]
    vec_copies[0].start()
    z_begin, z_arrive, z_relay, z_finish, z_settled = spread_steps(
        z_ref, every, (z_send, z_recv), 0, place()
    )
    own_z = pltpu.make_async_copy(z_ref, every.at[plane, wide_at], local_sem.at[1])
    own_z.start()
    main_sems = (main_send, main_recv)
    near_copies = []
    for chunk in range(CHUNKS):
        copy = remote(main_ref.at[other, chunk], near.at[chunk], main_sems, chunk, sibling)
        copy.start()
        near_copies.append(copy)

    def vec_far_step():
        vec_copies[0].wait_recv()
        vec_far[chip] = vec_ref[core] + vec_near[...]
        for k, target in enumerate(chips):
            copy = remote(vec_far.at[chip], vec_far.at[chip], vec_sems, 1 + k, target)
            copy.start()
            vec_copies.append(copy)

    def vec_deep_step():
        for copy in vec_copies[1:4]:
            copy.wait()
        vec_deep[plane] = (vec_far[0] + vec_far[1]) + (vec_far[2] + vec_far[3])
        for k, target in enumerate(planes):
            copy = remote(vec_deep.at[plane], vec_deep.at[plane], vec_sems, 4 + k, target)
            copy.start()
            vec_copies.append(copy)

    def vec_last_step():
        for copy in vec_copies[4:7]:
            copy.wait()
        vec_out_ref[core] = (vec_deep[0] + vec_deep[1]) + (vec_deep[2] + vec_deep[3])
        copy = remote(vec_out_ref.at[core], vec_out_ref.at[core], vec_sems, 7, sibling)
        copy.start()
        vec_copies.append(copy)

    far_sems = (far_send, far_recv)
    lows, highs = pl.ds(0, 2), pl.ds(2, 2)
    firsts = []

    def first_step(chunk):
        near_copies[chunk].wait_recv()

        @pl.loop(0, CHIPS * PLANES)
        def _(step):
            y, x, m = step // (SIDE * PLANES), lax.rem(step // PLANES, SIDE), lax.rem(step, PLANES)
            first[chunk, y, x, m] = (
                first[chunk, y, x, m].astype(jnp.float32)
                + near[chunk, y, x, m].astype(jnp.float32)
            ).astype(jnp.bfloat16)

        by_x = remote(
            first.at[chunk, :, 1 - x_at, lows], x_first.at[chunk], far_sems, chunk * 4, x_near
        )
        by_y = remote(
            first.at[chunk, 1 - y_at, :, highs], y_first.at[chunk], far_sems, chunk * 4 + 1, y_near
        )
        by_x.start()
        by_y.start()
        firsts.append((by_x, by_y))

    seconds = []

    def second_step(chunk):
        by_x, by_y = firsts[chunk]
        by_x.wait_recv()
        for y in range(SIDE):
            for m in range(2):
                first[chunk, y, x_at, m] = (
                    first[chunk, y, x_at, m].astype(jnp.float32)
                    + x_first[chunk, y, m].astype(jnp.float32)
                ).astype(jnp.bfloat16)
        next_y = remote(
            first.at[chunk, 1 - y_at, x_at, lows],
            y_second.at[chunk],
            far_sems,
            chunk * 4 + 2,
            y_near,
        )
        next_y.start()
        by_y.wait_recv()
        for x in range(SIDE):
            for m in range(2):
                first[chunk, y_at, x, 2 + m] = (
                    first[chunk, y_at, x, 2 + m].astype(jnp.float32)
                    + y_first[chunk, x, m].astype(jnp.float32)
                ).astype(jnp.bfloat16)
        next_x = remote(
            first.at[chunk, y_at, 1 - x_at, highs],
            x_second.at[chunk],
            far_sems,
            chunk * 4 + 3,
            x_near,
        )
        next_x.start()
        seconds.append((next_y, next_x))

    deep_sems = (deep_send, deep_recv)
    deep_copies = []

    def deep_step(chunk):
        next_y, next_x = seconds[chunk]
        next_y.wait_recv()
        for m in range(2):
            second[chunk, m] = (
                first[chunk, y_at, x_at, m].astype(jnp.float32)
                + y_second[chunk, m].astype(jnp.float32)
            ).astype(jnp.bfloat16)
        next_x.wait_recv()
        for m in range(2):
            second[chunk, 2 + m] = (
                first[chunk, y_at, x_at, 2 + m].astype(jnp.float32)
                + x_second[chunk, m].astype(jnp.float32)
            ).astype(jnp.bfloat16)
        copies = []
        for k, target in enumerate(planes):
            to_plane = lax.rem(plane + k + 1, PLANES)
            copy = remote(
                second.at[chunk, to_plane], deep.at[chunk, k], deep_sems, chunk * 3 + k, target
            )
            copy.start()
            copies.append(copy)
        deep_copies.append(copies)

    count = every.shape[2]
    features = proj_ref.shape[0]
    wide_count = CHIPS * CORES
    per_band = grad_ref.shape[0] // BANDS
    proj_sems = (proj_send, proj_recv)
    proj_copies = []

    def proj_near_step():
        total = jnp.zeros((features, D), jnp.float32)
        for block in range(PLANES * wide_count):
            rows = every[block % PLANES, block // PLANES]
            total = total + dot_tn(grad_ref[block], rows)
        proj_own[...] = total.astype(jnp.bfloat16).reshape(CHIPS, PROJ, D)
        for k, target in enumerate(chips):
            to_chip = lax.rem(chip + k + 1, CHIPS)
            copy = remote(proj_own.at[to_chip], proj_far.at[chip], proj_sems, k, target)
            copy.start()
            proj_copies.append(copy)
        proj_far[chip] = proj_own[chip]

    def proj_far_step():
        for copy in proj_copies:
            copy.wait()
        for k, target in enumerate(planes):
            to_plane = lax.rem(plane + k + 1, PLANES)
            copy = remote(proj_far.at[to_plane], proj_part.at[plane], proj_sems, 3 + k, target)
            copy.start()
            proj_copies.append(copy)
        proj_part[plane] = proj_far[plane]

    def publish_proj():
        for copy in proj_copies[3:]:
            copy.wait()
        publish(len(PIECES), proj_part, proj_natural(chip, core))

    done_sems = (done_send, done_recv)
    pass_sems = (pass_send, pass_recv)
    done_copies = []
    locals_done = []

    def natural(index, wide):
        _, size, base = PIECES[index]
        return sum_ref.at[pl.ds(pl.multiple_of(base + wide * size, 16), size)]

    def proj_natural(at_chip, at_core):
        return proj_sum_ref.at[at_core, :, at_chip]

    def publish(index, src, spot):
        copies = []
        for k, target in enumerate([sibling] + chips):
            copy = remote(src, spot, done_sems, index * 4 + k, target)
            copy.start()
            copies.append(copy)
        done_copies.append(copies)
        copy = pltpu.make_async_copy(src, spot, local_sem.at[2 + index])
        copy.start()
        locals_done.append(copy)

    def publish_step(chunk):
        for copy in deep_copies[chunk]:
            copy.wait_recv()
        value = second[chunk, plane].astype(jnp.float32)
        for k in range(3):
            value = value + deep[chunk, k].astype(jnp.float32)
        part[chunk * CHUNK : (chunk + 1) * CHUNK, :] = value.astype(jnp.bfloat16)
        for index, (offset, size, _) in enumerate(PIECES):
            if offset // CHUNK == chunk:
                publish(index, part.at[pl.ds(offset, size)], natural(index, wide_at))

    pass_copies = []

    def pass_step(index):
        for k in range(3):
            done_copies[index][1 + k].wait_recv()
            from_chip = lax.rem(chip + CHIPS - 1 - k, CHIPS)
            if index < len(PIECES):
                spot = natural(index, from_chip * CORES + core)
            else:
                spot = proj_natural(from_chip, core)
            copy = remote(spot, spot, pass_sems, index * 3 + k, sibling)
            copy.start()
            pass_copies.append(copy)

    def table_step():
        for block in range(PLANES * wide_count):
            rows = every[block % PLANES, block // PLANES]
            band, spot = divmod(block, per_band)
            table_ref[band * features : (band + 1) * features, spot * count : (spot + 1) * count] = (
                dot_nt(proj_ref[...], rows) + bias_ref[...]
            ).astype(jnp.bfloat16)

    text_rows = table_ref.shape[1]
    row_tiles = ids_ref.shape[1] // TEXT_TILE
    text_count = ids_ref.shape[0] * row_tiles

    def text_copy(step):
        slot = lax.rem(step, 2)
        lanes = pl.ds(pl.multiple_of(step * TEXT_TILE, TEXT_TILE), TEXT_TILE)
        return pltpu.make_async_copy(text_tiles.at[slot], text_ref.at[:, lanes], text_sem.at[slot])

    def text_steps(begin, end):
        @pl.loop(begin, end)
        def _(step):
            row = pl.ds(step // row_tiles, 1)
            start = lax.rem(step, row_tiles) * TEXT_TILE
            id_lanes = pl.ds(pl.multiple_of(start, TEXT_TILE), TEXT_TILE)
            ids = ids_ref[row, id_lanes]
            values = plain_dot(table_ref[...], band_onehot(ids, text_rows))
            band = jnp.where(mask_ref[row, id_lanes] > 0, ids // text_rows, -1)
            total = jnp.zeros((features, TEXT_TILE), jnp.float32)
            for b in range(BANDS):
                total = jnp.where(band == b, values[b * features : (b + 1) * features], total)

            @pl.when(step >= 2)
            def _():
                text_copy(step - 2).wait()

            text_tiles[lax.rem(step, 2)] = total
            text_copy(step).start()

    own_main.wait()
    z_begin()
    first_step(0)
    vec_far_step()
    first_step(1)
    z_arrive(1)
    first_step(2)
    z_relay(0)
    z_arrive(2)
    second_step(0)
    z_relay(1)
    z_arrive(3)
    second_step(1)
    z_finish(0)
    z_relay(2)
    second_step(2)
    deep_step(0)
    z_finish(1)
    z_relay(3)
    deep_step(1)
    z_finish(2)
    z_finish(3)
    deep_step(2)
    own_z.wait()
    z_settled()
    proj_near_step()
    vec_deep_step()
    publish_step(0)
    publish_step(1)
    proj_far_step()
    publish_step(2)
    table_step()
    vec_last_step()
    publish_proj()
    for index in range(len(PIECES) + 1):
        pass_step(index)
    for copies in done_copies:
        copies[0].wait_recv()
    for copy in pass_copies:
        copy.wait_recv()
    for copy in locals_done:
        copy.wait()

    gram_sems = (gram_send, gram_recv)

    def add_tile(tile, gradient):
        momentum_load(tile).wait()
        gradient = gradient.astype(jnp.float32)
        update = gradient + MUON_BETA * (MUON_BETA * momentum_tiles[tile] + gradient)
        high, low = halves(update)
        rows = pl.ds(pl.multiple_of(tile * TILE, TILE), TILE)
        high_ref[rows, :] = high
        low_ref[rows, :] = low

    @pl.when(wide_at == OWNERS[4])
    def _():
        loads = [
            pltpu.make_async_copy(
                proj_sum_ref.at[tile // PLANES, tile % PLANES],
                proj_tiles.at[tile],
                tile_sem.at[1, tile],
            )
            for tile in range(MOST_TILES)
        ]
        for copy in loads:
            copy.start()
        for copy in loads:
            copy.wait()

        @pl.loop(0, MOST_TILES)
        def _(tile):
            add_tile(tile, proj_tiles[tile].reshape(TILE, D))

    @pl.when((tile_count > 0) & (wide_at != OWNERS[4]))
    def _():
        def load(tile):
            source = pl.ds(pl.multiple_of((tile_first + tile) * TILE, TILE), TILE)
            return pltpu.make_async_copy(
                sum_ref.at[source], main_tiles.at[tile], tile_sem.at[1, tile]
            )

        @pl.loop(0, tile_count)
        def _(tile):
            load(tile).start()

        @pl.loop(0, tile_count)
        def _(tile):
            load(tile).wait()
            add_tile(tile, main_tiles[tile])

    for count_here in sorted(set(BLOCK_TILES)):

        @pl.when(tile_count == count_here)
        def _(count_here=count_here):
            high = high_ref[0 : count_here * TILE, :]
            cross = dot_tn(high, low_ref[0 : count_here * TILE, :])
            gram_ref[...] = dot_tn(high, high) + (cross + cross.T)

    def gram_copies(first_index):
        copies = []
        for k, target in enumerate(planes):
            to_plane = lax.rem(plane + k + 1, PLANES)
            if first_index == 0:
                src, dst = packs.at[to_plane], pieces.at[plane]
            else:
                src, dst = totals.at[plane], totals.at[plane]
            copies.append(remote(src, dst, gram_sems, first_index + k, target))
        return copies

    owning = tile_count > 0

    @pl.when(owning)
    def _():
        for t in range(PLANES):
            for strip, lane in ((t, 0), (STRIPS - 1 - t, 1)):
                begin = strip // 2 * TILE
                value = gram_ref[strip * STRIP : (strip + 1) * STRIP, begin:]
                width = D - begin
                at = 0 if lane == 0 else PACKED - width
                packs[t, :, at : at + width] = value
        for copy in gram_copies(0):
            copy.start()
        pieces[plane] = packs[plane]

    text_steps(0, text_count // 2)

    @pl.when(owning)
    def _():
        for copy in gram_copies(0):
            copy.wait()
        totals[plane] = (pieces[0] + pieces[1]) + (pieces[2] + pieces[3])
        for copy in gram_copies(3):
            copy.start()

    text_steps(text_count // 2, text_count)

    @pl.when(owning)
    def _():
        for copy in gram_copies(3):
            copy.wait()
        for t in range(PLANES):
            for strip, lane in ((t, 0), (STRIPS - 1 - t, 1)):
                begin = strip // 2 * TILE
                width = D - begin
                at = 0 if lane == 0 else PACKED - width
                gram_ref[strip * STRIP : (strip + 1) * STRIP, begin:] = totals[
                    t, :, at : at + width
                ]
        row_block = lax.broadcasted_iota(jnp.int32, (D, D), 0) // TILE
        lane_block = lax.broadcasted_iota(jnp.int32, (D, D), 1) // TILE
        value = gram_ref[...]
        gram_ref[...] = jnp.where(lane_block >= row_block, value, value.T)

    for copies in done_copies:
        for copy in copies:
            copy.wait_send()
    for copy in pass_copies:
        copy.wait_send()
    for copy in near_copies:
        copy.wait_send()
    for pair in firsts + seconds:
        for copy in pair:
            copy.wait_send()
    for copies in deep_copies:
        for copy in copies:
            copy.wait_send()
    vec_copies[0].wait_send()
    vec_copies[7].wait()
    text_copy(text_count - 2).wait()
    text_copy(text_count - 1).wait()


def settle(z_own, main, vec, grad_own, proj_own, bias_own, momentum, text_ids, text_mask):
    dma = pltpu.SemaphoreType.DMA
    f32, bf = jnp.float32, jnp.bfloat16
    features, tokens = proj_own.shape[0], text_ids.size
    rows = grad_own.shape[0] * grad_own.shape[1] // BANDS
    hbm = pl.BlockSpec(memory_space=pl.ANY)
    vmem = pl.BlockSpec(memory_space=pltpu.VMEM)
    grid = (CHUNKS, SIDE, SIDE, PLANES, CHUNK, D)
    return pl.pallas_call(
        settle_kernel,
        out_shape=(
            jax.ShapeDtypeStruct((features, tokens), f32),
            jax.ShapeDtypeStruct((MAIN_TILES * TILE, D), bf),
            jax.ShapeDtypeStruct((CORES, PLANES, CHIPS, PROJ, D), bf),
            jax.ShapeDtypeStruct((CORES, VROWS, D), f32),
            jax.ShapeDtypeStruct((D, D), f32),
            jax.ShapeDtypeStruct((MOST_TILES * TILE, D), bf),
            jax.ShapeDtypeStruct((MOST_TILES * TILE, D), bf),
        ),
        in_specs=[vmem, hbm, vmem, vmem, vmem, vmem, hbm, vmem, vmem],
        out_specs=(hbm, hbm, hbm, vmem, vmem, vmem, vmem),
        scratch_shapes=[
            pltpu.VMEM((PLANES, CHIPS * CORES) + z_own.shape, bf),
            pltpu.VMEM((BANDS * features, rows), bf),
            pltpu.VMEM((2, features, TEXT_TILE), f32),
            pltpu.VMEM(grid, bf),
            pltpu.VMEM(grid, bf),
            pltpu.VMEM((CHUNKS, SIDE, 2, CHUNK, D), bf),
            pltpu.VMEM((CHUNKS, SIDE, 2, CHUNK, D), bf),
            pltpu.VMEM((CHUNKS, 2, CHUNK, D), bf),
            pltpu.VMEM((CHUNKS, 2, CHUNK, D), bf),
            pltpu.VMEM((CHUNKS, PLANES, CHUNK, D), bf),
            pltpu.VMEM((CHUNKS, 3, CHUNK, D), bf),
            pltpu.VMEM((CHIPS, PROJ, D), bf),
            pltpu.VMEM((CHIPS, PROJ, D), bf),
            pltpu.VMEM((MAIN, D), bf),
            pltpu.VMEM((PLANES, PROJ, D), bf),
            pltpu.VMEM((VROWS, D), f32),
            pltpu.VMEM((CHIPS, VROWS, D), f32),
            pltpu.VMEM((PLANES, VROWS, D), f32),
            pltpu.VMEM((4, TILE, D), bf),
            pltpu.VMEM((MOST_TILES, CHIPS, PROJ, D), bf),
            pltpu.VMEM((MOST_TILES, TILE, D), f32),
            pltpu.VMEM((PLANES, STRIP, PACKED), f32),
            pltpu.VMEM((PLANES, STRIP, PACKED), f32),
            pltpu.VMEM((PLANES, STRIP, PACKED), f32),
            dma((8,)),
            dma((2, MOST_TILES)),
            dma((2,)),
            dma((6 + 9 * PLANES,)),
            dma((6 + 9 * PLANES,)),
            dma((CHUNKS,)),
            dma((CHUNKS,)),
            dma((CHUNKS * 4,)),
            dma((CHUNKS * 4,)),
            dma((CHUNKS * 3,)),
            dma((CHUNKS * 3,)),
            dma((20,)),
            dma((20,)),
            dma((15,)),
            dma((15,)),
            dma((6,)),
            dma((6,)),
            dma((8,)),
            dma((8,)),
            dma((6,)),
            dma((6,)),
        ],
        compiler_params=pltpu.CompilerParams(
            collective_id=3, has_side_effects=True, vmem_limit_bytes=58 * 2**20
        ),
        name="settle",
    )(
        z_own,
        main.reshape((CORES,) + grid),
        vec,
        grad_own,
        proj_own,
        bias_own,
        momentum,
        text_ids,
        text_mask,
    )


SHARES = ((6, 0, 0, 384), (7, 0, 384, 128), (2, 0, 512, 512), (4, 0, 1024, 512)) + (
    (0, 0, 1536, 512),
    (0, 512, 2048, 512),
)


def muon_kernel(
    gram_ref,
    high_ref,
    low_ref,
    out_ref,
    gram,
    poly,
    chain,
    chain_high,
    chain_low,
    rows_out,
    local_sem,
    rows_send,
    rows_recv,
):
    wide_at, plane, chip, core = place()
    sibling, chips, planes = neighbours(wide_at, plane, chip, core)
    x_wide, y_wide = across(wide_at, plane, chip, core)
    x_near, y_near = (x_wide, plane), (y_wide, plane)
    tile_count, _ = owner_tiles(wide_at)
    enter([sibling, x_near, y_near])

    @pl.when(tile_count > 0)
    def _():
        diagonal = lax.broadcasted_iota(jnp.int32, (D, D), 0) == lax.broadcasted_iota(
            jnp.int32, (D, D), 1
        )
        square = jnp.sum(jnp.where(diagonal, gram_ref[...], 0.0))
        inverse = 1.0 / (jnp.sqrt(jnp.full((1, 1), square)) + 1e-07)
        gram[...] = gram_ref[...] * (inverse * inverse)

        def make_poly():
            value = gram[...]
            parts = halves(value)
            diagonal = lax.broadcasted_iota(jnp.int32, (D, D), 0) == lax.broadcasted_iota(
                jnp.int32, (D, D), 1
            )
            poly[...] = (
                NEWTON_B * value
                + NEWTON_C * split_dot(parts, parts)
                + jnp.where(diagonal, NEWTON_A, 0.0)
            )

        def next_gram():
            parts = halves(poly[...])
            half_way = split_dot(halves(gram[...]), parts)
            gram[...] = split_dot(halves(half_way), parts)

        def extend():
            chain[...] = split_dot(halves(chain[...]), halves(poly[...]))

        make_poly()
        chain[...] = poly[...]
        next_gram()

        @pl.loop(0, 3)
        def _(sweep):
            make_poly()
            extend()
            next_gram()

        make_poly()
        extend()
        high, low = halves(chain[...] * inverse)
        chain_high[...] = high
        chain_low[...] = low

    sems = (rows_send, rows_recv)

    def share_copies(index):
        owner, source, begin, size = SHARES[index]
        owner_chip, owner_core = divmod(owner, CORES)
        mine = rows_out.at[pl.ds(source, size)]
        spot = out_ref.at[pl.ds(begin, size)]
        first = out_ref.at[pl.ds(begin, size // 2)]
        last = out_ref.at[pl.ds(begin + size // 2, size // 2)]
        base = index * 9
        roles = {
            "x": (owner_chip ^ 1) * CORES + owner_core,
            "y": (owner_chip ^ 2) * CORES + owner_core,
            "d": (owner_chip ^ 3) * CORES + owner_core,
        }
        sends = {
            "o": [
                (mine, spot, base, x_near),
                (mine, spot, base + 1, y_near),
                (mine, spot, base + 2, sibling),
            ],
            "x": [(first, first, base + 3, y_near), (spot, spot, base + 5, sibling)],
            "y": [(last, last, base + 4, x_near), (spot, spot, base + 6, sibling)],
            "d": [(first, first, base + 7, sibling), (last, last, base + 8, sibling)],
        }
        gets = {
            "x": [(spot, base)],
            "y": [(spot, base + 1)],
            "d": [(first, base + 3), (last, base + 4)],
            "so": [(spot, base + 2)],
            "sx": [(spot, base + 5)],
            "sy": [(spot, base + 6)],
            "sd": [(first, base + 7), (last, base + 8)],
        }
        roles["o"] = owner
        for role in ("o", "x", "y", "d"):
            at = roles[role]
            roles["s" + role] = at // CORES * CORES + 1 - at % CORES
        local = (mine, spot, local_sem.at[index])
        return roles, sends, gets, local

    def started(entry):
        src, dst, index, target = entry
        return remote(src, dst, sems, index, target)

    def arriving(entry):
        spot, index = entry
        return remote(spot, spot, sems, index, sibling)

    plans = [share_copies(index) for index in range(len(SHARES))]
    for (roles, sends, gets, local), (_, source, _, size) in zip(plans, SHARES):

        @pl.when(wide_at == roles["o"])
        def _(sends=sends, local=local, source=source, size=size):
            rows = slice(source, source + size)
            rows_out[rows, :] = split_dot(
                (high_ref[rows, :], low_ref[rows, :]), (chain_high[...], chain_low[...])
            ).astype(jnp.bfloat16)
            for entry in sends["o"]:
                started(entry).start()
            pltpu.make_async_copy(*local).start()

    for phase in (("x", "y"), ("d",)):
        for roles, sends, gets, local in plans:
            for role in phase:

                @pl.when(wide_at == roles[role])
                def _(sends=sends, gets=gets, role=role):
                    for got, entry in zip(gets[role] * 2, sends[role]):
                        if role == "d" or entry is sends[role][0]:
                            arriving(got).wait_recv()
                        started(entry).start()

    for roles, sends, gets, local in plans:
        for role in ("so", "sx", "sy", "sd"):

            @pl.when(wide_at == roles[role])
            def _(gets=gets, role=role):
                for got in gets[role]:
                    arriving(got).wait_recv()

        for role in ("o", "x", "y", "d"):

            @pl.when(wide_at == roles[role])
            def _(sends=sends, local=local, role=role):
                for entry in sends[role]:
                    started(entry).wait_send()
                if role == "o":
                    pltpu.make_async_copy(*local).wait()


def muon_rows(gram, high, low):
    dma = pltpu.SemaphoreType.DMA
    vmem = pl.BlockSpec(memory_space=pltpu.VMEM)
    total = (MAIN_TILES + MOST_TILES) * TILE
    return pl.pallas_call(
        muon_kernel,
        out_shape=jax.ShapeDtypeStruct((total, D), jnp.bfloat16),
        in_specs=[vmem] * 3,
        out_specs=pl.BlockSpec(memory_space=pl.ANY),
        scratch_shapes=[
            pltpu.VMEM((D, D), jnp.float32),
            pltpu.VMEM((D, D), jnp.float32),
            pltpu.VMEM((D, D), jnp.float32),
            pltpu.VMEM((D, D), jnp.bfloat16),
            pltpu.VMEM((D, D), jnp.bfloat16),
            pltpu.VMEM((MOST_TILES * TILE, D), jnp.bfloat16),
            dma((len(SHARES),)),
            dma((len(SHARES) * 9,)),
            dma((len(SHARES) * 9,)),
        ],
        compiler_params=pltpu.CompilerParams(
            collective_id=4, has_side_effects=True, vmem_limit_bytes=40 * 2**20
        ),
        name="muon_rows",
    )(gram, high, low)


def finish_kernel(main_ref, proj_ref, rows_ref, momentum_ref, master_ref, ema_ref, *outs):
    grad_ref, momentum_new_ref, weight_ref, ema_new_ref = outs
    tile = pl.program_id(0)
    height = rows_ref.shape[0]
    main = main_ref[...].astype(jnp.float32)
    proj = proj_ref[...].reshape(height, D).astype(jnp.float32)
    gradient = jnp.where(tile < MAIN_TILES * TILE // height, main, proj)
    grad_ref[0] = gradient
    momentum_new_ref[0] = MUON_BETA * momentum_ref[0] + gradient
    row = lax.broadcasted_iota(jnp.int32, (height, 1), 0) + tile * height
    scale = jnp.zeros((height, 1), jnp.float32)
    begin = 0
    for row_total, count in zip(matrix_rows(), BLOCK_TILES):
        inside = (row >= begin * TILE) & (row < (begin + count) * TILE)
        scale = jnp.where(inside, MUON_RATE * math.sqrt(row_total / D), scale)
        begin = begin + count
    weight = master_ref[0] * (1.0 - MUON_RATE * MUON_DECAY) - scale * rows_ref[...].astype(
        jnp.float32
    )
    weight_ref[0] = weight
    ema_new_ref[0] = EMA_DECAY * ema_ref[0] + (1.0 - EMA_DECAY) * weight


def finish(main_sum, proj_sum, rows, momentum, master, ema):
    height = 2 * TILE
    tall = height // TILE
    main_steps = MAIN_TILES // tall
    block = pl.BlockSpec((1, height, D), lambda i: (0, i, 0))
    proj = proj_sum.reshape((MOST_TILES,) + proj_sum.shape[2:])
    return pl.pallas_call(
        finish_kernel,
        grid=((MAIN_TILES + MOST_TILES) // tall,),
        out_shape=(jax.ShapeDtypeStruct(master.shape, jnp.float32),) * 4,
        in_specs=[
            pl.BlockSpec((height, D), lambda i: (jnp.minimum(i, main_steps - 1), 0)),
            pl.BlockSpec(
                (tall,) + proj.shape[1:], lambda i: (jnp.maximum(i - main_steps, 0), 0, 0, 0)
            ),
            pl.BlockSpec((height, D), lambda i: (i, 0)),
            block,
            block,
            block,
        ],
        out_specs=(block,) * 4,
        cost_estimate=pl.CostEstimate(
            flops=12 * master.size, bytes_accessed=32 * master.size, transcendentals=0
        ),
        compiler_params=pltpu.CompilerParams(vmem_limit_bytes=32 * 2**20),
        name="finish",
    )(main_sum, proj, rows, momentum, master, ema)

def two_part_dot(left, right):
    high, low = halves(left)
    return plain_dot(high, right) + plain_dot(low, right)


def normalize(values):
    center = values - jnp.mean(values, axis=-1, keepdims=True)
    spread = jnp.mean(center * center, axis=-1, keepdims=True)
    scale = lax.rsqrt(spread + 1e-05)
    return center * scale, scale


def normalize_back(grad, gain, hat, scale):
    grad_hat = grad * gain
    return scale * (
        grad_hat
        - jnp.mean(grad_hat, axis=-1, keepdims=True)
        - hat * jnp.mean(grad_hat * hat, axis=-1, keepdims=True)
    )


def over_rows(values):
    return jnp.sum(values, axis=0, keepdims=True)


def layer_kernel(
    master_ref,
    pieces_ref,
    table_ref,
    ids_ref,
    mask_ref,
    cot_ref,
    live_ref,
    param_ref,
    z_ref,
    main_ref,
    outgoing_ref,
    vec_ref,
    own_grad_ref,
    own_proj_ref,
    rows_ref,
    own_rows,
    every_ids,
    spots_ref,
    asked_ranks,
    asked_locals,
    incoming_ref,
    grad_ref,
    packed,
    text_total,
    onehot,
    hats,
    scales,
    normed,
    keys,
    probs,
    grad_kv,
    grad_normed,
    grad_pieces,
    active,
    slope,
    slides,
    sums,
    local_sem,
    tell_send,
    tell_recv,
    piece_send,
    piece_recv,
    table_send,
    table_recv,
    body_send,
    body_recv,
    proj_send,
    proj_recv,
):
    at = place()
    wide_at, plane, chip, core = at
    me = wide_at * PLANES + plane
    wide_count = CHIPS * CORES
    group_rows = table_ref.shape[0]
    cap = outgoing_ref.shape[0] // (wide_count * PLANES)
    entries = z_ref.shape[0]
    peers = [
        (lax.rem(wide_at + k // PLANES, wide_count), lax.rem(plane + k % PLANES, PLANES))
        for k in range(1, wide_count * PLANES)
    ]

    def spread_of(own, held, sems):
        return spread_steps(own, held, sems, 0, at)

    body_held = packed.at[:, :, pl.ds(0, MAIN)]
    proj_held = packed.at[:, :, pl.ds(MAIN, PART - MAIN)]
    body_spread = spread_of(body_held.at[plane, wide_at], body_held, (body_send, body_recv))
    proj_spread = spread_of(proj_held.at[plane, wide_at], proj_held, (proj_send, proj_recv))
    body_begin, body_arrive, body_relay, body_finish, body_settled = body_spread
    proj_begin, proj_arrive, proj_relay, proj_finish, proj_settled = proj_spread

    loads = []
    begin = 0
    block = 0
    for index, row_total in enumerate(matrix_rows()):
        height = row_total // PLANES
        size = height // wide_count
        copy = pltpu.make_async_copy(
            master_ref.at[pl.ds(pl.multiple_of(block + wide_at * size, 16), size)],
            own_rows.at[pl.ds(begin, size)],
            local_sem.at[index],
        )
        copy.start()
        loads.append(copy)
        begin = begin + size
        block = block + height
    enter(peers)
    tell_copies = []
    for index, target in enumerate(peers):
        copy = remote(pieces_ref, every_ids.at[me], (tell_send, tell_recv), index, target)
        copy.start()
        tell_copies.append(copy)
    every_ids[me] = pieces_ref[...]
    for copy in loads:
        copy.wait()
    packed[plane, wide_at] = own_rows[...].astype(jnp.bfloat16)
    piece_copies = []
    table_copies = []

    def piece_rows(device):
        return pl.ds(pl.multiple_of(device * cap, cap), cap)

    def send_pieces(begin, end):
        for index in range(begin, end):
            wide_to, plane_to = peers[index]
            copy = remote(
                outgoing_ref.at[piece_rows(wide_to * PLANES + plane_to)],
                incoming_ref.at[piece_rows(me)],
                (piece_send, piece_recv),
                index,
                (wide_to, plane_to),
            )
            copy.start()
            piece_copies.append(copy)

    def send_table(begin, end):
        for index in range(begin, end):
            wide_to, plane_to = peers[index]
            copy = remote(
                own_grad_ref.at[wide_to * PLANES + plane_to],
                grad_ref.at[me],
                (table_send, table_recv),
                index,
                (wide_to, plane_to),
            )
            copy.start()
            table_copies.append(copy)

    text_rows = own_grad_ref.shape[0] * own_grad_ref.shape[1] // BANDS
    features = cot_ref.shape[0]
    text_total[...] = jnp.zeros_like(text_total)

    row_tiles = ids_ref.shape[1] // TEXT_TILE

    def build_pieces():
        for copy in tell_copies:
            copy.wait()
        device_count = wide_count * PLANES
        slot_count = entries * PSLOTS
        asked_ids = jnp.concatenate([every_ids[:, slot, :] for slot in range(PSLOTS)], axis=1)
        own_ids = jnp.concatenate([pieces_ref[slot : slot + 1, :] for slot in range(PSLOTS)], axis=1)
        asked = asked_ids // group_rows == me
        own_group = own_ids // group_rows
        group_at = lax.broadcasted_iota(jnp.int32, (device_count, slot_count), 0)
        grouped = jnp.where(group_at == own_group, 1.0, 0.0)
        marks = jnp.concatenate([jnp.where(asked, 1.0, 0.0), grouped], axis=0).astype(jnp.bfloat16)
        earlier = jnp.where(
            lax.broadcasted_iota(jnp.int32, (slot_count, slot_count), 0)
            < lax.broadcasted_iota(jnp.int32, (slot_count, slot_count), 1),
            1.0,
            0.0,
        ).astype(jnp.bfloat16)
        ranks = plain_dot(marks, earlier)
        own_rank = over_rows(grouped * ranks[device_count:, :])
        spots = own_group * cap + own_rank.astype(jnp.int32)
        for slot in range(PSLOTS):
            spots_ref[slot + 1 : slot + 2, :] = spots[:, slot * entries : (slot + 1) * entries]
        asked_ranks[...] = jnp.where(asked, ranks[:device_count, :], -1.0)
        asked_locals[...] = (asked_ids - me * group_rows + 1).astype(jnp.float32)

        @pl.loop(0, device_count)
        def _(device):
            here = pl.ds(device, 1)
            rank_at = lax.broadcasted_iota(jnp.int32, (cap, slot_count), 0).astype(jnp.float32)
            rows = jnp.sum(
                jnp.where(rank_at == asked_ranks[here, :], asked_locals[here, :], 0.0),
                axis=1,
                keepdims=True,
            )
            rows_ref[piece_rows(device), :] = rows.astype(jnp.int32) - 1

        tile = 512
        for begin in range(0, device_count * cap, tile):
            row_at = lax.broadcasted_iota(jnp.int32, (tile, group_rows), 1)
            chosen = jnp.where(row_at == rows_ref[begin : begin + tile, :], 1.0, 0.0)
            outgoing_ref[begin : begin + tile, :] = plain_dot(
                chosen.astype(jnp.bfloat16), table_ref[...]
            ).astype(jnp.bfloat16)
        incoming_ref[piece_rows(me), :] = outgoing_ref[piece_rows(me), :]

    def text_steps(begin, end):
        @pl.loop(begin, end)
        def _(step):
            lanes = pl.ds(pl.multiple_of(step * TEXT_TILE, TEXT_TILE), TEXT_TILE)
            row = pl.ds(step // row_tiles, 1)
            start = lax.rem(step, row_tiles) * TEXT_TILE
            id_lanes = pl.ds(pl.multiple_of(start, TEXT_TILE), TEXT_TILE)
            ids = ids_ref[row, id_lanes]
            chosen = band_onehot(ids, text_rows)
            band = jnp.where(mask_ref[row, id_lanes] > 0, ids // text_rows, -1)
            cot = cot_ref[:, lanes].astype(jnp.float32)
            banded = jnp.concatenate(
                [jnp.where(band == b, cot, 0.0).astype(jnp.bfloat16) for b in range(BANDS)], axis=0
            )
            text_total[...] += dot_nt(chosen, banded)

    text_tiles = ids_ref.shape[0] * row_tiles
    body_begin()
    proj_begin()
    text_steps(0, 1)
    body_arrive(1)
    build_pieces()
    send_pieces(0, 6)
    text_steps(1, 3)
    body_relay(0)
    body_arrive(2)
    send_pieces(6, 12)
    text_steps(3, 5)
    body_arrive(3)
    body_relay(1)
    body_finish(0)
    send_pieces(12, 18)
    text_steps(5, 8)
    body_relay(2)
    body_finish(1)
    send_pieces(18, 24)
    text_steps(8, 11)
    body_relay(3)
    body_finish(2)
    send_pieces(24, 31)
    text_steps(11, 16)
    bias_total = jnp.zeros((1, features), jnp.float32)
    blocks = own_grad_ref.shape[0] // BANDS
    for b in range(BANDS):
        rounded = text_total[:, b * features : (b + 1) * features].astype(jnp.bfloat16)
        own_grad_ref[b * blocks : (b + 1) * blocks] = rounded.reshape(
            (blocks,) + own_grad_ref.shape[1:]
        )
        bias_total = bias_total + over_rows(rounded.astype(jnp.float32))
    grad_ref[me] = own_grad_ref[me]
    body_finish(3)
    proj_arrive(1)
    send_table(0, 8)
    proj_relay(0)
    proj_arrive(2)
    send_table(8, 16)
    proj_relay(1)
    proj_arrive(3)
    send_table(16, 31)
    proj_finish(0)
    body_settled()
    for copy in piece_copies:
        copy.wait()
    def weight_rows(begin, size, plane_at=None):
        rows = slice(begin, begin + size)
        if plane_at is None:
            return packed[:, :, rows, :].reshape(PLANES * wide_count * size, D)
        return packed[plane_at, :, rows, :].reshape(wide_count * size, D)

    qkv_at, out_at, up_at, down_at, proj_at = 0, 48, 64, 128, MAIN
    spot_count = incoming_ref.shape[0]
    gain_one, shift_one = param_ref[9:10, :], param_ref[10:11, :]
    gain_two, shift_two = param_ref[11:12, :], param_ref[12:13, :]
    gain_end, shift_end = param_ref[13:14, :], param_ref[14:15, :]

    def slot_rows(slot):
        return pl.ds(pl.multiple_of(slot * entries, entries), entries)

    def piece_lanes(slot):
        return pl.ds(pl.multiple_of((slot - 1) * entries, entries), entries)

    @pl.loop(1, SLOTS)
    def _(slot):
        places = lax.broadcasted_iota(jnp.int32, (spot_count, entries), 0)
        chosen = jnp.where(places == spots_ref[pl.ds(slot, 1), :], 1.0, 0.0).astype(jnp.bfloat16)
        onehot[:, piece_lanes(slot)] = chosen

    bounds = (0, 4 * entries, PSLOTS * entries)
    for begin, end in zip(bounds[:-1], bounds[1:]):
        hats[entries + begin : entries + end, :] = dot_tn(onehot[:, begin:end], incoming_ref[...])

    first_row = param_ref[0:1, :] + param_ref[1:2, :]
    hats[0:entries, :] = jnp.broadcast_to(param_ref[0:1, :], (entries, D))
    sums[...] = jnp.zeros_like(sums)

    @pl.loop(0, SLOTS)
    def _(slot):
        rows = slot_rows(slot)
        hat, scale = normalize(hats[rows, :] + param_ref[pl.ds(1 + slot, 1), :])
        hats[rows, :] = hat
        scales[rows, :] = jnp.broadcast_to(scale, (entries, 128))
        part = (hat * gain_one + shift_one).astype(jnp.bfloat16)
        normed[rows, :] = part

    wholes = SLOTS * entries
    tall = wholes // 2
    for begin in range(0, wholes, tall):
        rows = slice(begin, begin + tall)
        keys[rows, :] = dot_nt(normed[rows, :], weight_rows(qkv_at, 48)[D:, :])

    proj_relay(2)
    proj_finish(1)
    query = dot_nt(normed[0:entries, :], weight_rows(qkv_at, 48)[0:D, :])
    lane_head = lax.broadcasted_iota(jnp.int32, (D, 128), 0) // HDIM
    to_heads = jnp.where(
        lane_head == lax.broadcasted_iota(jnp.int32, (D, 128), 1), 1.0, 0.0
    ).astype(jnp.bfloat16)
    head_lane = lax.broadcasted_iota(jnp.int32, (128, D), 1) // HDIM
    from_heads = jnp.where(
        head_lane == lax.broadcasted_iota(jnp.int32, (128, D), 0), 1.0, 0.0
    ).astype(jnp.bfloat16)
    root = 1.0 / math.sqrt(HDIM)
    for slot in range(SLOTS):
        rows = slice(slot * entries, (slot + 1) * entries)
        grad_normed[rows, :] = query * keys[rows, 0:D]
    for begin in range(0, wholes, tall):
        rows = slice(begin, begin + tall)
        probs[rows, :] = two_part_dot(grad_normed[rows, :], to_heads) * root
    scores = []
    for slot in range(SLOTS):
        value = probs[slot * entries : (slot + 1) * entries, :]
        if slot > 0:
            value = jnp.where(live_ref[:, slot - 1 : slot] > 0, value, -1e30)
        scores.append(value)
    top = scores[0]
    for value in scores[1:]:
        top = jnp.maximum(top, value)
    scores = [jnp.exp(value - top) for value in scores]
    whole = scores[0]
    for value in scores[1:]:
        whole = whole + value
    for slot in range(SLOTS):
        probs[slot * entries : (slot + 1) * entries, :] = scores[slot] / whole
    for begin in range(0, wholes, tall):
        rows = slice(begin, begin + tall)
        grad_normed[rows, :] = two_part_dot(probs[rows, :], from_heads)
    attended = jnp.zeros((entries, D), jnp.float32)
    for slot in range(SLOTS):
        rows = slice(slot * entries, (slot + 1) * entries)
        attended = attended + grad_normed[rows, :] * keys[rows, D:]
    proj_relay(3)
    proj_finish(2)
    attended_bf = attended.astype(jnp.bfloat16)
    residual = first_row + dot_nt(attended_bf, weight_rows(out_at, 16))
    hat_two, scale_two = normalize(residual)
    normed_two = (hat_two * gain_two + shift_two).astype(jnp.bfloat16)
    span = 512
    second = residual + param_ref[19:20, :]
    for begin in range(0, FF, span):
        lanes = slice(begin, begin + span)
        bias = param_ref[15 + begin // span : 16 + begin // span, :]
        gate = dot_nt(normed_two, weight_rows(up_at, 64, begin // span)) + bias
        square = gate * gate
        bend = jnp.tanh(math.sqrt(2.0 / math.pi) * (gate + 0.044715 * square * gate))
        part = (0.5 * gate * (1.0 + bend)).astype(jnp.bfloat16)
        active[:, lanes] = part
        slope[:, lanes] = 0.5 * (1.0 + bend) + 0.5 * gate * (1.0 - bend * bend) * (
            math.sqrt(2.0 / math.pi) * (1.0 + 3.0 * 0.044715 * square)
        )
        second = second + plain_dot(part, weight_rows(down_at, 64, begin // span))
    hat_end, scale_end = normalize(second)
    z_ref[...] = (hat_end * gain_end + shift_end).astype(jnp.bfloat16)

    proj_finish(3)
    proj_settled()
    for copy in table_copies:
        copy.wait()
    own_proj_ref[...] = packed[me // wide_count, lax.rem(me, wide_count), MAIN:, :]
    grad_z = jnp.zeros((entries, D), jnp.float32)
    for source in range(0, grad_ref.shape[0], 2):
        pair = jnp.concatenate([grad_ref[source], grad_ref[source + 1]], axis=1)
        at_plane, at_wide = divmod(source, wide_count)
        grad_z = grad_z + plain_dot(
            pair, packed[at_plane, at_wide : at_wide + 2, MAIN:, :].reshape(2 * features, D)
        )
    vec_ref[...] = jnp.zeros_like(vec_ref)
    vec_ref[13:14, :] = over_rows(grad_z * hat_end)
    vec_ref[14:15, :] = over_rows(grad_z)
    grad_second = normalize_back(grad_z, gain_end, hat_end, scale_end)
    branch_two = grad_second.astype(jnp.bfloat16)
    vec_ref[19:20, :] = over_rows(branch_two.astype(jnp.float32))
    tile_lanes = D // features
    vec_ref[pl.ds(20 + me // tile_lanes, 1), :] = jnp.concatenate(
        [jnp.where(lax.rem(me, tile_lanes) == k, bias_total, 0.0) for k in range(tile_lanes)],
        axis=1,
    )

    def store(value, block, chunk, height, offset):
        for chip_at in range(CHIPS):
            for core_at in range(CORES):
                top = (chip_at * CORES + core_at) * height
                main_ref[core_at, chunk, chip_at, block, offset : offset + height, :] = value[
                    top : top + height, :
                ].astype(jnp.bfloat16)

    grad_two = jnp.zeros((entries, D), jnp.float32)
    for block in range(PLANES):
        lanes = slice(block * span, (block + 1) * span)
        store(dot_tn(active[:, lanes], branch_two), block, 0, 64, 0)
        gate_grad = (dot_nt(branch_two, weight_rows(down_at, 64, block)) * slope[:, lanes]).astype(jnp.bfloat16)
        vec_ref[15 + block : 16 + block, :] = over_rows(gate_grad.astype(jnp.float32))
        store(dot_tn(gate_grad, normed_two), block, 1, 64, 0)
        grad_two = grad_two + plain_dot(gate_grad, weight_rows(up_at, 64, block))
    vec_ref[11:12, :] = over_rows(grad_two * hat_two)
    vec_ref[12:13, :] = over_rows(grad_two)
    grad_residual = grad_second + normalize_back(grad_two, gain_two, hat_two, scale_two)
    branch_one = grad_residual.astype(jnp.bfloat16)
    grad_out = dot_tn(branch_one, attended_bf)
    for block in range(PLANES):
        store(grad_out[block * 128 : (block + 1) * 128, :], block, 2, 16, 0)
    grad_attended = plain_dot(branch_one, weight_rows(out_at, 16))

    for slot in range(SLOTS):
        rows = slice(slot * entries, (slot + 1) * entries)
        grad_kv[rows, D:] = (grad_normed[rows, :] * grad_attended).astype(jnp.bfloat16)
        grad_normed[rows, :] = grad_attended * keys[rows, D:]
    for begin in range(0, wholes, tall):
        rows = slice(begin, begin + tall)
        slides[rows, :] = two_part_dot(grad_normed[rows, :], to_heads)
    inner = jnp.zeros((entries, 128), jnp.float32)
    for slot in range(SLOTS):
        rows = slice(slot * entries, (slot + 1) * entries)
        inner = inner + probs[rows, :] * slides[rows, :]
    for slot in range(SLOTS):
        rows = slice(slot * entries, (slot + 1) * entries)
        slides[rows, :] = probs[rows, :] * (slides[rows, :] - inner)
    for begin in range(0, wholes, tall):
        rows = slice(begin, begin + tall)
        grad_normed[rows, :] = two_part_dot(slides[rows, :], from_heads) * root
    grad_query = jnp.zeros((entries, D), jnp.float32)
    for slot in range(SLOTS):
        rows = slice(slot * entries, (slot + 1) * entries)
        push = grad_normed[rows, :]
        grad_query = grad_query + push * keys[rows, 0:D]
        grad_kv[rows, 0:D] = (push * query).astype(jnp.bfloat16)
    query_bf = grad_query.astype(jnp.bfloat16)

    grad_q = dot_tn(query_bf, normed[0:entries, :])
    grad_k = dot_tn(grad_kv[:, 0:D], normed[...])
    grad_v = dot_tn(grad_kv[:, D:], normed[...])
    third = D * 3 // PLANES
    every = jnp.concatenate([grad_q, grad_k, grad_v], axis=0)
    for block in range(PLANES):
        store(every[block * third : (block + 1) * third, :], block, 2, 48, 16)

    for begin in range(0, wholes, tall):
        rows = slice(begin, begin + tall)
        grad_normed[rows, :] = plain_dot(grad_kv[rows, :], weight_rows(qkv_at, 48)[D:, :])

    grad_normed[0:entries, :] += plain_dot(query_bf, weight_rows(qkv_at, 48)[0:D, :])

    @pl.loop(0, SLOTS)
    def _(slot):
        rows = slot_rows(slot)
        grad = grad_normed[rows, :]
        hat = hats[rows, :]
        sums[0:1, :] += over_rows(grad * hat)
        sums[1:2, :] += over_rows(grad)
        grad_x = normalize_back(grad, gain_one, hat, scales[rows, 0:1])
        vec_ref[pl.ds(1 + slot, 1), :] = over_rows(grad_x)

        @pl.when(slot > 0)
        def _():
            grad_pieces[pl.ds(pl.multiple_of((slot - 1) * entries, entries), entries), :] = (
                grad_x.astype(jnp.bfloat16)
            )

    vec_ref[9:11, :] = sums[0:2, :]
    vec_ref[1:2, :] += over_rows(grad_residual)
    vec_ref[0:1, :] = vec_ref[1:2, :]
    tile = 256
    for begin in range(0, spot_count, tile):
        outgoing_ref[begin : begin + tile, :] = plain_dot(
            onehot[begin : begin + tile, :], grad_pieces[...]
        ).astype(jnp.bfloat16)


def layer(master, pieces, table, text_ids, text_mask, text_cot, slot_mask, params, cap):
    f32, bf = jnp.float32, jnp.bfloat16
    dma = pltpu.SemaphoreType.DMA
    count = PLANES * CHIPS * CORES
    entries = slot_mask.shape[0]
    features = text_cot.shape[0]
    rows = entries * SLOTS
    hbm = pl.BlockSpec(memory_space=pl.ANY)
    vmem = pl.BlockSpec(memory_space=pltpu.VMEM)
    spread_count = 6 + 9 * PLANES
    return pl.pallas_call(
        layer_kernel,
        out_shape=(
            jax.ShapeDtypeStruct((entries, D), bf),
            jax.ShapeDtypeStruct((CORES, CHUNKS, CHIPS, PLANES, CHUNK, D), bf),
            jax.ShapeDtypeStruct((count * cap, D), bf),
            jax.ShapeDtypeStruct((CORES * VROWS, D), f32),
            jax.ShapeDtypeStruct((count, entries, features), bf),
            jax.ShapeDtypeStruct((features, D), bf),
            jax.ShapeDtypeStruct((count * cap, 1), jnp.int32),
        ),
        in_specs=[hbm] + [vmem] * 7,
        out_specs=(vmem,) * 7,
        scratch_shapes=[
            pltpu.VMEM((PART, D), f32),
            pltpu.VMEM((count,) + pieces.shape, jnp.int32),
            pltpu.VMEM((SLOTS, entries), jnp.int32),
            pltpu.VMEM((count, entries * PSLOTS), f32),
            pltpu.VMEM((count, entries * PSLOTS), f32),
            pltpu.VMEM((count * cap, D), bf),
            pltpu.VMEM((count, entries, features), bf),
            pltpu.VMEM((PLANES, CHIPS * CORES, PART, D), bf),
            pltpu.VMEM((count * entries // BANDS, BANDS * features), f32),
            pltpu.VMEM((count * cap, entries * PSLOTS), bf),
            pltpu.VMEM((rows, D), f32),
            pltpu.VMEM((rows, 128), f32),
            pltpu.VMEM((rows, D), bf),
            pltpu.VMEM((rows, 2 * D), f32),
            pltpu.VMEM((rows, 128), f32),
            pltpu.VMEM((rows, 2 * D), bf),
            pltpu.VMEM((rows, D), f32),
            pltpu.VMEM((entries * PSLOTS, D), bf),
            pltpu.VMEM((entries, FF), bf),
            pltpu.VMEM((entries, FF), f32),
            pltpu.VMEM((rows, 128), f32),
            pltpu.VMEM((8, D), f32),
            dma((6,)),
        ]
        + [dma((count - 1,))] * 6
        + [dma((spread_count,))] * 4,
        compiler_params=pltpu.CompilerParams(
            collective_id=5, has_side_effects=True, vmem_limit_bytes=63 * 2**20
        ),
        name="layer",
    )(master, pieces, table, text_ids, text_mask, text_cot, slot_mask, params)


def piece_grad_kernel(rows_ref, grads_ref, out_ref):
    tile = out_ref.shape[0]
    at = lax.broadcasted_iota(jnp.int32, (tile, rows_ref.shape[1]), 0) + pl.program_id(0) * tile
    chosen = jnp.where(at == rows_ref[...], 1.0, 0.0).astype(jnp.bfloat16)
    out_ref[...] = plain_dot(chosen, grads_ref[...])


def add_piece_grads(rows, grads, group_rows):
    tile = 256
    return pl.pallas_call(
        piece_grad_kernel,
        grid=(group_rows // tile,),
        out_shape=jax.ShapeDtypeStruct((group_rows, D), jnp.float32),
        in_specs=[
            pl.BlockSpec(rows.shape, lambda i: (0, 0)),
            pl.BlockSpec(grads.shape, lambda i: (0, 0)),
        ],
        out_specs=pl.BlockSpec((tile, D), lambda i: (i, 0)),
        compiler_params=pltpu.CompilerParams(vmem_limit_bytes=24 * 2**20),
        name="add_piece_grads",
    )(rows, grads)


def on_device(
    piece_table,
    piece_ids,
    slot_mask,
    text_ids,
    text_mask,
    text_cot,
    mat_master,
    mat_momentum,
    mat_ema,
    vec_master,
    vec_moment1,
    vec_moment2,
    vec_ema,
):
    device_count = PLANES * CHIPS * CORES
    me = lax.axis_index("wide") * PLANES + lax.axis_index("narrow")
    entries = piece_ids.shape[0]
    group_rows = piece_table.shape[0]
    cap = piece_cap(group_rows)
    feature_rows = text_cot.shape[0]
    params = vec_master.reshape(-1, D)
    pieces = jnp.pad(piece_ids.T, ((0, SLOTS - PSLOTS), (0, 0)))
    (
        z_own,
        main,
        grad_outgoing,
        vec_rows,
        grad_own,
        proj_own,
        asked_rows,
    ) = layer(
        mat_master[0], pieces, piece_table, text_ids, text_mask, text_cot, slot_mask, params, cap
    )
    bias_out = vec_master[vec_master.shape[0] - OUTW :]
    bias_own = lax.dynamic_slice_in_dim(bias_out, me * feature_rows, feature_rows, 0)
    text_embeds, main_sum, proj_sum, vec_sum, gram, high, low = settle(
        z_own,
        main,
        vec_rows.reshape(CORES, VROWS, D),
        grad_own,
        proj_own,
        bias_own[:, None],
        mat_momentum[0],
        text_ids,
        text_mask,
    )
    vec_grad = vec_sum.reshape(-1)[: vec_master.shape[0]]
    grad_outgoing, _ = lax.optimization_barrier((grad_outgoing, gram))
    grad_incoming = lax.all_to_all(
        grad_outgoing.reshape(device_count, cap, D), BOTH, 0, 0, tiled=True
    ).reshape(device_count * cap, D)
    rows = muon_rows(gram, high, low)
    grad_block, momentum_block, weight_block, ema_block = finish(
        main_sum, proj_sum, rows, mat_momentum, mat_master, mat_ema
    )
    piece_grad = add_piece_grads(asked_rows.reshape(1, -1), grad_incoming, group_rows)
    return (
        text_embeds,
        piece_grad,
        grad_block,
        momentum_block,
        weight_block,
        ema_block,
    ) + adam(vec_grad, vec_master, vec_moment1, vec_moment2, vec_ema)


def solution(mesh):
    in_specs = (
        P(("wide", "narrow"), None),
        P(("wide", "narrow"), None),
        P(("wide", "narrow"), None),
        P(),
        P(),
        P(("wide", "narrow"), None),
        P("narrow", None, None),
        P("narrow", None, None),
        P("narrow", None, None),
        P(),
        P(),
        P(),
        P(),
    )
    out_specs = (
        P(("wide", "narrow"), None),
        P(("wide", "narrow"), None),
        P("narrow", None, None),
        P("narrow", None, None),
        P("narrow", None, None),
        P("narrow", None, None),
        P(),
        P(),
        P(),
        P(),
        P(),
    )
    fits = mesh.shape["wide"] == CHIPS * CORES and mesh.shape["narrow"] == PLANES
    step = on_device if fits else on_device_plain
    return jax.shard_map(
        step, mesh=mesh, in_specs=in_specs, out_specs=out_specs, check_vma=False
    )
```

```python
from functools import partial
import math

import jax
import jax.numpy as jnp
from jax import lax
from jax.experimental import pallas as pl
from jax.experimental.pallas import tpu as pltpu
from jax.sharding import PartitionSpec as P

D = 512
HEADS = 8
HDIM = 64
FF = 2048
OUTW = 4096
SLOTS = 8
PSLOTS = 7
STEP = 10


HIGHEST = lax.Precision.HIGHEST
HIGH = lax.Precision.HIGH
MUON_RATE = 0.5
MUON_DECAY = 0.01
MUON_BETA = 0.95
ADAM_RATE = 0.5
ADAM_BETA1 = 0.9
ADAM_BETA2 = 0.95
ADAM_EPSILON = 1e-08
EMA_DECAY = 0.8
NEWTON_A = 3.4445
NEWTON_B = -4.775
NEWTON_C = 2.0315


def matrix_rows():
    return (3 * D, D, FF, FF, OUTW)


def unpack(packed, narrow_count):
    matrices = []
    offset = 0
    for row_total in matrix_rows():
        height = row_total // narrow_count
        matrices.append(packed[:, offset : offset + height, :].reshape(row_total, packed.shape[2]))
        offset = offset + height
    return matrices


def pack(matrices, narrow_count):
    return jnp.concatenate(
        [
            matrix.reshape(narrow_count, matrix.shape[0] // narrow_count, matrix.shape[1])
            for matrix in matrices
        ],
        axis=1,
    )


def block_slices(block, narrow_count):
    segments = []
    offset = 0
    for row_total in matrix_rows():
        height = row_total // narrow_count
        segments.append(block[offset : offset + height])
        offset = offset + height
    return segments


def split_vectors(vector):
    lengths = (D, SLOTS * D, D, D, D, D, D, D, FF, D, OUTW)
    chosen = []
    offset = 0
    for length in lengths:
        chosen.append(vector[offset : offset + length])
        offset = offset + length
    chosen[1] = chosen[1].reshape(SLOTS, D)
    return chosen


def layer_norm(values, gain, shift):
    center = values - jnp.mean(values, axis=-1, keepdims=True)
    spread = jnp.mean(center * center, axis=-1, keepdims=True)
    return center * lax.rsqrt(spread + 1e-05) * gain + shift


def gelu_tanh(values):
    return jax.nn.gelu(values, approximate=True)


def attend(query_rows, key_rows, value_rows, live_slots):
    entry_count = query_rows.shape[0]
    query_heads = query_rows.reshape(entry_count, HEADS, HDIM)
    key_heads = key_rows.reshape(entry_count, SLOTS, HEADS, HDIM)
    value_heads = value_rows.reshape(entry_count, SLOTS, HEADS, HDIM)
    scores = jnp.einsum("ehd,eshd->ehs", query_heads, key_heads, precision=HIGHEST) / math.sqrt(
        HDIM
    )
    scores = jnp.where(live_slots[:, None, :], scores, -1e30)
    scores = scores - jnp.max(scores, axis=-1, keepdims=True)
    expped = jnp.exp(scores)
    probabilities = expped / jnp.sum(expped, axis=-1, keepdims=True)
    mixed_heads = jnp.einsum("ehs,eshd->ehd", probabilities, value_heads, precision=HIGHEST)
    return mixed_heads.reshape(entry_count, D)


PIECE_CAPS = {1024: 58, 256: 16}
BOTH = ("wide", "narrow")


def piece_cap(group_rows):
    cap = PIECE_CAPS.get(group_rows, group_rows)
    return -(-cap // 16) * 16


def contract_rows(left, right):
    return lax.dot_general(
        left, right, (((0,), (0,)), ((), ())), preferred_element_type=jnp.float32
    )


def gram_of(block):
    return lax.dot_general(block, block, (((0,), (0,)), ((), ())), precision=HIGHEST)


def adam(vec_grad, vec_master, vec_moment1, vec_moment2, vec_ema):
    moment_one = ADAM_BETA1 * vec_moment1 + (1.0 - ADAM_BETA1) * vec_grad
    moment_two = ADAM_BETA2 * vec_moment2 + (1.0 - ADAM_BETA2) * vec_grad * vec_grad
    corrected_one = moment_one / (1.0 - ADAM_BETA1**STEP)
    corrected_two = moment_two / (1.0 - ADAM_BETA2**STEP)
    vec_weight = vec_master - ADAM_RATE * corrected_one / (jnp.sqrt(corrected_two) + ADAM_EPSILON)
    vec_ema_new = EMA_DECAY * vec_ema + (1.0 - EMA_DECAY) * vec_weight
    return vec_grad, moment_one, moment_two, vec_weight, vec_ema_new


def on_device_plain(
    piece_table,
    piece_ids,
    slot_mask,
    text_ids,
    text_mask,
    text_cot,
    mat_master,
    mat_momentum,
    mat_ema,
    vec_master,
    vec_moment1,
    vec_moment2,
    vec_ema,
):
    narrow_count = lax.axis_size("narrow")
    wide_count = lax.axis_size("wide")
    device_count = narrow_count * wide_count
    wide_at = lax.axis_index("wide")
    narrow_at = lax.axis_index("narrow")
    me = wide_at * narrow_count + narrow_at
    block_rows = mat_master.shape[1]
    own_rows = block_rows // wide_count
    own_part = lax.dynamic_slice_in_dim(mat_master[0], wide_at * own_rows, own_rows, 0)
    packed_bf = lax.all_gather(
        own_part.astype(jnp.bfloat16), ("narrow", "wide"), axis=0, tiled=True
    ).reshape(narrow_count, block_rows, D)
    w_qkv, w_out, w_up, w_down, w_proj = unpack(packed_bf, narrow_count)
    (
        cls_vec,
        positions,
        ln1_gain,
        ln1_shift,
        ln2_gain,
        ln2_shift,
        final_gain,
        final_shift,
        bias_up,
        bias_down,
        bias_out,
    ) = split_vectors(vec_master)
    entries = piece_ids.shape[0]
    slot_ids = piece_ids.reshape(-1)
    slot_count = slot_ids.shape[0]
    group_rows = piece_table.shape[0]
    cap = piece_cap(group_rows)
    every_ids = lax.all_gather(slot_ids, BOTH, axis=0, tiled=False)
    asked = every_ids // group_rows == me
    before = (
        lax.broadcasted_iota(jnp.int32, (slot_count, slot_count), 0)
        < lax.broadcasted_iota(jnp.int32, (slot_count, slot_count), 1)
    )
    asked_rank = jnp.dot(
        asked.astype(jnp.bfloat16), before.astype(jnp.bfloat16), preferred_element_type=jnp.float32
    ).astype(jnp.int32)
    asked_rank = jnp.where(asked, asked_rank, -1)
    chosen = asked_rank[:, None, :] == lax.iota(jnp.int32, cap)[None, :, None]
    local_ids = every_ids - me * group_rows + 1
    asked_rows = jnp.sum(jnp.where(chosen, local_ids[:, None, :], 0), axis=2).reshape(-1) - 1
    asked_onehot = (
        asked_rows[:, None] == lax.iota(jnp.int32, group_rows)[None, :]
    ).astype(jnp.bfloat16)
    outgoing = jnp.dot(asked_onehot, piece_table, preferred_element_type=jnp.float32)
    incoming = lax.all_to_all(
        outgoing.astype(jnp.bfloat16).reshape(device_count, cap, D), BOTH, 0, 0, tiled=True
    ).reshape(device_count * cap, D)
    own_group = slot_ids // group_rows
    same = (own_group[:, None] == own_group[None, :]) & before.T
    own_rank = jnp.sum(same.astype(jnp.int32), axis=1)
    own_spot = own_group * cap + own_rank
    own_onehot = (
        own_spot[:, None] == lax.iota(jnp.int32, device_count * cap)[None, :]
    ).astype(jnp.bfloat16)
    looked = jnp.dot(own_onehot, incoming, preferred_element_type=jnp.float32)
    pieces = looked.reshape(entries, PSLOTS, D)

    flat_ids = text_ids.reshape(-1)
    flat_mask = text_mask.reshape(-1)
    token_count = flat_ids.shape[0]
    feature_rows = text_cot.shape[0]
    all_entries = entries * device_count
    block_len = min(512, token_count)
    entry_index = lax.iota(jnp.int32, all_entries)

    def text_block(step_index, grad_cols):
        begin_at = step_index * block_len
        ids_now = lax.dynamic_slice_in_dim(flat_ids, begin_at, block_len)
        keep_mask = lax.dynamic_slice_in_dim(flat_mask, begin_at, block_len)
        onehot = (entry_index[:, None] == ids_now[None, :]).astype(jnp.bfloat16)
        cot_now = lax.dynamic_slice_in_dim(text_cot, begin_at, block_len, 1)
        masked_cot = jnp.where(keep_mask[None, :] > 0, cot_now, jnp.zeros_like(cot_now))
        return grad_cols + lax.dot_general(
            masked_cot, onehot, (((1,), (1,)), ((), ())), preferred_element_type=jnp.float32
        )

    grad_cols = lax.fori_loop(
        0, token_count // block_len, text_block, jnp.zeros((feature_rows, all_entries), jnp.float32)
    )
    grad_table_cols = grad_cols.astype(jnp.bfloat16)
    grad_table = lax.all_to_all(grad_table_cols, BOTH, split_axis=1, concat_axis=0, tiled=True)
    grad_bias_own = jnp.sum(grad_table_cols.astype(jnp.float32), axis=1)
    grad_normed_three = contract_rows(grad_table, w_proj)

    first_slot = jnp.broadcast_to(cls_vec + positions[0], (entries, 1, D))
    slots_x = jnp.concatenate([first_slot, pieces + positions[1:]], axis=1)
    live_slots = jnp.concatenate([jnp.ones((entries, 1), jnp.int32), slot_mask], axis=1) > 0
    normed, norm1_pull = jax.vjp(layer_norm, slots_x, ln1_gain, ln1_shift)
    normed_bf = normed.astype(jnp.bfloat16)
    query_rows = jnp.einsum(
        "ed,fd->ef", normed_bf[:, 0], w_qkv[:D], preferred_element_type=jnp.float32
    )
    key_value = jnp.einsum("esd,fd->esf", normed_bf, w_qkv[D:], preferred_element_type=jnp.float32)
    attended, attend_pull = jax.vjp(
        partial(attend, live_slots=live_slots), query_rows, key_value[:, :, :D], key_value[:, :, D:]
    )
    attended_bf = attended.astype(jnp.bfloat16)
    residual = slots_x[:, 0] + jnp.einsum(
        "ed,fd->ef", attended_bf, w_out, preferred_element_type=jnp.float32
    )
    normed_two, norm2_pull = jax.vjp(layer_norm, residual, ln2_gain, ln2_shift)
    normed_two_bf = normed_two.astype(jnp.bfloat16)
    gate_in = (
        jnp.einsum("ed,fd->ef", normed_two_bf, w_up, preferred_element_type=jnp.float32) + bias_up
    )
    active, gelu_pull = jax.vjp(gelu_tanh, gate_in)
    active_bf = active.astype(jnp.bfloat16)
    second_residual = residual + (
        jnp.dot(active_bf, w_down, preferred_element_type=jnp.float32) + bias_down
    )
    normed_three, norm3_pull = jax.vjp(layer_norm, second_residual, final_gain, final_shift)
    normed_three_bf = normed_three.astype(jnp.bfloat16)
    every_normed = lax.all_gather(normed_three_bf, BOTH, axis=0, tiled=True)
    proj_own = lax.dynamic_slice_in_dim(w_proj, me * feature_rows, feature_rows, 0)
    bias_own = lax.dynamic_slice_in_dim(bias_out, me * feature_rows, feature_rows, 0)
    table_cols = (
        jnp.einsum("fd,ed->fe", proj_own, every_normed, preferred_element_type=jnp.float32)
        + bias_own[:, None]
    )
    text_embeds = jnp.take(table_cols, flat_ids, axis=1) * flat_mask[None, :].astype(jnp.float32)
    grad_proj_own = jnp.dot(grad_table_cols, every_normed, preferred_element_type=jnp.float32)

    grad_second, grad_final_gain, grad_final_shift = norm3_pull(grad_normed_three)
    grad_branch_two = grad_second.astype(jnp.bfloat16)
    grad_bias_down = jnp.sum(grad_branch_two.astype(jnp.float32), axis=0)
    grad_down = contract_rows(active_bf, grad_branch_two)
    grad_active = jnp.einsum(
        "ed,fd->ef", grad_branch_two, w_down, preferred_element_type=jnp.float32
    )
    (grad_gate,) = gelu_pull(grad_active)
    grad_gate_bf = grad_gate.astype(jnp.bfloat16)
    grad_bias_up = jnp.sum(grad_gate_bf.astype(jnp.float32), axis=0)
    grad_up = contract_rows(grad_gate_bf, normed_two_bf)
    grad_normed_two = jnp.dot(grad_gate_bf, w_up, preferred_element_type=jnp.float32)
    grad_residual_norm, grad_ln2_gain, grad_ln2_shift = norm2_pull(grad_normed_two)
    grad_residual = grad_second + grad_residual_norm
    grad_branch_one = grad_residual.astype(jnp.bfloat16)
    grad_out_w = contract_rows(grad_branch_one, attended_bf)
    grad_attended = jnp.dot(grad_branch_one, w_out, preferred_element_type=jnp.float32)
    grad_query, grad_keys, grad_values = attend_pull(grad_attended)
    grad_query_bf = grad_query.astype(jnp.bfloat16)
    grad_kv = jnp.concatenate(
        [grad_keys.astype(jnp.bfloat16), grad_values.astype(jnp.bfloat16)], axis=2
    )
    grad_q_w = contract_rows(grad_query_bf, normed_bf[:, 0])
    grad_kv_w = jnp.einsum("esf,esd->fd", grad_kv, normed_bf, preferred_element_type=jnp.float32)
    grad_normed = jnp.einsum("esf,fd->esd", grad_kv, w_qkv[D:], preferred_element_type=jnp.float32)
    grad_normed = grad_normed.at[:, 0].add(
        jnp.dot(grad_query_bf, w_qkv[:D], preferred_element_type=jnp.float32)
    )
    grad_slots, grad_ln1_gain, grad_ln1_shift = norm1_pull(grad_normed)
    grad_first = grad_slots[:, 0] + grad_residual
    grad_cls = jnp.sum(grad_first, axis=0)
    grad_pos = jnp.concatenate([grad_cls[None], jnp.sum(grad_slots[:, 1:], axis=0)], axis=0)
    grad_pieces = grad_slots[:, 1:].astype(jnp.bfloat16).reshape(-1, D)
    grad_outgoing = contract_rows(own_onehot, grad_pieces).astype(jnp.bfloat16)
    grad_incoming = lax.all_to_all(
        grad_outgoing.reshape(device_count, cap, D), BOTH, 0, 0, tiled=True
    ).reshape(device_count * cap, D)
    piece_grad = contract_rows(asked_onehot, grad_incoming)

    vec_local = jnp.concatenate(
        [
            grad_cls,
            grad_pos.reshape(-1),
            grad_ln1_gain,
            grad_ln1_shift,
            grad_ln2_gain,
            grad_ln2_shift,
            grad_final_gain,
            grad_final_shift,
            grad_bias_up,
            grad_bias_down,
            lax.dynamic_update_slice_in_dim(
                jnp.zeros((OUTW,), jnp.float32), grad_bias_own, me * feature_rows, 0
            ),
        ]
    )
    vec_grad = lax.psum(vec_local, BOTH)
    grad_qkv = jnp.concatenate([grad_q_w, grad_kv_w], axis=0)
    packed_term = jnp.concatenate(
        [
            matrix.reshape(narrow_count, matrix.shape[0] // narrow_count, D)
            for matrix in (grad_qkv, grad_out_w, grad_up, grad_down)
        ],
        axis=1,
    )
    term_rows = packed_term.shape[1]
    share = term_rows // wide_count
    packed_term = (
        packed_term.astype(jnp.bfloat16)
        .reshape(narrow_count, wide_count, share, D)
        .transpose(1, 0, 2, 3)
        .reshape(device_count, share, D)
    )
    terms = lax.all_to_all(packed_term, BOTH, 0, 0, tiled=True)
    share_sum = jnp.sum(terms.astype(jnp.float32), axis=0)
    main_grad = lax.all_gather(share_sum.astype(jnp.bfloat16), "wide", axis=0, tiled=True)
    proj_grad = lax.all_gather(grad_proj_own.astype(jnp.bfloat16), BOTH, axis=0, tiled=True)
    proj_rows = OUTW // narrow_count
    proj_grad = lax.dynamic_slice_in_dim(proj_grad, narrow_at * proj_rows, proj_rows, 0)
    grad_block = jnp.concatenate([main_grad, proj_grad], axis=0).astype(jnp.float32)
    momentum_block = MUON_BETA * mat_momentum[0] + grad_block
    update_block = grad_block + MUON_BETA * momentum_block
    segments = block_slices(update_block, narrow_count)
    grams = lax.psum(jnp.stack([gram_of(segment) for segment in segments]), "narrow")
    new_segments = []
    for position, (row_total, master_seg, segment) in enumerate(
        zip(matrix_rows(), block_slices(mat_master[0], narrow_count), segments)
    ):
        square = jnp.sum(jnp.diagonal(grams[position]))
        norm = jnp.sqrt(square) + 1e-07
        gram = grams[position] / (norm * norm)
        chain = None
        for sweep_index in range(5):
            squared = jnp.dot(gram, gram, precision=HIGH)
            poly = NEWTON_B * gram + NEWTON_C * squared + NEWTON_A * jnp.eye(D, dtype=jnp.float32)
            chain = poly if chain is None else jnp.dot(chain, poly, precision=HIGH)
            if sweep_index < 4:
                gram = jnp.dot(jnp.dot(gram, poly, precision=HIGH), poly, precision=HIGH)
        ortho = jnp.dot(segment / norm, chain, precision=HIGH)
        new_segments.append(
            master_seg * (1.0 - MUON_RATE * MUON_DECAY)
            - MUON_RATE * math.sqrt(row_total / D) * ortho
        )
    weight_block = jnp.concatenate(new_segments, axis=0)[None]
    ema_block = EMA_DECAY * mat_ema + (1.0 - EMA_DECAY) * weight_block
    return (
        text_embeds,
        piece_grad,
        grad_block[None],
        momentum_block[None],
        weight_block,
        ema_block,
    ) + adam(vec_grad, vec_master, vec_moment1, vec_moment2, vec_ema)


MESH_ID = pl.DeviceIdType.MESH
CORES = 2
CHIPS = 4
PLANES = 4
MAIN = 192
CHUNKS = 3
CHUNK = MAIN // CHUNKS
PROJ = 32
PART = MAIN + PLANES * PROJ
VROWS = 16


def place():
    wide_at = lax.axis_index("wide")
    plane = lax.axis_index("narrow")
    chip = wide_at // CORES
    core = lax.rem(wide_at, CORES)
    return wide_at, plane, chip, core


def enter(targets):
    barrier = pltpu.get_barrier_semaphore()
    for target in targets:
        pl.semaphore_signal(barrier, inc=1, device_id=target, device_id_type=MESH_ID)
    pl.semaphore_wait(barrier, len(targets))


def neighbours(wide_at, plane, chip, core):
    sibling = (chip * CORES + 1 - core, plane)
    chips = [(lax.rem(chip + k, CHIPS) * CORES + core, plane) for k in range(1, CHIPS)]
    planes = [(wide_at, lax.rem(plane + k, PLANES)) for k in range(1, PLANES)]
    return sibling, chips, planes


def remote(src, dst, sems, index, target):
    return pltpu.make_async_remote_copy(
        src_ref=src,
        dst_ref=dst,
        send_sem=sems[0].at[index],
        recv_sem=sems[1].at[index],
        device_id=target,
        device_id_type=MESH_ID,
    )

OWNERS = (6, 7, 2, 4, 0)
BLOCK_TILES = (3, 1, 4, 4, 8)
MOST_TILES = max(BLOCK_TILES)
MAIN_TILES = 12
BANDS = 4
TEXT_TILE = 512
TILE = 128
SIDE = 2
STRIPS = 8
STRIP = D // STRIPS
PACKED = 640
PIECES = ((0, 64, 1024), (64, 64, 512), (128, 16, 384), (144, 48, 0))


def halves(value):
    high = value.astype(jnp.bfloat16)
    return high, (value - high.astype(jnp.float32)).astype(jnp.bfloat16)


def plain_dot(left, right):
    return jnp.dot(left, right, preferred_element_type=jnp.float32)


def split_dot(left, right):
    return plain_dot(left[0], right[0]) + (
        plain_dot(left[0], right[1]) + plain_dot(left[1], right[0])
    )


def dot_nt(left, right):
    return lax.dot_general(
        left, right, (((1,), (1,)), ((), ())), preferred_element_type=jnp.float32
    )


def dot_tn(left, right):
    return lax.dot_general(
        left, right, (((0,), (0,)), ((), ())), preferred_element_type=jnp.float32
    )


def band_onehot(ids, rows):
    place_in = lax.rem(ids, rows)
    spots = lax.broadcasted_iota(jnp.int32, (rows, ids.shape[1]), 0)
    return jnp.where(spots == place_in, 1.0, 0.0).astype(jnp.bfloat16)


def across(wide_at, plane, chip, core):
    x_at = lax.rem(chip, SIDE)
    x_chip = chip + 1 - 2 * x_at
    y_chip = lax.rem(chip + SIDE, CHIPS)
    return x_chip * CORES + core, y_chip * CORES + core


def owner_tiles(wide_at):
    tile_count = jnp.int32(0)
    tile_first = jnp.int32(0)
    begin = 0
    for owner, count in zip(OWNERS, BLOCK_TILES):
        tile_count = tile_count + jnp.where(wide_at == owner, count, 0)
        tile_first = tile_first + jnp.where(wide_at == owner, begin, 0)
        begin = begin + count
    return tile_count, tile_first


def spread_steps(own, held, sems, base, at):
    wide_at, plane, chip, core = at
    sibling = (chip * CORES + 1 - core, plane)
    x_wide, y_wide = across(wide_at, plane, chip, core)
    x_near, y_near = (x_wide, plane), (y_wide, plane)
    diagonal_wide = (CHIPS - 1 - chip) * CORES + core
    half = own.shape[0] // 2
    tops, bottoms = pl.ds(0, half), pl.ds(half, half)
    above, below = (wide_at, plane + 1), (wide_at, plane - 1)

    def climb(distance, source, src):
        spot = held.at[source, wide_at]
        return remote(spot if src is None else src, spot, sems, base + distance - 1, above)

    def sink(distance, source, src):
        spot = held.at[source, wide_at]
        return remote(spot if src is None else src, spot, sems, base + 2 + distance, below)

    def plane_copy(source, kind, src=None):
        index = base + 6 + 9 * source + kind
        own_spot = held.at[source, wide_at]
        x_spot, y_spot = held.at[source, x_wide], held.at[source, y_wide]
        far_spot = held.at[source, diagonal_wide]
        if kind in (0, 1, 2):
            target = (x_near, y_near, sibling)[kind]
            return remote(own_spot if src is None else src, own_spot, sems, index, target)
        if kind == 3:
            return remote(x_spot.at[tops], x_spot.at[tops], sems, index, y_near)
        if kind == 5:
            return remote(y_spot.at[bottoms], y_spot.at[bottoms], sems, index, x_near)
        if kind in (4, 6):
            spot = x_spot if kind == 4 else y_spot
            return remote(spot, spot, sems, index, sibling)
        rows = tops if kind == 7 else bottoms
        return remote(far_spot.at[rows], far_spot.at[rows], sems, index, sibling)

    def plane_send(source, src=None):
        for kind in (0, 1, 2):
            plane_copy(source, kind, src).start()

    def begin():
        @pl.when(plane < PLANES - 1)
        def _():
            climb(1, plane, own).start()

        @pl.when(plane > 0)
        def _():
            sink(1, plane, own).start()

        plane_send(plane, own)

    def arrive(distance):
        @pl.when(plane >= distance)
        def _():
            source = plane - distance
            climb(distance, source, None).wait_recv()
            if distance < PLANES - 1:

                @pl.when(plane < PLANES - 1)
                def _():
                    climb(distance + 1, source, None).start()

            plane_send(source)

        @pl.when(plane + distance < PLANES)
        def _():
            source = plane + distance
            sink(distance, source, None).wait_recv()
            if distance < PLANES - 1:

                @pl.when(plane > 0)
                def _():
                    sink(distance + 1, source, None).start()

            plane_send(source)

    def at_distance(distance, step):
        if distance == 0:
            step(plane)
            return

        @pl.when(plane >= distance)
        def _():
            step(plane - distance)

        @pl.when(plane + distance < PLANES)
        def _():
            step(plane + distance)

    def relay_one(source):
        plane_copy(source, 0).wait_recv()
        plane_copy(source, 3).start()
        plane_copy(source, 4).start()
        plane_copy(source, 1).wait_recv()
        plane_copy(source, 5).start()
        plane_copy(source, 6).start()

    def finish_one(source):
        plane_copy(source, 3).wait_recv()
        plane_copy(source, 7).start()
        plane_copy(source, 5).wait_recv()
        plane_copy(source, 8).start()

    def settle_one(source):
        for kind in (2, 4, 6, 7, 8):
            plane_copy(source, kind).wait_recv()
        for kind in range(9):
            plane_copy(source, kind).wait_send()

    def relay(distance):
        at_distance(distance, relay_one)

    def finish(distance):
        at_distance(distance, finish_one)

    def settled():
        for distance in range(PLANES):
            at_distance(distance, settle_one)
        for distance in range(1, PLANES):
            source = plane - distance + 1

            @pl.when((plane < PLANES - 1) & (source >= 0))
            def _(distance=distance, source=source):
                climb(distance, source, None).wait_send()

            down_source = plane + distance - 1

            @pl.when((plane > 0) & (down_source < PLANES))
            def _(distance=distance, down_source=down_source):
                sink(distance, down_source, None).wait_send()

    return begin, arrive, relay, finish, settled


def settle_kernel(
    z_ref,
    main_ref,
    vec_ref,
    grad_ref,
    proj_ref,
    bias_ref,
    momentum_ref,
    ids_ref,
    mask_ref,
    text_ref,
    sum_ref,
    proj_sum_ref,
    vec_out_ref,
    gram_ref,
    high_ref,
    low_ref,
    every,
    table_ref,
    text_tiles,
    near,
    first,
    x_first,
    y_first,
    x_second,
    y_second,
    second,
    deep,
    proj_own,
    proj_far,
    part,
    proj_part,
    vec_near,
    vec_far,
    vec_deep,
    main_tiles,
    proj_tiles,
    momentum_tiles,
    packs,
    pieces,
    totals,
    local_sem,
    tile_sem,
    text_sem,
    z_send,
    z_recv,
    main_send,
    main_recv,
    far_send,
    far_recv,
    deep_send,
    deep_recv,
    done_send,
    done_recv,
    pass_send,
    pass_recv,
    proj_send,
    proj_recv,
    vec_send,
    vec_recv,
    gram_send,
    gram_recv,
):
    wide_at, plane, chip, core = place()
    sibling, chips, planes = neighbours(wide_at, plane, chip, core)
    x_wide, y_wide = across(wide_at, plane, chip, core)
    x_near, y_near = (x_wide, plane), (y_wide, plane)
    diagonal_wide = (CHIPS - 1 - chip) * CORES + core
    other = 1 - core
    x_at = lax.rem(chip, SIDE)
    y_at = chip // SIDE
    tile_count, tile_first = owner_tiles(wide_at)

    own_main = pltpu.make_async_copy(main_ref.at[core], first, local_sem.at[0])
    own_main.start()

    def momentum_load(tile):
        source = pl.ds(pl.multiple_of((tile_first + tile) * TILE, TILE), TILE)
        return pltpu.make_async_copy(
            momentum_ref.at[source], momentum_tiles.at[tile], tile_sem.at[0, tile]
        )

    @pl.loop(0, tile_count)
    def _(tile):
        momentum_load(tile).start()

    enter([sibling] + chips + planes)

    vec_sems = (vec_send, vec_recv)
    vec_copies = [remote(vec_ref.at[other], vec_near, vec_sems, 0, sibling)]
    vec_copies[0].start()
    z_begin, z_arrive, z_relay, z_finish, z_settled = spread_steps(
        z_ref, every, (z_send, z_recv), 0, place()
    )
    own_z = pltpu.make_async_copy(z_ref, every.at[plane, wide_at], local_sem.at[1])
    own_z.start()
    main_sems = (main_send, main_recv)
    near_copies = []
    for chunk in range(CHUNKS):
        copy = remote(main_ref.at[other, chunk], near.at[chunk], main_sems, chunk, sibling)
        copy.start()
        near_copies.append(copy)

    def vec_far_step():
        vec_copies[0].wait_recv()
        vec_far[chip] = vec_ref[core] + vec_near[...]
        for k, target in enumerate(chips):
            copy = remote(vec_far.at[chip], vec_far.at[chip], vec_sems, 1 + k, target)
            copy.start()
            vec_copies.append(copy)

    def vec_deep_step():
        for copy in vec_copies[1:4]:
            copy.wait()
        vec_deep[plane] = (vec_far[0] + vec_far[1]) + (vec_far[2] + vec_far[3])
        for k, target in enumerate(planes):
            copy = remote(vec_deep.at[plane], vec_deep.at[plane], vec_sems, 4 + k, target)
            copy.start()
            vec_copies.append(copy)

    def vec_last_step():
        for copy in vec_copies[4:7]:
            copy.wait()
        vec_out_ref[core] = (vec_deep[0] + vec_deep[1]) + (vec_deep[2] + vec_deep[3])
        copy = remote(vec_out_ref.at[core], vec_out_ref.at[core], vec_sems, 7, sibling)
        copy.start()
        vec_copies.append(copy)

    far_sems = (far_send, far_recv)
    lows, highs = pl.ds(0, 2), pl.ds(2, 2)
    firsts = []

    def first_step(chunk):
        near_copies[chunk].wait_recv()

        @pl.loop(0, CHIPS * PLANES)
        def _(step):
            y, x, m = step // (SIDE * PLANES), lax.rem(step // PLANES, SIDE), lax.rem(step, PLANES)
            first[chunk, y, x, m] = (
                first[chunk, y, x, m].astype(jnp.float32)
                + near[chunk, y, x, m].astype(jnp.float32)
            ).astype(jnp.bfloat16)

        by_x = remote(
            first.at[chunk, :, 1 - x_at, lows], x_first.at[chunk], far_sems, chunk * 4, x_near
        )
        by_y = remote(
            first.at[chunk, 1 - y_at, :, highs], y_first.at[chunk], far_sems, chunk * 4 + 1, y_near
        )
        by_x.start()
        by_y.start()
        firsts.append((by_x, by_y))

    seconds = []

    def second_step(chunk):
        by_x, by_y = firsts[chunk]
        by_x.wait_recv()
        for y in range(SIDE):
            for m in range(2):
                first[chunk, y, x_at, m] = (
                    first[chunk, y, x_at, m].astype(jnp.float32)
                    + x_first[chunk, y, m].astype(jnp.float32)
                ).astype(jnp.bfloat16)
        next_y = remote(
            first.at[chunk, 1 - y_at, x_at, lows],
            y_second.at[chunk],
            far_sems,
            chunk * 4 + 2,
            y_near,
        )
        next_y.start()
        by_y.wait_recv()
        for x in range(SIDE):
            for m in range(2):
                first[chunk, y_at, x, 2 + m] = (
                    first[chunk, y_at, x, 2 + m].astype(jnp.float32)
                    + y_first[chunk, x, m].astype(jnp.float32)
                ).astype(jnp.bfloat16)
        next_x = remote(
            first.at[chunk, y_at, 1 - x_at, highs],
            x_second.at[chunk],
            far_sems,
            chunk * 4 + 3,
            x_near,
        )
        next_x.start()
        seconds.append((next_y, next_x))

    deep_sems = (deep_send, deep_recv)
    deep_copies = []

    def deep_step(chunk):
        next_y, next_x = seconds[chunk]
        next_y.wait_recv()
        for m in range(2):
            second[chunk, m] = (
                first[chunk, y_at, x_at, m].astype(jnp.float32)
                + y_second[chunk, m].astype(jnp.float32)
            ).astype(jnp.bfloat16)
        next_x.wait_recv()
        for m in range(2):
            second[chunk, 2 + m] = (
                first[chunk, y_at, x_at, 2 + m].astype(jnp.float32)
                + x_second[chunk, m].astype(jnp.float32)
            ).astype(jnp.bfloat16)
        copies = []
        for k, target in enumerate(planes):
            to_plane = lax.rem(plane + k + 1, PLANES)
            copy = remote(
                second.at[chunk, to_plane], deep.at[chunk, k], deep_sems, chunk * 3 + k, target
            )
            copy.start()
            copies.append(copy)
        deep_copies.append(copies)

    count = every.shape[2]
    features = proj_ref.shape[0]
    wide_count = CHIPS * CORES
    per_band = grad_ref.shape[0] // BANDS
    proj_sems = (proj_send, proj_recv)
    proj_copies = []

    def proj_near_step():
        total = jnp.zeros((features, D), jnp.float32)
        for block in range(PLANES * wide_count):
            rows = every[block % PLANES, block // PLANES]
            total = total + dot_tn(grad_ref[block], rows)
        proj_own[...] = total.astype(jnp.bfloat16).reshape(CHIPS, PROJ, D)
        for k, target in enumerate(chips):
            to_chip = lax.rem(chip + k + 1, CHIPS)
            copy = remote(proj_own.at[to_chip], proj_far.at[chip], proj_sems, k, target)
            copy.start()
            proj_copies.append(copy)
        proj_far[chip] = proj_own[chip]

    def proj_far_step():
        for copy in proj_copies:
            copy.wait()
        for k, target in enumerate(planes):
            to_plane = lax.rem(plane + k + 1, PLANES)
            copy = remote(proj_far.at[to_plane], proj_part.at[plane], proj_sems, 3 + k, target)
            copy.start()
            proj_copies.append(copy)
        proj_part[plane] = proj_far[plane]

    def publish_proj():
        for copy in proj_copies[3:]:
            copy.wait()
        publish(len(PIECES), proj_part, proj_natural(chip, core))

    done_sems = (done_send, done_recv)
    pass_sems = (pass_send, pass_recv)
    done_copies = []
    locals_done = []

    def natural(index, wide):
        _, size, base = PIECES[index]
        return sum_ref.at[pl.ds(pl.multiple_of(base + wide * size, 16), size)]

    def proj_natural(at_chip, at_core):
        return proj_sum_ref.at[at_core, :, at_chip]

    def publish(index, src, spot):
        copies = []
        for k, target in enumerate([sibling] + chips):
            copy = remote(src, spot, done_sems, index * 4 + k, target)
            copy.start()
            copies.append(copy)
        done_copies.append(copies)
        copy = pltpu.make_async_copy(src, spot, local_sem.at[2 + index])
        copy.start()
        locals_done.append(copy)

    def publish_step(chunk):
        for copy in deep_copies[chunk]:
            copy.wait_recv()
        value = second[chunk, plane].astype(jnp.float32)
        for k in range(3):
            value = value + deep[chunk, k].astype(jnp.float32)
        part[chunk * CHUNK : (chunk + 1) * CHUNK, :] = value.astype(jnp.bfloat16)
        for index, (offset, size, _) in enumerate(PIECES):
            if offset // CHUNK == chunk:
                publish(index, part.at[pl.ds(offset, size)], natural(index, wide_at))

    pass_copies = []

    def pass_step(index):
        for k in range(3):
            done_copies[index][1 + k].wait_recv()
            from_chip = lax.rem(chip + CHIPS - 1 - k, CHIPS)
            if index < len(PIECES):
                spot = natural(index, from_chip * CORES + core)
            else:
                spot = proj_natural(from_chip, core)
            copy = remote(spot, spot, pass_sems, index * 3 + k, sibling)
            copy.start()
            pass_copies.append(copy)

    def table_step():
        for block in range(PLANES * wide_count):
            rows = every[block % PLANES, block // PLANES]
            band, spot = divmod(block, per_band)
            table_ref[band * features : (band + 1) * features, spot * count : (spot + 1) * count] = (
                dot_nt(proj_ref[...], rows) + bias_ref[...]
            ).astype(jnp.bfloat16)

    text_rows = table_ref.shape[1]
    row_tiles = ids_ref.shape[1] // TEXT_TILE
    text_count = ids_ref.shape[0] * row_tiles

    def text_copy(step):
        slot = lax.rem(step, 2)
        lanes = pl.ds(pl.multiple_of(step * TEXT_TILE, TEXT_TILE), TEXT_TILE)
        return pltpu.make_async_copy(text_tiles.at[slot], text_ref.at[:, lanes], text_sem.at[slot])

    def text_steps(begin, end):
        @pl.loop(begin, end)
        def _(step):
            row = pl.ds(step // row_tiles, 1)
            start = lax.rem(step, row_tiles) * TEXT_TILE
            id_lanes = pl.ds(pl.multiple_of(start, TEXT_TILE), TEXT_TILE)
            ids = ids_ref[row, id_lanes]
            values = plain_dot(table_ref[...], band_onehot(ids, text_rows))
            band = jnp.where(mask_ref[row, id_lanes] > 0, ids // text_rows, -1)
            total = jnp.zeros((features, TEXT_TILE), jnp.float32)
            for b in range(BANDS):
                total = jnp.where(band == b, values[b * features : (b + 1) * features], total)

            @pl.when(step >= 2)
            def _():
                text_copy(step - 2).wait()

            text_tiles[lax.rem(step, 2)] = total
            text_copy(step).start()

    own_main.wait()
    z_begin()
    first_step(0)
    vec_far_step()
    first_step(1)
    z_arrive(1)
    first_step(2)
    z_relay(0)
    z_arrive(2)
    second_step(0)
    z_relay(1)
    z_arrive(3)
    second_step(1)
    z_finish(0)
    z_relay(2)
    second_step(2)
    deep_step(0)
    z_finish(1)
    z_relay(3)
    deep_step(1)
    z_finish(2)
    z_finish(3)
    deep_step(2)
    own_z.wait()
    z_settled()
    proj_near_step()
    vec_deep_step()
    publish_step(0)
    publish_step(1)
    proj_far_step()
    publish_step(2)
    table_step()
    vec_last_step()
    publish_proj()
    for index in range(len(PIECES) + 1):
        pass_step(index)
    for copies in done_copies:
        copies[0].wait_recv()
    for copy in pass_copies:
        copy.wait_recv()
    for copy in locals_done:
        copy.wait()

    gram_sems = (gram_send, gram_recv)

    def add_tile(tile, gradient):
        momentum_load(tile).wait()
        gradient = gradient.astype(jnp.float32)
        update = gradient + MUON_BETA * (MUON_BETA * momentum_tiles[tile] + gradient)
        high, low = halves(update)
        rows = pl.ds(pl.multiple_of(tile * TILE, TILE), TILE)
        high_ref[rows, :] = high
        low_ref[rows, :] = low

    @pl.when(wide_at == OWNERS[4])
    def _():
        loads = [
            pltpu.make_async_copy(
                proj_sum_ref.at[tile // PLANES, tile % PLANES],
                proj_tiles.at[tile],
                tile_sem.at[1, tile],
            )
            for tile in range(MOST_TILES)
        ]
        for copy in loads:
            copy.start()
        for copy in loads:
            copy.wait()

        @pl.loop(0, MOST_TILES)
        def _(tile):
            add_tile(tile, proj_tiles[tile].reshape(TILE, D))

    @pl.when((tile_count > 0) & (wide_at != OWNERS[4]))
    def _():
        def load(tile):
            source = pl.ds(pl.multiple_of((tile_first + tile) * TILE, TILE), TILE)
            return pltpu.make_async_copy(
                sum_ref.at[source], main_tiles.at[tile], tile_sem.at[1, tile]
            )

        @pl.loop(0, tile_count)
        def _(tile):
            load(tile).start()

        @pl.loop(0, tile_count)
        def _(tile):
            load(tile).wait()
            add_tile(tile, main_tiles[tile])

    for count_here in sorted(set(BLOCK_TILES)):

        @pl.when(tile_count == count_here)
        def _(count_here=count_here):
            high = high_ref[0 : count_here * TILE, :]
            cross = dot_tn(high, low_ref[0 : count_here * TILE, :])
            gram_ref[...] = dot_tn(high, high) + (cross + cross.T)

    def gram_copies(first_index):
        copies = []
        for k, target in enumerate(planes):
            to_plane = lax.rem(plane + k + 1, PLANES)
            if first_index == 0:
                src, dst = packs.at[to_plane], pieces.at[plane]
            else:
                src, dst = totals.at[plane], totals.at[plane]
            copies.append(remote(src, dst, gram_sems, first_index + k, target))
        return copies

    owning = tile_count > 0

    @pl.when(owning)
    def _():
        for t in range(PLANES):
            for strip, lane in ((t, 0), (STRIPS - 1 - t, 1)):
                begin = strip // 2 * TILE
                value = gram_ref[strip * STRIP : (strip + 1) * STRIP, begin:]
                width = D - begin
                at = 0 if lane == 0 else PACKED - width
                packs[t, :, at : at + width] = value
        for copy in gram_copies(0):
            copy.start()
        pieces[plane] = packs[plane]

    text_steps(0, text_count // 2)

    @pl.when(owning)
    def _():
        for copy in gram_copies(0):
            copy.wait()
        totals[plane] = (pieces[0] + pieces[1]) + (pieces[2] + pieces[3])
        for copy in gram_copies(3):
            copy.start()

    text_steps(text_count // 2, text_count)

    @pl.when(owning)
    def _():
        for copy in gram_copies(3):
            copy.wait()
        for t in range(PLANES):
            for strip, lane in ((t, 0), (STRIPS - 1 - t, 1)):
                begin = strip // 2 * TILE
                width = D - begin
                at = 0 if lane == 0 else PACKED - width
                gram_ref[strip * STRIP : (strip + 1) * STRIP, begin:] = totals[
                    t, :, at : at + width
                ]
        row_block = lax.broadcasted_iota(jnp.int32, (D, D), 0) // TILE
        lane_block = lax.broadcasted_iota(jnp.int32, (D, D), 1) // TILE
        value = gram_ref[...]
        gram_ref[...] = jnp.where(lane_block >= row_block, value, value.T)

    for copies in done_copies:
        for copy in copies:
            copy.wait_send()
    for copy in pass_copies:
        copy.wait_send()
    for copy in near_copies:
        copy.wait_send()
    for pair in firsts + seconds:
        for copy in pair:
            copy.wait_send()
    for copies in deep_copies:
        for copy in copies:
            copy.wait_send()
    vec_copies[0].wait_send()
    vec_copies[7].wait()
    text_copy(text_count - 2).wait()
    text_copy(text_count - 1).wait()


def settle(z_own, main, vec, grad_own, proj_own, bias_own, momentum, text_ids, text_mask):
    dma = pltpu.SemaphoreType.DMA
    f32, bf = jnp.float32, jnp.bfloat16
    features, tokens = proj_own.shape[0], text_ids.size
    rows = grad_own.shape[0] * grad_own.shape[1] // BANDS
    hbm = pl.BlockSpec(memory_space=pl.ANY)
    vmem = pl.BlockSpec(memory_space=pltpu.VMEM)
    grid = (CHUNKS, SIDE, SIDE, PLANES, CHUNK, D)
    return pl.pallas_call(
        settle_kernel,
        out_shape=(
            jax.ShapeDtypeStruct((features, tokens), f32),
            jax.ShapeDtypeStruct((MAIN_TILES * TILE, D), bf),
            jax.ShapeDtypeStruct((CORES, PLANES, CHIPS, PROJ, D), bf),
            jax.ShapeDtypeStruct((CORES, VROWS, D), f32),
            jax.ShapeDtypeStruct((D, D), f32),
            jax.ShapeDtypeStruct((MOST_TILES * TILE, D), bf),
            jax.ShapeDtypeStruct((MOST_TILES * TILE, D), bf),
        ),
        in_specs=[vmem, hbm, vmem, vmem, vmem, vmem, hbm, vmem, vmem],
        out_specs=(hbm, hbm, hbm, vmem, vmem, vmem, vmem),
        scratch_shapes=[
            pltpu.VMEM((PLANES, CHIPS * CORES) + z_own.shape, bf),
            pltpu.VMEM((BANDS * features, rows), bf),
            pltpu.VMEM((2, features, TEXT_TILE), f32),
            pltpu.VMEM(grid, bf),
            pltpu.VMEM(grid, bf),
            pltpu.VMEM((CHUNKS, SIDE, 2, CHUNK, D), bf),
            pltpu.VMEM((CHUNKS, SIDE, 2, CHUNK, D), bf),
            pltpu.VMEM((CHUNKS, 2, CHUNK, D), bf),
            pltpu.VMEM((CHUNKS, 2, CHUNK, D), bf),
            pltpu.VMEM((CHUNKS, PLANES, CHUNK, D), bf),
            pltpu.VMEM((CHUNKS, 3, CHUNK, D), bf),
            pltpu.VMEM((CHIPS, PROJ, D), bf),
            pltpu.VMEM((CHIPS, PROJ, D), bf),
            pltpu.VMEM((MAIN, D), bf),
            pltpu.VMEM((PLANES, PROJ, D), bf),
            pltpu.VMEM((VROWS, D), f32),
            pltpu.VMEM((CHIPS, VROWS, D), f32),
            pltpu.VMEM((PLANES, VROWS, D), f32),
            pltpu.VMEM((4, TILE, D), bf),
            pltpu.VMEM((MOST_TILES, CHIPS, PROJ, D), bf),
            pltpu.VMEM((MOST_TILES, TILE, D), f32),
            pltpu.VMEM((PLANES, STRIP, PACKED), f32),
            pltpu.VMEM((PLANES, STRIP, PACKED), f32),
            pltpu.VMEM((PLANES, STRIP, PACKED), f32),
            dma((8,)),
            dma((2, MOST_TILES)),
            dma((2,)),
            dma((6 + 9 * PLANES,)),
            dma((6 + 9 * PLANES,)),
            dma((CHUNKS,)),
            dma((CHUNKS,)),
            dma((CHUNKS * 4,)),
            dma((CHUNKS * 4,)),
            dma((CHUNKS * 3,)),
            dma((CHUNKS * 3,)),
            dma((20,)),
            dma((20,)),
            dma((15,)),
            dma((15,)),
            dma((6,)),
            dma((6,)),
            dma((8,)),
            dma((8,)),
            dma((6,)),
            dma((6,)),
        ],
        compiler_params=pltpu.CompilerParams(
            collective_id=3, has_side_effects=True, vmem_limit_bytes=58 * 2**20
        ),
        name="settle",
    )(
        z_own,
        main.reshape((CORES,) + grid),
        vec,
        grad_own,
        proj_own,
        bias_own,
        momentum,
        text_ids,
        text_mask,
    )


SHARES = ((6, 0, 0, 384), (7, 0, 384, 128), (2, 0, 512, 512), (4, 0, 1024, 512)) + (
    (0, 0, 1536, 512),
    (0, 512, 2048, 512),
)


def muon_kernel(
    gram_ref,
    high_ref,
    low_ref,
    out_ref,
    gram,
    poly,
    chain,
    chain_high,
    chain_low,
    rows_out,
    local_sem,
    rows_send,
    rows_recv,
):
    wide_at, plane, chip, core = place()
    sibling, chips, planes = neighbours(wide_at, plane, chip, core)
    x_wide, y_wide = across(wide_at, plane, chip, core)
    x_near, y_near = (x_wide, plane), (y_wide, plane)
    tile_count, _ = owner_tiles(wide_at)
    enter([sibling, x_near, y_near])

    @pl.when(tile_count > 0)
    def _():
        diagonal = lax.broadcasted_iota(jnp.int32, (D, D), 0) == lax.broadcasted_iota(
            jnp.int32, (D, D), 1
        )
        square = jnp.sum(jnp.where(diagonal, gram_ref[...], 0.0))
        inverse = 1.0 / (jnp.sqrt(jnp.full((1, 1), square)) + 1e-07)
        gram[...] = gram_ref[...] * (inverse * inverse)

        def make_poly():
            value = gram[...]
            parts = halves(value)
            diagonal = lax.broadcasted_iota(jnp.int32, (D, D), 0) == lax.broadcasted_iota(
                jnp.int32, (D, D), 1
            )
            poly[...] = (
                NEWTON_B * value
                + NEWTON_C * split_dot(parts, parts)
                + jnp.where(diagonal, NEWTON_A, 0.0)
            )

        def next_gram():
            parts = halves(poly[...])
            half_way = split_dot(halves(gram[...]), parts)
            gram[...] = split_dot(halves(half_way), parts)

        def extend():
            chain[...] = split_dot(halves(chain[...]), halves(poly[...]))

        make_poly()
        chain[...] = poly[...]
        next_gram()

        @pl.loop(0, 3)
        def _(sweep):
            make_poly()
            extend()
            next_gram()

        make_poly()
        extend()
        high, low = halves(chain[...] * inverse)
        chain_high[...] = high
        chain_low[...] = low

    sems = (rows_send, rows_recv)

    def share_copies(index):
        owner, source, begin, size = SHARES[index]
        owner_chip, owner_core = divmod(owner, CORES)
        mine = rows_out.at[pl.ds(source, size)]
        spot = out_ref.at[pl.ds(begin, size)]
        first = out_ref.at[pl.ds(begin, size // 2)]
        last = out_ref.at[pl.ds(begin + size // 2, size // 2)]
        base = index * 9
        roles = {
            "x": (owner_chip ^ 1) * CORES + owner_core,
            "y": (owner_chip ^ 2) * CORES + owner_core,
            "d": (owner_chip ^ 3) * CORES + owner_core,
        }
        sends = {
            "o": [
                (mine, spot, base, x_near),
                (mine, spot, base + 1, y_near),
                (mine, spot, base + 2, sibling),
            ],
            "x": [(first, first, base + 3, y_near), (spot, spot, base + 5, sibling)],
            "y": [(last, last, base + 4, x_near), (spot, spot, base + 6, sibling)],
            "d": [(first, first, base + 7, sibling), (last, last, base + 8, sibling)],
        }
        gets = {
            "x": [(spot, base)],
            "y": [(spot, base + 1)],
            "d": [(first, base + 3), (last, base + 4)],
            "so": [(spot, base + 2)],
            "sx": [(spot, base + 5)],
            "sy": [(spot, base + 6)],
            "sd": [(first, base + 7), (last, base + 8)],
        }
        roles["o"] = owner
        for role in ("o", "x", "y", "d"):
            at = roles[role]
            roles["s" + role] = at // CORES * CORES + 1 - at % CORES
        local = (mine, spot, local_sem.at[index])
        return roles, sends, gets, local

    def started(entry):
        src, dst, index, target = entry
        return remote(src, dst, sems, index, target)

    def arriving(entry):
        spot, index = entry
        return remote(spot, spot, sems, index, sibling)

    plans = [share_copies(index) for index in range(len(SHARES))]
    for (roles, sends, gets, local), (_, source, _, size) in zip(plans, SHARES):

        @pl.when(wide_at == roles["o"])
        def _(sends=sends, local=local, source=source, size=size):
            rows = slice(source, source + size)
            rows_out[rows, :] = split_dot(
                (high_ref[rows, :], low_ref[rows, :]), (chain_high[...], chain_low[...])
            ).astype(jnp.bfloat16)
            for entry in sends["o"]:
                started(entry).start()
            pltpu.make_async_copy(*local).start()

    for phase in (("x", "y"), ("d",)):
        for roles, sends, gets, local in plans:
            for role in phase:

                @pl.when(wide_at == roles[role])
                def _(sends=sends, gets=gets, role=role):
                    for got, entry in zip(gets[role] * 2, sends[role]):
                        if role == "d" or entry is sends[role][0]:
                            arriving(got).wait_recv()
                        started(entry).start()

    for roles, sends, gets, local in plans:
        for role in ("so", "sx", "sy", "sd"):

            @pl.when(wide_at == roles[role])
            def _(gets=gets, role=role):
                for got in gets[role]:
                    arriving(got).wait_recv()

        for role in ("o", "x", "y", "d"):

            @pl.when(wide_at == roles[role])
            def _(sends=sends, local=local, role=role):
                for entry in sends[role]:
                    started(entry).wait_send()
                if role == "o":
                    pltpu.make_async_copy(*local).wait()


def muon_rows(gram, high, low):
    dma = pltpu.SemaphoreType.DMA
    vmem = pl.BlockSpec(memory_space=pltpu.VMEM)
    total = (MAIN_TILES + MOST_TILES) * TILE
    return pl.pallas_call(
        muon_kernel,
        out_shape=jax.ShapeDtypeStruct((total, D), jnp.bfloat16),
        in_specs=[vmem] * 3,
        out_specs=pl.BlockSpec(memory_space=pl.ANY),
        scratch_shapes=[
            pltpu.VMEM((D, D), jnp.float32),
            pltpu.VMEM((D, D), jnp.float32),
            pltpu.VMEM((D, D), jnp.float32),
            pltpu.VMEM((D, D), jnp.bfloat16),
            pltpu.VMEM((D, D), jnp.bfloat16),
            pltpu.VMEM((MOST_TILES * TILE, D), jnp.bfloat16),
            dma((len(SHARES),)),
            dma((len(SHARES) * 9,)),
            dma((len(SHARES) * 9,)),
        ],
        compiler_params=pltpu.CompilerParams(
            collective_id=4, has_side_effects=True, vmem_limit_bytes=60 * 2**20
        ),
        name="muon_rows",
    )(gram, high, low)


def finish_kernel(main_ref, proj_ref, rows_ref, momentum_ref, master_ref, ema_ref, *outs):
    grad_ref, momentum_new_ref, weight_ref, ema_new_ref = outs
    tile = pl.program_id(0)
    height = rows_ref.shape[0]
    main = main_ref[...].astype(jnp.float32)
    proj = proj_ref[...].reshape(height, D).astype(jnp.float32)
    gradient = jnp.where(tile < MAIN_TILES * TILE // height, main, proj)
    grad_ref[0] = gradient
    momentum_new_ref[0] = MUON_BETA * momentum_ref[0] + gradient
    row = lax.broadcasted_iota(jnp.int32, (height, 1), 0) + tile * height
    scale = jnp.zeros((height, 1), jnp.float32)
    begin = 0
    for row_total, count in zip(matrix_rows(), BLOCK_TILES):
        inside = (row >= begin * TILE) & (row < (begin + count) * TILE)
        scale = jnp.where(inside, MUON_RATE * math.sqrt(row_total / D), scale)
        begin = begin + count
    weight = master_ref[0] * (1.0 - MUON_RATE * MUON_DECAY) - scale * rows_ref[...].astype(
        jnp.float32
    )
    weight_ref[0] = weight
    ema_new_ref[0] = EMA_DECAY * ema_ref[0] + (1.0 - EMA_DECAY) * weight


def finish(main_sum, proj_sum, rows, momentum, master, ema):
    height = 2 * TILE
    tall = height // TILE
    main_steps = MAIN_TILES // tall
    block = pl.BlockSpec((1, height, D), lambda i: (0, i, 0))
    proj = proj_sum.reshape((MOST_TILES,) + proj_sum.shape[2:])
    return pl.pallas_call(
        finish_kernel,
        grid=((MAIN_TILES + MOST_TILES) // tall,),
        out_shape=(jax.ShapeDtypeStruct(master.shape, jnp.float32),) * 4,
        in_specs=[
            pl.BlockSpec((height, D), lambda i: (jnp.minimum(i, main_steps - 1), 0)),
            pl.BlockSpec(
                (tall,) + proj.shape[1:], lambda i: (jnp.maximum(i - main_steps, 0), 0, 0, 0)
            ),
            pl.BlockSpec((height, D), lambda i: (i, 0)),
            block,
            block,
            block,
        ],
        out_specs=(block,) * 4,
        cost_estimate=pl.CostEstimate(
            flops=12 * master.size, bytes_accessed=32 * master.size, transcendentals=0
        ),
        compiler_params=pltpu.CompilerParams(vmem_limit_bytes=32 * 2**20),
        name="finish",
    )(main_sum, proj, rows, momentum, master, ema)

def two_part_dot(left, right):
    high, low = halves(left)
    return plain_dot(high, right) + plain_dot(low, right)


def normalize(values):
    center = values - jnp.mean(values, axis=-1, keepdims=True)
    spread = jnp.mean(center * center, axis=-1, keepdims=True)
    scale = lax.rsqrt(spread + 1e-05)
    return center * scale, scale


def normalize_back(grad, gain, hat, scale):
    grad_hat = grad * gain
    return scale * (
        grad_hat
        - jnp.mean(grad_hat, axis=-1, keepdims=True)
        - hat * jnp.mean(grad_hat * hat, axis=-1, keepdims=True)
    )


def over_rows(values):
    return jnp.sum(values, axis=0, keepdims=True)


def plane_sums(first, near_copies, near, buffers, far_sems, deep_sems):
    x_first, y_first, x_second, y_second, second, deep = buffers
    wide_at, plane, chip, core = place()
    _, _, planes = neighbours(wide_at, plane, chip, core)
    x_wide, y_wide = across(wide_at, plane, chip, core)
    x_near, y_near = (x_wide, plane), (y_wide, plane)
    x_at, y_at = lax.rem(chip, SIDE), chip // SIDE
    lows, highs = pl.ds(0, 2), pl.ds(2, 2)
    sent = []
    waiting = {}

    def start(src, dst, sems, index, target):
        copy = remote(src, dst, sems, index, target)
        copy.start()
        sent.append(copy)
        return copy

    def add(left, right):
        return (left.astype(jnp.float32) + right.astype(jnp.float32)).astype(jnp.bfloat16)

    def first_step(chunk):
        near_copies[chunk].wait_recv()

        @pl.loop(0, CHIPS * PLANES)
        def _(step):
            y, x, m = step // (SIDE * PLANES), lax.rem(step // PLANES, SIDE), lax.rem(step, PLANES)
            first[chunk, y, x, m] = add(first[chunk, y, x, m], near[chunk, y, x, m])

        base = chunk * 4
        waiting["x", chunk] = start(
            first.at[chunk, :, 1 - x_at, lows], x_first.at[chunk], far_sems, base, x_near
        )
        waiting["y", chunk] = start(
            first.at[chunk, 1 - y_at, :, highs], y_first.at[chunk], far_sems, base + 1, y_near
        )

    def second_step(chunk):
        base = chunk * 4
        waiting["x", chunk].wait_recv()
        for y in range(SIDE):
            for m in range(2):
                first[chunk, y, x_at, m] = add(first[chunk, y, x_at, m], x_first[chunk, y, m])
        waiting["yy", chunk] = start(
            first.at[chunk, 1 - y_at, x_at, lows], y_second.at[chunk], far_sems, base + 2, y_near
        )
        waiting["y", chunk].wait_recv()
        for x in range(SIDE):
            for m in range(2):
                first[chunk, y_at, x, 2 + m] = add(
                    first[chunk, y_at, x, 2 + m], y_first[chunk, x, m]
                )
        waiting["xx", chunk] = start(
            first.at[chunk, y_at, 1 - x_at, highs], x_second.at[chunk], far_sems, base + 3, x_near
        )

    def deep_step(chunk):
        waiting["yy", chunk].wait_recv()
        for m in range(2):
            second[chunk, m] = add(first[chunk, y_at, x_at, m], y_second[chunk, m])
        waiting["xx", chunk].wait_recv()
        for m in range(2):
            second[chunk, 2 + m] = add(first[chunk, y_at, x_at, 2 + m], x_second[chunk, m])
        for k, target in enumerate(planes):
            to_plane = lax.rem(plane + k + 1, PLANES)
            waiting["z", chunk, k] = start(
                second.at[chunk, to_plane], deep.at[chunk, k], deep_sems, chunk * 3 + k, target
            )

    def total(chunk):
        value = second[chunk, plane].astype(jnp.float32)
        for k in range(3):
            waiting["z", chunk, k].wait_recv()
            value = value + deep[chunk, k].astype(jnp.float32)
        return value

    def sums_settled():
        for copy in sent:
            copy.wait_send()

    return first_step, second_step, deep_step, total, sums_settled


def sum_scratch(chunks):
    dma = pltpu.SemaphoreType.DMA
    bf = jnp.bfloat16
    return [
        pltpu.VMEM((chunks, SIDE, 2, CHUNK, D), bf),
        pltpu.VMEM((chunks, SIDE, 2, CHUNK, D), bf),
        pltpu.VMEM((chunks, 2, CHUNK, D), bf),
        pltpu.VMEM((chunks, 2, CHUNK, D), bf),
        pltpu.VMEM((chunks, PLANES, CHUNK, D), bf),
        pltpu.VMEM((chunks, 3, CHUNK, D), bf),
        dma((chunks * 4,)),
        dma((chunks * 4,)),
        dma((chunks * 3,)),
        dma((chunks * 3,)),
    ]


def layer_kernel(
    master_ref,
    pieces_ref,
    table_ref,
    ids_ref,
    mask_ref,
    cot_ref,
    live_ref,
    param_ref,
    z_ref,
    main_ref,
    outgoing_ref,
    vec_ref,
    own_grad_ref,
    own_proj_ref,
    rows_ref,
    own_rows,
    every_ids,
    spots_ref,
    asked_ranks,
    asked_locals,
    incoming_ref,
    proj_rows,
    proj_stage,
    packed,
    text_total,
    onehot,
    hats,
    scales,
    normed,
    keys,
    probs,
    grad_kv,
    grad_normed,
    grad_pieces,
    active,
    slope,
    slides,
    sums,
    local_sem,
    x_first,
    y_first,
    x_second,
    y_second,
    second_sum,
    deep,
    far_send,
    far_recv,
    deep_send,
    deep_recv,
    tell_send,
    tell_recv,
    piece_send,
    piece_recv,
    near_send,
    near_recv,
    body_send,
    body_recv,
    proj_send,
    proj_recv,
):
    at = place()
    wide_at, plane, chip, core = at
    me = wide_at * PLANES + plane
    wide_count = CHIPS * CORES
    group_rows = table_ref.shape[0]
    cap = outgoing_ref.shape[0] // (wide_count * PLANES)
    entries = z_ref.shape[0]
    peers = [
        (lax.rem(wide_at + k // PLANES, wide_count), lax.rem(plane + k % PLANES, PLANES))
        for k in range(1, wide_count * PLANES)
    ]

    sibling, _, planes = neighbours(*at)
    body_begin, body_arrive, body_relay, body_finish, body_settled = spread_steps(
        packed.at[plane, wide_at], packed, (body_send, body_recv), 0, at
    )
    holds_proj = plane == chip
    proj_sems = (proj_send, proj_recv)
    features = cot_ref.shape[0]

    def proj_load():
        begin = master_ref.shape[0] - OUTW // PLANES + core * PLANES * features
        source = pl.ds(pl.multiple_of(begin, 16), PLANES * features)
        return pltpu.make_async_copy(master_ref.at[source], proj_rows, local_sem.at[4])

    def proj_copy(k):
        to_plane = lax.rem(plane + k + 1, PLANES)
        return remote(proj_stage.at[to_plane], own_proj_ref, proj_sems, k, planes[k])

    @pl.when(holds_proj)
    def _():
        proj_load().start()

    loads = []
    begin = 0
    block = 0
    for index, row_total in enumerate(matrix_rows()[:4]):
        height = row_total // PLANES
        size = height // wide_count
        copy = pltpu.make_async_copy(
            master_ref.at[pl.ds(pl.multiple_of(block + wide_at * size, 16), size)],
            own_rows.at[pl.ds(begin, size)],
            local_sem.at[index],
        )
        copy.start()
        loads.append(copy)
        begin = begin + size
        block = block + height
    enter(peers)
    tell_copies = []
    for index, target in enumerate(peers):
        copy = remote(pieces_ref, every_ids.at[me], (tell_send, tell_recv), index, target)
        copy.start()
        tell_copies.append(copy)
    every_ids[me] = pieces_ref[...]
    for copy in loads:
        copy.wait()
    packed[plane, wide_at] = own_rows[...].astype(jnp.bfloat16)

    def proj_begin():
        @pl.when(holds_proj)
        def _():
            proj_load().wait()
            proj_stage[...] = proj_rows[...].astype(jnp.bfloat16).reshape(proj_stage.shape)
            for k in range(PLANES - 1):
                proj_copy(k).start()
            own_proj_ref[...] = proj_stage[plane]

    piece_copies = []

    def piece_rows(device):
        return pl.ds(pl.multiple_of(device * cap, cap), cap)

    def send_pieces(begin, end):
        for index in range(begin, end):
            wide_to, plane_to = peers[index]
            copy = remote(
                outgoing_ref.at[piece_rows(wide_to * PLANES + plane_to)],
                incoming_ref.at[piece_rows(me)],
                (piece_send, piece_recv),
                index,
                (wide_to, plane_to),
            )
            copy.start()
            piece_copies.append(copy)

    near_copies = []
    dz_first, dz_second, dz_deep, dz_total, dz_settled = plane_sums(
        main_ref.at[core],
        near_copies,
        grad_kv,
        (x_first, y_first, x_second, y_second, second_sum, deep),
        (far_send, far_recv),
        (deep_send, deep_recv),
    )

    def dz_begin():
        @pl.when(jnp.logical_not(holds_proj))
        def _():
            k = lax.rem(plane - chip - 1 + PLANES, PLANES)
            remote(proj_stage.at[0], own_proj_ref, proj_sems, k, sibling).wait_recv()

        proj = own_proj_ref[...]
        for wide in range(wide_count):
            block = own_grad_ref[wide * PLANES : (wide + 1) * PLANES]
            value = plain_dot(block.reshape(PLANES * entries, features), proj)
            value = value.astype(jnp.bfloat16).reshape(PLANES, entries, D)
            y, x = divmod(wide // CORES, SIDE)
            for part in range(entries // CHUNK):
                main_ref[wide % CORES, part, y, x] = value[:, part * CHUNK : (part + 1) * CHUNK, :]
        for part in range(entries // CHUNK):
            copy = remote(
                main_ref.at[1 - core, part],
                grad_kv.at[part],
                (near_send, near_recv),
                part,
                sibling,
            )
            copy.start()
            near_copies.append(copy)

    text_rows = own_grad_ref.shape[0] * own_grad_ref.shape[1] // BANDS
    text_total[...] = jnp.zeros_like(text_total)

    row_tiles = ids_ref.shape[1] // TEXT_TILE

    def build_pieces():
        for copy in tell_copies:
            copy.wait()
        device_count = wide_count * PLANES
        slot_count = entries * PSLOTS
        asked_ids = jnp.concatenate([every_ids[:, slot, :] for slot in range(PSLOTS)], axis=1)
        own_ids = jnp.concatenate([pieces_ref[slot : slot + 1, :] for slot in range(PSLOTS)], axis=1)
        asked = asked_ids // group_rows == me
        own_group = own_ids // group_rows
        group_at = lax.broadcasted_iota(jnp.int32, (device_count, slot_count), 0)
        grouped = jnp.where(group_at == own_group, 1.0, 0.0)
        marks = jnp.concatenate([jnp.where(asked, 1.0, 0.0), grouped], axis=0).astype(jnp.bfloat16)
        earlier = jnp.where(
            lax.broadcasted_iota(jnp.int32, (slot_count, slot_count), 0)
            < lax.broadcasted_iota(jnp.int32, (slot_count, slot_count), 1),
            1.0,
            0.0,
        ).astype(jnp.bfloat16)
        ranks = plain_dot(marks, earlier)
        own_rank = over_rows(grouped * ranks[device_count:, :])
        spots = own_group * cap + own_rank.astype(jnp.int32)
        for slot in range(PSLOTS):
            spots_ref[slot + 1 : slot + 2, :] = spots[:, slot * entries : (slot + 1) * entries]
        asked_ranks[...] = jnp.where(asked, ranks[:device_count, :], -1.0)
        asked_locals[...] = (asked_ids - me * group_rows + 1).astype(jnp.float32)

        @pl.loop(0, device_count)
        def _(device):
            here = pl.ds(device, 1)
            rank_at = lax.broadcasted_iota(jnp.int32, (cap, slot_count), 0).astype(jnp.float32)
            rows = jnp.sum(
                jnp.where(rank_at == asked_ranks[here, :], asked_locals[here, :], 0.0),
                axis=1,
                keepdims=True,
            )
            rows_ref[piece_rows(device), :] = rows.astype(jnp.int32) - 1

        tile = 512
        for begin in range(0, device_count * cap, tile):
            row_at = lax.broadcasted_iota(jnp.int32, (tile, group_rows), 1)
            chosen = jnp.where(row_at == rows_ref[begin : begin + tile, :], 1.0, 0.0)
            outgoing_ref[begin : begin + tile, :] = plain_dot(
                chosen.astype(jnp.bfloat16), table_ref[...]
            ).astype(jnp.bfloat16)
        incoming_ref[piece_rows(me), :] = outgoing_ref[piece_rows(me), :]

    def text_steps(begin, end):
        @pl.loop(begin, end)
        def _(step):
            lanes = pl.ds(pl.multiple_of(step * TEXT_TILE, TEXT_TILE), TEXT_TILE)
            row = pl.ds(step // row_tiles, 1)
            start = lax.rem(step, row_tiles) * TEXT_TILE
            id_lanes = pl.ds(pl.multiple_of(start, TEXT_TILE), TEXT_TILE)
            ids = ids_ref[row, id_lanes]
            chosen = band_onehot(ids, text_rows)
            band = jnp.where(mask_ref[row, id_lanes] > 0, ids // text_rows, -1)
            cot = cot_ref[:, lanes].astype(jnp.float32)
            banded = jnp.concatenate(
                [jnp.where(band == b, cot, 0.0).astype(jnp.bfloat16) for b in range(BANDS)], axis=0
            )
            text_total[...] += dot_nt(chosen, banded)

    text_tiles = ids_ref.shape[0] * row_tiles
    body_begin()
    proj_begin()
    text_steps(0, 1)
    body_arrive(1)
    build_pieces()
    send_pieces(0, 6)
    text_steps(1, 4)
    body_relay(0)
    body_arrive(2)
    send_pieces(6, 12)
    text_steps(4, 8)
    body_arrive(3)
    body_relay(1)
    body_finish(0)
    send_pieces(12, 16)
    text_steps(8, 12)
    body_relay(2)
    body_finish(1)
    send_pieces(16, 20)
    text_steps(12, 16)
    bias_total = jnp.zeros((1, features), jnp.float32)
    blocks = own_grad_ref.shape[0] // BANDS
    for b in range(BANDS):
        rounded = text_total[:, b * features : (b + 1) * features].astype(jnp.bfloat16)
        own_grad_ref[b * blocks : (b + 1) * blocks] = rounded.reshape(
            (blocks,) + own_grad_ref.shape[1:]
        )
        bias_total = bias_total + over_rows(rounded.astype(jnp.float32))
    dz_begin()
    body_relay(3)
    body_finish(2)
    send_pieces(20, 24)
    dz_first(0)
    dz_first(1)
    send_pieces(24, 28)
    body_finish(3)
    dz_second(0)
    send_pieces(28, 31)
    dz_second(1)
    dz_deep(0)
    dz_deep(1)
    body_settled()
    for copy in piece_copies:
        copy.wait()
    def weight_rows(begin, size, plane_at=None):
        rows = slice(begin, begin + size)
        if plane_at is None:
            return packed[:, :, rows, :].reshape(PLANES * wide_count * size, D)
        return packed[plane_at, :, rows, :].reshape(wide_count * size, D)

    qkv_at, out_at, up_at, down_at = 0, 48, 64, 128
    spot_count = incoming_ref.shape[0]
    gain_one, shift_one = param_ref[9:10, :], param_ref[10:11, :]
    gain_two, shift_two = param_ref[11:12, :], param_ref[12:13, :]
    gain_end, shift_end = param_ref[13:14, :], param_ref[14:15, :]

    def slot_rows(slot):
        return pl.ds(pl.multiple_of(slot * entries, entries), entries)

    def piece_lanes(slot):
        return pl.ds(pl.multiple_of((slot - 1) * entries, entries), entries)

    @pl.loop(1, SLOTS)
    def _(slot):
        places = lax.broadcasted_iota(jnp.int32, (spot_count, entries), 0)
        chosen = jnp.where(places == spots_ref[pl.ds(slot, 1), :], 1.0, 0.0).astype(jnp.bfloat16)
        onehot[:, piece_lanes(slot)] = chosen

    bounds = (0, 4 * entries, PSLOTS * entries)
    for begin, end in zip(bounds[:-1], bounds[1:]):
        hats[entries + begin : entries + end, :] = dot_tn(onehot[:, begin:end], incoming_ref[...])

    first_row = param_ref[0:1, :] + param_ref[1:2, :]
    hats[0:entries, :] = jnp.broadcast_to(param_ref[0:1, :], (entries, D))
    sums[...] = jnp.zeros_like(sums)

    @pl.loop(0, SLOTS)
    def _(slot):
        rows = slot_rows(slot)
        hat, scale = normalize(hats[rows, :] + param_ref[pl.ds(1 + slot, 1), :])
        hats[rows, :] = hat
        scales[rows, :] = jnp.broadcast_to(scale, (entries, 128))
        part = (hat * gain_one + shift_one).astype(jnp.bfloat16)
        normed[rows, :] = part

    wholes = SLOTS * entries
    tall = wholes // 2
    for begin in range(0, wholes, tall):
        rows = slice(begin, begin + tall)
        keys[rows, :] = dot_nt(normed[rows, :], weight_rows(qkv_at, 48)[D:, :])

    query = dot_nt(normed[0:entries, :], weight_rows(qkv_at, 48)[0:D, :])
    lane_head = lax.broadcasted_iota(jnp.int32, (D, 128), 0) // HDIM
    to_heads = jnp.where(
        lane_head == lax.broadcasted_iota(jnp.int32, (D, 128), 1), 1.0, 0.0
    ).astype(jnp.bfloat16)
    head_lane = lax.broadcasted_iota(jnp.int32, (128, D), 1) // HDIM
    from_heads = jnp.where(
        head_lane == lax.broadcasted_iota(jnp.int32, (128, D), 0), 1.0, 0.0
    ).astype(jnp.bfloat16)
    root = 1.0 / math.sqrt(HDIM)
    for slot in range(SLOTS):
        rows = slice(slot * entries, (slot + 1) * entries)
        grad_normed[rows, :] = query * keys[rows, 0:D]
    for begin in range(0, wholes, tall):
        rows = slice(begin, begin + tall)
        probs[rows, :] = two_part_dot(grad_normed[rows, :], to_heads) * root
    scores = []
    for slot in range(SLOTS):
        value = probs[slot * entries : (slot + 1) * entries, :]
        if slot > 0:
            value = jnp.where(live_ref[:, slot - 1 : slot] > 0, value, -1e30)
        scores.append(value)
    top = scores[0]
    for value in scores[1:]:
        top = jnp.maximum(top, value)
    scores = [jnp.exp(value - top) for value in scores]
    whole = scores[0]
    for value in scores[1:]:
        whole = whole + value
    for slot in range(SLOTS):
        probs[slot * entries : (slot + 1) * entries, :] = scores[slot] / whole
    for begin in range(0, wholes, tall):
        rows = slice(begin, begin + tall)
        grad_normed[rows, :] = two_part_dot(probs[rows, :], from_heads)
    attended = jnp.zeros((entries, D), jnp.float32)
    for slot in range(SLOTS):
        rows = slice(slot * entries, (slot + 1) * entries)
        attended = attended + grad_normed[rows, :] * keys[rows, D:]
    attended_bf = attended.astype(jnp.bfloat16)
    residual = first_row + dot_nt(attended_bf, weight_rows(out_at, 16))
    hat_two, scale_two = normalize(residual)
    normed_two = (hat_two * gain_two + shift_two).astype(jnp.bfloat16)
    span = 512
    second = residual + param_ref[19:20, :]
    for begin in range(0, FF, span):
        lanes = slice(begin, begin + span)
        bias = param_ref[15 + begin // span : 16 + begin // span, :]
        gate = dot_nt(normed_two, weight_rows(up_at, 64, begin // span)) + bias
        square = gate * gate
        bend = jnp.tanh(math.sqrt(2.0 / math.pi) * (gate + 0.044715 * square * gate))
        part = (0.5 * gate * (1.0 + bend)).astype(jnp.bfloat16)
        active[:, lanes] = part
        slope[:, lanes] = 0.5 * (1.0 + bend) + 0.5 * gate * (1.0 - bend * bend) * (
            math.sqrt(2.0 / math.pi) * (1.0 + 3.0 * 0.044715 * square)
        )
        second = second + plain_dot(part, weight_rows(down_at, 64, begin // span))
    hat_end, scale_end = normalize(second)
    z_ref[...] = (hat_end * gain_end + shift_end).astype(jnp.bfloat16)

    grad_z = jnp.concatenate([dz_total(part) for part in range(entries // CHUNK)], axis=0)
    for copy in near_copies:
        copy.wait_send()
    dz_settled()

    @pl.when(holds_proj)
    def _():
        for k in range(PLANES - 1):
            proj_copy(k).wait_send()

    vec_ref[...] = jnp.zeros_like(vec_ref)
    vec_ref[13:14, :] = over_rows(grad_z * hat_end)
    vec_ref[14:15, :] = over_rows(grad_z)
    grad_second = normalize_back(grad_z, gain_end, hat_end, scale_end)
    branch_two = grad_second.astype(jnp.bfloat16)
    vec_ref[19:20, :] = over_rows(branch_two.astype(jnp.float32))
    tile_lanes = D // features
    vec_ref[pl.ds(20 + me // tile_lanes, 1), :] = jnp.concatenate(
        [jnp.where(lax.rem(me, tile_lanes) == k, bias_total, 0.0) for k in range(tile_lanes)],
        axis=1,
    )

    def store(value, block, chunk, height, offset):
        for chip_at in range(CHIPS):
            for core_at in range(CORES):
                top = (chip_at * CORES + core_at) * height
                y, x = divmod(chip_at, SIDE)
                main_ref[core_at, chunk, y, x, block, offset : offset + height, :] = value[
                    top : top + height, :
                ].astype(jnp.bfloat16)

    grad_two = jnp.zeros((entries, D), jnp.float32)
    for block in range(PLANES):
        lanes = slice(block * span, (block + 1) * span)
        store(dot_tn(active[:, lanes], branch_two), block, 0, 64, 0)
        gate_grad = (dot_nt(branch_two, weight_rows(down_at, 64, block)) * slope[:, lanes]).astype(jnp.bfloat16)
        vec_ref[15 + block : 16 + block, :] = over_rows(gate_grad.astype(jnp.float32))
        store(dot_tn(gate_grad, normed_two), block, 1, 64, 0)
        grad_two = grad_two + plain_dot(gate_grad, weight_rows(up_at, 64, block))
    vec_ref[11:12, :] = over_rows(grad_two * hat_two)
    vec_ref[12:13, :] = over_rows(grad_two)
    grad_residual = grad_second + normalize_back(grad_two, gain_two, hat_two, scale_two)
    branch_one = grad_residual.astype(jnp.bfloat16)
    grad_out = dot_tn(branch_one, attended_bf)
    for block in range(PLANES):
        store(grad_out[block * 128 : (block + 1) * 128, :], block, 2, 16, 0)
    grad_attended = plain_dot(branch_one, weight_rows(out_at, 16))
    halves_of = entries // CHUNK

    def store_kv(kind, slot, value):
        y, x = divmod(slot // 2, SIDE)
        begin = slot % 2 * halves_of
        grad_kv[kind, y, x, begin : begin + halves_of] = value.astype(jnp.bfloat16).reshape(
            halves_of, CHUNK, D
        )


    for slot in range(SLOTS):
        rows = slice(slot * entries, (slot + 1) * entries)
        store_kv(1, slot, grad_normed[rows, :] * grad_attended)
        grad_normed[rows, :] = grad_attended * keys[rows, D:]
    for begin in range(0, wholes, tall):
        rows = slice(begin, begin + tall)
        slides[rows, :] = two_part_dot(grad_normed[rows, :], to_heads)
    inner = jnp.zeros((entries, 128), jnp.float32)
    for slot in range(SLOTS):
        rows = slice(slot * entries, (slot + 1) * entries)
        inner = inner + probs[rows, :] * slides[rows, :]
    for slot in range(SLOTS):
        rows = slice(slot * entries, (slot + 1) * entries)
        slides[rows, :] = probs[rows, :] * (slides[rows, :] - inner)
    for begin in range(0, wholes, tall):
        rows = slice(begin, begin + tall)
        grad_normed[rows, :] = two_part_dot(slides[rows, :], from_heads) * root
    grad_query = jnp.zeros((entries, D), jnp.float32)
    for slot in range(SLOTS):
        rows = slice(slot * entries, (slot + 1) * entries)
        push = grad_normed[rows, :]
        grad_query = grad_query + push * keys[rows, 0:D]
        store_kv(0, slot, push * query)
    query_bf = grad_query.astype(jnp.bfloat16)

    grad_q = dot_tn(query_bf, normed[0:entries, :])
    grad_keys = grad_kv[0].reshape(wholes, D)
    grad_values = grad_kv[1].reshape(wholes, D)
    grad_k = dot_tn(grad_keys, normed[...])
    grad_v = dot_tn(grad_values, normed[...])
    third = D * 3 // PLANES
    every = jnp.concatenate([grad_q, grad_k, grad_v], axis=0)
    for block in range(PLANES):
        store(every[block * third : (block + 1) * third, :], block, 2, 48, 16)

    for begin in range(0, wholes, tall):
        rows = slice(begin, begin + tall)
        grad_normed[rows, :] = plain_dot(
            grad_keys[rows, :], weight_rows(qkv_at, 48)[D : 2 * D, :]
        ) + plain_dot(grad_values[rows, :], weight_rows(qkv_at, 48)[2 * D :, :])

    grad_normed[0:entries, :] += plain_dot(query_bf, weight_rows(qkv_at, 48)[0:D, :])

    @pl.loop(0, SLOTS)
    def _(slot):
        rows = slot_rows(slot)
        grad = grad_normed[rows, :]
        hat = hats[rows, :]
        sums[0:1, :] += over_rows(grad * hat)
        sums[1:2, :] += over_rows(grad)
        grad_x = normalize_back(grad, gain_one, hat, scales[rows, 0:1])
        vec_ref[pl.ds(1 + slot, 1), :] = over_rows(grad_x)

        @pl.when(slot > 0)
        def _():
            grad_pieces[pl.ds(pl.multiple_of((slot - 1) * entries, entries), entries), :] = (
                grad_x.astype(jnp.bfloat16)
            )

    vec_ref[9:11, :] = sums[0:2, :]
    vec_ref[1:2, :] += over_rows(grad_residual)
    vec_ref[0:1, :] = vec_ref[1:2, :]
    tile = 256
    for begin in range(0, spot_count, tile):
        outgoing_ref[begin : begin + tile, :] = plain_dot(
            onehot[begin : begin + tile, :], grad_pieces[...]
        ).astype(jnp.bfloat16)


def layer(master, pieces, table, text_ids, text_mask, text_cot, slot_mask, params, cap):
    f32, bf = jnp.float32, jnp.bfloat16
    dma = pltpu.SemaphoreType.DMA
    count = PLANES * CHIPS * CORES
    entries = slot_mask.shape[0]
    features = text_cot.shape[0]
    rows = entries * SLOTS
    hbm = pl.BlockSpec(memory_space=pl.ANY)
    vmem = pl.BlockSpec(memory_space=pltpu.VMEM)
    spread_count = 6 + 9 * PLANES
    return pl.pallas_call(
        layer_kernel,
        out_shape=(
            jax.ShapeDtypeStruct((entries, D), bf),
            jax.ShapeDtypeStruct((CORES, CHUNKS, SIDE, SIDE, PLANES, CHUNK, D), bf),
            jax.ShapeDtypeStruct((count * cap, D), bf),
            jax.ShapeDtypeStruct((CORES * VROWS, D), f32),
            jax.ShapeDtypeStruct((count, entries, features), bf),
            jax.ShapeDtypeStruct((features, D), bf),
            jax.ShapeDtypeStruct((count * cap, 1), jnp.int32),
        ),
        in_specs=[hbm] + [vmem] * 7,
        out_specs=(vmem,) * 7,
        scratch_shapes=[
            pltpu.VMEM((MAIN, D), f32),
            pltpu.VMEM((count,) + pieces.shape, jnp.int32),
            pltpu.VMEM((SLOTS, entries), jnp.int32),
            pltpu.VMEM((count, entries * PSLOTS), f32),
            pltpu.VMEM((count, entries * PSLOTS), f32),
            pltpu.VMEM((count * cap, D), bf),
            pltpu.VMEM((PLANES * features, D), f32),
            pltpu.VMEM((PLANES, features, D), bf),
            pltpu.VMEM((PLANES, CHIPS * CORES, MAIN, D), bf),
            pltpu.VMEM((count * entries // BANDS, BANDS * features), f32),
            pltpu.VMEM((count * cap, entries * PSLOTS), bf),
            pltpu.VMEM((rows, D), f32),
            pltpu.VMEM((rows, 128), f32),
            pltpu.VMEM((rows, D), bf),
            pltpu.VMEM((rows, 2 * D), f32),
            pltpu.VMEM((rows, 128), f32),
            pltpu.VMEM((2, SIDE, SIDE, PLANES, CHUNK, D), bf),
            pltpu.VMEM((rows, D), f32),
            pltpu.VMEM((entries * PSLOTS, D), bf),
            pltpu.VMEM((entries, FF), bf),
            pltpu.VMEM((entries, FF), f32),
            pltpu.VMEM((rows, 128), f32),
            pltpu.VMEM((8, D), f32),
            dma((5,)),
        ]
        + sum_scratch(entries // CHUNK)
        + [dma((count - 1,))] * 4
        + [dma((entries // CHUNK,))] * 2
        + [dma((spread_count,))] * 2
        + [dma((PLANES - 1,))] * 2,
        compiler_params=pltpu.CompilerParams(
            collective_id=5, has_side_effects=True, vmem_limit_bytes=63 * 2**20
        ),
        name="layer",
    )(master, pieces, table, text_ids, text_mask, text_cot, slot_mask, params)


def piece_grad_kernel(rows_ref, grads_ref, out_ref):
    tile = out_ref.shape[0]
    at = lax.broadcasted_iota(jnp.int32, (tile, rows_ref.shape[1]), 0) + pl.program_id(0) * tile
    chosen = jnp.where(at == rows_ref[...], 1.0, 0.0).astype(jnp.bfloat16)
    out_ref[...] = plain_dot(chosen, grads_ref[...])


def add_piece_grads(rows, grads, group_rows):
    tile = 256
    return pl.pallas_call(
        piece_grad_kernel,
        grid=(group_rows // tile,),
        out_shape=jax.ShapeDtypeStruct((group_rows, D), jnp.float32),
        in_specs=[
            pl.BlockSpec(rows.shape, lambda i: (0, 0)),
            pl.BlockSpec(grads.shape, lambda i: (0, 0)),
        ],
        out_specs=pl.BlockSpec((tile, D), lambda i: (i, 0)),
        compiler_params=pltpu.CompilerParams(vmem_limit_bytes=24 * 2**20),
        name="add_piece_grads",
    )(rows, grads)


def on_device(
    piece_table,
    piece_ids,
    slot_mask,
    text_ids,
    text_mask,
    text_cot,
    mat_master,
    mat_momentum,
    mat_ema,
    vec_master,
    vec_moment1,
    vec_moment2,
    vec_ema,
):
    device_count = PLANES * CHIPS * CORES
    me = lax.axis_index("wide") * PLANES + lax.axis_index("narrow")
    entries = piece_ids.shape[0]
    group_rows = piece_table.shape[0]
    cap = piece_cap(group_rows)
    feature_rows = text_cot.shape[0]
    params = vec_master.reshape(-1, D)
    pieces = jnp.pad(piece_ids.T, ((0, SLOTS - PSLOTS), (0, 0)))
    (
        z_own,
        main,
        grad_outgoing,
        vec_rows,
        grad_own,
        proj_own,
        asked_rows,
    ) = layer(
        mat_master[0], pieces, piece_table, text_ids, text_mask, text_cot, slot_mask, params, cap
    )
    bias_out = vec_master[vec_master.shape[0] - OUTW :]
    bias_own = lax.dynamic_slice_in_dim(bias_out, me * feature_rows, feature_rows, 0)
    text_embeds, main_sum, proj_sum, vec_sum, gram, high, low = settle(
        z_own,
        main,
        vec_rows.reshape(CORES, VROWS, D),
        grad_own,
        proj_own,
        bias_own[:, None],
        mat_momentum[0],
        text_ids,
        text_mask,
    )
    vec_grad = vec_sum.reshape(-1)[: vec_master.shape[0]]
    grad_outgoing, _ = lax.optimization_barrier((grad_outgoing, gram))
    grad_incoming = lax.all_to_all(
        grad_outgoing.reshape(device_count, cap, D), BOTH, 0, 0, tiled=True
    ).reshape(device_count * cap, D)
    rows = muon_rows(gram, high, low)
    grad_block, momentum_block, weight_block, ema_block = finish(
        main_sum, proj_sum, rows, mat_momentum, mat_master, mat_ema
    )
    piece_grad = add_piece_grads(asked_rows.reshape(1, -1), grad_incoming, group_rows)
    return (
        text_embeds,
        piece_grad,
        grad_block,
        momentum_block,
        weight_block,
        ema_block,
    ) + adam(vec_grad, vec_master, vec_moment1, vec_moment2, vec_ema)


def solution(mesh):
    in_specs = (
        P(("wide", "narrow"), None),
        P(("wide", "narrow"), None),
        P(("wide", "narrow"), None),
        P(),
        P(),
        P(("wide", "narrow"), None),
        P("narrow", None, None),
        P("narrow", None, None),
        P("narrow", None, None),
        P(),
        P(),
        P(),
        P(),
    )
    out_specs = (
        P(("wide", "narrow"), None),
        P(("wide", "narrow"), None),
        P("narrow", None, None),
        P("narrow", None, None),
        P("narrow", None, None),
        P("narrow", None, None),
        P(),
        P(),
        P(),
        P(),
        P(),
    )
    fits = mesh.shape["wide"] == CHIPS * CORES and mesh.shape["narrow"] == PLANES
    step = on_device if fits else on_device_plain
    return jax.shard_map(
        step, mesh=mesh, in_specs=in_specs, out_specs=out_specs, check_vma=False
    )
```

```python
from functools import partial
import math

import jax
import jax.numpy as jnp
from jax import lax
from jax.experimental import pallas as pl
from jax.experimental.pallas import tpu as pltpu
from jax.sharding import PartitionSpec as P

D = 512
HEADS = 8
HDIM = 64
FF = 2048
OUTW = 4096
SLOTS = 8
PSLOTS = 7
STEP = 10


HIGHEST = lax.Precision.HIGHEST
HIGH = lax.Precision.HIGH
MUON_RATE = 0.5
MUON_DECAY = 0.01
MUON_BETA = 0.95
ADAM_RATE = 0.5
ADAM_BETA1 = 0.9
ADAM_BETA2 = 0.95
ADAM_EPSILON = 1e-08
EMA_DECAY = 0.8
NEWTON_A = 3.4445
NEWTON_B = -4.775
NEWTON_C = 2.0315


def matrix_rows():
    return (3 * D, D, FF, FF, OUTW)


def unpack(packed, narrow_count):
    matrices = []
    offset = 0
    for row_total in matrix_rows():
        height = row_total // narrow_count
        matrices.append(packed[:, offset : offset + height, :].reshape(row_total, packed.shape[2]))
        offset = offset + height
    return matrices


def pack(matrices, narrow_count):
    return jnp.concatenate(
        [
            matrix.reshape(narrow_count, matrix.shape[0] // narrow_count, matrix.shape[1])
            for matrix in matrices
        ],
        axis=1,
    )


def block_slices(block, narrow_count):
    segments = []
    offset = 0
    for row_total in matrix_rows():
        height = row_total // narrow_count
        segments.append(block[offset : offset + height])
        offset = offset + height
    return segments


def split_vectors(vector):
    lengths = (D, SLOTS * D, D, D, D, D, D, D, FF, D, OUTW)
    chosen = []
    offset = 0
    for length in lengths:
        chosen.append(vector[offset : offset + length])
        offset = offset + length
    chosen[1] = chosen[1].reshape(SLOTS, D)
    return chosen


def layer_norm(values, gain, shift):
    center = values - jnp.mean(values, axis=-1, keepdims=True)
    spread = jnp.mean(center * center, axis=-1, keepdims=True)
    return center * lax.rsqrt(spread + 1e-05) * gain + shift


def gelu_tanh(values):
    return jax.nn.gelu(values, approximate=True)


def attend(query_rows, key_rows, value_rows, live_slots):
    entry_count = query_rows.shape[0]
    query_heads = query_rows.reshape(entry_count, HEADS, HDIM)
    key_heads = key_rows.reshape(entry_count, SLOTS, HEADS, HDIM)
    value_heads = value_rows.reshape(entry_count, SLOTS, HEADS, HDIM)
    scores = jnp.einsum("ehd,eshd->ehs", query_heads, key_heads, precision=HIGHEST) / math.sqrt(
        HDIM
    )
    scores = jnp.where(live_slots[:, None, :], scores, -1e30)
    scores = scores - jnp.max(scores, axis=-1, keepdims=True)
    expped = jnp.exp(scores)
    probabilities = expped / jnp.sum(expped, axis=-1, keepdims=True)
    mixed_heads = jnp.einsum("ehs,eshd->ehd", probabilities, value_heads, precision=HIGHEST)
    return mixed_heads.reshape(entry_count, D)


PIECE_CAPS = {1024: 58, 256: 16}
BOTH = ("wide", "narrow")


def piece_cap(group_rows):
    cap = PIECE_CAPS.get(group_rows, group_rows)
    return -(-cap // 16) * 16


def contract_rows(left, right):
    return lax.dot_general(
        left, right, (((0,), (0,)), ((), ())), preferred_element_type=jnp.float32
    )


def gram_of(block):
    return lax.dot_general(block, block, (((0,), (0,)), ((), ())), precision=HIGHEST)


def adam(vec_grad, vec_master, vec_moment1, vec_moment2, vec_ema):
    moment_one = ADAM_BETA1 * vec_moment1 + (1.0 - ADAM_BETA1) * vec_grad
    moment_two = ADAM_BETA2 * vec_moment2 + (1.0 - ADAM_BETA2) * vec_grad * vec_grad
    corrected_one = moment_one / (1.0 - ADAM_BETA1**STEP)
    corrected_two = moment_two / (1.0 - ADAM_BETA2**STEP)
    vec_weight = vec_master - ADAM_RATE * corrected_one / (jnp.sqrt(corrected_two) + ADAM_EPSILON)
    vec_ema_new = EMA_DECAY * vec_ema + (1.0 - EMA_DECAY) * vec_weight
    return vec_grad, moment_one, moment_two, vec_weight, vec_ema_new


def on_device_plain(
    piece_table,
    piece_ids,
    slot_mask,
    text_ids,
    text_mask,
    text_cot,
    mat_master,
    mat_momentum,
    mat_ema,
    vec_master,
    vec_moment1,
    vec_moment2,
    vec_ema,
):
    narrow_count = lax.axis_size("narrow")
    wide_count = lax.axis_size("wide")
    device_count = narrow_count * wide_count
    wide_at = lax.axis_index("wide")
    narrow_at = lax.axis_index("narrow")
    me = wide_at * narrow_count + narrow_at
    block_rows = mat_master.shape[1]
    own_rows = block_rows // wide_count
    own_part = lax.dynamic_slice_in_dim(mat_master[0], wide_at * own_rows, own_rows, 0)
    packed_bf = lax.all_gather(
        own_part.astype(jnp.bfloat16), ("narrow", "wide"), axis=0, tiled=True
    ).reshape(narrow_count, block_rows, D)
    w_qkv, w_out, w_up, w_down, w_proj = unpack(packed_bf, narrow_count)
    (
        cls_vec,
        positions,
        ln1_gain,
        ln1_shift,
        ln2_gain,
        ln2_shift,
        final_gain,
        final_shift,
        bias_up,
        bias_down,
        bias_out,
    ) = split_vectors(vec_master)
    entries = piece_ids.shape[0]
    slot_ids = piece_ids.reshape(-1)
    slot_count = slot_ids.shape[0]
    group_rows = piece_table.shape[0]
    cap = piece_cap(group_rows)
    every_ids = lax.all_gather(slot_ids, BOTH, axis=0, tiled=False)
    asked = every_ids // group_rows == me
    before = (
        lax.broadcasted_iota(jnp.int32, (slot_count, slot_count), 0)
        < lax.broadcasted_iota(jnp.int32, (slot_count, slot_count), 1)
    )
    asked_rank = jnp.dot(
        asked.astype(jnp.bfloat16), before.astype(jnp.bfloat16), preferred_element_type=jnp.float32
    ).astype(jnp.int32)
    asked_rank = jnp.where(asked, asked_rank, -1)
    chosen = asked_rank[:, None, :] == lax.iota(jnp.int32, cap)[None, :, None]
    local_ids = every_ids - me * group_rows + 1
    asked_rows = jnp.sum(jnp.where(chosen, local_ids[:, None, :], 0), axis=2).reshape(-1) - 1
    asked_onehot = (
        asked_rows[:, None] == lax.iota(jnp.int32, group_rows)[None, :]
    ).astype(jnp.bfloat16)
    outgoing = jnp.dot(asked_onehot, piece_table, preferred_element_type=jnp.float32)
    incoming = lax.all_to_all(
        outgoing.astype(jnp.bfloat16).reshape(device_count, cap, D), BOTH, 0, 0, tiled=True
    ).reshape(device_count * cap, D)
    own_group = slot_ids // group_rows
    same = (own_group[:, None] == own_group[None, :]) & before.T
    own_rank = jnp.sum(same.astype(jnp.int32), axis=1)
    own_spot = own_group * cap + own_rank
    own_onehot = (
        own_spot[:, None] == lax.iota(jnp.int32, device_count * cap)[None, :]
    ).astype(jnp.bfloat16)
    looked = jnp.dot(own_onehot, incoming, preferred_element_type=jnp.float32)
    pieces = looked.reshape(entries, PSLOTS, D)

    flat_ids = text_ids.reshape(-1)
    flat_mask = text_mask.reshape(-1)
    token_count = flat_ids.shape[0]
    feature_rows = text_cot.shape[0]
    all_entries = entries * device_count
    block_len = min(512, token_count)
    entry_index = lax.iota(jnp.int32, all_entries)

    def text_block(step_index, grad_cols):
        begin_at = step_index * block_len
        ids_now = lax.dynamic_slice_in_dim(flat_ids, begin_at, block_len)
        keep_mask = lax.dynamic_slice_in_dim(flat_mask, begin_at, block_len)
        onehot = (entry_index[:, None] == ids_now[None, :]).astype(jnp.bfloat16)
        cot_now = lax.dynamic_slice_in_dim(text_cot, begin_at, block_len, 1)
        masked_cot = jnp.where(keep_mask[None, :] > 0, cot_now, jnp.zeros_like(cot_now))
        return grad_cols + lax.dot_general(
            masked_cot, onehot, (((1,), (1,)), ((), ())), preferred_element_type=jnp.float32
        )

    grad_cols = lax.fori_loop(
        0, token_count // block_len, text_block, jnp.zeros((feature_rows, all_entries), jnp.float32)
    )
    grad_table_cols = grad_cols.astype(jnp.bfloat16)
    grad_table = lax.all_to_all(grad_table_cols, BOTH, split_axis=1, concat_axis=0, tiled=True)
    grad_bias_own = jnp.sum(grad_table_cols.astype(jnp.float32), axis=1)
    grad_normed_three = contract_rows(grad_table, w_proj)

    first_slot = jnp.broadcast_to(cls_vec + positions[0], (entries, 1, D))
    slots_x = jnp.concatenate([first_slot, pieces + positions[1:]], axis=1)
    live_slots = jnp.concatenate([jnp.ones((entries, 1), jnp.int32), slot_mask], axis=1) > 0
    normed, norm1_pull = jax.vjp(layer_norm, slots_x, ln1_gain, ln1_shift)
    normed_bf = normed.astype(jnp.bfloat16)
    query_rows = jnp.einsum(
        "ed,fd->ef", normed_bf[:, 0], w_qkv[:D], preferred_element_type=jnp.float32
    )
    key_value = jnp.einsum("esd,fd->esf", normed_bf, w_qkv[D:], preferred_element_type=jnp.float32)
    attended, attend_pull = jax.vjp(
        partial(attend, live_slots=live_slots), query_rows, key_value[:, :, :D], key_value[:, :, D:]
    )
    attended_bf = attended.astype(jnp.bfloat16)
    residual = slots_x[:, 0] + jnp.einsum(
        "ed,fd->ef", attended_bf, w_out, preferred_element_type=jnp.float32
    )
    normed_two, norm2_pull = jax.vjp(layer_norm, residual, ln2_gain, ln2_shift)
    normed_two_bf = normed_two.astype(jnp.bfloat16)
    gate_in = (
        jnp.einsum("ed,fd->ef", normed_two_bf, w_up, preferred_element_type=jnp.float32) + bias_up
    )
    active, gelu_pull = jax.vjp(gelu_tanh, gate_in)
    active_bf = active.astype(jnp.bfloat16)
    second_residual = residual + (
        jnp.dot(active_bf, w_down, preferred_element_type=jnp.float32) + bias_down
    )
    normed_three, norm3_pull = jax.vjp(layer_norm, second_residual, final_gain, final_shift)
    normed_three_bf = normed_three.astype(jnp.bfloat16)
    every_normed = lax.all_gather(normed_three_bf, BOTH, axis=0, tiled=True)
    proj_own = lax.dynamic_slice_in_dim(w_proj, me * feature_rows, feature_rows, 0)
    bias_own = lax.dynamic_slice_in_dim(bias_out, me * feature_rows, feature_rows, 0)
    table_cols = (
        jnp.einsum("fd,ed->fe", proj_own, every_normed, preferred_element_type=jnp.float32)
        + bias_own[:, None]
    )
    text_embeds = jnp.take(table_cols, flat_ids, axis=1) * flat_mask[None, :].astype(jnp.float32)
    grad_proj_own = jnp.dot(grad_table_cols, every_normed, preferred_element_type=jnp.float32)

    grad_second, grad_final_gain, grad_final_shift = norm3_pull(grad_normed_three)
    grad_branch_two = grad_second.astype(jnp.bfloat16)
    grad_bias_down = jnp.sum(grad_branch_two.astype(jnp.float32), axis=0)
    grad_down = contract_rows(active_bf, grad_branch_two)
    grad_active = jnp.einsum(
        "ed,fd->ef", grad_branch_two, w_down, preferred_element_type=jnp.float32
    )
    (grad_gate,) = gelu_pull(grad_active)
    grad_gate_bf = grad_gate.astype(jnp.bfloat16)
    grad_bias_up = jnp.sum(grad_gate_bf.astype(jnp.float32), axis=0)
    grad_up = contract_rows(grad_gate_bf, normed_two_bf)
    grad_normed_two = jnp.dot(grad_gate_bf, w_up, preferred_element_type=jnp.float32)
    grad_residual_norm, grad_ln2_gain, grad_ln2_shift = norm2_pull(grad_normed_two)
    grad_residual = grad_second + grad_residual_norm
    grad_branch_one = grad_residual.astype(jnp.bfloat16)
    grad_out_w = contract_rows(grad_branch_one, attended_bf)
    grad_attended = jnp.dot(grad_branch_one, w_out, preferred_element_type=jnp.float32)
    grad_query, grad_keys, grad_values = attend_pull(grad_attended)
    grad_query_bf = grad_query.astype(jnp.bfloat16)
    grad_kv = jnp.concatenate(
        [grad_keys.astype(jnp.bfloat16), grad_values.astype(jnp.bfloat16)], axis=2
    )
    grad_q_w = contract_rows(grad_query_bf, normed_bf[:, 0])
    grad_kv_w = jnp.einsum("esf,esd->fd", grad_kv, normed_bf, preferred_element_type=jnp.float32)
    grad_normed = jnp.einsum("esf,fd->esd", grad_kv, w_qkv[D:], preferred_element_type=jnp.float32)
    grad_normed = grad_normed.at[:, 0].add(
        jnp.dot(grad_query_bf, w_qkv[:D], preferred_element_type=jnp.float32)
    )
    grad_slots, grad_ln1_gain, grad_ln1_shift = norm1_pull(grad_normed)
    grad_first = grad_slots[:, 0] + grad_residual
    grad_cls = jnp.sum(grad_first, axis=0)
    grad_pos = jnp.concatenate([grad_cls[None], jnp.sum(grad_slots[:, 1:], axis=0)], axis=0)
    grad_pieces = grad_slots[:, 1:].astype(jnp.bfloat16).reshape(-1, D)
    grad_outgoing = contract_rows(own_onehot, grad_pieces).astype(jnp.bfloat16)
    grad_incoming = lax.all_to_all(
        grad_outgoing.reshape(device_count, cap, D), BOTH, 0, 0, tiled=True
    ).reshape(device_count * cap, D)
    piece_grad = contract_rows(asked_onehot, grad_incoming)

    vec_local = jnp.concatenate(
        [
            grad_cls,
            grad_pos.reshape(-1),
            grad_ln1_gain,
            grad_ln1_shift,
            grad_ln2_gain,
            grad_ln2_shift,
            grad_final_gain,
            grad_final_shift,
            grad_bias_up,
            grad_bias_down,
            lax.dynamic_update_slice_in_dim(
                jnp.zeros((OUTW,), jnp.float32), grad_bias_own, me * feature_rows, 0
            ),
        ]
    )
    vec_grad = lax.psum(vec_local, BOTH)
    grad_qkv = jnp.concatenate([grad_q_w, grad_kv_w], axis=0)
    packed_term = jnp.concatenate(
        [
            matrix.reshape(narrow_count, matrix.shape[0] // narrow_count, D)
            for matrix in (grad_qkv, grad_out_w, grad_up, grad_down)
        ],
        axis=1,
    )
    term_rows = packed_term.shape[1]
    share = term_rows // wide_count
    packed_term = (
        packed_term.astype(jnp.bfloat16)
        .reshape(narrow_count, wide_count, share, D)
        .transpose(1, 0, 2, 3)
        .reshape(device_count, share, D)
    )
    terms = lax.all_to_all(packed_term, BOTH, 0, 0, tiled=True)
    share_sum = jnp.sum(terms.astype(jnp.float32), axis=0)
    main_grad = lax.all_gather(share_sum.astype(jnp.bfloat16), "wide", axis=0, tiled=True)
    proj_grad = lax.all_gather(grad_proj_own.astype(jnp.bfloat16), BOTH, axis=0, tiled=True)
    proj_rows = OUTW // narrow_count
    proj_grad = lax.dynamic_slice_in_dim(proj_grad, narrow_at * proj_rows, proj_rows, 0)
    grad_block = jnp.concatenate([main_grad, proj_grad], axis=0).astype(jnp.float32)
    momentum_block = MUON_BETA * mat_momentum[0] + grad_block
    update_block = grad_block + MUON_BETA * momentum_block
    segments = block_slices(update_block, narrow_count)
    grams = lax.psum(jnp.stack([gram_of(segment) for segment in segments]), "narrow")
    new_segments = []
    for position, (row_total, master_seg, segment) in enumerate(
        zip(matrix_rows(), block_slices(mat_master[0], narrow_count), segments)
    ):
        square = jnp.sum(jnp.diagonal(grams[position]))
        norm = jnp.sqrt(square) + 1e-07
        gram = grams[position] / (norm * norm)
        chain = None
        for sweep_index in range(5):
            squared = jnp.dot(gram, gram, precision=HIGH)
            poly = NEWTON_B * gram + NEWTON_C * squared + NEWTON_A * jnp.eye(D, dtype=jnp.float32)
            chain = poly if chain is None else jnp.dot(chain, poly, precision=HIGH)
            if sweep_index < 4:
                gram = jnp.dot(jnp.dot(gram, poly, precision=HIGH), poly, precision=HIGH)
        ortho = jnp.dot(segment / norm, chain, precision=HIGH)
        new_segments.append(
            master_seg * (1.0 - MUON_RATE * MUON_DECAY)
            - MUON_RATE * math.sqrt(row_total / D) * ortho
        )
    weight_block = jnp.concatenate(new_segments, axis=0)[None]
    ema_block = EMA_DECAY * mat_ema + (1.0 - EMA_DECAY) * weight_block
    return (
        text_embeds,
        piece_grad,
        grad_block[None],
        momentum_block[None],
        weight_block,
        ema_block,
    ) + adam(vec_grad, vec_master, vec_moment1, vec_moment2, vec_ema)


MESH_ID = pl.DeviceIdType.MESH
CORES = 2
CHIPS = 4
PLANES = 4
MAIN = 192
CHUNKS = 3
CHUNK = MAIN // CHUNKS
PROJ = 32
PART = MAIN + PLANES * PROJ
VROWS = 16


def place():
    wide_at = lax.axis_index("wide")
    plane = lax.axis_index("narrow")
    chip = wide_at // CORES
    core = lax.rem(wide_at, CORES)
    return wide_at, plane, chip, core


def enter(targets):
    barrier = pltpu.get_barrier_semaphore()
    for target in targets:
        pl.semaphore_signal(barrier, inc=1, device_id=target, device_id_type=MESH_ID)
    pl.semaphore_wait(barrier, len(targets))


def neighbours(wide_at, plane, chip, core):
    sibling = (chip * CORES + 1 - core, plane)
    chips = [(lax.rem(chip + k, CHIPS) * CORES + core, plane) for k in range(1, CHIPS)]
    planes = [(wide_at, lax.rem(plane + k, PLANES)) for k in range(1, PLANES)]
    return sibling, chips, planes


def remote(src, dst, sems, index, target):
    return pltpu.make_async_remote_copy(
        src_ref=src,
        dst_ref=dst,
        send_sem=sems[0].at[index],
        recv_sem=sems[1].at[index],
        device_id=target,
        device_id_type=MESH_ID,
    )

OWNERS = (6, 7, 2, 4, 0)
BLOCK_TILES = (3, 1, 4, 4, 8)
MOST_TILES = max(BLOCK_TILES)
MAIN_TILES = 12
BANDS = 4
TEXT_TILE = 512
TILE = 128
SIDE = 2
STRIPS = 8
STRIP = D // STRIPS
PACKED = 640
PIECES = ((0, 64, 1024), (64, 64, 512), (128, 16, 384), (144, 48, 0))


def halves(value):
    high = value.astype(jnp.bfloat16)
    return high, (value - high.astype(jnp.float32)).astype(jnp.bfloat16)


def plain_dot(left, right):
    return jnp.dot(left, right, preferred_element_type=jnp.float32)


def split_dot(left, right):
    return plain_dot(left[0], right[0]) + (
        plain_dot(left[0], right[1]) + plain_dot(left[1], right[0])
    )


def dot_nt(left, right):
    return lax.dot_general(
        left, right, (((1,), (1,)), ((), ())), preferred_element_type=jnp.float32
    )


def dot_tn(left, right):
    return lax.dot_general(
        left, right, (((0,), (0,)), ((), ())), preferred_element_type=jnp.float32
    )


def band_onehot(ids, rows):
    place_in = lax.rem(ids, rows)
    spots = lax.broadcasted_iota(jnp.int32, (rows, ids.shape[1]), 0)
    return jnp.where(spots == place_in, 1.0, 0.0).astype(jnp.bfloat16)


def across(wide_at, plane, chip, core):
    x_at = lax.rem(chip, SIDE)
    x_chip = chip + 1 - 2 * x_at
    y_chip = lax.rem(chip + SIDE, CHIPS)
    return x_chip * CORES + core, y_chip * CORES + core


def owner_tiles(wide_at):
    tile_count = jnp.int32(0)
    tile_first = jnp.int32(0)
    begin = 0
    for owner, count in zip(OWNERS, BLOCK_TILES):
        tile_count = tile_count + jnp.where(wide_at == owner, count, 0)
        tile_first = tile_first + jnp.where(wide_at == owner, begin, 0)
        begin = begin + count
    return tile_count, tile_first


def spread_steps(own, held, sems, base, at):
    wide_at, plane, chip, core = at
    sibling = (chip * CORES + 1 - core, plane)
    x_wide, y_wide = across(wide_at, plane, chip, core)
    x_near, y_near = (x_wide, plane), (y_wide, plane)
    diagonal_wide = (CHIPS - 1 - chip) * CORES + core
    half = own.shape[0] // 2
    tops, bottoms = pl.ds(0, half), pl.ds(half, half)
    above, below = (wide_at, plane + 1), (wide_at, plane - 1)

    def climb(distance, source, src):
        spot = held.at[source, wide_at]
        return remote(spot if src is None else src, spot, sems, base + distance - 1, above)

    def sink(distance, source, src):
        spot = held.at[source, wide_at]
        return remote(spot if src is None else src, spot, sems, base + 2 + distance, below)

    def plane_copy(source, kind, src=None):
        index = base + 6 + 9 * source + kind
        own_spot = held.at[source, wide_at]
        x_spot, y_spot = held.at[source, x_wide], held.at[source, y_wide]
        far_spot = held.at[source, diagonal_wide]
        if kind in (0, 1, 2):
            target = (x_near, y_near, sibling)[kind]
            return remote(own_spot if src is None else src, own_spot, sems, index, target)
        if kind == 3:
            return remote(x_spot.at[tops], x_spot.at[tops], sems, index, y_near)
        if kind == 5:
            return remote(y_spot.at[bottoms], y_spot.at[bottoms], sems, index, x_near)
        if kind in (4, 6):
            spot = x_spot if kind == 4 else y_spot
            return remote(spot, spot, sems, index, sibling)
        rows = tops if kind == 7 else bottoms
        return remote(far_spot.at[rows], far_spot.at[rows], sems, index, sibling)

    def plane_send(source, src=None):
        for kind in (0, 1, 2):
            plane_copy(source, kind, src).start()

    def begin():
        @pl.when(plane < PLANES - 1)
        def _():
            climb(1, plane, own).start()

        @pl.when(plane > 0)
        def _():
            sink(1, plane, own).start()

        plane_send(plane, own)

    def arrive(distance):
        @pl.when(plane >= distance)
        def _():
            source = plane - distance
            climb(distance, source, None).wait_recv()
            if distance < PLANES - 1:

                @pl.when(plane < PLANES - 1)
                def _():
                    climb(distance + 1, source, None).start()

            plane_send(source)

        @pl.when(plane + distance < PLANES)
        def _():
            source = plane + distance
            sink(distance, source, None).wait_recv()
            if distance < PLANES - 1:

                @pl.when(plane > 0)
                def _():
                    sink(distance + 1, source, None).start()

            plane_send(source)

    def at_distance(distance, step):
        if distance == 0:
            step(plane)
            return

        @pl.when(plane >= distance)
        def _():
            step(plane - distance)

        @pl.when(plane + distance < PLANES)
        def _():
            step(plane + distance)

    def relay_one(source):
        plane_copy(source, 0).wait_recv()
        plane_copy(source, 3).start()
        plane_copy(source, 4).start()
        plane_copy(source, 1).wait_recv()
        plane_copy(source, 5).start()
        plane_copy(source, 6).start()

    def finish_one(source):
        plane_copy(source, 3).wait_recv()
        plane_copy(source, 7).start()
        plane_copy(source, 5).wait_recv()
        plane_copy(source, 8).start()

    def settle_one(source):
        for kind in (2, 4, 6, 7, 8):
            plane_copy(source, kind).wait_recv()
        for kind in range(9):
            plane_copy(source, kind).wait_send()

    def relay(distance):
        at_distance(distance, relay_one)

    def finish(distance):
        at_distance(distance, finish_one)

    def settled():
        for distance in range(PLANES):
            at_distance(distance, settle_one)
        for distance in range(1, PLANES):
            source = plane - distance + 1

            @pl.when((plane < PLANES - 1) & (source >= 0))
            def _(distance=distance, source=source):
                climb(distance, source, None).wait_send()

            down_source = plane + distance - 1

            @pl.when((plane > 0) & (down_source < PLANES))
            def _(distance=distance, down_source=down_source):
                sink(distance, down_source, None).wait_send()

    return begin, arrive, relay, finish, settled


SHARES = ((6, 0, 0, 384), (7, 0, 384, 128), (2, 0, 512, 512), (4, 0, 1024, 512)) + (
    (0, 0, 1536, 512),
    (0, 512, 2048, 512),
)


def settle_kernel(
    every,
    part,
    vec_ref,
    grad_ref,
    proj_ref,
    bias_ref,
    momentum_ref,
    ids_ref,
    mask_ref,
    outgoing_ref,
    text_ref,
    sum_ref,
    proj_sum_ref,
    vec_out_ref,
    rows_ref,
    incoming_ref,
    gram_ref,
    high_ref,
    low_ref,
    poly,
    chain,
    chain_high,
    chain_low,
    rows_out,
    table_ref,
    text_tiles,
    proj_own,
    proj_far,
    proj_part,
    vec_near,
    vec_far,
    vec_deep,
    main_tiles,
    proj_tiles,
    momentum_tiles,
    packs,
    pieces,
    totals,
    local_sem,
    tile_sem,
    text_sem,
    done_send,
    done_recv,
    pass_send,
    pass_recv,
    proj_send,
    proj_recv,
    vec_send,
    vec_recv,
    gram_send,
    gram_recv,
    share_sem,
    rows_send,
    rows_recv,
    piece_send,
    piece_recv,
):
    wide_at, plane, chip, core = place()
    sibling, chips, planes = neighbours(wide_at, plane, chip, core)
    x_wide, y_wide = across(wide_at, plane, chip, core)
    x_near, y_near = (x_wide, plane), (y_wide, plane)
    diagonal_wide = (CHIPS - 1 - chip) * CORES + core
    other = 1 - core
    x_at = lax.rem(chip, SIDE)
    y_at = chip // SIDE
    tile_count, tile_first = owner_tiles(wide_at)

    def momentum_load(tile):
        source = pl.ds(pl.multiple_of((tile_first + tile) * TILE, TILE), TILE)
        return pltpu.make_async_copy(
            momentum_ref.at[source], momentum_tiles.at[tile], tile_sem.at[0, tile]
        )

    @pl.loop(0, tile_count)
    def _(tile):
        momentum_load(tile).start()

    wide_count = CHIPS * CORES
    peers = [
        (lax.rem(wide_at + k // PLANES, wide_count), lax.rem(plane + k % PLANES, PLANES))
        for k in range(1, wide_count * PLANES)
    ]
    enter(peers)
    me = wide_at * PLANES + plane
    cap = outgoing_ref.shape[0] // (wide_count * PLANES)

    def piece_rows(device):
        return pl.ds(pl.multiple_of(device * cap, cap), cap)

    def piece_copy(index):
        wide_to, plane_to = peers[index]
        return remote(
            outgoing_ref.at[piece_rows(wide_to * PLANES + plane_to)],
            incoming_ref.at[piece_rows(me)],
            (piece_send, piece_recv),
            index,
            (wide_to, plane_to),
        )

    def send_pieces(begin, end):
        for index in range(begin, end):
            piece_copy(index).start()

    own_pieces = pltpu.make_async_copy(
        outgoing_ref.at[piece_rows(me)], incoming_ref.at[piece_rows(me)], local_sem.at[7]
    )
    own_pieces.start()

    vec_sems = (vec_send, vec_recv)
    vec_copies = [remote(vec_ref.at[other], vec_near, vec_sems, 0, sibling)]
    vec_copies[0].start()
    def vec_far_step():
        vec_copies[0].wait_recv()
        vec_far[chip] = vec_ref[core] + vec_near[...]
        for k, target in enumerate(chips):
            copy = remote(vec_far.at[chip], vec_far.at[chip], vec_sems, 1 + k, target)
            copy.start()
            vec_copies.append(copy)

    def vec_deep_step():
        for copy in vec_copies[1:4]:
            copy.wait()
        vec_deep[plane] = (vec_far[0] + vec_far[1]) + (vec_far[2] + vec_far[3])
        for k, target in enumerate(planes):
            copy = remote(vec_deep.at[plane], vec_deep.at[plane], vec_sems, 4 + k, target)
            copy.start()
            vec_copies.append(copy)

    def vec_last_step():
        for copy in vec_copies[4:7]:
            copy.wait()
        vec_out_ref[core] = (vec_deep[0] + vec_deep[1]) + (vec_deep[2] + vec_deep[3])
        copy = remote(vec_out_ref.at[core], vec_out_ref.at[core], vec_sems, 7, sibling)
        copy.start()
        vec_copies.append(copy)

    count = every.shape[2]
    features = proj_ref.shape[0]
    wide_count = CHIPS * CORES
    per_band = grad_ref.shape[0] // BANDS
    proj_sems = (proj_send, proj_recv)
    proj_copies = []

    def proj_near_step():
        total = jnp.zeros((features, D), jnp.float32)
        for block in range(PLANES * wide_count):
            rows = every[block % PLANES, block // PLANES]
            total = total + dot_tn(grad_ref[block], rows)
        proj_own[...] = total.astype(jnp.bfloat16).reshape(CHIPS, PROJ, D)
        for k, target in enumerate(chips):
            to_chip = lax.rem(chip + k + 1, CHIPS)
            copy = remote(proj_own.at[to_chip], proj_far.at[chip], proj_sems, k, target)
            copy.start()
            proj_copies.append(copy)
        proj_far[chip] = proj_own[chip]

    def proj_far_step():
        for copy in proj_copies:
            copy.wait()
        for k, target in enumerate(planes):
            to_plane = lax.rem(plane + k + 1, PLANES)
            copy = remote(proj_far.at[to_plane], proj_part.at[plane], proj_sems, 3 + k, target)
            copy.start()
            proj_copies.append(copy)
        proj_part[plane] = proj_far[plane]

    def publish_proj():
        for copy in proj_copies[3:]:
            copy.wait()
        publish(len(PIECES), proj_part, proj_natural(chip, core))

    done_sems = (done_send, done_recv)
    pass_sems = (pass_send, pass_recv)
    done_copies = {}
    locals_done = {}

    def natural(index, wide):
        _, size, base = PIECES[index]
        return sum_ref.at[pl.ds(pl.multiple_of(base + wide * size, 16), size)]

    def proj_natural(at_chip, at_core):
        return proj_sum_ref.at[at_core, :, at_chip]

    def publish(index, src, spot):
        copies = []
        for k, target in enumerate([sibling] + chips):
            copy = remote(src, spot, done_sems, index * 4 + k, target)
            copy.start()
            copies.append(copy)
        done_copies[index] = copies
        copy = pltpu.make_async_copy(src, spot, local_sem.at[2 + index])
        copy.start()
        locals_done[index] = copy

    def publish_step(chunk):
        for index, (offset, size, _) in enumerate(PIECES):
            if offset // CHUNK == chunk:
                publish(index, part.at[pl.ds(offset, size)], natural(index, wide_at))

    pass_copies = {}

    def pass_step(index):
        pass_copies[index] = []
        for k in range(3):
            done_copies[index][1 + k].wait_recv()
            from_chip = lax.rem(chip + CHIPS - 1 - k, CHIPS)
            if index < len(PIECES):
                spot = natural(index, from_chip * CORES + core)
            else:
                spot = proj_natural(from_chip, core)
            copy = remote(spot, spot, pass_sems, index * 3 + k, sibling)
            copy.start()
            pass_copies[index].append(copy)

    def table_step():
        for block in range(PLANES * wide_count):
            rows = every[block % PLANES, block // PLANES]
            band, spot = divmod(block, per_band)
            table_ref[band * features : (band + 1) * features, spot * count : (spot + 1) * count] = (
                dot_nt(proj_ref[...], rows) + bias_ref[...]
            ).astype(jnp.bfloat16)

    text_rows = table_ref.shape[1]
    row_tiles = ids_ref.shape[1] // TEXT_TILE
    text_count = ids_ref.shape[0] * row_tiles

    def text_copy(step):
        slot = lax.rem(step, 2)
        lanes = pl.ds(pl.multiple_of(step * TEXT_TILE, TEXT_TILE), TEXT_TILE)
        return pltpu.make_async_copy(text_tiles.at[slot], text_ref.at[:, lanes], text_sem.at[slot])

    def text_steps(begin, end):
        @pl.loop(begin, end)
        def _(step):
            row = pl.ds(step // row_tiles, 1)
            start = lax.rem(step, row_tiles) * TEXT_TILE
            id_lanes = pl.ds(pl.multiple_of(start, TEXT_TILE), TEXT_TILE)
            ids = ids_ref[row, id_lanes]
            values = plain_dot(table_ref[...], band_onehot(ids, text_rows))
            band = jnp.where(mask_ref[row, id_lanes] > 0, ids // text_rows, -1)
            total = jnp.zeros((features, TEXT_TILE), jnp.float32)
            for b in range(BANDS):
                total = jnp.where(band == b, values[b * features : (b + 1) * features], total)

            @pl.when(step >= 2)
            def _():
                text_copy(step - 2).wait()

            text_tiles[lax.rem(step, 2)] = total
            text_copy(step).start()

    def settle_piece(index):
        done_copies[index][0].wait_recv()
        for copy in pass_copies[index]:
            copy.wait_recv()
        locals_done[index].wait()

    gram_sems = (gram_send, gram_recv)

    def add_tile(tile, gradient):
        momentum_load(tile).wait()
        gradient = gradient.astype(jnp.float32)
        update = gradient + MUON_BETA * (MUON_BETA * momentum_tiles[tile] + gradient)
        high, low = halves(update)
        rows = pl.ds(pl.multiple_of(tile * TILE, TILE), TILE)
        high_ref[rows, :] = high
        low_ref[rows, :] = low

    early = (wide_at == OWNERS[0]) | (wide_at == OWNERS[1])
    late = (tile_count > 0) & jnp.logical_not(early)

    def proj_tiles_step():
        loads = [
            pltpu.make_async_copy(
                proj_sum_ref.at[tile // PLANES, tile % PLANES],
                proj_tiles.at[tile],
                tile_sem.at[1, tile],
            )
            for tile in range(MOST_TILES)
        ]
        for copy in loads:
            copy.start()
        for copy in loads:
            copy.wait()

        @pl.loop(0, MOST_TILES)
        def _(tile):
            add_tile(tile, proj_tiles[tile].reshape(TILE, D))

    def main_tiles_step():
        def load(tile):
            source = pl.ds(pl.multiple_of((tile_first + tile) * TILE, TILE), TILE)
            return pltpu.make_async_copy(
                sum_ref.at[source], main_tiles.at[tile], tile_sem.at[1, tile]
            )

        @pl.loop(0, tile_count)
        def _(tile):
            load(tile).start()

        @pl.loop(0, tile_count)
        def _(tile):
            load(tile).wait()
            add_tile(tile, main_tiles[tile])

    def gram_product(count_here):
        high = high_ref[0 : count_here * TILE, :]
        cross = dot_tn(high, low_ref[0 : count_here * TILE, :])
        gram_ref[...] = dot_tn(high, high) + (cross + cross.T)

    def gram_copies(first_index):
        copies = []
        for k, target in enumerate(planes):
            to_plane = lax.rem(plane + k + 1, PLANES)
            if first_index == 0:
                src, dst = packs.at[to_plane], pieces.at[plane]
            else:
                src, dst = totals.at[plane], totals.at[plane]
            copies.append(remote(src, dst, gram_sems, first_index + k, target))
        return copies

    def gram_send_step():
        for t in range(PLANES):
            for strip, lane in ((t, 0), (STRIPS - 1 - t, 1)):
                begin = strip // 2 * TILE
                value = gram_ref[strip * STRIP : (strip + 1) * STRIP, begin:]
                width = D - begin
                at = 0 if lane == 0 else PACKED - width
                packs[t, :, at : at + width] = value
        for copy in gram_copies(0):
            copy.start()
        pieces[plane] = packs[plane]

    def gram_early_step():
        @pl.when(early)
        def _():
            main_tiles_step()

        for owner, count_here in zip(OWNERS[:2], BLOCK_TILES[:2]):

            @pl.when(wide_at == owner)
            def _(count_here=count_here):
                gram_product(count_here)

        @pl.when(early)
        def _():
            gram_send_step()

    def gram_late_step():
        @pl.when(wide_at == OWNERS[4])
        def _():
            proj_tiles_step()
            gram_product(BLOCK_TILES[4])

        @pl.when(late & (wide_at != OWNERS[4]))
        def _():
            main_tiles_step()
            gram_product(BLOCK_TILES[3])

        @pl.when(late)
        def _():
            gram_send_step()

    def gram_total_step(here):
        @pl.when(here)
        def _():
            for copy in gram_copies(0):
                copy.wait()
            totals[plane] = (pieces[0] + pieces[1]) + (pieces[2] + pieces[3])
            for copy in gram_copies(3):
                copy.start()

    def gram_whole_step():
        @pl.when(tile_count > 0)
        def _():
            for copy in gram_copies(3):
                copy.wait()
            for t in range(PLANES):
                for strip, lane in ((t, 0), (STRIPS - 1 - t, 1)):
                    begin = strip // 2 * TILE
                    width = D - begin
                    at = 0 if lane == 0 else PACKED - width
                    gram_ref[strip * STRIP : (strip + 1) * STRIP, begin:] = totals[
                        t, :, at : at + width
                    ]
            row_block = lax.broadcasted_iota(jnp.int32, (D, D), 0) // TILE
            lane_block = lax.broadcasted_iota(jnp.int32, (D, D), 1) // TILE
            value = gram_ref[...]
            gram_ref[...] = jnp.where(lane_block >= row_block, value, value.T)

    def chain_step():
        diagonal = lax.broadcasted_iota(jnp.int32, (D, D), 0) == lax.broadcasted_iota(
            jnp.int32, (D, D), 1
        )
        square = jnp.sum(jnp.where(diagonal, gram_ref[...], 0.0))
        inverse = 1.0 / (jnp.sqrt(jnp.full((1, 1), square)) + 1e-07)
        gram_ref[...] = gram_ref[...] * (inverse * inverse)

        def make_poly():
            value = gram_ref[...]
            parts = halves(value)
            diagonal = lax.broadcasted_iota(jnp.int32, (D, D), 0) == lax.broadcasted_iota(
                jnp.int32, (D, D), 1
            )
            poly[...] = (
                NEWTON_B * value
                + NEWTON_C * split_dot(parts, parts)
                + jnp.where(diagonal, NEWTON_A, 0.0)
            )

        def next_gram():
            parts = halves(poly[...])
            half_way = split_dot(halves(gram_ref[...]), parts)
            gram_ref[...] = split_dot(halves(half_way), parts)

        def extend():
            chain[...] = split_dot(halves(chain[...]), halves(poly[...]))

        make_poly()
        chain[...] = poly[...]
        next_gram()

        @pl.loop(0, 3)
        def _(sweep):
            make_poly()
            extend()
            next_gram()

        make_poly()
        extend()
        high, low = halves(chain[...] * inverse)
        chain_high[...] = high
        chain_low[...] = low

    proj_near_step()
    publish_step(2)
    publish_step(0)
    publish_step(1)
    vec_far_step()
    pass_step(2)
    pass_step(3)
    proj_far_step()
    pass_step(0)
    pass_step(1)
    vec_deep_step()
    table_step()
    settle_piece(2)
    settle_piece(3)
    publish_proj()
    gram_early_step()
    vec_last_step()
    settle_piece(0)
    settle_piece(1)
    pass_step(4)
    settle_piece(4)
    gram_late_step()
    text_steps(0, text_count // 2)
    gram_total_step(tile_count > 0)
    text_steps(text_count // 2, text_count)
    gram_whole_step()
    send_pieces(0, len(peers))
    @pl.when(tile_count > 0)
    def _():
        chain_step()


    share_sems = (rows_send, rows_recv)

    def share_copies(index):
        owner, source, begin, size = SHARES[index]
        owner_chip, owner_core = divmod(owner, CORES)
        mine = rows_out.at[pl.ds(source, size)]
        spot = rows_ref.at[pl.ds(begin, size)]
        first = rows_ref.at[pl.ds(begin, size // 2)]
        last = rows_ref.at[pl.ds(begin + size // 2, size // 2)]
        base = index * 9
        roles = {
            "x": (owner_chip ^ 1) * CORES + owner_core,
            "y": (owner_chip ^ 2) * CORES + owner_core,
            "d": (owner_chip ^ 3) * CORES + owner_core,
        }
        sends = {
            "o": [
                (mine, spot, base, x_near),
                (mine, spot, base + 1, y_near),
                (mine, spot, base + 2, sibling),
            ],
            "x": [(first, first, base + 3, y_near), (spot, spot, base + 5, sibling)],
            "y": [(last, last, base + 4, x_near), (spot, spot, base + 6, sibling)],
            "d": [(first, first, base + 7, sibling), (last, last, base + 8, sibling)],
        }
        gets = {
            "x": [(spot, base)],
            "y": [(spot, base + 1)],
            "d": [(first, base + 3), (last, base + 4)],
            "so": [(spot, base + 2)],
            "sx": [(spot, base + 5)],
            "sy": [(spot, base + 6)],
            "sd": [(first, base + 7), (last, base + 8)],
        }
        roles["o"] = owner
        for role in ("o", "x", "y", "d"):
            at = roles[role]
            roles["s" + role] = at // CORES * CORES + 1 - at % CORES
        local = (mine, spot, share_sem.at[index])
        return roles, sends, gets, local

    def started(entry):
        src, dst, index, target = entry
        return remote(src, dst, share_sems, index, target)

    def arriving(entry):
        spot, index = entry
        return remote(spot, spot, share_sems, index, sibling)

    plans = [share_copies(index) for index in range(len(SHARES))]
    for (roles, sends, gets, local), (_, source, _, size) in zip(plans, SHARES):

        @pl.when(wide_at == roles["o"])
        def _(sends=sends, local=local, source=source, size=size):
            rows = slice(source, source + size)
            rows_out[rows, :] = split_dot(
                (high_ref[rows, :], low_ref[rows, :]), (chain_high[...], chain_low[...])
            ).astype(jnp.bfloat16)
            for entry in sends["o"]:
                started(entry).start()
            pltpu.make_async_copy(*local).start()

    for phase in (("x", "y"), ("d",)):
        for roles, sends, gets, local in plans:
            for role in phase:

                @pl.when(wide_at == roles[role])
                def _(sends=sends, gets=gets, role=role):
                    for got, entry in zip(gets[role] * 2, sends[role]):
                        if role == "d" or entry is sends[role][0]:
                            arriving(got).wait_recv()
                        started(entry).start()

    for roles, sends, gets, local in plans:
        for role in ("so", "sx", "sy", "sd"):

            @pl.when(wide_at == roles[role])
            def _(gets=gets, role=role):
                for got in gets[role]:
                    arriving(got).wait_recv()

        for role in ("o", "x", "y", "d"):

            @pl.when(wide_at == roles[role])
            def _(sends=sends, local=local, role=role):
                for entry in sends[role]:
                    started(entry).wait_send()
                if role == "o":
                    pltpu.make_async_copy(*local).wait()


    for copies in list(done_copies.values()) + list(pass_copies.values()):
        for copy in copies:
            copy.wait_send()
    vec_copies[0].wait_send()
    vec_copies[7].wait()
    text_copy(text_count - 2).wait()
    text_copy(text_count - 1).wait()
    own_pieces.wait()
    for index in range(len(peers)):
        piece_copy(index).wait()


def settle(every, part, vec, grad_own, proj_own, bias_own, momentum, text_ids, text_mask, outgoing):
    dma = pltpu.SemaphoreType.DMA
    f32, bf = jnp.float32, jnp.bfloat16
    features, tokens = proj_own.shape[0], text_ids.size
    rows = grad_own.shape[0] * grad_own.shape[1] // BANDS
    hbm = pl.BlockSpec(memory_space=pl.ANY)
    vmem = pl.BlockSpec(memory_space=pltpu.VMEM)
    return pl.pallas_call(
        settle_kernel,
        out_shape=(
            jax.ShapeDtypeStruct((features, tokens), f32),
            jax.ShapeDtypeStruct((MAIN_TILES * TILE, D), bf),
            jax.ShapeDtypeStruct((CORES, PLANES, CHIPS, PROJ, D), bf),
            jax.ShapeDtypeStruct((CORES, VROWS, D), f32),
            jax.ShapeDtypeStruct(((MAIN_TILES + MOST_TILES) * TILE, D), bf),
            jax.ShapeDtypeStruct(outgoing.shape, bf),
        ),
        in_specs=[vmem, vmem, vmem, vmem, vmem, vmem, hbm, vmem, vmem, hbm],
        out_specs=(hbm, hbm, hbm, vmem, hbm, hbm),
        scratch_shapes=[
            pltpu.VMEM((D, D), f32),
            pltpu.VMEM((MOST_TILES * TILE, D), bf),
            pltpu.VMEM((MOST_TILES * TILE, D), bf),
            pltpu.VMEM((D, D), f32),
            pltpu.VMEM((D, D), f32),
            pltpu.VMEM((D, D), bf),
            pltpu.VMEM((D, D), bf),
            pltpu.VMEM((MOST_TILES * TILE, D), bf),
            pltpu.VMEM((BANDS * features, rows), bf),
            pltpu.VMEM((2, features, TEXT_TILE), f32),
            pltpu.VMEM((CHIPS, PROJ, D), bf),
            pltpu.VMEM((CHIPS, PROJ, D), bf),
            pltpu.VMEM((PLANES, PROJ, D), bf),
            pltpu.VMEM((VROWS, D), f32),
            pltpu.VMEM((CHIPS, VROWS, D), f32),
            pltpu.VMEM((PLANES, VROWS, D), f32),
            pltpu.VMEM((4, TILE, D), bf),
            pltpu.VMEM((MOST_TILES, CHIPS, PROJ, D), bf),
            pltpu.VMEM((MOST_TILES, TILE, D), f32),
            pltpu.VMEM((PLANES, STRIP, PACKED), f32),
            pltpu.VMEM((PLANES, STRIP, PACKED), f32),
            pltpu.VMEM((PLANES, STRIP, PACKED), f32),
            dma((8,)),
            dma((2, MOST_TILES)),
            dma((2,)),
            dma((20,)),
            dma((20,)),
            dma((15,)),
            dma((15,)),
            dma((6,)),
            dma((6,)),
            dma((8,)),
            dma((8,)),
            dma((6,)),
            dma((6,)),
            dma((len(SHARES),)),
            dma((len(SHARES) * 9,)),
            dma((len(SHARES) * 9,)),
            dma((PLANES * CHIPS * CORES - 1,)),
            dma((PLANES * CHIPS * CORES - 1,)),
        ],
        compiler_params=pltpu.CompilerParams(
            collective_id=3, has_side_effects=True, vmem_limit_bytes=58 * 2**20
        ),
        name="settle",
    )(
        every,
        part,
        vec,
        grad_own,
        proj_own,
        bias_own,
        momentum,
        text_ids,
        text_mask,
        outgoing,
    )


def finish_kernel(main_ref, proj_ref, rows_ref, momentum_ref, master_ref, ema_ref, *outs):
    grad_ref, momentum_new_ref, weight_ref, ema_new_ref = outs
    tile = pl.program_id(0)
    height = rows_ref.shape[0]
    main = main_ref[...].astype(jnp.float32)
    proj = proj_ref[...].reshape(height, D).astype(jnp.float32)
    gradient = jnp.where(tile < MAIN_TILES * TILE // height, main, proj)
    grad_ref[0] = gradient
    momentum_new_ref[0] = MUON_BETA * momentum_ref[0] + gradient
    row = lax.broadcasted_iota(jnp.int32, (height, 1), 0) + tile * height
    scale = jnp.zeros((height, 1), jnp.float32)
    begin = 0
    for row_total, count in zip(matrix_rows(), BLOCK_TILES):
        inside = (row >= begin * TILE) & (row < (begin + count) * TILE)
        scale = jnp.where(inside, MUON_RATE * math.sqrt(row_total / D), scale)
        begin = begin + count
    weight = master_ref[0] * (1.0 - MUON_RATE * MUON_DECAY) - scale * rows_ref[...].astype(
        jnp.float32
    )
    weight_ref[0] = weight
    ema_new_ref[0] = EMA_DECAY * ema_ref[0] + (1.0 - EMA_DECAY) * weight


def finish(main_sum, proj_sum, rows, momentum, master, ema):
    height = 2 * TILE
    tall = height // TILE
    main_steps = MAIN_TILES // tall
    block = pl.BlockSpec((1, height, D), lambda i: (0, i, 0))
    proj = proj_sum.reshape((MOST_TILES,) + proj_sum.shape[2:])
    return pl.pallas_call(
        finish_kernel,
        grid=((MAIN_TILES + MOST_TILES) // tall,),
        out_shape=(jax.ShapeDtypeStruct(master.shape, jnp.float32),) * 4,
        in_specs=[
            pl.BlockSpec((height, D), lambda i: (jnp.minimum(i, main_steps - 1), 0)),
            pl.BlockSpec(
                (tall,) + proj.shape[1:], lambda i: (jnp.maximum(i - main_steps, 0), 0, 0, 0)
            ),
            pl.BlockSpec((height, D), lambda i: (i, 0)),
            block,
            block,
            block,
        ],
        out_specs=(block,) * 4,
        cost_estimate=pl.CostEstimate(
            flops=12 * master.size, bytes_accessed=32 * master.size, transcendentals=0
        ),
        compiler_params=pltpu.CompilerParams(vmem_limit_bytes=62 * 2**20),
        name="finish",
    )(main_sum, proj, rows, momentum, master, ema)

def two_part_dot(left, right):
    high, low = halves(left)
    return plain_dot(high, right) + plain_dot(low, right)


def normalize(values):
    center = values - jnp.mean(values, axis=-1, keepdims=True)
    spread = jnp.mean(center * center, axis=-1, keepdims=True)
    scale = lax.rsqrt(spread + 1e-05)
    return center * scale, scale


def normalize_back(grad, gain, hat, scale):
    grad_hat = grad * gain
    return scale * (
        grad_hat
        - jnp.mean(grad_hat, axis=-1, keepdims=True)
        - hat * jnp.mean(grad_hat * hat, axis=-1, keepdims=True)
    )


def over_rows(values):
    return jnp.sum(values, axis=0, keepdims=True)


def plane_sums(first, near_copies, near, buffers, far_sems, deep_sems):
    x_first, y_first, x_second, y_second, second, deep = buffers
    wide_at, plane, chip, core = place()
    _, _, planes = neighbours(wide_at, plane, chip, core)
    x_wide, y_wide = across(wide_at, plane, chip, core)
    x_near, y_near = (x_wide, plane), (y_wide, plane)
    x_at, y_at = lax.rem(chip, SIDE), chip // SIDE
    lows, highs = pl.ds(0, 2), pl.ds(2, 2)
    sent = []
    waiting = {}

    def start(src, dst, sems, index, target):
        copy = remote(src, dst, sems, index, target)
        copy.start()
        sent.append(copy)
        return copy

    def add(left, right):
        return (left.astype(jnp.float32) + right.astype(jnp.float32)).astype(jnp.bfloat16)

    def first_step(chunk):
        near_copies[chunk].wait_recv()

        @pl.loop(0, CHIPS * PLANES)
        def _(step):
            y, x, m = step // (SIDE * PLANES), lax.rem(step // PLANES, SIDE), lax.rem(step, PLANES)
            first[chunk, y, x, m] = add(first[chunk, y, x, m], near[chunk, y, x, m])

        base = chunk * 4
        waiting["x", chunk] = start(
            first.at[chunk, :, 1 - x_at, lows], x_first.at[chunk], far_sems, base, x_near
        )
        waiting["y", chunk] = start(
            first.at[chunk, 1 - y_at, :, highs], y_first.at[chunk], far_sems, base + 1, y_near
        )

    def second_step(chunk):
        base = chunk * 4
        waiting["x", chunk].wait_recv()
        for y in range(SIDE):
            for m in range(2):
                first[chunk, y, x_at, m] = add(first[chunk, y, x_at, m], x_first[chunk, y, m])
        waiting["yy", chunk] = start(
            first.at[chunk, 1 - y_at, x_at, lows], y_second.at[chunk], far_sems, base + 2, y_near
        )
        waiting["y", chunk].wait_recv()
        for x in range(SIDE):
            for m in range(2):
                first[chunk, y_at, x, 2 + m] = add(
                    first[chunk, y_at, x, 2 + m], y_first[chunk, x, m]
                )
        waiting["xx", chunk] = start(
            first.at[chunk, y_at, 1 - x_at, highs], x_second.at[chunk], far_sems, base + 3, x_near
        )

    def deep_step(chunk):
        waiting["yy", chunk].wait_recv()
        for m in range(2):
            second[chunk, m] = add(first[chunk, y_at, x_at, m], y_second[chunk, m])
        waiting["xx", chunk].wait_recv()
        for m in range(2):
            second[chunk, 2 + m] = add(first[chunk, y_at, x_at, 2 + m], x_second[chunk, m])
        for k, target in enumerate(planes):
            to_plane = lax.rem(plane + k + 1, PLANES)
            waiting["z", chunk, k] = start(
                second.at[chunk, to_plane], deep.at[chunk, k], deep_sems, chunk * 3 + k, target
            )

    def total(chunk):
        value = second[chunk, plane].astype(jnp.float32)
        for k in range(3):
            waiting["z", chunk, k].wait_recv()
            value = value + deep[chunk, k].astype(jnp.float32)
        return value

    def sums_settled():
        for copy in sent:
            copy.wait_send()

    return first_step, second_step, deep_step, total, sums_settled


def sum_scratch(chunks):
    dma = pltpu.SemaphoreType.DMA
    bf = jnp.bfloat16
    return [
        pltpu.VMEM((chunks, SIDE, 2, CHUNK, D), bf),
        pltpu.VMEM((chunks, SIDE, 2, CHUNK, D), bf),
        pltpu.VMEM((chunks, 2, CHUNK, D), bf),
        pltpu.VMEM((chunks, 2, CHUNK, D), bf),
        pltpu.VMEM((chunks, PLANES, CHUNK, D), bf),
        pltpu.VMEM((chunks, 3, CHUNK, D), bf),
        dma((chunks * 4,)),
        dma((chunks * 4,)),
        dma((chunks * 3,)),
        dma((chunks * 3,)),
    ]


def layer_kernel(
    master_ref,
    pieces_ref,
    table_ref,
    ids_ref,
    mask_ref,
    cot_ref,
    live_ref,
    param_ref,
    every_ref,
    part_ref,
    outgoing_ref,
    vec_ref,
    own_grad_ref,
    own_proj_ref,
    rows_ref,
    main_ref,
    own_rows,
    every_ids,
    spots_ref,
    asked_ranks,
    asked_locals,
    incoming_ref,
    proj_rows,
    proj_stage,
    z_ref,
    packed,
    text_total,
    onehot,
    hats,
    scales,
    normed,
    keys,
    probs,
    grad_kv,
    grad_normed,
    grad_pieces,
    active,
    slope,
    slides,
    sums,
    local_sem,
    x_first,
    y_first,
    x_second,
    y_second,
    second_sum,
    deep,
    far_send,
    far_recv,
    deep_send,
    deep_recv,
    tell_send,
    tell_recv,
    piece_send,
    piece_recv,
    near_send,
    near_recv,
    main_near,
    main_x_first,
    main_y_first,
    main_x_second,
    main_y_second,
    main_second,
    main_deep,
    main_far_send,
    main_far_recv,
    main_deep_send,
    main_deep_recv,
    main_send,
    main_recv,
    body_send,
    body_recv,
    proj_send,
    proj_recv,
    z_send,
    z_recv,
):
    at = place()
    wide_at, plane, chip, core = at
    me = wide_at * PLANES + plane
    wide_count = CHIPS * CORES
    group_rows = table_ref.shape[0]
    cap = outgoing_ref.shape[0] // (wide_count * PLANES)
    entries = z_ref.shape[0]
    peers = [
        (lax.rem(wide_at + k // PLANES, wide_count), lax.rem(plane + k % PLANES, PLANES))
        for k in range(1, wide_count * PLANES)
    ]

    sibling, _, planes = neighbours(*at)
    body_begin, body_arrive, body_relay, body_finish, body_settled = spread_steps(
        packed.at[plane, wide_at], packed, (body_send, body_recv), 0, at
    )
    z_begin, z_arrive, z_relay, z_finish, z_settled = spread_steps(
        z_ref, every_ref, (z_send, z_recv), 0, at
    )
    holds_proj = plane == chip
    proj_sems = (proj_send, proj_recv)
    features = cot_ref.shape[0]

    def proj_load():
        begin = master_ref.shape[0] - OUTW // PLANES + core * PLANES * features
        source = pl.ds(pl.multiple_of(begin, 16), PLANES * features)
        return pltpu.make_async_copy(master_ref.at[source], proj_rows, local_sem.at[4])

    def proj_copy(k):
        to_plane = lax.rem(plane + k + 1, PLANES)
        return remote(proj_stage.at[to_plane], own_proj_ref, proj_sems, k, planes[k])

    @pl.when(holds_proj)
    def _():
        proj_load().start()

    loads = []
    begin = 0
    block = 0
    for index, row_total in enumerate(matrix_rows()[:4]):
        height = row_total // PLANES
        size = height // wide_count
        copy = pltpu.make_async_copy(
            master_ref.at[pl.ds(pl.multiple_of(block + wide_at * size, 16), size)],
            own_rows.at[pl.ds(begin, size)],
            local_sem.at[index],
        )
        copy.start()
        loads.append(copy)
        begin = begin + size
        block = block + height
    enter(peers)
    every_ids[me] = jnp.concatenate(
        [pieces_ref[...], jnp.zeros((SLOTS - PSLOTS, entries), jnp.int32)], axis=0
    )
    tell_copies = []
    for index, target in enumerate(peers):
        copy = remote(every_ids.at[me], every_ids.at[me], (tell_send, tell_recv), index, target)
        copy.start()
        tell_copies.append(copy)
    for copy in loads:
        copy.wait()
    packed[plane, wide_at] = own_rows[...].astype(jnp.bfloat16)

    def proj_begin():
        @pl.when(holds_proj)
        def _():
            proj_load().wait()
            proj_stage[...] = proj_rows[...].astype(jnp.bfloat16).reshape(proj_stage.shape)
            for k in range(PLANES - 1):
                proj_copy(k).start()
            own_proj_ref[...] = proj_stage[plane]

    piece_copies = []

    def piece_rows(device):
        return pl.ds(pl.multiple_of(device * cap, cap), cap)

    def send_pieces(begin, end):
        for index in range(begin, end):
            wide_to, plane_to = peers[index]
            copy = remote(
                outgoing_ref.at[piece_rows(wide_to * PLANES + plane_to)],
                incoming_ref.at[piece_rows(me)],
                (piece_send, piece_recv),
                index,
                (wide_to, plane_to),
            )
            copy.start()
            piece_copies.append(copy)

    near_copies = []
    dz_first, dz_second, dz_deep, dz_total, dz_settled = plane_sums(
        main_ref.at[core],
        near_copies,
        grad_kv,
        (x_first, y_first, x_second, y_second, second_sum, deep),
        (far_send, far_recv),
        (deep_send, deep_recv),
    )

    main_copies = {}
    main_first, main_then, main_last, main_total, main_settled = plane_sums(
        main_ref.at[core],
        main_copies,
        main_near,
        (main_x_first, main_y_first, main_x_second, main_y_second, main_second, main_deep),
        (main_far_send, main_far_recv),
        (main_deep_send, main_deep_recv),
    )

    def main_begin(chunk):
        copy = remote(
            main_ref.at[1 - core, chunk],
            main_near.at[chunk],
            (main_send, main_recv),
            chunk,
            sibling,
        )
        copy.start()
        main_copies[chunk] = copy

    def dz_begin():
        @pl.when(jnp.logical_not(holds_proj))
        def _():
            k = lax.rem(plane - chip - 1 + PLANES, PLANES)
            remote(proj_stage.at[0], own_proj_ref, proj_sems, k, sibling).wait_recv()

        proj = own_proj_ref[...]
        for wide in range(wide_count):
            block = own_grad_ref[wide * PLANES : (wide + 1) * PLANES]
            value = plain_dot(block.reshape(PLANES * entries, features), proj)
            value = value.astype(jnp.bfloat16).reshape(PLANES, entries, D)
            y, x = divmod(wide // CORES, SIDE)
            for part in range(entries // CHUNK):
                main_ref[wide % CORES, part, y, x] = value[:, part * CHUNK : (part + 1) * CHUNK, :]
        for part in range(entries // CHUNK):
            copy = remote(
                main_ref.at[1 - core, part],
                grad_kv.at[part],
                (near_send, near_recv),
                part,
                sibling,
            )
            copy.start()
            near_copies.append(copy)

    text_rows = own_grad_ref.shape[0] * own_grad_ref.shape[1] // BANDS
    text_total[...] = jnp.zeros_like(text_total)

    row_tiles = ids_ref.shape[1] // TEXT_TILE

    def build_pieces():
        for copy in tell_copies:
            copy.wait()
        device_count = wide_count * PLANES
        slot_count = entries * PSLOTS
        asked_ids = jnp.concatenate([every_ids[:, slot, :] for slot in range(PSLOTS)], axis=1)
        own_ids = jnp.concatenate([pieces_ref[slot : slot + 1, :] for slot in range(PSLOTS)], axis=1)
        asked = asked_ids // group_rows == me
        own_group = own_ids // group_rows
        group_at = lax.broadcasted_iota(jnp.int32, (device_count, slot_count), 0)
        grouped = jnp.where(group_at == own_group, 1.0, 0.0)
        marks = jnp.concatenate([jnp.where(asked, 1.0, 0.0), grouped], axis=0).astype(jnp.bfloat16)
        earlier = jnp.where(
            lax.broadcasted_iota(jnp.int32, (slot_count, slot_count), 0)
            < lax.broadcasted_iota(jnp.int32, (slot_count, slot_count), 1),
            1.0,
            0.0,
        ).astype(jnp.bfloat16)
        ranks = plain_dot(marks, earlier)
        own_rank = over_rows(grouped * ranks[device_count:, :])
        spots = own_group * cap + own_rank.astype(jnp.int32)
        for slot in range(PSLOTS):
            spots_ref[slot + 1 : slot + 2, :] = spots[:, slot * entries : (slot + 1) * entries]
        asked_ranks[...] = jnp.where(asked, ranks[:device_count, :], -1.0)
        asked_locals[...] = (asked_ids - me * group_rows + 1).astype(jnp.float32)

        @pl.loop(0, device_count)
        def _(device):
            here = pl.ds(device, 1)
            rank_at = lax.broadcasted_iota(jnp.int32, (cap, slot_count), 0).astype(jnp.float32)
            rows = jnp.sum(
                jnp.where(rank_at == asked_ranks[here, :], asked_locals[here, :], 0.0),
                axis=1,
                keepdims=True,
            )
            rows_ref[piece_rows(device), :] = rows.astype(jnp.int32) - 1

        tile = 512
        for begin in range(0, device_count * cap, tile):
            row_at = lax.broadcasted_iota(jnp.int32, (tile, group_rows), 1)
            chosen = jnp.where(row_at == rows_ref[begin : begin + tile, :], 1.0, 0.0)
            outgoing_ref[begin : begin + tile, :] = plain_dot(
                chosen.astype(jnp.bfloat16), table_ref[...]
            ).astype(jnp.bfloat16)
        incoming_ref[piece_rows(me), :] = outgoing_ref[piece_rows(me), :]

    def text_steps(begin, end):
        @pl.loop(begin, end)
        def _(step):
            lanes = pl.ds(pl.multiple_of(step * TEXT_TILE, TEXT_TILE), TEXT_TILE)
            row = pl.ds(step // row_tiles, 1)
            start = lax.rem(step, row_tiles) * TEXT_TILE
            id_lanes = pl.ds(pl.multiple_of(start, TEXT_TILE), TEXT_TILE)
            ids = ids_ref[row, id_lanes]
            chosen = band_onehot(ids, text_rows)
            band = jnp.where(mask_ref[row, id_lanes] > 0, ids // text_rows, -1)
            cot = cot_ref[:, lanes].astype(jnp.float32)
            banded = jnp.concatenate(
                [jnp.where(band == b, cot, 0.0).astype(jnp.bfloat16) for b in range(BANDS)], axis=0
            )
            text_total[...] += dot_nt(chosen, banded)

    text_tiles = ids_ref.shape[0] * row_tiles
    body_begin()
    proj_begin()
    text_steps(0, 1)
    body_arrive(1)
    build_pieces()
    send_pieces(0, 6)
    text_steps(1, 4)
    body_relay(0)
    body_arrive(2)
    send_pieces(6, 12)
    text_steps(4, 8)
    body_arrive(3)
    body_relay(1)
    body_finish(0)
    send_pieces(12, 16)
    text_steps(8, 12)
    body_relay(2)
    body_finish(1)
    send_pieces(16, 20)
    text_steps(12, 16)
    bias_total = jnp.zeros((1, features), jnp.float32)
    blocks = own_grad_ref.shape[0] // BANDS
    for b in range(BANDS):
        rounded = text_total[:, b * features : (b + 1) * features].astype(jnp.bfloat16)
        own_grad_ref[b * blocks : (b + 1) * blocks] = rounded.reshape(
            (blocks,) + own_grad_ref.shape[1:]
        )
        bias_total = bias_total + over_rows(rounded.astype(jnp.float32))
    dz_begin()
    body_relay(3)
    body_finish(2)
    send_pieces(20, 24)
    dz_first(0)
    dz_first(1)
    send_pieces(24, 28)
    body_finish(3)
    dz_second(0)
    send_pieces(28, 31)
    dz_second(1)
    dz_deep(0)
    dz_deep(1)
    body_settled()
    for copy in piece_copies:
        copy.wait()
    def weight_rows(begin, size, plane_at=None):
        rows = slice(begin, begin + size)
        if plane_at is None:
            return packed[:, :, rows, :].reshape(PLANES * wide_count * size, D)
        return packed[plane_at, :, rows, :].reshape(wide_count * size, D)

    qkv_at, out_at, up_at, down_at = 0, 48, 64, 128
    spot_count = incoming_ref.shape[0]
    gain_one, shift_one = param_ref[9:10, :], param_ref[10:11, :]
    gain_two, shift_two = param_ref[11:12, :], param_ref[12:13, :]
    gain_end, shift_end = param_ref[13:14, :], param_ref[14:15, :]

    def slot_rows(slot):
        return pl.ds(pl.multiple_of(slot * entries, entries), entries)

    def piece_lanes(slot):
        return pl.ds(pl.multiple_of((slot - 1) * entries, entries), entries)

    @pl.loop(1, SLOTS)
    def _(slot):
        places = lax.broadcasted_iota(jnp.int32, (spot_count, entries), 0)
        chosen = jnp.where(places == spots_ref[pl.ds(slot, 1), :], 1.0, 0.0).astype(jnp.bfloat16)
        onehot[:, piece_lanes(slot)] = chosen

    bounds = (0, 4 * entries, PSLOTS * entries)
    for begin, end in zip(bounds[:-1], bounds[1:]):
        hats[entries + begin : entries + end, :] = dot_tn(onehot[:, begin:end], incoming_ref[...])

    first_row = param_ref[0:1, :] + param_ref[1:2, :]
    hats[0:entries, :] = jnp.broadcast_to(param_ref[0:1, :], (entries, D))
    sums[...] = jnp.zeros_like(sums)

    @pl.loop(0, SLOTS)
    def _(slot):
        rows = slot_rows(slot)
        hat, scale = normalize(hats[rows, :] + param_ref[pl.ds(1 + slot, 1), :])
        hats[rows, :] = hat
        scales[rows, :] = jnp.broadcast_to(scale, (entries, 128))
        part = (hat * gain_one + shift_one).astype(jnp.bfloat16)
        normed[rows, :] = part

    wholes = SLOTS * entries
    tall = wholes // 2
    for begin in range(0, wholes, tall):
        rows = slice(begin, begin + tall)
        keys[rows, :] = dot_nt(normed[rows, :], weight_rows(qkv_at, 48)[D:, :])

    query = dot_nt(normed[0:entries, :], weight_rows(qkv_at, 48)[0:D, :])
    lane_head = lax.broadcasted_iota(jnp.int32, (D, 128), 0) // HDIM
    to_heads = jnp.where(
        lane_head == lax.broadcasted_iota(jnp.int32, (D, 128), 1), 1.0, 0.0
    ).astype(jnp.bfloat16)
    head_lane = lax.broadcasted_iota(jnp.int32, (128, D), 1) // HDIM
    from_heads = jnp.where(
        head_lane == lax.broadcasted_iota(jnp.int32, (128, D), 0), 1.0, 0.0
    ).astype(jnp.bfloat16)
    root = 1.0 / math.sqrt(HDIM)
    for slot in range(SLOTS):
        rows = slice(slot * entries, (slot + 1) * entries)
        grad_normed[rows, :] = query * keys[rows, 0:D]
    for begin in range(0, wholes, tall):
        rows = slice(begin, begin + tall)
        probs[rows, :] = two_part_dot(grad_normed[rows, :], to_heads) * root
    live = jnp.concatenate(
        [live_ref[...].astype(jnp.float32), jnp.zeros((1, entries), jnp.float32)], axis=0
    ).T
    scores = []
    for slot in range(SLOTS):
        value = probs[slot * entries : (slot + 1) * entries, :]
        if slot > 0:
            value = jnp.where(live[:, slot - 1 : slot] > 0, value, -1e30)
        scores.append(value)
    top = scores[0]
    for value in scores[1:]:
        top = jnp.maximum(top, value)
    scores = [jnp.exp(value - top) for value in scores]
    whole = scores[0]
    for value in scores[1:]:
        whole = whole + value
    for slot in range(SLOTS):
        probs[slot * entries : (slot + 1) * entries, :] = scores[slot] / whole
    for begin in range(0, wholes, tall):
        rows = slice(begin, begin + tall)
        grad_normed[rows, :] = two_part_dot(probs[rows, :], from_heads)
    attended = jnp.zeros((entries, D), jnp.float32)
    for slot in range(SLOTS):
        rows = slice(slot * entries, (slot + 1) * entries)
        attended = attended + grad_normed[rows, :] * keys[rows, D:]
    attended_bf = attended.astype(jnp.bfloat16)
    residual = first_row + dot_nt(attended_bf, weight_rows(out_at, 16))
    hat_two, scale_two = normalize(residual)
    normed_two = (hat_two * gain_two + shift_two).astype(jnp.bfloat16)
    span = 512
    second = residual + param_ref[19:20, :]
    for begin in range(0, FF, span):
        lanes = slice(begin, begin + span)
        bias = param_ref[15 + begin // span : 16 + begin // span, :]
        gate = dot_nt(normed_two, weight_rows(up_at, 64, begin // span)) + bias
        square = gate * gate
        bend = jnp.tanh(math.sqrt(2.0 / math.pi) * (gate + 0.044715 * square * gate))
        part = (0.5 * gate * (1.0 + bend)).astype(jnp.bfloat16)
        active[:, lanes] = part
        slope[:, lanes] = 0.5 * (1.0 + bend) + 0.5 * gate * (1.0 - bend * bend) * (
            math.sqrt(2.0 / math.pi) * (1.0 + 3.0 * 0.044715 * square)
        )
        second = second + plain_dot(part, weight_rows(down_at, 64, begin // span))
    hat_end, scale_end = normalize(second)
    z_ref[...] = (hat_end * gain_end + shift_end).astype(jnp.bfloat16)

    z_begin()
    own_z = pltpu.make_async_copy(z_ref, every_ref.at[plane, wide_at], local_sem.at[5])
    own_z.start()
    z_arrive(1)
    grad_z = jnp.concatenate([dz_total(part) for part in range(entries // CHUNK)], axis=0)
    for copy in near_copies:
        copy.wait_send()
    dz_settled()

    @pl.when(holds_proj)
    def _():
        for k in range(PLANES - 1):
            proj_copy(k).wait_send()

    vec_ref[...] = jnp.zeros_like(vec_ref)
    vec_ref[13:14, :] = over_rows(grad_z * hat_end)
    vec_ref[14:15, :] = over_rows(grad_z)
    grad_second = normalize_back(grad_z, gain_end, hat_end, scale_end)
    branch_two = grad_second.astype(jnp.bfloat16)
    vec_ref[19:20, :] = over_rows(branch_two.astype(jnp.float32))
    tile_lanes = D // features
    vec_ref[pl.ds(20 + me // tile_lanes, 1), :] = jnp.concatenate(
        [jnp.where(lax.rem(me, tile_lanes) == k, bias_total, 0.0) for k in range(tile_lanes)],
        axis=1,
    )

    def store(value, block, chunk, height, offset):
        for chip_at in range(CHIPS):
            for core_at in range(CORES):
                top = (chip_at * CORES + core_at) * height
                y, x = divmod(chip_at, SIDE)
                main_ref[core_at, chunk, y, x, block, offset : offset + height, :] = value[
                    top : top + height, :
                ].astype(jnp.bfloat16)

    z_relay(0)
    z_arrive(2)
    grad_two = jnp.zeros((entries, D), jnp.float32)
    for block in range(PLANES):
        lanes = slice(block * span, (block + 1) * span)
        store(dot_tn(active[:, lanes], branch_two), block, 0, 64, 0)
        gate_grad = (dot_nt(branch_two, weight_rows(down_at, 64, block)) * slope[:, lanes]).astype(jnp.bfloat16)
        vec_ref[15 + block : 16 + block, :] = over_rows(gate_grad.astype(jnp.float32))
        store(dot_tn(gate_grad, normed_two), block, 1, 64, 0)
        grad_two = grad_two + plain_dot(gate_grad, weight_rows(up_at, 64, block))
    main_begin(0)
    main_begin(1)
    z_relay(1)
    z_arrive(3)
    vec_ref[11:12, :] = over_rows(grad_two * hat_two)
    vec_ref[12:13, :] = over_rows(grad_two)
    grad_residual = grad_second + normalize_back(grad_two, gain_two, hat_two, scale_two)
    branch_one = grad_residual.astype(jnp.bfloat16)
    grad_out = dot_tn(branch_one, attended_bf)
    for block in range(PLANES):
        store(grad_out[block * 128 : (block + 1) * 128, :], block, 2, 16, 0)
    grad_attended = plain_dot(branch_one, weight_rows(out_at, 16))
    main_first(0)
    main_first(1)
    z_finish(0)
    z_relay(2)
    halves_of = entries // CHUNK

    def store_kv(kind, slot, value):
        y, x = divmod(slot // 2, SIDE)
        begin = slot % 2 * halves_of
        grad_kv[kind, y, x, begin : begin + halves_of] = value.astype(jnp.bfloat16).reshape(
            halves_of, CHUNK, D
        )


    for slot in range(SLOTS):
        rows = slice(slot * entries, (slot + 1) * entries)
        store_kv(1, slot, grad_normed[rows, :] * grad_attended)
        grad_normed[rows, :] = grad_attended * keys[rows, D:]
    for begin in range(0, wholes, tall):
        rows = slice(begin, begin + tall)
        slides[rows, :] = two_part_dot(grad_normed[rows, :], to_heads)
    inner = jnp.zeros((entries, 128), jnp.float32)
    for slot in range(SLOTS):
        rows = slice(slot * entries, (slot + 1) * entries)
        inner = inner + probs[rows, :] * slides[rows, :]
    for slot in range(SLOTS):
        rows = slice(slot * entries, (slot + 1) * entries)
        slides[rows, :] = probs[rows, :] * (slides[rows, :] - inner)
    for begin in range(0, wholes, tall):
        rows = slice(begin, begin + tall)
        grad_normed[rows, :] = two_part_dot(slides[rows, :], from_heads) * root
    grad_query = jnp.zeros((entries, D), jnp.float32)
    for slot in range(SLOTS):
        rows = slice(slot * entries, (slot + 1) * entries)
        push = grad_normed[rows, :]
        grad_query = grad_query + push * keys[rows, 0:D]
        store_kv(0, slot, push * query)
    z_finish(1)
    z_relay(3)
    query_bf = grad_query.astype(jnp.bfloat16)

    grad_q = dot_tn(query_bf, normed[0:entries, :])
    grad_keys = grad_kv[0].reshape(wholes, D)
    grad_values = grad_kv[1].reshape(wholes, D)
    grad_k = dot_tn(grad_keys, normed[...])
    grad_v = dot_tn(grad_values, normed[...])
    third = D * 3 // PLANES
    every = jnp.concatenate([grad_q, grad_k, grad_v], axis=0)
    for block in range(PLANES):
        store(every[block * third : (block + 1) * third, :], block, 2, 48, 16)

    main_begin(2)
    main_then(0)
    for begin in range(0, wholes, tall):
        rows = slice(begin, begin + tall)
        grad_normed[rows, :] = plain_dot(
            grad_keys[rows, :], weight_rows(qkv_at, 48)[D : 2 * D, :]
        ) + plain_dot(grad_values[rows, :], weight_rows(qkv_at, 48)[2 * D :, :])

    grad_normed[0:entries, :] += plain_dot(query_bf, weight_rows(qkv_at, 48)[0:D, :])

    @pl.loop(0, SLOTS)
    def _(slot):
        rows = slot_rows(slot)
        grad = grad_normed[rows, :]
        hat = hats[rows, :]
        sums[0:1, :] += over_rows(grad * hat)
        sums[1:2, :] += over_rows(grad)
        grad_x = normalize_back(grad, gain_one, hat, scales[rows, 0:1])
        vec_ref[pl.ds(1 + slot, 1), :] = over_rows(grad_x)

        @pl.when(slot > 0)
        def _():
            grad_pieces[pl.ds(pl.multiple_of((slot - 1) * entries, entries), entries), :] = (
                grad_x.astype(jnp.bfloat16)
            )

    main_first(2)
    z_finish(2)
    z_finish(3)
    main_then(1)
    vec_ref[9:11, :] = sums[0:2, :]
    vec_ref[1:2, :] += over_rows(grad_residual)
    vec_ref[0:1, :] = vec_ref[1:2, :]
    tile = 256
    for begin in range(0, spot_count, tile):
        outgoing_ref[begin : begin + tile, :] = plain_dot(
            onehot[begin : begin + tile, :], grad_pieces[...]
        ).astype(jnp.bfloat16)
    main_last(0)
    main_then(2)
    main_last(1)
    main_last(2)
    for chunk in range(CHUNKS):
        part_ref[chunk * CHUNK : (chunk + 1) * CHUNK, :] = main_total(chunk).astype(jnp.bfloat16)
    own_z.wait()
    z_settled()
    main_settled()
    for chunk in range(CHUNKS):
        main_copies[chunk].wait_send()


def layer(master, pieces, table, text_ids, text_mask, text_cot, slot_mask, params, cap):
    f32, bf = jnp.float32, jnp.bfloat16
    dma = pltpu.SemaphoreType.DMA
    count = PLANES * CHIPS * CORES
    entries = slot_mask.shape[1]
    features = text_cot.shape[0]
    rows = entries * SLOTS
    hbm = pl.BlockSpec(memory_space=pl.ANY)
    vmem = pl.BlockSpec(memory_space=pltpu.VMEM)
    spread_count = 6 + 9 * PLANES
    return pl.pallas_call(
        layer_kernel,
        out_shape=(
            jax.ShapeDtypeStruct((PLANES, CHIPS * CORES, entries, D), bf),
            jax.ShapeDtypeStruct((MAIN, D), bf),
            jax.ShapeDtypeStruct((count * cap, D), bf),
            jax.ShapeDtypeStruct((CORES * VROWS, D), f32),
            jax.ShapeDtypeStruct((count, entries, features), bf),
            jax.ShapeDtypeStruct((features, D), bf),
            jax.ShapeDtypeStruct((count * cap, 1), jnp.int32),
        ),
        in_specs=[hbm] + [vmem] * 7,
        out_specs=(hbm,) + (vmem,) * 6,
        scratch_shapes=[
            pltpu.VMEM((CORES, CHUNKS, SIDE, SIDE, PLANES, CHUNK, D), bf),
            pltpu.VMEM((MAIN, D), f32),
            pltpu.VMEM((count, SLOTS, entries), jnp.int32),
            pltpu.VMEM((SLOTS, entries), jnp.int32),
            pltpu.VMEM((count, entries * PSLOTS), f32),
            pltpu.VMEM((count, entries * PSLOTS), f32),
            pltpu.VMEM((count * cap, D), bf),
            pltpu.VMEM((PLANES * features, D), f32),
            pltpu.VMEM((PLANES, features, D), bf),
            pltpu.VMEM((entries, D), bf),
            pltpu.VMEM((PLANES, CHIPS * CORES, MAIN, D), bf),
            pltpu.VMEM((count * entries // BANDS, BANDS * features), f32),
            pltpu.VMEM((count * cap, entries * PSLOTS), bf),
            pltpu.VMEM((rows, D), f32),
            pltpu.VMEM((rows, 128), f32),
            pltpu.VMEM((rows, D), bf),
            pltpu.VMEM((rows, 2 * D), f32),
            pltpu.VMEM((rows, 128), f32),
            pltpu.VMEM((2, SIDE, SIDE, PLANES, CHUNK, D), bf),
            pltpu.VMEM((rows, D), f32),
            pltpu.VMEM((entries * PSLOTS, D), bf),
            pltpu.VMEM((entries, FF), bf),
            pltpu.VMEM((entries, FF), f32),
            pltpu.VMEM((rows, 128), f32),
            pltpu.VMEM((8, D), f32),
            dma((6,)),
        ]
        + sum_scratch(entries // CHUNK)
        + [dma((count - 1,))] * 4
        + [dma((entries // CHUNK,))] * 2
        + [pltpu.VMEM((CHUNKS, SIDE, SIDE, PLANES, CHUNK, D), bf)]
        + sum_scratch(CHUNKS)
        + [dma((CHUNKS,))] * 2
        + [dma((spread_count,))] * 2
        + [dma((PLANES - 1,))] * 2
        + [dma((spread_count,))] * 2,
        compiler_params=pltpu.CompilerParams(
            collective_id=5, has_side_effects=True, vmem_limit_bytes=63 * 2**20
        ),
        name="layer",
    )(master, pieces, table, text_ids, text_mask, text_cot, slot_mask, params)


def piece_grad_kernel(rows_ref, grads_ref, out_ref):
    tile = out_ref.shape[0]
    at = lax.broadcasted_iota(jnp.int32, (tile, rows_ref.shape[1]), 0) + pl.program_id(0) * tile
    chosen = jnp.where(at == rows_ref[...], 1.0, 0.0).astype(jnp.bfloat16)
    out_ref[...] = plain_dot(chosen, grads_ref[...])


def add_piece_grads(rows, grads, group_rows):
    tile = 256
    return pl.pallas_call(
        piece_grad_kernel,
        grid=(group_rows // tile,),
        out_shape=jax.ShapeDtypeStruct((group_rows, D), jnp.float32),
        in_specs=[
            pl.BlockSpec(rows.shape, lambda i: (0, 0)),
            pl.BlockSpec(grads.shape, lambda i: (0, 0)),
        ],
        out_specs=pl.BlockSpec((tile, D), lambda i: (i, 0)),
        compiler_params=pltpu.CompilerParams(vmem_limit_bytes=24 * 2**20),
        name="add_piece_grads",
    )(rows, grads)


def on_device(
    piece_table,
    piece_ids,
    slot_mask,
    text_ids,
    text_mask,
    text_cot,
    mat_master,
    mat_momentum,
    mat_ema,
    vec_master,
    vec_moment1,
    vec_moment2,
    vec_ema,
):
    me = lax.axis_index("wide") * PLANES + lax.axis_index("narrow")
    entries = piece_ids.shape[0]
    group_rows = piece_table.shape[0]
    cap = piece_cap(group_rows)
    feature_rows = text_cot.shape[0]
    params = vec_master.reshape(-1, D)
    pieces = piece_ids.T
    (
        every,
        part,
        grad_outgoing,
        vec_rows,
        grad_own,
        proj_own,
        asked_rows,
    ) = layer(
        mat_master[0], pieces, piece_table, text_ids, text_mask, text_cot, slot_mask.T, params, cap
    )
    bias_out = vec_master[vec_master.shape[0] - OUTW :]
    bias_own = lax.dynamic_slice_in_dim(bias_out, me * feature_rows, feature_rows, 0)
    text_embeds, main_sum, proj_sum, vec_sum, rows, grad_incoming = settle(
        every,
        part,
        vec_rows.reshape(CORES, VROWS, D),
        grad_own,
        proj_own,
        bias_own[:, None],
        mat_momentum[0],
        text_ids,
        text_mask,
        grad_outgoing,
    )
    vec_grad = vec_sum.reshape(-1)[: vec_master.shape[0]]
    grad_block, momentum_block, weight_block, ema_block = finish(
        main_sum, proj_sum, rows, mat_momentum, mat_master, mat_ema
    )
    piece_grad = add_piece_grads(asked_rows.reshape(1, -1), grad_incoming, group_rows)
    return (
        text_embeds,
        piece_grad,
        grad_block,
        momentum_block,
        weight_block,
        ema_block,
    ) + adam(vec_grad, vec_master, vec_moment1, vec_moment2, vec_ema)


def solution(mesh):
    in_specs = (
        P(("wide", "narrow"), None),
        P(("wide", "narrow"), None),
        P(("wide", "narrow"), None),
        P(),
        P(),
        P(("wide", "narrow"), None),
        P("narrow", None, None),
        P("narrow", None, None),
        P("narrow", None, None),
        P(),
        P(),
        P(),
        P(),
    )
    out_specs = (
        P(("wide", "narrow"), None),
        P(("wide", "narrow"), None),
        P("narrow", None, None),
        P("narrow", None, None),
        P("narrow", None, None),
        P("narrow", None, None),
        P(),
        P(),
        P(),
        P(),
        P(),
    )
    fits = mesh.shape["wide"] == CHIPS * CORES and mesh.shape["narrow"] == PLANES
    step = on_device if fits else on_device_plain
    return jax.shard_map(
        step, mesh=mesh, in_specs=in_specs, out_specs=out_specs, check_vma=False
    )
```

```python
from functools import partial
import math

import jax
import jax.numpy as jnp
from jax import lax
from jax.experimental import pallas as pl
from jax.experimental.pallas import tpu as pltpu
from jax.sharding import PartitionSpec as P

D = 512
HEADS = 8
HDIM = 64
FF = 2048
OUTW = 4096
SLOTS = 8
PSLOTS = 7
STEP = 10


HIGHEST = lax.Precision.HIGHEST
HIGH = lax.Precision.HIGH
MUON_RATE = 0.5
MUON_DECAY = 0.01
MUON_BETA = 0.95
ADAM_RATE = 0.5
ADAM_BETA1 = 0.9
ADAM_BETA2 = 0.95
ADAM_EPSILON = 1e-08
EMA_DECAY = 0.8
NEWTON_A = 3.4445
NEWTON_B = -4.775
NEWTON_C = 2.0315


def matrix_rows():
    return (3 * D, D, FF, FF, OUTW)


def unpack(packed, narrow_count):
    matrices = []
    offset = 0
    for row_total in matrix_rows():
        height = row_total // narrow_count
        matrices.append(packed[:, offset : offset + height, :].reshape(row_total, packed.shape[2]))
        offset = offset + height
    return matrices


def pack(matrices, narrow_count):
    return jnp.concatenate(
        [
            matrix.reshape(narrow_count, matrix.shape[0] // narrow_count, matrix.shape[1])
            for matrix in matrices
        ],
        axis=1,
    )


def block_slices(block, narrow_count):
    segments = []
    offset = 0
    for row_total in matrix_rows():
        height = row_total // narrow_count
        segments.append(block[offset : offset + height])
        offset = offset + height
    return segments


def split_vectors(vector):
    lengths = (D, SLOTS * D, D, D, D, D, D, D, FF, D, OUTW)
    chosen = []
    offset = 0
    for length in lengths:
        chosen.append(vector[offset : offset + length])
        offset = offset + length
    chosen[1] = chosen[1].reshape(SLOTS, D)
    return chosen


def layer_norm(values, gain, shift):
    center = values - jnp.mean(values, axis=-1, keepdims=True)
    spread = jnp.mean(center * center, axis=-1, keepdims=True)
    return center * lax.rsqrt(spread + 1e-05) * gain + shift


def gelu_tanh(values):
    return jax.nn.gelu(values, approximate=True)


def attend(query_rows, key_rows, value_rows, live_slots):
    entry_count = query_rows.shape[0]
    query_heads = query_rows.reshape(entry_count, HEADS, HDIM)
    key_heads = key_rows.reshape(entry_count, SLOTS, HEADS, HDIM)
    value_heads = value_rows.reshape(entry_count, SLOTS, HEADS, HDIM)
    scores = jnp.einsum("ehd,eshd->ehs", query_heads, key_heads, precision=HIGHEST) / math.sqrt(
        HDIM
    )
    scores = jnp.where(live_slots[:, None, :], scores, -1e30)
    scores = scores - jnp.max(scores, axis=-1, keepdims=True)
    expped = jnp.exp(scores)
    probabilities = expped / jnp.sum(expped, axis=-1, keepdims=True)
    mixed_heads = jnp.einsum("ehs,eshd->ehd", probabilities, value_heads, precision=HIGHEST)
    return mixed_heads.reshape(entry_count, D)


PIECE_CAPS = {1024: 58, 256: 16}
BOTH = ("wide", "narrow")


def piece_cap(group_rows):
    cap = PIECE_CAPS.get(group_rows, group_rows)
    return -(-cap // 16) * 16


def contract_rows(left, right):
    return lax.dot_general(
        left, right, (((0,), (0,)), ((), ())), preferred_element_type=jnp.float32
    )


def gram_of(block):
    return lax.dot_general(block, block, (((0,), (0,)), ((), ())), precision=HIGHEST)


def adam(vec_grad, vec_master, vec_moment1, vec_moment2, vec_ema):
    moment_one = ADAM_BETA1 * vec_moment1 + (1.0 - ADAM_BETA1) * vec_grad
    moment_two = ADAM_BETA2 * vec_moment2 + (1.0 - ADAM_BETA2) * vec_grad * vec_grad
    corrected_one = moment_one / (1.0 - ADAM_BETA1**STEP)
    corrected_two = moment_two / (1.0 - ADAM_BETA2**STEP)
    vec_weight = vec_master - ADAM_RATE * corrected_one / (jnp.sqrt(corrected_two) + ADAM_EPSILON)
    vec_ema_new = EMA_DECAY * vec_ema + (1.0 - EMA_DECAY) * vec_weight
    return vec_grad, moment_one, moment_two, vec_weight, vec_ema_new


def on_device_plain(
    piece_table,
    piece_ids,
    slot_mask,
    text_ids,
    text_mask,
    text_cot,
    mat_master,
    mat_momentum,
    mat_ema,
    vec_master,
    vec_moment1,
    vec_moment2,
    vec_ema,
):
    narrow_count = lax.axis_size("narrow")
    wide_count = lax.axis_size("wide")
    device_count = narrow_count * wide_count
    wide_at = lax.axis_index("wide")
    narrow_at = lax.axis_index("narrow")
    me = wide_at * narrow_count + narrow_at
    block_rows = mat_master.shape[1]
    own_rows = block_rows // wide_count
    own_part = lax.dynamic_slice_in_dim(mat_master[0], wide_at * own_rows, own_rows, 0)
    packed_bf = lax.all_gather(
        own_part.astype(jnp.bfloat16), ("narrow", "wide"), axis=0, tiled=True
    ).reshape(narrow_count, block_rows, D)
    w_qkv, w_out, w_up, w_down, w_proj = unpack(packed_bf, narrow_count)
    (
        cls_vec,
        positions,
        ln1_gain,
        ln1_shift,
        ln2_gain,
        ln2_shift,
        final_gain,
        final_shift,
        bias_up,
        bias_down,
        bias_out,
    ) = split_vectors(vec_master)
    entries = piece_ids.shape[0]
    slot_ids = piece_ids.reshape(-1)
    slot_count = slot_ids.shape[0]
    group_rows = piece_table.shape[0]
    cap = piece_cap(group_rows)
    every_ids = lax.all_gather(slot_ids, BOTH, axis=0, tiled=False)
    asked = every_ids // group_rows == me
    before = (
        lax.broadcasted_iota(jnp.int32, (slot_count, slot_count), 0)
        < lax.broadcasted_iota(jnp.int32, (slot_count, slot_count), 1)
    )
    asked_rank = jnp.dot(
        asked.astype(jnp.bfloat16), before.astype(jnp.bfloat16), preferred_element_type=jnp.float32
    ).astype(jnp.int32)
    asked_rank = jnp.where(asked, asked_rank, -1)
    chosen = asked_rank[:, None, :] == lax.iota(jnp.int32, cap)[None, :, None]
    local_ids = every_ids - me * group_rows + 1
    asked_rows = jnp.sum(jnp.where(chosen, local_ids[:, None, :], 0), axis=2).reshape(-1) - 1
    asked_onehot = (
        asked_rows[:, None] == lax.iota(jnp.int32, group_rows)[None, :]
    ).astype(jnp.bfloat16)
    outgoing = jnp.dot(asked_onehot, piece_table, preferred_element_type=jnp.float32)
    incoming = lax.all_to_all(
        outgoing.astype(jnp.bfloat16).reshape(device_count, cap, D), BOTH, 0, 0, tiled=True
    ).reshape(device_count * cap, D)
    own_group = slot_ids // group_rows
    same = (own_group[:, None] == own_group[None, :]) & before.T
    own_rank = jnp.sum(same.astype(jnp.int32), axis=1)
    own_spot = own_group * cap + own_rank
    own_onehot = (
        own_spot[:, None] == lax.iota(jnp.int32, device_count * cap)[None, :]
    ).astype(jnp.bfloat16)
    looked = jnp.dot(own_onehot, incoming, preferred_element_type=jnp.float32)
    pieces = looked.reshape(entries, PSLOTS, D)

    flat_ids = text_ids.reshape(-1)
    flat_mask = text_mask.reshape(-1)
    token_count = flat_ids.shape[0]
    feature_rows = text_cot.shape[0]
    all_entries = entries * device_count
    block_len = min(512, token_count)
    entry_index = lax.iota(jnp.int32, all_entries)

    def text_block(step_index, grad_cols):
        begin_at = step_index * block_len
        ids_now = lax.dynamic_slice_in_dim(flat_ids, begin_at, block_len)
        keep_mask = lax.dynamic_slice_in_dim(flat_mask, begin_at, block_len)
        onehot = (entry_index[:, None] == ids_now[None, :]).astype(jnp.bfloat16)
        cot_now = lax.dynamic_slice_in_dim(text_cot, begin_at, block_len, 1)
        masked_cot = jnp.where(keep_mask[None, :] > 0, cot_now, jnp.zeros_like(cot_now))
        return grad_cols + lax.dot_general(
            masked_cot, onehot, (((1,), (1,)), ((), ())), preferred_element_type=jnp.float32
        )

    grad_cols = lax.fori_loop(
        0, token_count // block_len, text_block, jnp.zeros((feature_rows, all_entries), jnp.float32)
    )
    grad_table_cols = grad_cols.astype(jnp.bfloat16)
    grad_table = lax.all_to_all(grad_table_cols, BOTH, split_axis=1, concat_axis=0, tiled=True)
    grad_bias_own = jnp.sum(grad_table_cols.astype(jnp.float32), axis=1)
    grad_normed_three = contract_rows(grad_table, w_proj)

    first_slot = jnp.broadcast_to(cls_vec + positions[0], (entries, 1, D))
    slots_x = jnp.concatenate([first_slot, pieces + positions[1:]], axis=1)
    live_slots = jnp.concatenate([jnp.ones((entries, 1), jnp.int32), slot_mask], axis=1) > 0
    normed, norm1_pull = jax.vjp(layer_norm, slots_x, ln1_gain, ln1_shift)
    normed_bf = normed.astype(jnp.bfloat16)
    query_rows = jnp.einsum(
        "ed,fd->ef", normed_bf[:, 0], w_qkv[:D], preferred_element_type=jnp.float32
    )
    key_value = jnp.einsum("esd,fd->esf", normed_bf, w_qkv[D:], preferred_element_type=jnp.float32)
    attended, attend_pull = jax.vjp(
        partial(attend, live_slots=live_slots), query_rows, key_value[:, :, :D], key_value[:, :, D:]
    )
    attended_bf = attended.astype(jnp.bfloat16)
    residual = slots_x[:, 0] + jnp.einsum(
        "ed,fd->ef", attended_bf, w_out, preferred_element_type=jnp.float32
    )
    normed_two, norm2_pull = jax.vjp(layer_norm, residual, ln2_gain, ln2_shift)
    normed_two_bf = normed_two.astype(jnp.bfloat16)
    gate_in = (
        jnp.einsum("ed,fd->ef", normed_two_bf, w_up, preferred_element_type=jnp.float32) + bias_up
    )
    active, gelu_pull = jax.vjp(gelu_tanh, gate_in)
    active_bf = active.astype(jnp.bfloat16)
    second_residual = residual + (
        jnp.dot(active_bf, w_down, preferred_element_type=jnp.float32) + bias_down
    )
    normed_three, norm3_pull = jax.vjp(layer_norm, second_residual, final_gain, final_shift)
    normed_three_bf = normed_three.astype(jnp.bfloat16)
    every_normed = lax.all_gather(normed_three_bf, BOTH, axis=0, tiled=True)
    proj_own = lax.dynamic_slice_in_dim(w_proj, me * feature_rows, feature_rows, 0)
    bias_own = lax.dynamic_slice_in_dim(bias_out, me * feature_rows, feature_rows, 0)
    table_cols = (
        jnp.einsum("fd,ed->fe", proj_own, every_normed, preferred_element_type=jnp.float32)
        + bias_own[:, None]
    )
    text_embeds = jnp.take(table_cols, flat_ids, axis=1) * flat_mask[None, :].astype(jnp.float32)
    grad_proj_own = jnp.dot(grad_table_cols, every_normed, preferred_element_type=jnp.float32)

    grad_second, grad_final_gain, grad_final_shift = norm3_pull(grad_normed_three)
    grad_branch_two = grad_second.astype(jnp.bfloat16)
    grad_bias_down = jnp.sum(grad_branch_two.astype(jnp.float32), axis=0)
    grad_down = contract_rows(active_bf, grad_branch_two)
    grad_active = jnp.einsum(
        "ed,fd->ef", grad_branch_two, w_down, preferred_element_type=jnp.float32
    )
    (grad_gate,) = gelu_pull(grad_active)
    grad_gate_bf = grad_gate.astype(jnp.bfloat16)
    grad_bias_up = jnp.sum(grad_gate_bf.astype(jnp.float32), axis=0)
    grad_up = contract_rows(grad_gate_bf, normed_two_bf)
    grad_normed_two = jnp.dot(grad_gate_bf, w_up, preferred_element_type=jnp.float32)
    grad_residual_norm, grad_ln2_gain, grad_ln2_shift = norm2_pull(grad_normed_two)
    grad_residual = grad_second + grad_residual_norm
    grad_branch_one = grad_residual.astype(jnp.bfloat16)
    grad_out_w = contract_rows(grad_branch_one, attended_bf)
    grad_attended = jnp.dot(grad_branch_one, w_out, preferred_element_type=jnp.float32)
    grad_query, grad_keys, grad_values = attend_pull(grad_attended)
    grad_query_bf = grad_query.astype(jnp.bfloat16)
    grad_kv = jnp.concatenate(
        [grad_keys.astype(jnp.bfloat16), grad_values.astype(jnp.bfloat16)], axis=2
    )
    grad_q_w = contract_rows(grad_query_bf, normed_bf[:, 0])
    grad_kv_w = jnp.einsum("esf,esd->fd", grad_kv, normed_bf, preferred_element_type=jnp.float32)
    grad_normed = jnp.einsum("esf,fd->esd", grad_kv, w_qkv[D:], preferred_element_type=jnp.float32)
    grad_normed = grad_normed.at[:, 0].add(
        jnp.dot(grad_query_bf, w_qkv[:D], preferred_element_type=jnp.float32)
    )
    grad_slots, grad_ln1_gain, grad_ln1_shift = norm1_pull(grad_normed)
    grad_first = grad_slots[:, 0] + grad_residual
    grad_cls = jnp.sum(grad_first, axis=0)
    grad_pos = jnp.concatenate([grad_cls[None], jnp.sum(grad_slots[:, 1:], axis=0)], axis=0)
    grad_pieces = grad_slots[:, 1:].astype(jnp.bfloat16).reshape(-1, D)
    grad_outgoing = contract_rows(own_onehot, grad_pieces).astype(jnp.bfloat16)
    grad_incoming = lax.all_to_all(
        grad_outgoing.reshape(device_count, cap, D), BOTH, 0, 0, tiled=True
    ).reshape(device_count * cap, D)
    piece_grad = contract_rows(asked_onehot, grad_incoming)

    vec_local = jnp.concatenate(
        [
            grad_cls,
            grad_pos.reshape(-1),
            grad_ln1_gain,
            grad_ln1_shift,
            grad_ln2_gain,
            grad_ln2_shift,
            grad_final_gain,
            grad_final_shift,
            grad_bias_up,
            grad_bias_down,
            lax.dynamic_update_slice_in_dim(
                jnp.zeros((OUTW,), jnp.float32), grad_bias_own, me * feature_rows, 0
            ),
        ]
    )
    vec_grad = lax.psum(vec_local, BOTH)
    grad_qkv = jnp.concatenate([grad_q_w, grad_kv_w], axis=0)
    packed_term = jnp.concatenate(
        [
            matrix.reshape(narrow_count, matrix.shape[0] // narrow_count, D)
            for matrix in (grad_qkv, grad_out_w, grad_up, grad_down)
        ],
        axis=1,
    )
    term_rows = packed_term.shape[1]
    share = term_rows // wide_count
    packed_term = (
        packed_term.astype(jnp.bfloat16)
        .reshape(narrow_count, wide_count, share, D)
        .transpose(1, 0, 2, 3)
        .reshape(device_count, share, D)
    )
    terms = lax.all_to_all(packed_term, BOTH, 0, 0, tiled=True)
    share_sum = jnp.sum(terms.astype(jnp.float32), axis=0)
    main_grad = lax.all_gather(share_sum.astype(jnp.bfloat16), "wide", axis=0, tiled=True)
    proj_grad = lax.all_gather(grad_proj_own.astype(jnp.bfloat16), BOTH, axis=0, tiled=True)
    proj_rows = OUTW // narrow_count
    proj_grad = lax.dynamic_slice_in_dim(proj_grad, narrow_at * proj_rows, proj_rows, 0)
    grad_block = jnp.concatenate([main_grad, proj_grad], axis=0).astype(jnp.float32)
    momentum_block = MUON_BETA * mat_momentum[0] + grad_block
    update_block = grad_block + MUON_BETA * momentum_block
    segments = block_slices(update_block, narrow_count)
    grams = lax.psum(jnp.stack([gram_of(segment) for segment in segments]), "narrow")
    new_segments = []
    for position, (row_total, master_seg, segment) in enumerate(
        zip(matrix_rows(), block_slices(mat_master[0], narrow_count), segments)
    ):
        square = jnp.sum(jnp.diagonal(grams[position]))
        norm = jnp.sqrt(square) + 1e-07
        gram = grams[position] / (norm * norm)
        chain = None
        for sweep_index in range(5):
            squared = jnp.dot(gram, gram, precision=HIGH)
            poly = NEWTON_B * gram + NEWTON_C * squared + NEWTON_A * jnp.eye(D, dtype=jnp.float32)
            chain = poly if chain is None else jnp.dot(chain, poly, precision=HIGH)
            if sweep_index < 4:
                gram = jnp.dot(jnp.dot(gram, poly, precision=HIGH), poly, precision=HIGH)
        ortho = jnp.dot(segment / norm, chain, precision=HIGH)
        new_segments.append(
            master_seg * (1.0 - MUON_RATE * MUON_DECAY)
            - MUON_RATE * math.sqrt(row_total / D) * ortho
        )
    weight_block = jnp.concatenate(new_segments, axis=0)[None]
    ema_block = EMA_DECAY * mat_ema + (1.0 - EMA_DECAY) * weight_block
    return (
        text_embeds,
        piece_grad,
        grad_block[None],
        momentum_block[None],
        weight_block,
        ema_block,
    ) + adam(vec_grad, vec_master, vec_moment1, vec_moment2, vec_ema)


MESH_ID = pl.DeviceIdType.MESH
CORES = 2
CHIPS = 4
PLANES = 4
MAIN = 192
CHUNKS = 3
CHUNK = MAIN // CHUNKS
PROJ = 32
PART = MAIN + PLANES * PROJ
VROWS = 16


def place():
    wide_at = lax.axis_index("wide")
    plane = lax.axis_index("narrow")
    chip = wide_at // CORES
    core = lax.rem(wide_at, CORES)
    return wide_at, plane, chip, core


def enter(targets):
    barrier = pltpu.get_barrier_semaphore()
    for target in targets:
        pl.semaphore_signal(barrier, inc=1, device_id=target, device_id_type=MESH_ID)
    pl.semaphore_wait(barrier, len(targets))


def neighbours(wide_at, plane, chip, core):
    sibling = (chip * CORES + 1 - core, plane)
    chips = [(lax.rem(chip + k, CHIPS) * CORES + core, plane) for k in range(1, CHIPS)]
    planes = [(wide_at, lax.rem(plane + k, PLANES)) for k in range(1, PLANES)]
    return sibling, chips, planes


def remote(src, dst, sems, index, target):
    return pltpu.make_async_remote_copy(
        src_ref=src,
        dst_ref=dst,
        send_sem=sems[0].at[index],
        recv_sem=sems[1].at[index],
        device_id=target,
        device_id_type=MESH_ID,
    )

OWNERS = (6, 7, 2, 4, 0)
BLOCK_TILES = (3, 1, 4, 4, 8)
MOST_TILES = max(BLOCK_TILES)
MAIN_TILES = 12
BANDS = 4
TEXT_TILE = 512
TILE = 128
SIDE = 2
STRIPS = 8
STRIP = D // STRIPS
PACKED = 640
PIECES = ((0, 64, 1024), (64, 64, 512), (128, 16, 384), (144, 48, 0))


def halves(value):
    high = value.astype(jnp.bfloat16)
    return high, (value - high.astype(jnp.float32)).astype(jnp.bfloat16)


def plain_dot(left, right):
    return jnp.dot(left, right, preferred_element_type=jnp.float32)


def split_dot(left, right):
    return plain_dot(left[0], right[0]) + (
        plain_dot(left[0], right[1]) + plain_dot(left[1], right[0])
    )


def dot_nt(left, right):
    return lax.dot_general(
        left, right, (((1,), (1,)), ((), ())), preferred_element_type=jnp.float32
    )


def dot_tn(left, right):
    return lax.dot_general(
        left, right, (((0,), (0,)), ((), ())), preferred_element_type=jnp.float32
    )


def band_onehot(ids, rows):
    place_in = lax.rem(ids, rows)
    spots = lax.broadcasted_iota(jnp.int32, (rows, ids.shape[1]), 0)
    return jnp.where(spots == place_in, 1.0, 0.0).astype(jnp.bfloat16)


def across(wide_at, plane, chip, core):
    x_at = lax.rem(chip, SIDE)
    x_chip = chip + 1 - 2 * x_at
    y_chip = lax.rem(chip + SIDE, CHIPS)
    return x_chip * CORES + core, y_chip * CORES + core


def owner_tiles(wide_at):
    tile_count = jnp.int32(0)
    tile_first = jnp.int32(0)
    begin = 0
    for owner, count in zip(OWNERS, BLOCK_TILES):
        tile_count = tile_count + jnp.where(wide_at == owner, count, 0)
        tile_first = tile_first + jnp.where(wide_at == owner, begin, 0)
        begin = begin + count
    return tile_count, tile_first


def spread_steps(own, held, sems, base, at):
    wide_at, plane, chip, core = at
    sibling = (chip * CORES + 1 - core, plane)
    x_wide, y_wide = across(wide_at, plane, chip, core)
    x_near, y_near = (x_wide, plane), (y_wide, plane)
    diagonal_wide = (CHIPS - 1 - chip) * CORES + core
    half = own.shape[0] // 2
    tops, bottoms = pl.ds(0, half), pl.ds(half, half)
    above, below = (wide_at, plane + 1), (wide_at, plane - 1)

    def climb(distance, source, src):
        spot = held.at[source, wide_at]
        return remote(spot if src is None else src, spot, sems, base + distance - 1, above)

    def sink(distance, source, src):
        spot = held.at[source, wide_at]
        return remote(spot if src is None else src, spot, sems, base + 2 + distance, below)

    def plane_copy(source, kind, src=None):
        index = base + 6 + 9 * source + kind
        own_spot = held.at[source, wide_at]
        x_spot, y_spot = held.at[source, x_wide], held.at[source, y_wide]
        far_spot = held.at[source, diagonal_wide]
        if kind in (0, 1, 2):
            target = (x_near, y_near, sibling)[kind]
            return remote(own_spot if src is None else src, own_spot, sems, index, target)
        if kind == 3:
            return remote(x_spot.at[tops], x_spot.at[tops], sems, index, y_near)
        if kind == 5:
            return remote(y_spot.at[bottoms], y_spot.at[bottoms], sems, index, x_near)
        if kind in (4, 6):
            spot = x_spot if kind == 4 else y_spot
            return remote(spot, spot, sems, index, sibling)
        rows = tops if kind == 7 else bottoms
        return remote(far_spot.at[rows], far_spot.at[rows], sems, index, sibling)

    def plane_send(source, src=None):
        for kind in (0, 1, 2):
            plane_copy(source, kind, src).start()

    def begin():
        @pl.when(plane < PLANES - 1)
        def _():
            climb(1, plane, own).start()

        @pl.when(plane > 0)
        def _():
            sink(1, plane, own).start()

        plane_send(plane, own)

    def arrive(distance):
        @pl.when(plane >= distance)
        def _():
            source = plane - distance
            climb(distance, source, None).wait_recv()
            if distance < PLANES - 1:

                @pl.when(plane < PLANES - 1)
                def _():
                    climb(distance + 1, source, None).start()

            plane_send(source)

        @pl.when(plane + distance < PLANES)
        def _():
            source = plane + distance
            sink(distance, source, None).wait_recv()
            if distance < PLANES - 1:

                @pl.when(plane > 0)
                def _():
                    sink(distance + 1, source, None).start()

            plane_send(source)

    def at_distance(distance, step):
        if distance == 0:
            step(plane)
            return

        @pl.when(plane >= distance)
        def _():
            step(plane - distance)

        @pl.when(plane + distance < PLANES)
        def _():
            step(plane + distance)

    def relay_one(source):
        plane_copy(source, 0).wait_recv()
        plane_copy(source, 3).start()
        plane_copy(source, 4).start()
        plane_copy(source, 1).wait_recv()
        plane_copy(source, 5).start()
        plane_copy(source, 6).start()

    def finish_one(source):
        plane_copy(source, 3).wait_recv()
        plane_copy(source, 7).start()
        plane_copy(source, 5).wait_recv()
        plane_copy(source, 8).start()

    def settle_one(source):
        for kind in (2, 4, 6, 7, 8):
            plane_copy(source, kind).wait_recv()
        for kind in range(9):
            plane_copy(source, kind).wait_send()

    def relay(distance):
        at_distance(distance, relay_one)

    def finish(distance):
        at_distance(distance, finish_one)

    def settled():
        for distance in range(PLANES):
            at_distance(distance, settle_one)
        for distance in range(1, PLANES):
            source = plane - distance + 1

            @pl.when((plane < PLANES - 1) & (source >= 0))
            def _(distance=distance, source=source):
                climb(distance, source, None).wait_send()

            down_source = plane + distance - 1

            @pl.when((plane > 0) & (down_source < PLANES))
            def _(distance=distance, down_source=down_source):
                sink(distance, down_source, None).wait_send()

    return begin, arrive, relay, finish, settled


SHARES = ((6, 0, 0, 384), (7, 0, 384, 128), (2, 0, 512, 512), (4, 0, 1024, 512)) + (
    (0, 0, 1536, 512),
    (0, 512, 2048, 512),
)


def settle_kernel(
    every,
    part,
    vec_ref,
    grad_ref,
    proj_ref,
    bias_ref,
    momentum_ref,
    ids_ref,
    mask_ref,
    outgoing_ref,
    text_ref,
    sum_ref,
    proj_sum_ref,
    vec_out_ref,
    rows_ref,
    incoming_ref,
    gram_ref,
    high_ref,
    low_ref,
    poly,
    chain,
    chain_high,
    chain_low,
    rows_out,
    table_ref,
    text_tiles,
    proj_own,
    proj_far,
    proj_part,
    vec_near,
    vec_far,
    vec_deep,
    main_tiles,
    proj_tiles,
    momentum_tiles,
    packs,
    pieces,
    totals,
    local_sem,
    tile_sem,
    text_sem,
    done_send,
    done_recv,
    pass_send,
    pass_recv,
    proj_send,
    proj_recv,
    vec_send,
    vec_recv,
    gram_send,
    gram_recv,
    share_sem,
    rows_send,
    rows_recv,
    piece_send,
    piece_recv,
):
    wide_at, plane, chip, core = place()
    sibling, chips, planes = neighbours(wide_at, plane, chip, core)
    x_wide, y_wide = across(wide_at, plane, chip, core)
    x_near, y_near = (x_wide, plane), (y_wide, plane)
    diagonal_wide = (CHIPS - 1 - chip) * CORES + core
    other = 1 - core
    x_at = lax.rem(chip, SIDE)
    y_at = chip // SIDE
    tile_count, tile_first = owner_tiles(wide_at)

    def momentum_load(tile):
        source = pl.ds(pl.multiple_of((tile_first + tile) * TILE, TILE), TILE)
        return pltpu.make_async_copy(
            momentum_ref.at[source], momentum_tiles.at[tile], tile_sem.at[0, tile]
        )

    @pl.loop(0, tile_count)
    def _(tile):
        momentum_load(tile).start()

    wide_count = CHIPS * CORES
    peers = [
        (lax.rem(wide_at + k // PLANES, wide_count), lax.rem(plane + k % PLANES, PLANES))
        for k in range(1, wide_count * PLANES)
    ]
    enter(peers)
    me = wide_at * PLANES + plane
    cap = outgoing_ref.shape[0] // (wide_count * PLANES)

    def piece_rows(device):
        return pl.ds(pl.multiple_of(device * cap, cap), cap)

    def piece_copy(index):
        wide_to, plane_to = peers[index]
        return remote(
            outgoing_ref.at[piece_rows(wide_to * PLANES + plane_to)],
            incoming_ref.at[piece_rows(me)],
            (piece_send, piece_recv),
            index,
            (wide_to, plane_to),
        )

    def send_pieces(begin, end):
        for index in range(begin, end):
            piece_copy(index).start()

    own_pieces = pltpu.make_async_copy(
        outgoing_ref.at[piece_rows(me)], incoming_ref.at[piece_rows(me)], local_sem.at[7]
    )
    own_pieces.start()

    vec_sems = (vec_send, vec_recv)
    vec_copies = [remote(vec_ref.at[other], vec_near, vec_sems, 0, sibling)]
    vec_copies[0].start()
    def vec_far_step():
        vec_copies[0].wait_recv()
        vec_far[chip] = vec_ref[core] + vec_near[...]
        for k, target in enumerate(chips):
            copy = remote(vec_far.at[chip], vec_far.at[chip], vec_sems, 1 + k, target)
            copy.start()
            vec_copies.append(copy)

    def vec_deep_step():
        for copy in vec_copies[1:4]:
            copy.wait()
        vec_deep[plane] = (vec_far[0] + vec_far[1]) + (vec_far[2] + vec_far[3])
        for k, target in enumerate(planes):
            copy = remote(vec_deep.at[plane], vec_deep.at[plane], vec_sems, 4 + k, target)
            copy.start()
            vec_copies.append(copy)

    def vec_last_step():
        for copy in vec_copies[4:7]:
            copy.wait()
        vec_out_ref[core] = (vec_deep[0] + vec_deep[1]) + (vec_deep[2] + vec_deep[3])
        copy = remote(vec_out_ref.at[core], vec_out_ref.at[core], vec_sems, 7, sibling)
        copy.start()
        vec_copies.append(copy)

    count = every.shape[2]
    features = proj_ref.shape[0]
    wide_count = CHIPS * CORES
    per_band = grad_ref.shape[0] // BANDS
    proj_sems = (proj_send, proj_recv)
    proj_copies = []

    def proj_near_step():
        total = jnp.zeros((features, D), jnp.float32)
        for block in range(PLANES * wide_count):
            rows = every[block % PLANES, block // PLANES]
            total = total + dot_tn(grad_ref[block], rows)
        proj_own[...] = total.astype(jnp.bfloat16).reshape(CHIPS, PROJ, D)
        for k, target in enumerate(chips):
            to_chip = lax.rem(chip + k + 1, CHIPS)
            copy = remote(proj_own.at[to_chip], proj_far.at[chip], proj_sems, k, target)
            copy.start()
            proj_copies.append(copy)
        proj_far[chip] = proj_own[chip]

    def proj_far_step():
        for copy in proj_copies:
            copy.wait()
        for k, target in enumerate(planes):
            to_plane = lax.rem(plane + k + 1, PLANES)
            copy = remote(proj_far.at[to_plane], proj_part.at[plane], proj_sems, 3 + k, target)
            copy.start()
            proj_copies.append(copy)
        proj_part[plane] = proj_far[plane]

    def publish_proj():
        for copy in proj_copies[3:]:
            copy.wait()
        publish(len(PIECES), proj_part, proj_natural(chip, core))

    done_sems = (done_send, done_recv)
    pass_sems = (pass_send, pass_recv)
    done_copies = {}
    locals_done = {}

    def natural(index, wide):
        _, size, base = PIECES[index]
        return sum_ref.at[pl.ds(pl.multiple_of(base + wide * size, 16), size)]

    def proj_natural(at_chip, at_core):
        return proj_sum_ref.at[at_core, :, at_chip]

    def publish(index, src, spot):
        copies = []
        for k, target in enumerate([sibling] + chips):
            copy = remote(src, spot, done_sems, index * 4 + k, target)
            copy.start()
            copies.append(copy)
        done_copies[index] = copies
        copy = pltpu.make_async_copy(src, spot, local_sem.at[2 + index])
        copy.start()
        locals_done[index] = copy

    def publish_step(chunk):
        for index, (offset, size, _) in enumerate(PIECES):
            if offset // CHUNK == chunk:
                publish(index, part.at[pl.ds(offset, size)], natural(index, wide_at))

    pass_copies = {}

    def pass_step(index):
        pass_copies[index] = []
        for k in range(3):
            done_copies[index][1 + k].wait_recv()
            from_chip = lax.rem(chip + CHIPS - 1 - k, CHIPS)
            if index < len(PIECES):
                spot = natural(index, from_chip * CORES + core)
            else:
                spot = proj_natural(from_chip, core)
            copy = remote(spot, spot, pass_sems, index * 3 + k, sibling)
            copy.start()
            pass_copies[index].append(copy)

    def table_step():
        for block in range(PLANES * wide_count):
            rows = every[block % PLANES, block // PLANES]
            band, spot = divmod(block, per_band)
            table_ref[band * features : (band + 1) * features, spot * count : (spot + 1) * count] = (
                dot_nt(proj_ref[...], rows) + bias_ref[...]
            ).astype(jnp.bfloat16)

    text_rows = table_ref.shape[1]
    row_tiles = ids_ref.shape[1] // TEXT_TILE
    text_count = ids_ref.shape[0] * row_tiles

    def text_copy(step):
        slot = lax.rem(step, 2)
        lanes = pl.ds(pl.multiple_of(step * TEXT_TILE, TEXT_TILE), TEXT_TILE)
        return pltpu.make_async_copy(text_tiles.at[slot], text_ref.at[:, lanes], text_sem.at[slot])

    def text_steps(begin, end):
        @pl.loop(begin, end)
        def _(step):
            row = pl.ds(step // row_tiles, 1)
            start = lax.rem(step, row_tiles) * TEXT_TILE
            id_lanes = pl.ds(pl.multiple_of(start, TEXT_TILE), TEXT_TILE)
            ids = ids_ref[row, id_lanes]
            values = plain_dot(table_ref[...], band_onehot(ids, text_rows))
            band = jnp.where(mask_ref[row, id_lanes] > 0, ids // text_rows, -1)
            total = jnp.zeros((features, TEXT_TILE), jnp.float32)
            for b in range(BANDS):
                total = jnp.where(band == b, values[b * features : (b + 1) * features], total)

            @pl.when(step >= 2)
            def _():
                text_copy(step - 2).wait()

            text_tiles[lax.rem(step, 2)] = total
            text_copy(step).start()

    def settle_piece(index):
        done_copies[index][0].wait_recv()
        for copy in pass_copies[index]:
            copy.wait_recv()
        locals_done[index].wait()

    gram_sems = (gram_send, gram_recv)

    def add_tile(tile, gradient):
        momentum_load(tile).wait()
        gradient = gradient.astype(jnp.float32)
        update = gradient + MUON_BETA * (MUON_BETA * momentum_tiles[tile] + gradient)
        high, low = halves(update)
        rows = pl.ds(pl.multiple_of(tile * TILE, TILE), TILE)
        high_ref[rows, :] = high
        low_ref[rows, :] = low

    early = (wide_at == OWNERS[0]) | (wide_at == OWNERS[1])
    late = (tile_count > 0) & jnp.logical_not(early)

    def proj_tiles_step():
        loads = [
            pltpu.make_async_copy(
                proj_sum_ref.at[tile // PLANES, tile % PLANES],
                proj_tiles.at[tile],
                tile_sem.at[1, tile],
            )
            for tile in range(MOST_TILES)
        ]
        for copy in loads:
            copy.start()
        for copy in loads:
            copy.wait()

        @pl.loop(0, MOST_TILES)
        def _(tile):
            add_tile(tile, proj_tiles[tile].reshape(TILE, D))

    def main_tiles_step():
        def load(tile):
            source = pl.ds(pl.multiple_of((tile_first + tile) * TILE, TILE), TILE)
            return pltpu.make_async_copy(
                sum_ref.at[source], main_tiles.at[tile], tile_sem.at[1, tile]
            )

        @pl.loop(0, tile_count)
        def _(tile):
            load(tile).start()

        @pl.loop(0, tile_count)
        def _(tile):
            load(tile).wait()
            add_tile(tile, main_tiles[tile])

    def gram_product(count_here):
        high = high_ref[0 : count_here * TILE, :]
        cross = dot_tn(high, low_ref[0 : count_here * TILE, :])
        gram_ref[...] = dot_tn(high, high) + (cross + cross.T)

    def gram_copies(first_index):
        copies = []
        for k, target in enumerate(planes):
            to_plane = lax.rem(plane + k + 1, PLANES)
            if first_index == 0:
                src, dst = packs.at[to_plane], pieces.at[plane]
            else:
                src, dst = totals.at[plane], totals.at[plane]
            copies.append(remote(src, dst, gram_sems, first_index + k, target))
        return copies

    def gram_send_step():
        for t in range(PLANES):
            for strip, lane in ((t, 0), (STRIPS - 1 - t, 1)):
                begin = strip // 2 * TILE
                value = gram_ref[strip * STRIP : (strip + 1) * STRIP, begin:]
                width = D - begin
                at = 0 if lane == 0 else PACKED - width
                packs[t, :, at : at + width] = value
        for copy in gram_copies(0):
            copy.start()
        pieces[plane] = packs[plane]

    def gram_early_step():
        @pl.when(early)
        def _():
            main_tiles_step()

        for owner, count_here in zip(OWNERS[:2], BLOCK_TILES[:2]):

            @pl.when(wide_at == owner)
            def _(count_here=count_here):
                gram_product(count_here)

        @pl.when(early)
        def _():
            gram_send_step()

    def gram_late_step():
        @pl.when(wide_at == OWNERS[4])
        def _():
            proj_tiles_step()
            gram_product(BLOCK_TILES[4])

        @pl.when(late & (wide_at != OWNERS[4]))
        def _():
            main_tiles_step()
            gram_product(BLOCK_TILES[3])

        @pl.when(late)
        def _():
            gram_send_step()

    def gram_total_step(here):
        @pl.when(here)
        def _():
            for copy in gram_copies(0):
                copy.wait()
            totals[plane] = (pieces[0] + pieces[1]) + (pieces[2] + pieces[3])
            for copy in gram_copies(3):
                copy.start()

    def gram_whole_step():
        @pl.when(tile_count > 0)
        def _():
            for copy in gram_copies(3):
                copy.wait()
            for t in range(PLANES):
                for strip, lane in ((t, 0), (STRIPS - 1 - t, 1)):
                    begin = strip // 2 * TILE
                    width = D - begin
                    at = 0 if lane == 0 else PACKED - width
                    gram_ref[strip * STRIP : (strip + 1) * STRIP, begin:] = totals[
                        t, :, at : at + width
                    ]
            row_block = lax.broadcasted_iota(jnp.int32, (D, D), 0) // TILE
            lane_block = lax.broadcasted_iota(jnp.int32, (D, D), 1) // TILE
            value = gram_ref[...]
            gram_ref[...] = jnp.where(lane_block >= row_block, value, value.T)

    def chain_step():
        diagonal = lax.broadcasted_iota(jnp.int32, (D, D), 0) == lax.broadcasted_iota(
            jnp.int32, (D, D), 1
        )
        square = jnp.sum(jnp.where(diagonal, gram_ref[...], 0.0))
        inverse = 1.0 / (jnp.sqrt(jnp.full((1, 1), square)) + 1e-07)
        gram_ref[...] = gram_ref[...] * (inverse * inverse)

        def make_poly():
            value = gram_ref[...]
            parts = halves(value)
            diagonal = lax.broadcasted_iota(jnp.int32, (D, D), 0) == lax.broadcasted_iota(
                jnp.int32, (D, D), 1
            )
            poly[...] = (
                NEWTON_B * value
                + NEWTON_C * split_dot(parts, parts)
                + jnp.where(diagonal, NEWTON_A, 0.0)
            )

        def next_gram():
            parts = halves(poly[...])
            half_way = split_dot(halves(gram_ref[...]), parts)
            gram_ref[...] = split_dot(halves(half_way), parts)

        def extend():
            chain[...] = split_dot(halves(chain[...]), halves(poly[...]))

        make_poly()
        chain[...] = poly[...]
        next_gram()

        @pl.loop(0, 3)
        def _(sweep):
            make_poly()
            extend()
            next_gram()

        make_poly()
        extend()
        high, low = halves(chain[...] * inverse)
        chain_high[...] = high
        chain_low[...] = low

    proj_near_step()
    publish_step(2)
    publish_step(0)
    publish_step(1)
    vec_far_step()
    proj_far_step()
    pass_step(2)
    pass_step(3)
    publish_proj()
    pass_step(0)
    pass_step(1)
    settle_piece(2)
    settle_piece(3)
    gram_early_step()
    pass_step(4)
    settle_piece(0)
    settle_piece(1)
    settle_piece(4)
    gram_late_step()
    vec_deep_step()
    table_step()
    text_steps(0, 5)
    gram_total_step(tile_count > 0)
    vec_last_step()
    text_steps(5, text_count)
    gram_whole_step()
    send_pieces(0, len(peers))
    @pl.when(tile_count > 0)
    def _():
        chain_step()


    share_sems = (rows_send, rows_recv)

    def share_copies(index):
        owner, source, begin, size = SHARES[index]
        owner_chip, owner_core = divmod(owner, CORES)
        mine = rows_out.at[pl.ds(source, size)]
        spot = rows_ref.at[pl.ds(begin, size)]
        first = rows_ref.at[pl.ds(begin, size // 2)]
        last = rows_ref.at[pl.ds(begin + size // 2, size // 2)]
        base = index * 9
        roles = {
            "x": (owner_chip ^ 1) * CORES + owner_core,
            "y": (owner_chip ^ 2) * CORES + owner_core,
            "d": (owner_chip ^ 3) * CORES + owner_core,
        }
        sends = {
            "o": [
                (mine, spot, base, x_near),
                (mine, spot, base + 1, y_near),
                (mine, spot, base + 2, sibling),
            ],
            "x": [(first, first, base + 3, y_near), (spot, spot, base + 5, sibling)],
            "y": [(last, last, base + 4, x_near), (spot, spot, base + 6, sibling)],
            "d": [(first, first, base + 7, sibling), (last, last, base + 8, sibling)],
        }
        gets = {
            "x": [(spot, base)],
            "y": [(spot, base + 1)],
            "d": [(first, base + 3), (last, base + 4)],
            "so": [(spot, base + 2)],
            "sx": [(spot, base + 5)],
            "sy": [(spot, base + 6)],
            "sd": [(first, base + 7), (last, base + 8)],
        }
        roles["o"] = owner
        for role in ("o", "x", "y", "d"):
            at = roles[role]
            roles["s" + role] = at // CORES * CORES + 1 - at % CORES
        local = (mine, spot, share_sem.at[index])
        return roles, sends, gets, local

    def started(entry):
        src, dst, index, target = entry
        return remote(src, dst, share_sems, index, target)

    def arriving(entry):
        spot, index = entry
        return remote(spot, spot, share_sems, index, sibling)

    plans = [share_copies(index) for index in range(len(SHARES))]
    for (roles, sends, gets, local), (_, source, _, size) in zip(plans, SHARES):

        @pl.when(wide_at == roles["o"])
        def _(sends=sends, local=local, source=source, size=size):
            rows = slice(source, source + size)
            rows_out[rows, :] = split_dot(
                (high_ref[rows, :], low_ref[rows, :]), (chain_high[...], chain_low[...])
            ).astype(jnp.bfloat16)
            for entry in sends["o"]:
                started(entry).start()
            pltpu.make_async_copy(*local).start()

    for phase in (("x", "y"), ("d",)):
        for roles, sends, gets, local in plans:
            for role in phase:

                @pl.when(wide_at == roles[role])
                def _(sends=sends, gets=gets, role=role):
                    for got, entry in zip(gets[role] * 2, sends[role]):
                        if role == "d" or entry is sends[role][0]:
                            arriving(got).wait_recv()
                        started(entry).start()

    for roles, sends, gets, local in plans:
        for role in ("so", "sx", "sy", "sd"):

            @pl.when(wide_at == roles[role])
            def _(gets=gets, role=role):
                for got in gets[role]:
                    arriving(got).wait_recv()

        for role in ("o", "x", "y", "d"):

            @pl.when(wide_at == roles[role])
            def _(sends=sends, local=local, role=role):
                for entry in sends[role]:
                    started(entry).wait_send()
                if role == "o":
                    pltpu.make_async_copy(*local).wait()


    for copies in list(done_copies.values()) + list(pass_copies.values()):
        for copy in copies:
            copy.wait_send()
    vec_copies[0].wait_send()
    vec_copies[7].wait()
    text_copy(text_count - 2).wait()
    text_copy(text_count - 1).wait()
    own_pieces.wait()
    for index in range(len(peers)):
        piece_copy(index).wait()


def settle(every, part, vec, grad_own, proj_own, bias_own, momentum, text_ids, text_mask, outgoing):
    dma = pltpu.SemaphoreType.DMA
    f32, bf = jnp.float32, jnp.bfloat16
    features, tokens = proj_own.shape[0], text_ids.size
    rows = grad_own.shape[0] * grad_own.shape[1] // BANDS
    hbm = pl.BlockSpec(memory_space=pl.ANY)
    vmem = pl.BlockSpec(memory_space=pltpu.VMEM)
    return pl.pallas_call(
        settle_kernel,
        out_shape=(
            jax.ShapeDtypeStruct((features, tokens), f32),
            jax.ShapeDtypeStruct((MAIN_TILES * TILE, D), bf),
            jax.ShapeDtypeStruct((CORES, PLANES, CHIPS, PROJ, D), bf),
            jax.ShapeDtypeStruct((CORES, VROWS, D), f32),
            jax.ShapeDtypeStruct(((MAIN_TILES + MOST_TILES) * TILE, D), bf),
            jax.ShapeDtypeStruct(outgoing.shape, bf),
        ),
        in_specs=[vmem, vmem, vmem, vmem, vmem, vmem, hbm, vmem, vmem, hbm],
        out_specs=(hbm, hbm, hbm, vmem, hbm, hbm),
        scratch_shapes=[
            pltpu.VMEM((D, D), f32),
            pltpu.VMEM((MOST_TILES * TILE, D), bf),
            pltpu.VMEM((MOST_TILES * TILE, D), bf),
            pltpu.VMEM((D, D), f32),
            pltpu.VMEM((D, D), f32),
            pltpu.VMEM((D, D), bf),
            pltpu.VMEM((D, D), bf),
            pltpu.VMEM((MOST_TILES * TILE, D), bf),
            pltpu.VMEM((BANDS * features, rows), bf),
            pltpu.VMEM((2, features, TEXT_TILE), f32),
            pltpu.VMEM((CHIPS, PROJ, D), bf),
            pltpu.VMEM((CHIPS, PROJ, D), bf),
            pltpu.VMEM((PLANES, PROJ, D), bf),
            pltpu.VMEM((VROWS, D), f32),
            pltpu.VMEM((CHIPS, VROWS, D), f32),
            pltpu.VMEM((PLANES, VROWS, D), f32),
            pltpu.VMEM((4, TILE, D), bf),
            pltpu.VMEM((MOST_TILES, CHIPS, PROJ, D), bf),
            pltpu.VMEM((MOST_TILES, TILE, D), f32),
            pltpu.VMEM((PLANES, STRIP, PACKED), f32),
            pltpu.VMEM((PLANES, STRIP, PACKED), f32),
            pltpu.VMEM((PLANES, STRIP, PACKED), f32),
            dma((8,)),
            dma((2, MOST_TILES)),
            dma((2,)),
            dma((20,)),
            dma((20,)),
            dma((15,)),
            dma((15,)),
            dma((6,)),
            dma((6,)),
            dma((8,)),
            dma((8,)),
            dma((6,)),
            dma((6,)),
            dma((len(SHARES),)),
            dma((len(SHARES) * 9,)),
            dma((len(SHARES) * 9,)),
            dma((PLANES * CHIPS * CORES - 1,)),
            dma((PLANES * CHIPS * CORES - 1,)),
        ],
        compiler_params=pltpu.CompilerParams(
            collective_id=3, has_side_effects=True, vmem_limit_bytes=58 * 2**20
        ),
        name="settle",
    )(
        every,
        part,
        vec,
        grad_own,
        proj_own,
        bias_own,
        momentum,
        text_ids,
        text_mask,
        outgoing,
    )


def finish_kernel(main_ref, proj_ref, rows_ref, momentum_ref, master_ref, ema_ref, *outs):
    grad_ref, momentum_new_ref, weight_ref, ema_new_ref = outs
    tile = pl.program_id(0)
    height = rows_ref.shape[0]
    main = main_ref[...].astype(jnp.float32)
    proj = proj_ref[...].reshape(height, D).astype(jnp.float32)
    gradient = jnp.where(tile < MAIN_TILES * TILE // height, main, proj)
    grad_ref[0] = gradient
    momentum_new_ref[0] = MUON_BETA * momentum_ref[0] + gradient
    row = lax.broadcasted_iota(jnp.int32, (height, 1), 0) + tile * height
    scale = jnp.zeros((height, 1), jnp.float32)
    begin = 0
    for row_total, count in zip(matrix_rows(), BLOCK_TILES):
        inside = (row >= begin * TILE) & (row < (begin + count) * TILE)
        scale = jnp.where(inside, MUON_RATE * math.sqrt(row_total / D), scale)
        begin = begin + count
    weight = master_ref[0] * (1.0 - MUON_RATE * MUON_DECAY) - scale * rows_ref[...].astype(
        jnp.float32
    )
    weight_ref[0] = weight
    ema_new_ref[0] = EMA_DECAY * ema_ref[0] + (1.0 - EMA_DECAY) * weight


def finish(main_sum, proj_sum, rows, momentum, master, ema):
    height = 4 * TILE
    tall = height // TILE
    main_steps = MAIN_TILES // tall
    block = pl.BlockSpec((1, height, D), lambda i: (0, i, 0))
    proj = proj_sum.reshape((MOST_TILES,) + proj_sum.shape[2:])
    return pl.pallas_call(
        finish_kernel,
        grid=((MAIN_TILES + MOST_TILES) // tall,),
        out_shape=(jax.ShapeDtypeStruct(master.shape, jnp.float32),) * 4,
        in_specs=[
            pl.BlockSpec((height, D), lambda i: (jnp.minimum(i, main_steps - 1), 0)),
            pl.BlockSpec(
                (tall,) + proj.shape[1:], lambda i: (jnp.maximum(i - main_steps, 0), 0, 0, 0)
            ),
            pl.BlockSpec((height, D), lambda i: (i, 0)),
            block,
            block,
            block,
        ],
        out_specs=(block,) * 4,
        cost_estimate=pl.CostEstimate(
            flops=12 * master.size, bytes_accessed=32 * master.size, transcendentals=0
        ),
        compiler_params=pltpu.CompilerParams(vmem_limit_bytes=62 * 2**20),
        name="finish",
    )(main_sum, proj, rows, momentum, master, ema)

def two_part_dot(left, right):
    high, low = halves(left)
    return plain_dot(high, right) + plain_dot(low, right)


def normalize(values):
    center = values - jnp.mean(values, axis=-1, keepdims=True)
    spread = jnp.mean(center * center, axis=-1, keepdims=True)
    scale = lax.rsqrt(spread + 1e-05)
    return center * scale, scale


def normalize_back(grad, gain, hat, scale):
    grad_hat = grad * gain
    return scale * (
        grad_hat
        - jnp.mean(grad_hat, axis=-1, keepdims=True)
        - hat * jnp.mean(grad_hat * hat, axis=-1, keepdims=True)
    )


def over_rows(values):
    return jnp.sum(values, axis=0, keepdims=True)


def plane_sums(first, near_copies, near, buffers, far_sems, deep_sems):
    x_first, y_first, x_second, y_second, second, deep = buffers
    wide_at, plane, chip, core = place()
    _, _, planes = neighbours(wide_at, plane, chip, core)
    x_wide, y_wide = across(wide_at, plane, chip, core)
    x_near, y_near = (x_wide, plane), (y_wide, plane)
    x_at, y_at = lax.rem(chip, SIDE), chip // SIDE
    lows, highs = pl.ds(0, 2), pl.ds(2, 2)
    sent = []
    waiting = {}

    def start(src, dst, sems, index, target):
        copy = remote(src, dst, sems, index, target)
        copy.start()
        sent.append(copy)
        return copy

    def add(left, right):
        return (left.astype(jnp.float32) + right.astype(jnp.float32)).astype(jnp.bfloat16)

    def first_step(chunk):
        near_copies[chunk].wait_recv()

        @pl.loop(0, CHIPS * PLANES)
        def _(step):
            y, x, m = step // (SIDE * PLANES), lax.rem(step // PLANES, SIDE), lax.rem(step, PLANES)
            first[chunk, y, x, m] = add(first[chunk, y, x, m], near[chunk, y, x, m])

        base = chunk * 4
        waiting["x", chunk] = start(
            first.at[chunk, :, 1 - x_at, lows], x_first.at[chunk], far_sems, base, x_near
        )
        waiting["y", chunk] = start(
            first.at[chunk, 1 - y_at, :, highs], y_first.at[chunk], far_sems, base + 1, y_near
        )

    def second_step(chunk):
        base = chunk * 4
        waiting["x", chunk].wait_recv()
        for y in range(SIDE):
            for m in range(2):
                first[chunk, y, x_at, m] = add(first[chunk, y, x_at, m], x_first[chunk, y, m])
        waiting["yy", chunk] = start(
            first.at[chunk, 1 - y_at, x_at, lows], y_second.at[chunk], far_sems, base + 2, y_near
        )
        waiting["y", chunk].wait_recv()
        for x in range(SIDE):
            for m in range(2):
                first[chunk, y_at, x, 2 + m] = add(
                    first[chunk, y_at, x, 2 + m], y_first[chunk, x, m]
                )
        waiting["xx", chunk] = start(
            first.at[chunk, y_at, 1 - x_at, highs], x_second.at[chunk], far_sems, base + 3, x_near
        )

    def deep_step(chunk):
        waiting["yy", chunk].wait_recv()
        for m in range(2):
            second[chunk, m] = add(first[chunk, y_at, x_at, m], y_second[chunk, m])
        waiting["xx", chunk].wait_recv()
        for m in range(2):
            second[chunk, 2 + m] = add(first[chunk, y_at, x_at, 2 + m], x_second[chunk, m])
        for k, target in enumerate(planes):
            to_plane = lax.rem(plane + k + 1, PLANES)
            waiting["z", chunk, k] = start(
                second.at[chunk, to_plane], deep.at[chunk, k], deep_sems, chunk * 3 + k, target
            )

    def total(chunk):
        value = second[chunk, plane].astype(jnp.float32)
        for k in range(3):
            waiting["z", chunk, k].wait_recv()
            value = value + deep[chunk, k].astype(jnp.float32)
        return value

    def sums_settled():
        for copy in sent:
            copy.wait_send()

    return first_step, second_step, deep_step, total, sums_settled


def sum_scratch(chunks):
    dma = pltpu.SemaphoreType.DMA
    bf = jnp.bfloat16
    return [
        pltpu.VMEM((chunks, SIDE, 2, CHUNK, D), bf),
        pltpu.VMEM((chunks, SIDE, 2, CHUNK, D), bf),
        pltpu.VMEM((chunks, 2, CHUNK, D), bf),
        pltpu.VMEM((chunks, 2, CHUNK, D), bf),
        pltpu.VMEM((chunks, PLANES, CHUNK, D), bf),
        pltpu.VMEM((chunks, 3, CHUNK, D), bf),
        dma((chunks * 4,)),
        dma((chunks * 4,)),
        dma((chunks * 3,)),
        dma((chunks * 3,)),
    ]


def layer_kernel(
    master_ref,
    pieces_ref,
    table_ref,
    ids_ref,
    mask_ref,
    cot_ref,
    live_ref,
    param_ref,
    every_ref,
    part_ref,
    outgoing_ref,
    vec_ref,
    own_grad_ref,
    own_proj_ref,
    rows_ref,
    main_ref,
    own_rows,
    every_ids,
    spots_ref,
    asked_ranks,
    asked_locals,
    incoming_ref,
    proj_rows,
    proj_stage,
    z_ref,
    packed,
    text_total,
    onehot,
    hats,
    scales,
    normed,
    keys,
    probs,
    grad_kv,
    grad_normed,
    grad_pieces,
    active,
    slope,
    slides,
    sums,
    local_sem,
    x_first,
    y_first,
    x_second,
    y_second,
    second_sum,
    deep,
    far_send,
    far_recv,
    deep_send,
    deep_recv,
    tell_send,
    tell_recv,
    piece_send,
    piece_recv,
    near_send,
    near_recv,
    main_near,
    main_x_first,
    main_y_first,
    main_x_second,
    main_y_second,
    main_second,
    main_deep,
    main_far_send,
    main_far_recv,
    main_deep_send,
    main_deep_recv,
    main_send,
    main_recv,
    body_send,
    body_recv,
    proj_send,
    proj_recv,
    z_send,
    z_recv,
):
    at = place()
    wide_at, plane, chip, core = at
    me = wide_at * PLANES + plane
    wide_count = CHIPS * CORES
    group_rows = table_ref.shape[0]
    cap = outgoing_ref.shape[0] // (wide_count * PLANES)
    entries = z_ref.shape[0]
    peers = [
        (lax.rem(wide_at + k // PLANES, wide_count), lax.rem(plane + k % PLANES, PLANES))
        for k in range(1, wide_count * PLANES)
    ]

    sibling, _, planes = neighbours(*at)
    body_begin, body_arrive, body_relay, body_finish, body_settled = spread_steps(
        packed.at[plane, wide_at], packed, (body_send, body_recv), 0, at
    )
    z_begin, z_arrive, z_relay, z_finish, z_settled = spread_steps(
        z_ref, every_ref, (z_send, z_recv), 0, at
    )
    holds_proj = plane == chip
    proj_sems = (proj_send, proj_recv)
    features = cot_ref.shape[0]

    def proj_load():
        begin = master_ref.shape[0] - OUTW // PLANES + core * PLANES * features
        source = pl.ds(pl.multiple_of(begin, 16), PLANES * features)
        return pltpu.make_async_copy(master_ref.at[source], proj_rows, local_sem.at[4])

    def proj_copy(k):
        to_plane = lax.rem(plane + k + 1, PLANES)
        return remote(proj_stage.at[to_plane], own_proj_ref, proj_sems, k, planes[k])

    @pl.when(holds_proj)
    def _():
        proj_load().start()

    loads = []
    begin = 0
    block = 0
    for index, row_total in enumerate(matrix_rows()[:4]):
        height = row_total // PLANES
        size = height // wide_count
        copy = pltpu.make_async_copy(
            master_ref.at[pl.ds(pl.multiple_of(block + wide_at * size, 16), size)],
            own_rows.at[pl.ds(begin, size)],
            local_sem.at[index],
        )
        copy.start()
        loads.append(copy)
        begin = begin + size
        block = block + height
    enter(peers)
    every_ids[me] = jnp.concatenate(
        [pieces_ref[...], jnp.zeros((SLOTS - PSLOTS, entries), jnp.int32)], axis=0
    )
    tell_copies = []
    for index, target in enumerate(peers):
        copy = remote(every_ids.at[me], every_ids.at[me], (tell_send, tell_recv), index, target)
        copy.start()
        tell_copies.append(copy)
    for copy in loads:
        copy.wait()
    packed[plane, wide_at] = own_rows[...].astype(jnp.bfloat16)

    def proj_begin():
        @pl.when(holds_proj)
        def _():
            proj_load().wait()
            proj_stage[...] = proj_rows[...].astype(jnp.bfloat16).reshape(proj_stage.shape)
            for k in range(PLANES - 1):
                proj_copy(k).start()
            own_proj_ref[...] = proj_stage[plane]

    piece_copies = []

    def piece_rows(device):
        return pl.ds(pl.multiple_of(device * cap, cap), cap)

    def send_pieces(begin, end):
        for index in range(begin, end):
            wide_to, plane_to = peers[index]
            copy = remote(
                outgoing_ref.at[piece_rows(wide_to * PLANES + plane_to)],
                incoming_ref.at[piece_rows(me)],
                (piece_send, piece_recv),
                index,
                (wide_to, plane_to),
            )
            copy.start()
            piece_copies.append(copy)

    near_copies = []
    dz_first, dz_second, dz_deep, dz_total, dz_settled = plane_sums(
        main_ref.at[core],
        near_copies,
        grad_kv,
        (x_first, y_first, x_second, y_second, second_sum, deep),
        (far_send, far_recv),
        (deep_send, deep_recv),
    )

    main_copies = {}
    main_first, main_then, main_last, main_total, main_settled = plane_sums(
        main_ref.at[core],
        main_copies,
        main_near,
        (main_x_first, main_y_first, main_x_second, main_y_second, main_second, main_deep),
        (main_far_send, main_far_recv),
        (main_deep_send, main_deep_recv),
    )

    def main_begin(chunk):
        copy = remote(
            main_ref.at[1 - core, chunk],
            main_near.at[chunk],
            (main_send, main_recv),
            chunk,
            sibling,
        )
        copy.start()
        main_copies[chunk] = copy

    def dz_begin():
        @pl.when(jnp.logical_not(holds_proj))
        def _():
            k = lax.rem(plane - chip - 1 + PLANES, PLANES)
            remote(proj_stage.at[0], own_proj_ref, proj_sems, k, sibling).wait_recv()

        proj = own_proj_ref[...]
        for wide in range(wide_count):
            block = own_grad_ref[wide * PLANES : (wide + 1) * PLANES]
            value = plain_dot(block.reshape(PLANES * entries, features), proj)
            value = value.astype(jnp.bfloat16).reshape(PLANES, entries, D)
            y, x = divmod(wide // CORES, SIDE)
            for part in range(entries // CHUNK):
                main_ref[wide % CORES, part, y, x] = value[:, part * CHUNK : (part + 1) * CHUNK, :]
        for part in range(entries // CHUNK):
            copy = remote(
                main_ref.at[1 - core, part],
                grad_kv.at[part],
                (near_send, near_recv),
                part,
                sibling,
            )
            copy.start()
            near_copies.append(copy)

    text_rows = own_grad_ref.shape[0] * own_grad_ref.shape[1] // BANDS
    text_total[...] = jnp.zeros_like(text_total)

    row_tiles = ids_ref.shape[1] // TEXT_TILE

    def build_pieces():
        for copy in tell_copies:
            copy.wait()
        device_count = wide_count * PLANES
        slot_count = entries * PSLOTS
        asked_ids = jnp.concatenate([every_ids[:, slot, :] for slot in range(PSLOTS)], axis=1)
        own_ids = jnp.concatenate([pieces_ref[slot : slot + 1, :] for slot in range(PSLOTS)], axis=1)
        asked = asked_ids // group_rows == me
        own_group = own_ids // group_rows
        group_at = lax.broadcasted_iota(jnp.int32, (device_count, slot_count), 0)
        grouped = jnp.where(group_at == own_group, 1.0, 0.0)
        marks = jnp.concatenate([jnp.where(asked, 1.0, 0.0), grouped], axis=0).astype(jnp.bfloat16)
        earlier = jnp.where(
            lax.broadcasted_iota(jnp.int32, (slot_count, slot_count), 0)
            < lax.broadcasted_iota(jnp.int32, (slot_count, slot_count), 1),
            1.0,
            0.0,
        ).astype(jnp.bfloat16)
        ranks = plain_dot(marks, earlier)
        own_rank = over_rows(grouped * ranks[device_count:, :])
        spots = own_group * cap + own_rank.astype(jnp.int32)
        for slot in range(PSLOTS):
            spots_ref[slot + 1 : slot + 2, :] = spots[:, slot * entries : (slot + 1) * entries]
        asked_ranks[...] = jnp.where(asked, ranks[:device_count, :], -1.0)
        asked_locals[...] = (asked_ids - me * group_rows + 1).astype(jnp.float32)

        @pl.loop(0, device_count)
        def _(device):
            here = pl.ds(device, 1)
            rank_at = lax.broadcasted_iota(jnp.int32, (cap, slot_count), 0).astype(jnp.float32)
            rows = jnp.sum(
                jnp.where(rank_at == asked_ranks[here, :], asked_locals[here, :], 0.0),
                axis=1,
                keepdims=True,
            )
            rows_ref[piece_rows(device), :] = rows.astype(jnp.int32) - 1

        tile = 512
        for begin in range(0, device_count * cap, tile):
            row_at = lax.broadcasted_iota(jnp.int32, (tile, group_rows), 1)
            chosen = jnp.where(row_at == rows_ref[begin : begin + tile, :], 1.0, 0.0)
            outgoing_ref[begin : begin + tile, :] = plain_dot(
                chosen.astype(jnp.bfloat16), table_ref[...]
            ).astype(jnp.bfloat16)
        incoming_ref[piece_rows(me), :] = outgoing_ref[piece_rows(me), :]

    def text_steps(begin, end):
        @pl.loop(begin, end)
        def _(step):
            lanes = pl.ds(pl.multiple_of(step * TEXT_TILE, TEXT_TILE), TEXT_TILE)
            row = pl.ds(step // row_tiles, 1)
            start = lax.rem(step, row_tiles) * TEXT_TILE
            id_lanes = pl.ds(pl.multiple_of(start, TEXT_TILE), TEXT_TILE)
            ids = ids_ref[row, id_lanes]
            chosen = band_onehot(ids, text_rows)
            band = jnp.where(mask_ref[row, id_lanes] > 0, ids // text_rows, -1)
            cot = cot_ref[:, lanes].astype(jnp.float32)
            banded = jnp.concatenate(
                [jnp.where(band == b, cot, 0.0).astype(jnp.bfloat16) for b in range(BANDS)], axis=0
            )
            text_total[...] += dot_nt(chosen, banded)

    text_tiles = ids_ref.shape[0] * row_tiles
    body_begin()
    proj_begin()
    text_steps(0, 1)
    body_arrive(1)
    build_pieces()
    send_pieces(0, 6)
    text_steps(1, 4)
    body_relay(0)
    body_arrive(2)
    send_pieces(6, 12)
    text_steps(4, 8)
    body_arrive(3)
    body_relay(1)
    body_finish(0)
    send_pieces(12, 16)
    text_steps(8, 12)
    body_relay(2)
    body_finish(1)
    send_pieces(16, 20)
    text_steps(12, 16)
    bias_total = jnp.zeros((1, features), jnp.float32)
    blocks = own_grad_ref.shape[0] // BANDS
    for b in range(BANDS):
        rounded = text_total[:, b * features : (b + 1) * features].astype(jnp.bfloat16)
        own_grad_ref[b * blocks : (b + 1) * blocks] = rounded.reshape(
            (blocks,) + own_grad_ref.shape[1:]
        )
        bias_total = bias_total + over_rows(rounded.astype(jnp.float32))
    dz_begin()
    body_relay(3)
    body_finish(2)
    send_pieces(20, 24)
    dz_first(0)
    dz_first(1)
    send_pieces(24, 28)
    body_finish(3)
    dz_second(0)
    send_pieces(28, 31)
    dz_second(1)
    dz_deep(0)
    dz_deep(1)
    body_settled()
    for copy in piece_copies:
        copy.wait()
    def weight_rows(begin, size, plane_at=None):
        rows = slice(begin, begin + size)
        if plane_at is None:
            return packed[:, :, rows, :].reshape(PLANES * wide_count * size, D)
        return packed[plane_at, :, rows, :].reshape(wide_count * size, D)

    qkv_at, out_at, up_at, down_at = 0, 48, 64, 128
    spot_count = incoming_ref.shape[0]
    gain_one, shift_one = param_ref[9:10, :], param_ref[10:11, :]
    gain_two, shift_two = param_ref[11:12, :], param_ref[12:13, :]
    gain_end, shift_end = param_ref[13:14, :], param_ref[14:15, :]

    def slot_rows(slot):
        return pl.ds(pl.multiple_of(slot * entries, entries), entries)

    def piece_lanes(slot):
        return pl.ds(pl.multiple_of((slot - 1) * entries, entries), entries)

    @pl.loop(1, SLOTS)
    def _(slot):
        places = lax.broadcasted_iota(jnp.int32, (spot_count, entries), 0)
        chosen = jnp.where(places == spots_ref[pl.ds(slot, 1), :], 1.0, 0.0).astype(jnp.bfloat16)
        onehot[:, piece_lanes(slot)] = chosen

    bounds = (0, 4 * entries, PSLOTS * entries)
    for begin, end in zip(bounds[:-1], bounds[1:]):
        hats[entries + begin : entries + end, :] = dot_tn(onehot[:, begin:end], incoming_ref[...])

    first_row = param_ref[0:1, :] + param_ref[1:2, :]
    hats[0:entries, :] = jnp.broadcast_to(param_ref[0:1, :], (entries, D))
    sums[...] = jnp.zeros_like(sums)

    @pl.loop(0, SLOTS)
    def _(slot):
        rows = slot_rows(slot)
        hat, scale = normalize(hats[rows, :] + param_ref[pl.ds(1 + slot, 1), :])
        hats[rows, :] = hat
        scales[rows, :] = jnp.broadcast_to(scale, (entries, 128))
        part = (hat * gain_one + shift_one).astype(jnp.bfloat16)
        normed[rows, :] = part

    wholes = SLOTS * entries
    tall = wholes // 2
    for begin in range(0, wholes, tall):
        rows = slice(begin, begin + tall)
        keys[rows, :] = dot_nt(normed[rows, :], weight_rows(qkv_at, 48)[D:, :])

    query = dot_nt(normed[0:entries, :], weight_rows(qkv_at, 48)[0:D, :])
    lane_head = lax.broadcasted_iota(jnp.int32, (D, 128), 0) // HDIM
    to_heads = jnp.where(
        lane_head == lax.broadcasted_iota(jnp.int32, (D, 128), 1), 1.0, 0.0
    ).astype(jnp.bfloat16)
    head_lane = lax.broadcasted_iota(jnp.int32, (128, D), 1) // HDIM
    from_heads = jnp.where(
        head_lane == lax.broadcasted_iota(jnp.int32, (128, D), 0), 1.0, 0.0
    ).astype(jnp.bfloat16)
    root = 1.0 / math.sqrt(HDIM)
    for slot in range(SLOTS):
        rows = slice(slot * entries, (slot + 1) * entries)
        grad_normed[rows, :] = query * keys[rows, 0:D]
    for begin in range(0, wholes, tall):
        rows = slice(begin, begin + tall)
        probs[rows, :] = two_part_dot(grad_normed[rows, :], to_heads) * root
    live = jnp.concatenate(
        [live_ref[...].astype(jnp.float32), jnp.zeros((1, entries), jnp.float32)], axis=0
    ).T
    scores = []
    for slot in range(SLOTS):
        value = probs[slot * entries : (slot + 1) * entries, :]
        if slot > 0:
            value = jnp.where(live[:, slot - 1 : slot] > 0, value, -1e30)
        scores.append(value)
    top = scores[0]
    for value in scores[1:]:
        top = jnp.maximum(top, value)
    scores = [jnp.exp(value - top) for value in scores]
    whole = scores[0]
    for value in scores[1:]:
        whole = whole + value
    for slot in range(SLOTS):
        probs[slot * entries : (slot + 1) * entries, :] = scores[slot] / whole
    for begin in range(0, wholes, tall):
        rows = slice(begin, begin + tall)
        grad_normed[rows, :] = two_part_dot(probs[rows, :], from_heads)
    attended = jnp.zeros((entries, D), jnp.float32)
    for slot in range(SLOTS):
        rows = slice(slot * entries, (slot + 1) * entries)
        attended = attended + grad_normed[rows, :] * keys[rows, D:]
    attended_bf = attended.astype(jnp.bfloat16)
    residual = first_row + dot_nt(attended_bf, weight_rows(out_at, 16))
    hat_two, scale_two = normalize(residual)
    normed_two = (hat_two * gain_two + shift_two).astype(jnp.bfloat16)
    span = 512
    second = residual + param_ref[19:20, :]
    for begin in range(0, FF, span):
        lanes = slice(begin, begin + span)
        bias = param_ref[15 + begin // span : 16 + begin // span, :]
        gate = dot_nt(normed_two, weight_rows(up_at, 64, begin // span)) + bias
        square = gate * gate
        bend = jnp.tanh(math.sqrt(2.0 / math.pi) * (gate + 0.044715 * square * gate))
        part = (0.5 * gate * (1.0 + bend)).astype(jnp.bfloat16)
        active[:, lanes] = part
        slope[:, lanes] = 0.5 * (1.0 + bend) + 0.5 * gate * (1.0 - bend * bend) * (
            math.sqrt(2.0 / math.pi) * (1.0 + 3.0 * 0.044715 * square)
        )
        second = second + plain_dot(part, weight_rows(down_at, 64, begin // span))
    hat_end, scale_end = normalize(second)
    z_ref[...] = (hat_end * gain_end + shift_end).astype(jnp.bfloat16)

    z_begin()
    own_z = pltpu.make_async_copy(z_ref, every_ref.at[plane, wide_at], local_sem.at[5])
    own_z.start()
    z_arrive(1)
    grad_z = jnp.concatenate([dz_total(part) for part in range(entries // CHUNK)], axis=0)
    for copy in near_copies:
        copy.wait_send()
    dz_settled()

    @pl.when(holds_proj)
    def _():
        for k in range(PLANES - 1):
            proj_copy(k).wait_send()

    vec_ref[...] = jnp.zeros_like(vec_ref)
    vec_ref[13:14, :] = over_rows(grad_z * hat_end)
    vec_ref[14:15, :] = over_rows(grad_z)
    grad_second = normalize_back(grad_z, gain_end, hat_end, scale_end)
    branch_two = grad_second.astype(jnp.bfloat16)
    vec_ref[19:20, :] = over_rows(branch_two.astype(jnp.float32))
    tile_lanes = D // features
    vec_ref[pl.ds(20 + me // tile_lanes, 1), :] = jnp.concatenate(
        [jnp.where(lax.rem(me, tile_lanes) == k, bias_total, 0.0) for k in range(tile_lanes)],
        axis=1,
    )

    def store(value, block, chunk, height, offset):
        for chip_at in range(CHIPS):
            for core_at in range(CORES):
                top = (chip_at * CORES + core_at) * height
                y, x = divmod(chip_at, SIDE)
                main_ref[core_at, chunk, y, x, block, offset : offset + height, :] = value[
                    top : top + height, :
                ].astype(jnp.bfloat16)

    z_relay(0)
    z_arrive(2)
    grad_two = jnp.zeros((entries, D), jnp.float32)
    for block in range(PLANES):
        lanes = slice(block * span, (block + 1) * span)
        store(dot_tn(active[:, lanes], branch_two), block, 0, 64, 0)
        gate_grad = (dot_nt(branch_two, weight_rows(down_at, 64, block)) * slope[:, lanes]).astype(jnp.bfloat16)
        vec_ref[15 + block : 16 + block, :] = over_rows(gate_grad.astype(jnp.float32))
        store(dot_tn(gate_grad, normed_two), block, 1, 64, 0)
        grad_two = grad_two + plain_dot(gate_grad, weight_rows(up_at, 64, block))
    main_begin(0)
    main_begin(1)
    z_relay(1)
    z_arrive(3)
    vec_ref[11:12, :] = over_rows(grad_two * hat_two)
    vec_ref[12:13, :] = over_rows(grad_two)
    grad_residual = grad_second + normalize_back(grad_two, gain_two, hat_two, scale_two)
    branch_one = grad_residual.astype(jnp.bfloat16)
    grad_out = dot_tn(branch_one, attended_bf)
    for block in range(PLANES):
        store(grad_out[block * 128 : (block + 1) * 128, :], block, 2, 16, 0)
    grad_attended = plain_dot(branch_one, weight_rows(out_at, 16))
    main_first(0)
    main_first(1)
    z_finish(0)
    z_relay(2)
    halves_of = entries // CHUNK

    def store_kv(kind, slot, value):
        y, x = divmod(slot // 2, SIDE)
        begin = slot % 2 * halves_of
        grad_kv[kind, y, x, begin : begin + halves_of] = value.astype(jnp.bfloat16).reshape(
            halves_of, CHUNK, D
        )


    for slot in range(SLOTS):
        rows = slice(slot * entries, (slot + 1) * entries)
        store_kv(1, slot, grad_normed[rows, :] * grad_attended)
        grad_normed[rows, :] = grad_attended * keys[rows, D:]
    for begin in range(0, wholes, tall):
        rows = slice(begin, begin + tall)
        slides[rows, :] = two_part_dot(grad_normed[rows, :], to_heads)
    inner = jnp.zeros((entries, 128), jnp.float32)
    for slot in range(SLOTS):
        rows = slice(slot * entries, (slot + 1) * entries)
        inner = inner + probs[rows, :] * slides[rows, :]
    for slot in range(SLOTS):
        rows = slice(slot * entries, (slot + 1) * entries)
        slides[rows, :] = probs[rows, :] * (slides[rows, :] - inner)
    for begin in range(0, wholes, tall):
        rows = slice(begin, begin + tall)
        grad_normed[rows, :] = two_part_dot(slides[rows, :], from_heads) * root
    grad_query = jnp.zeros((entries, D), jnp.float32)
    for slot in range(SLOTS):
        rows = slice(slot * entries, (slot + 1) * entries)
        push = grad_normed[rows, :]
        grad_query = grad_query + push * keys[rows, 0:D]
        store_kv(0, slot, push * query)
    z_finish(1)
    z_relay(3)
    query_bf = grad_query.astype(jnp.bfloat16)

    grad_q = dot_tn(query_bf, normed[0:entries, :])
    grad_keys = grad_kv[0].reshape(wholes, D)
    grad_values = grad_kv[1].reshape(wholes, D)
    grad_k = dot_tn(grad_keys, normed[...])
    grad_v = dot_tn(grad_values, normed[...])
    third = D * 3 // PLANES
    every = jnp.concatenate([grad_q, grad_k, grad_v], axis=0)
    for block in range(PLANES):
        store(every[block * third : (block + 1) * third, :], block, 2, 48, 16)

    main_begin(2)
    main_then(0)
    for begin in range(0, wholes, tall):
        rows = slice(begin, begin + tall)
        grad_normed[rows, :] = plain_dot(
            grad_keys[rows, :], weight_rows(qkv_at, 48)[D : 2 * D, :]
        ) + plain_dot(grad_values[rows, :], weight_rows(qkv_at, 48)[2 * D :, :])

    grad_normed[0:entries, :] += plain_dot(query_bf, weight_rows(qkv_at, 48)[0:D, :])

    @pl.loop(0, SLOTS)
    def _(slot):
        rows = slot_rows(slot)
        grad = grad_normed[rows, :]
        hat = hats[rows, :]
        sums[0:1, :] += over_rows(grad * hat)
        sums[1:2, :] += over_rows(grad)
        grad_x = normalize_back(grad, gain_one, hat, scales[rows, 0:1])
        vec_ref[pl.ds(1 + slot, 1), :] = over_rows(grad_x)

        @pl.when(slot > 0)
        def _():
            grad_pieces[pl.ds(pl.multiple_of((slot - 1) * entries, entries), entries), :] = (
                grad_x.astype(jnp.bfloat16)
            )

    main_first(2)
    z_finish(2)
    z_finish(3)
    main_then(1)
    vec_ref[9:11, :] = sums[0:2, :]
    vec_ref[1:2, :] += over_rows(grad_residual)
    vec_ref[0:1, :] = vec_ref[1:2, :]
    tile = 256
    for begin in range(0, spot_count, tile):
        outgoing_ref[begin : begin + tile, :] = plain_dot(
            onehot[begin : begin + tile, :], grad_pieces[...]
        ).astype(jnp.bfloat16)
    main_last(0)
    main_then(2)
    main_last(1)
    main_last(2)
    for chunk in range(CHUNKS):
        part_ref[chunk * CHUNK : (chunk + 1) * CHUNK, :] = main_total(chunk).astype(jnp.bfloat16)
    own_z.wait()
    z_settled()
    main_settled()
    for chunk in range(CHUNKS):
        main_copies[chunk].wait_send()


def layer(master, pieces, table, text_ids, text_mask, text_cot, slot_mask, params, cap):
    f32, bf = jnp.float32, jnp.bfloat16
    dma = pltpu.SemaphoreType.DMA
    count = PLANES * CHIPS * CORES
    entries = slot_mask.shape[1]
    features = text_cot.shape[0]
    rows = entries * SLOTS
    hbm = pl.BlockSpec(memory_space=pl.ANY)
    vmem = pl.BlockSpec(memory_space=pltpu.VMEM)
    spread_count = 6 + 9 * PLANES
    return pl.pallas_call(
        layer_kernel,
        out_shape=(
            jax.ShapeDtypeStruct((PLANES, CHIPS * CORES, entries, D), bf),
            jax.ShapeDtypeStruct((MAIN, D), bf),
            jax.ShapeDtypeStruct((count * cap, D), bf),
            jax.ShapeDtypeStruct((CORES * VROWS, D), f32),
            jax.ShapeDtypeStruct((count, entries, features), bf),
            jax.ShapeDtypeStruct((features, D), bf),
            jax.ShapeDtypeStruct((count * cap, 1), jnp.int32),
        ),
        in_specs=[hbm] + [vmem] * 7,
        out_specs=(hbm,) + (vmem,) * 6,
        scratch_shapes=[
            pltpu.VMEM((CORES, CHUNKS, SIDE, SIDE, PLANES, CHUNK, D), bf),
            pltpu.VMEM((MAIN, D), f32),
            pltpu.VMEM((count, SLOTS, entries), jnp.int32),
            pltpu.VMEM((SLOTS, entries), jnp.int32),
            pltpu.VMEM((count, entries * PSLOTS), f32),
            pltpu.VMEM((count, entries * PSLOTS), f32),
            pltpu.VMEM((count * cap, D), bf),
            pltpu.VMEM((PLANES * features, D), f32),
            pltpu.VMEM((PLANES, features, D), bf),
            pltpu.VMEM((entries, D), bf),
            pltpu.VMEM((PLANES, CHIPS * CORES, MAIN, D), bf),
            pltpu.VMEM((count * entries // BANDS, BANDS * features), f32),
            pltpu.VMEM((count * cap, entries * PSLOTS), bf),
            pltpu.VMEM((rows, D), f32),
            pltpu.VMEM((rows, 128), f32),
            pltpu.VMEM((rows, D), bf),
            pltpu.VMEM((rows, 2 * D), f32),
            pltpu.VMEM((rows, 128), f32),
            pltpu.VMEM((2, SIDE, SIDE, PLANES, CHUNK, D), bf),
            pltpu.VMEM((rows, D), f32),
            pltpu.VMEM((entries * PSLOTS, D), bf),
            pltpu.VMEM((entries, FF), bf),
            pltpu.VMEM((entries, FF), f32),
            pltpu.VMEM((rows, 128), f32),
            pltpu.VMEM((8, D), f32),
            dma((6,)),
        ]
        + sum_scratch(entries // CHUNK)
        + [dma((count - 1,))] * 4
        + [dma((entries // CHUNK,))] * 2
        + [pltpu.VMEM((CHUNKS, SIDE, SIDE, PLANES, CHUNK, D), bf)]
        + sum_scratch(CHUNKS)
        + [dma((CHUNKS,))] * 2
        + [dma((spread_count,))] * 2
        + [dma((PLANES - 1,))] * 2
        + [dma((spread_count,))] * 2,
        compiler_params=pltpu.CompilerParams(
            collective_id=5, has_side_effects=True, vmem_limit_bytes=63 * 2**20
        ),
        name="layer",
    )(master, pieces, table, text_ids, text_mask, text_cot, slot_mask, params)


def piece_grad_kernel(rows_ref, grads_ref, out_ref):
    tile = out_ref.shape[0]
    at = lax.broadcasted_iota(jnp.int32, (tile, rows_ref.shape[1]), 0) + pl.program_id(0) * tile
    chosen = jnp.where(at == rows_ref[...], 1.0, 0.0).astype(jnp.bfloat16)
    out_ref[...] = plain_dot(chosen, grads_ref[...])


def add_piece_grads(rows, grads, group_rows):
    tile = 256
    return pl.pallas_call(
        piece_grad_kernel,
        grid=(group_rows // tile,),
        out_shape=jax.ShapeDtypeStruct((group_rows, D), jnp.float32),
        in_specs=[
            pl.BlockSpec(rows.shape, lambda i: (0, 0)),
            pl.BlockSpec(grads.shape, lambda i: (0, 0)),
        ],
        out_specs=pl.BlockSpec((tile, D), lambda i: (i, 0)),
        compiler_params=pltpu.CompilerParams(vmem_limit_bytes=24 * 2**20),
        name="add_piece_grads",
    )(rows, grads)


def on_device(
    piece_table,
    piece_ids,
    slot_mask,
    text_ids,
    text_mask,
    text_cot,
    mat_master,
    mat_momentum,
    mat_ema,
    vec_master,
    vec_moment1,
    vec_moment2,
    vec_ema,
):
    me = lax.axis_index("wide") * PLANES + lax.axis_index("narrow")
    entries = piece_ids.shape[0]
    group_rows = piece_table.shape[0]
    cap = piece_cap(group_rows)
    feature_rows = text_cot.shape[0]
    params = vec_master.reshape(-1, D)
    pieces = piece_ids.T
    (
        every,
        part,
        grad_outgoing,
        vec_rows,
        grad_own,
        proj_own,
        asked_rows,
    ) = layer(
        mat_master[0], pieces, piece_table, text_ids, text_mask, text_cot, slot_mask.T, params, cap
    )
    bias_out = vec_master[vec_master.shape[0] - OUTW :]
    bias_own = lax.dynamic_slice_in_dim(bias_out, me * feature_rows, feature_rows, 0)
    text_embeds, main_sum, proj_sum, vec_sum, rows, grad_incoming = settle(
        every,
        part,
        vec_rows.reshape(CORES, VROWS, D),
        grad_own,
        proj_own,
        bias_own[:, None],
        mat_momentum[0],
        text_ids,
        text_mask,
        grad_outgoing,
    )
    vec_grad = vec_sum.reshape(-1)[: vec_master.shape[0]]
    grad_block, momentum_block, weight_block, ema_block = finish(
        main_sum, proj_sum, rows, mat_momentum, mat_master, mat_ema
    )
    piece_grad = add_piece_grads(asked_rows.reshape(1, -1), grad_incoming, group_rows)
    return (
        text_embeds,
        piece_grad,
        grad_block,
        momentum_block,
        weight_block,
        ema_block,
    ) + adam(vec_grad, vec_master, vec_moment1, vec_moment2, vec_ema)


def solution(mesh):
    in_specs = (
        P(("wide", "narrow"), None),
        P(("wide", "narrow"), None),
        P(("wide", "narrow"), None),
        P(),
        P(),
        P(("wide", "narrow"), None),
        P("narrow", None, None),
        P("narrow", None, None),
        P("narrow", None, None),
        P(),
        P(),
        P(),
        P(),
    )
    out_specs = (
        P(("wide", "narrow"), None),
        P(("wide", "narrow"), None),
        P("narrow", None, None),
        P("narrow", None, None),
        P("narrow", None, None),
        P("narrow", None, None),
        P(),
        P(),
        P(),
        P(),
        P(),
    )
    fits = mesh.shape["wide"] == CHIPS * CORES and mesh.shape["narrow"] == PLANES
    step = on_device if fits else on_device_plain
    return jax.shard_map(
        step, mesh=mesh, in_specs=in_specs, out_specs=out_specs, check_vma=False
    )
```
